32 devices in a mesh: area: 16 (over z, x, core), snap: 2 (over y).
Axes of the slice: x: 2, y: 2, z: 4, core: 2. Of those that a mesh axis runs over, the one named last changes fastest.
Arguments:
- phasor_readings: float32 [64, 32768], P('snap', 'area')
- reading_error_spread: float32 [32768], P('area'), may hold values from 1 to 100
- starting_voltages: float32 [64, 32768], P('snap', 'area'), may hold values from -6 to 6
- derivative_pieces: bfloat16 [256, 4, 128, 128], P('area'), may hold values from -0.25 to 0.25
- derivative_tile_position: int32 [16, 16, 4], P('area'), may hold values from 0 to 23, as said below
- frontier_voltage_pieces: int32 [16, 2, 4], P('area'), may hold values from -1 to 15, as said below
- holder_line_order: int32 [16, 16, 256], P('area'), may hold values from -1 to 2047, as said below
- hub_line_order: int32 [16, 16, 256], P('area'), may hold values from -1 to 2047, as said below
- reciprocal_normal_operator: bfloat16 [32768, 2048], P(('area', 'snap'))
Outputs:
- state: float32 [64, 32768], P('snap', 'area')
The draws below stay inside these ranges and needn't reach their ends.
Inputs may be any that keep to these rules, and one draw needn't show every extreme that they name: holder_line_order[d, c] lists the owner rows of area d that concentrator c handles, at most 256 of them, then -1; every owner row appears exactly once over all concentrators; some pair holds exactly 256. hub_line_order[c, d] lists the rows of concentrator c matching holder_line_order[d, c] entry by entry, with -1 at the same places; every concentrator row appears exactly once. `derivative_tile_position`: the 4 slots of one measurement block are distinct. frontier_voltage_pieces[a, 0] lists distinct blocks sent to area a - 1 and frontier_voltage_pieces[a, 1] those sent to area a + 1, 1 to 4 of them then -1; the list of area 0 toward lower and of the last area toward upper are all -1; some list holds 4.
All inputs are finite; a program needn't handle non-finite values.
Results may differ from the reference program's by a relative error of at most 0.0022.
Values may be sent and summed in bfloat16 or wider, within the bound.
No kernel may reach another device: no remote copies, remote signals or barrier semaphores. Data moves between devices by JAX's collectives and lax.ppermute only.
A program may use at most 64 MiB of HBM per device.

```python
import math
import jax
import jax.numpy as jnp
from jax import lax

NS = 2048
BLK = 128
MEASURE_BLOCKS = 16
TOUCHED_BLOCKS = 4
TIES = 4
ITERS = 2
NB = 16
SLOT_COUNT = 24
READING_LINES = 2048
CONTROL_AREAS = 16
SNAPS = 64
CAP = 256


def route_tables(key):
    base = jax.random.fold_in(key, 11)
    key_pair, key_order, key_cycle, key_owner, key_conc = jax.random.split(base, 5)
    half = CAP // 2
    paired = jax.random.randint(key_pair, (CONTROL_AREAS // 2,), 0, half + 1).at[0].set(half)
    amounts = jnp.stack([half + paired, half - paired], axis=1).reshape(CONTROL_AREAS)
    amounts = amounts[jax.random.permutation(key_order, CONTROL_AREAS)]
    cycle = jax.random.permutation(key_cycle, CONTROL_AREAS)
    counts = amounts[(cycle[None, :] - cycle[:, None]) % CONTROL_AREAS]
    places = jnp.arange(CAP)
    owner_perm = jax.vmap(lambda subset_key: jax.random.permutation(subset_key, READING_LINES))(jax.random.split(key_owner, CONTROL_AREAS))
    conc_perm = jax.vmap(lambda subset_key: jax.random.permutation(subset_key, READING_LINES))(jax.random.split(key_conc, CONTROL_AREAS))
    owner_start = jnp.cumsum(counts, axis=0) - counts
    conc_start = jnp.cumsum(counts, axis=1) - counts
    owner_pos = jnp.clip(owner_start.T[:, :, None] + places[None, None, :], 0, READING_LINES - 1)
    conc_pos = jnp.clip(conc_start[:, :, None] + places[None, None, :], 0, READING_LINES - 1)
    owner_rows = jax.vmap(lambda perm, where_at: perm[where_at])(owner_perm, owner_pos)
    conc_rows = jax.vmap(lambda perm, where_at: perm[where_at])(conc_perm, conc_pos)
    owner_table = jnp.where(places[None, None, :] < counts.T[:, :, None], owner_rows, -1)
    conc_table = jnp.where(places[None, None, :] < counts[:, :, None], conc_rows, -1)
    return (owner_table.astype(jnp.int32), conc_table.astype(jnp.int32))


def draw_holder_line_order(key, part):
    return route_tables(key)[0]


def draw_hub_line_order(key, part):
    return route_tables(key)[1]


def draw_frontier_voltage_pieces(key, part):
    key_perm, key_count, key_full = jax.random.split(jax.random.fold_in(key, 23), 3)
    permutation_list = jax.vmap(lambda subset_key: jax.random.permutation(subset_key, NB))(jax.random.split(key_perm, CONTROL_AREAS * 2))
    permutation_list = permutation_list[:, :TIES].reshape(CONTROL_AREAS, 2, TIES)
    counts = jax.random.randint(key_count, (CONTROL_AREAS, 2), 1, TIES + 1)
    full_area = jax.random.randint(key_full, (), 1, CONTROL_AREAS - 1)
    counts = counts.at[full_area, 0].set(TIES)
    counts = counts.at[0, 0].set(0).at[CONTROL_AREAS - 1, 1].set(0)
    live = jnp.arange(TIES)[None, None, :] < counts[:, :, None]
    return jnp.where(live, permutation_list, -1).astype(jnp.int32)


def draw_derivative_tile_position(key, part):
    split_keys = jax.random.split(jax.random.fold_in(key, 31), CONTROL_AREAS * MEASURE_BLOCKS)
    permutation_list = jax.vmap(lambda subset_key: jax.random.permutation(subset_key, SLOT_COUNT))(split_keys)[:, :TOUCHED_BLOCKS]
    return permutation_list.reshape(CONTROL_AREAS, MEASURE_BLOCKS, TOUCHED_BLOCKS).astype(jnp.int32)


def draw_reciprocal_normal_operator(key, part):
    key_noise, key_diag = jax.random.split(jax.random.fold_in(key, 41))
    total_rows = CONTROL_AREAS * NS
    noise = jax.random.normal(key_noise, (total_rows, NS), jnp.float32)
    diagonal = jax.random.uniform(key_diag, (total_rows, 1), jnp.float32, 2.0, 6.0)
    position = (jnp.arange(total_rows) % NS)[:, None]
    matrix = noise * (2.5 / math.sqrt(NS)) + jnp.where(position == jnp.arange(NS)[None, :], diagonal, 0.0)
    return matrix.astype(jnp.bfloat16)


def draw_phasor_readings(key, part):
    key_base, key_row, key_col = jax.random.split(jax.random.fold_in(key, 53), 3)
    columns = CONTROL_AREAS * READING_LINES
    row_scale = jnp.exp(jax.random.uniform(key_row, (1, columns), jnp.float32, math.log(0.5), math.log(5.0)))
    ramp = jnp.arange(SNAPS, dtype=jnp.float32) / max(SNAPS - 1, 1)
    jitter = jax.random.uniform(key_col, (SNAPS, 1), jnp.float32, 0.8, 1.25)
    col_scale = jnp.exp(ramp * math.log(10.0))[:, None] * jitter
    base = jax.random.normal(key_base, (SNAPS, columns), jnp.float32)
    return base * row_scale * col_scale


def block_scale(rng, dims, cuts, least, high):
    loudness = 1.0
    for dim, shards_of in cuts:
        heights = jax.random.uniform(jax.random.fold_in(jax.random.fold_in(rng, 6), dim), (shards_of,), jnp.float32, least / len(cuts), high / len(cuts))
        loudness = loudness * jnp.repeat(jnp.exp(heights), dims[dim] // shards_of).reshape((-1,) + (1,) * (len(dims) - 1 - dim))
    return loudness


def normal_values(stream_key, dims, scale, reach, shards=(), kind=jnp.bfloat16):
    result = jax.random.normal(stream_key, dims, jnp.float32) * scale
    if len(shards) > 0:
        result = block_scale(stream_key, dims, shards, -0.22, 0.18) * result
    return jnp.clip(result, min=-reach, max=reach).astype(kind)


def setup_inputs(seed: int = 0) -> dict:
    key_of = jax.random.split(jax.random.key(seed), 10)
    return {
        "phasor_readings": draw_phasor_readings(jax.random.fold_in(key_of[9], 71), 0),
        "reading_error_spread": jnp.clip(jnp.exp(math.log(100.0) - 4.6051702 * jax.random.uniform(key_of[1], (CONTROL_AREAS * READING_LINES,), jnp.float32) ** block_scale(key_of[1], (CONTROL_AREAS * READING_LINES,), ((0, 16),), -0.2, 0.2)), 1.0, 100.0),
        "starting_voltages": normal_values(key_of[2], (SNAPS, CONTROL_AREAS * NS), 1.0, 6.0, ((0, 2), (1, 16)), jnp.float32),
        "derivative_pieces": normal_values(key_of[3], (CONTROL_AREAS * MEASURE_BLOCKS, TOUCHED_BLOCKS, BLK, BLK), (TOUCHED_BLOCKS * BLK) ** -0.5, 0.25, ((0, 16),)),
        "derivative_tile_position": draw_derivative_tile_position(jax.random.fold_in(key_of[9], 71), 0),
        "frontier_voltage_pieces": draw_frontier_voltage_pieces(jax.random.fold_in(key_of[9], 71), 0),
        "holder_line_order": draw_holder_line_order(jax.random.fold_in(key_of[9], 71), 0),
        "hub_line_order": draw_hub_line_order(jax.random.fold_in(key_of[9], 71), 0),
        "reciprocal_normal_operator": draw_reciprocal_normal_operator(jax.random.fold_in(key_of[9], 71), 0),
    }


HIGHEST_PRECISION = lax.Precision.HIGHEST


def take_blocks(blocks, listing):
    safe = jnp.maximum(listing, 0)
    taken = jax.vmap(lambda values, where_at: values[:, where_at])(blocks, safe)
    return jnp.where((listing >= 0)[:, None, :, None], taken, 0.0)


def put_blocks(values, listing):
    onehot_table = (listing[:, :, None] == jnp.arange(NB, dtype=jnp.int32)[None, None, :]).astype(jnp.float32)
    return jnp.einsum("astc,atb->asbc", values, onehot_table, precision=HIGHEST_PRECISION)


def reference(phasor_readings, reading_error_spread, starting_voltages, derivative_pieces, derivative_tile_position, frontier_voltage_pieces, holder_line_order, hub_line_order, reciprocal_normal_operator):
    region_sequence = holder_line_order.shape[0]
    capture_number = phasor_readings.shape[0]
    valid = holder_line_order >= 0
    owner_index = jnp.arange(region_sequence, dtype=jnp.int32)[:, None, None] * READING_LINES + holder_line_order
    conc_swap = jnp.transpose(hub_line_order, (1, 0, 2))
    conc_index = jnp.arange(region_sequence, dtype=jnp.int32)[None, :, None] * READING_LINES + conc_swap
    target = jnp.where(valid, owner_index, region_sequence * READING_LINES).reshape(-1).astype(jnp.int32)
    provider_lines = jnp.zeros((region_sequence * READING_LINES,), jnp.int32).at[target].set(conc_index.reshape(-1).astype(jnp.int32), mode="drop")
    observed_quantities = jnp.transpose(phasor_readings[:, provider_lines].reshape(capture_number, region_sequence, READING_LINES), (1, 0, 2))
    noise_variance = reading_error_spread[provider_lines].reshape(region_sequence, READING_LINES)
    tiles = derivative_pieces.reshape(region_sequence, MEASURE_BLOCKS, TOUCHED_BLOCKS, BLK, BLK)
    gains = reciprocal_normal_operator.reshape(region_sequence, NS, NS)
    current = jnp.transpose(starting_voltages.reshape(capture_number, region_sequence, NB, BLK), (1, 0, 2, 3))
    empty = jnp.zeros((1, capture_number, TIES, BLK), jnp.float32)
    slot_lookup = (derivative_tile_position.reshape(region_sequence, MEASURE_BLOCKS * TOUCHED_BLOCKS)[:, :, None] == jnp.arange(SLOT_COUNT, dtype=jnp.int32)[None, None, :]).astype(jnp.float32)

    def predict(inputs):
        tile, slot_column_index, augmented = inputs
        chosen = augmented[:, slot_column_index].astype(jnp.float32)
        return jnp.einsum("jkrc,sjkc->sjr", tile.astype(jnp.float32), chosen, precision=HIGHEST_PRECISION).reshape(capture_number, READING_LINES)

    def pull(inputs):
        tile, onehot_table, weighted = inputs
        tile_grad = jnp.einsum("jkrc,sjr->sjkc", tile.astype(jnp.float32), weighted.reshape(capture_number, MEASURE_BLOCKS, BLK).astype(jnp.float32), precision=HIGHEST_PRECISION)
        return jnp.einsum("sxc,xn->snc", tile_grad.reshape(capture_number, MEASURE_BLOCKS * TOUCHED_BLOCKS, BLK), onehot_table, precision=HIGHEST_PRECISION)

    def apply_gain(inputs):
        gradient, matrix = inputs
        return jnp.dot(gradient, matrix.T, preferred_element_type=jnp.float32)

    for step_index in range(ITERS):
        from_below = jnp.concatenate([empty, take_blocks(current, frontier_voltage_pieces[:, 1])[:-1]], axis=0)
        from_above = jnp.concatenate([take_blocks(current, frontier_voltage_pieces[:, 0])[1:], empty], axis=0)
        augmented = jnp.concatenate([current, from_below, from_above], axis=2).astype(jnp.bfloat16)
        predicted = lax.map(predict, (tiles, derivative_tile_position, augmented))
        residual_rows = observed_quantities - predicted
        spread = jnp.sum(residual_rows * residual_rows, axis=1) / capture_number
        weighted = (residual_rows / (noise_variance + spread)[:, None, :]).astype(jnp.bfloat16)
        slot_grad = lax.map(pull, (tiles, slot_lookup, weighted))
        below_slots = slot_grad[:, :, NB:NB + TIES]
        above_slots = slot_grad[:, :, NB + TIES:]
        back_upper = jnp.concatenate([below_slots[1:], empty], axis=0)
        back_lower = jnp.concatenate([empty, above_slots[:-1]], axis=0)
        gradient = slot_grad[:, :, :NB] + put_blocks(back_upper, frontier_voltage_pieces[:, 1]) + put_blocks(back_lower, frontier_voltage_pieces[:, 0])
        flat_grad = gradient.reshape(region_sequence, capture_number, NS).astype(jnp.bfloat16)
        update = lax.map(apply_gain, (flat_grad, gains))
        current = current + update.reshape(region_sequence, capture_number, NB, BLK)
    return jnp.transpose(current.reshape(region_sequence, capture_number, NS), (1, 0, 2)).reshape(capture_number, region_sequence * NS)
```

```python
import functools

import jax
import jax.numpy as jnp
from jax import lax
from jax.experimental import pallas as pl
from jax.experimental.pallas import tpu as pltpu
from jax.sharding import PartitionSpec as P

BLK = 128
ITERS = 2
F32 = jnp.float32
BF16 = jnp.bfloat16
NT = (((1,), (1,)), ((), ()))
VMEM = pl.BlockSpec(memory_space=pltpu.VMEM)
SMEM = pl.BlockSpec(memory_space=pltpu.SMEM)


def call(kernel, outs, ins, args, scratch=(), flops=0, bytes_accessed=0, name=None):
    return pl.pallas_call(
        kernel,
        out_shape=outs,
        in_specs=ins,
        out_specs=jax.tree.map(lambda _: VMEM, outs),
        scratch_shapes=list(scratch),
        compiler_params=pltpu.CompilerParams(vmem_limit_bytes=40 * 1024 * 1024),
        cost_estimate=pl.CostEstimate(
            flops=flops, bytes_accessed=bytes_accessed, transcendentals=0
        ),
        name=name,
    )(*args)


def lane_gather(values, lanes):
    return jnp.take_along_axis(values, lanes, axis=1, mode="promise_in_bounds")


def rows_iota(shape):
    return lax.broadcasted_iota(jnp.int32, shape, 0)


def pack_kernel(z_ref, v_ref, hub_ref, out_ref, slot_ref):
    snaps, lines = z_ref.shape
    blocks = lines // BLK
    chunks, width = hub_ref.shape
    groups = width // BLK
    for d in range(chunks):
        for g in range(groups):
            slot_ref[d, g : g + 1] = hub_ref[d : d + 1, g * BLK : (g + 1) * BLK]

    def chunk(d, carry):
        tail = jnp.zeros((16, BLK), F32)
        for g in range(groups):
            slot = slot_ref[d, g : g + 1]
            high = jnp.right_shift(slot, 7)
            low = jnp.bitwise_and(slot, 127)
            lanes = jnp.broadcast_to(low, (snaps, BLK))
            block_of = jnp.broadcast_to(high, (snaps, BLK))
            picked = jnp.zeros((snaps, BLK), F32)
            for b in range(blocks):
                found = lane_gather(z_ref[:, b * BLK : (b + 1) * BLK], lanes)
                picked = jnp.where(block_of == b, found, picked)
            out_ref[d, g * snaps : (g + 1) * snaps, :] = picked.astype(BF16)
            found = lane_gather(v_ref[...], jnp.broadcast_to(low, (blocks, BLK)))
            mine = rows_iota((blocks, BLK)) == high
            variance = jnp.sum(jnp.where(mine, found, 0.0), axis=0, keepdims=True)
            upper = variance.astype(BF16).astype(F32)
            row = rows_iota((16, BLK))
            tail = jnp.where(row == 2 * g, upper, tail)
            tail = jnp.where(row == 2 * g + 1, variance - upper, tail)
        out_ref[d, groups * snaps :, :] = tail.astype(BF16)
        return carry

    lax.fori_loop(0, chunks, chunk, 0)


def inverse_kernel(own_ref, group_ref, lane_ref):
    chunks, width = own_ref.shape
    blocks = group_ref.shape[0]
    groups = width // BLK
    total = jnp.zeros((2 * blocks, BLK), F32)
    lane = lax.broadcasted_iota(jnp.int32, (2 * blocks, width), 1)
    row = rows_iota((2 * blocks, width))
    in_group = jnp.bitwise_and(lane, 127)
    group_in = jnp.right_shift(lane, 7)
    for d in range(chunks):
        owned = own_ref[d : d + 1, :]
        high = jnp.right_shift(owned, 7)
        low = jnp.bitwise_and(owned, 127)
        label = jnp.where(row < blocks, group_in + d * groups, in_group)
        hit = jnp.bitwise_and(row, blocks - 1) == high
        left = jnp.where(hit, label.astype(F32), 0.0).astype(BF16)
        right = jnp.where(rows_iota((BLK, width)) == low, 1.0, 0.0).astype(BF16)
        total += lax.dot_general(left, right, NT, preferred_element_type=F32)
    group_ref[...] = total[:blocks].astype(jnp.int32)
    lane_ref[...] = total[blocks:].astype(jnp.int32)


def unpack_kernel(message_ref, group_ref, lane_ref, z_ref, v_ref, wide_ref, upper_ref):
    chunks = message_ref.shape[0]
    snaps, lines = z_ref.shape
    blocks = lines // BLK
    groups = (message_ref.shape[1] - 16) // snaps
    for d in range(chunks):
        tail = message_ref[d, groups * snaps :, :].astype(F32)
        for g in range(groups):
            at = d * groups + g
            wide_ref[at] = message_ref[d, g * snaps : (g + 1) * snaps, :].astype(F32)
            upper_ref[at : at + 1, :] = tail[2 * g : 2 * g + 1] + tail[2 * g + 1 : 2 * g + 2]
    total = chunks * groups

    def block(b, carry):
        group = group_ref[pl.ds(b, 1), :]
        lane = lane_ref[pl.ds(b, 1), :]
        lanes = jnp.broadcast_to(lane, (snaps, BLK))
        group_of = jnp.broadcast_to(group, (snaps, BLK))
        picked = jnp.zeros((snaps, BLK), F32)
        for g in range(total):
            picked = jnp.where(group_of == g, lane_gather(wide_ref[g], lanes), picked)
        columns = pl.ds(pl.multiple_of(b * BLK, BLK), BLK)
        z_ref[:, columns] = picked.astype(BF16)
        found = lane_gather(upper_ref[...], jnp.broadcast_to(lane, (total, BLK)))
        mine = rows_iota((total, BLK)) == group
        v_ref[:, columns] = jnp.sum(jnp.where(mine, found, 0.0), axis=0, keepdims=True)
        return carry

    lax.fori_loop(0, blocks, block, 0)


def pick(source, listing_ref, side, out_ref):
    for t in range(out_ref.shape[0]):
        b = listing_ref[side, t]
        block = source(jnp.maximum(b, 0))
        out_ref[t] = jnp.where(b >= 0, block, jnp.zeros_like(block))


def first_states_kernel(own_ref, others_ref, ties_ref, aug_ref, lower_ref, upper_ref):
    snaps = own_ref.shape[0]
    for b in range(aug_ref.shape[0]):
        columns = slice(b * BLK, (b + 1) * BLK)
        aug_ref[b, :snaps] = own_ref[:, columns].astype(BF16)
        for i in range(others_ref.shape[0]):
            aug_ref[b, (i + 1) * snaps : (i + 2) * snaps] = others_ref[i, :, columns].astype(BF16)
    pick(lambda b: aug_ref[b], ties_ref, 0, lower_ref)
    pick(lambda b: aug_ref[b], ties_ref, 1, upper_ref)


def join_states_kernel(mine_ref, others_ref, ties_ref, aug_ref, lower_ref, upper_ref):
    held, everything = mine_ref.shape[:2]
    members = others_ref.shape[0] + 1
    snaps = everything // members
    me = lax.axis_index("snap")
    aug_ref[pl.ds(me * held, held)] = mine_ref[...]
    for i in range(1, members):
        at = lax.rem(me + members - i, members) * held
        for j in range(members):
            to = (j - i) % members
            aug_ref[pl.ds(at, held), to * snaps : (to + 1) * snaps] = others_ref[
                i - 1, :, j * snaps : (j + 1) * snaps
            ]
    pick(lambda b: aug_ref[b], ties_ref, 0, lower_ref)
    pick(lambda b: aug_ref[b], ties_ref, 1, upper_ref)


def slots_into(slots_ref, aug_ref, below_ref, above_ref):
    own = aug_ref.shape[0]
    ties = below_ref.shape[0]
    slots_ref[:own] = aug_ref[...]
    slots_ref[own : own + ties] = below_ref[...]
    slots_ref[own + ties :] = above_ref[...]


def predicted(j, slots_ref, tiles_ref, place_ref):
    touched = tiles_ref.shape[1]
    chosen = jnp.concatenate([slots_ref[place_ref[j, k]] for k in range(touched)], axis=1)
    weights = jnp.concatenate([tiles_ref[j, k] for k in range(touched)], axis=1)
    return lax.dot_general(chosen, weights, NT, preferred_element_type=F32)


def predict_kernel(aug_ref, below_ref, above_ref, tiles_ref, place_ref, out_ref, slots_ref):
    slots_into(slots_ref, aug_ref, below_ref, above_ref)
    for j in range(tiles_ref.shape[0]):
        out_ref[:, j * BLK : (j + 1) * BLK] = predicted(j, slots_ref, tiles_ref, place_ref)


def pull(j, guess, z_ref, others_ref, v_ref, tiles_ref, place_ref, total_ref):
    columns = slice(j * BLK, (j + 1) * BLK)
    readings = [z_ref[:, columns]] + [o[:, columns] for o in split(others_ref)]
    resid = jnp.concatenate(readings, axis=0).astype(F32) - guess
    spread = jnp.sum(resid * resid, axis=0, keepdims=True) / resid.shape[0]
    weighted = (resid / (v_ref[:, columns] + spread)).astype(BF16)
    touched = tiles_ref.shape[1]
    weights = jnp.concatenate([tiles_ref[j, k] for k in range(touched)], axis=1)
    part = jnp.dot(weighted, weights, preferred_element_type=F32)
    for k in range(touched):
        n = place_ref[j, k]
        total_ref[n] += part[:, k * BLK : (k + 1) * BLK]


def split(ref):
    return [ref.at[i] for i in range(ref.shape[0])]


def give(total_ref, own_ref, below_ref, above_ref):
    own = own_ref.shape[0]
    ties = below_ref.shape[0]
    own_ref[...] = total_ref[:own]
    below_ref[...] = total_ref[own : own + ties]
    above_ref[...] = total_ref[own + ties :]


def pull_kernel(
    guess_ref, z_ref, others_ref, v_ref, tiles_ref, place_ref, own_ref, below_ref, above_ref, total_ref
):
    total_ref[...] = jnp.zeros_like(total_ref)
    for j in range(tiles_ref.shape[0]):
        guess = guess_ref[:, j * BLK : (j + 1) * BLK]
        pull(j, guess, z_ref, others_ref, v_ref, tiles_ref, place_ref, total_ref)
    give(total_ref, own_ref, below_ref, above_ref)


def predict_pull_kernel(
    aug_ref, below_in_ref, above_in_ref, z_ref, others_ref, v_ref, tiles_ref, place_ref,
    own_ref, below_ref, above_ref, slots_ref, total_ref,
):
    slots_into(slots_ref, aug_ref, below_in_ref, above_in_ref)
    total_ref[...] = jnp.zeros_like(total_ref)
    for j in range(tiles_ref.shape[0]):
        guess = predicted(j, slots_ref, tiles_ref, place_ref)
        pull(j, guess, z_ref, others_ref, v_ref, tiles_ref, place_ref, total_ref)
    give(total_ref, own_ref, below_ref, above_ref)


def full_gradient(grad_ref, back_upper_ref, back_lower_ref, ties_ref, work_ref):
    work_ref[...] = grad_ref[...]
    for side, back_ref in ((1, back_upper_ref), (0, back_lower_ref)):
        for t in range(back_ref.shape[0]):
            b = ties_ref[side, t]

            @pl.when(b >= 0)
            def _(b=b, t=t, back_ref=back_ref):
                work_ref[b] += back_ref[t]

    return jnp.concatenate([work_ref[b].astype(BF16) for b in range(work_ref.shape[0])], axis=1)


def first_update_kernel(
    grad_ref, back_upper_ref, back_lower_ref, ties_ref, gain_ref, x_ref, x_others_ref,
    state_ref, message_ref, work_ref,
):
    gradient = full_gradient(grad_ref, back_upper_ref, back_lower_ref, ties_ref, work_ref)
    held = state_ref.shape[0]
    me = lax.axis_index("snap")
    for i in range(held):
        rows = gain_ref[i * BLK : (i + 1) * BLK, :]
        update = lax.dot_general(gradient, rows, NT, preferred_element_type=F32)
        columns = pl.ds(pl.multiple_of((me * held + i) * BLK, BLK), BLK)
        parts = [x_ref[:, columns]] + [o[:, columns] for o in split(x_others_ref)]
        state = jnp.concatenate(parts, axis=0) + update
        state_ref[i] = state
        message_ref[i] = state.astype(BF16)


def last_update_kernel(
    grad_ref, back_upper_ref, back_lower_ref, ties_ref, gain_ref, state_ref, mine_ref, send_ref, work_ref
):
    gradient = full_gradient(grad_ref, back_upper_ref, back_lower_ref, ties_ref, work_ref)
    snaps = mine_ref.shape[0]
    for i in range(state_ref.shape[0]):
        rows = gain_ref[i * BLK : (i + 1) * BLK, :]
        update = lax.dot_general(gradient, rows, NT, preferred_element_type=F32)
        state = state_ref[i] + update
        columns = slice(i * BLK, (i + 1) * BLK)
        mine_ref[:, columns] = state[:snaps]
        for j in range(send_ref.shape[0]):
            send_ref[j, :, columns] = state[(j + 1) * snaps : (j + 2) * snaps]


def finish_kernel(mine_ref, others_ref, out_ref):
    width = mine_ref.shape[1]
    members = others_ref.shape[0] + 1
    me = lax.axis_index("snap")
    out_ref[:, pl.ds(pl.multiple_of(me * width, BLK), width)] = mine_ref[...]
    for i in range(1, members):
        at = lax.rem(me + members - i, members) * width
        out_ref[:, pl.ds(pl.multiple_of(at, BLK), width)] = others_ref[i - 1]


def along_area(block, distance):
    areas = range(lax.axis_size("area"))
    route = [(i - distance, i) for i in areas if i - distance in areas]
    return lax.ppermute(block, "area", route)


def from_snap(block, distance):
    members = lax.axis_size("snap")
    return lax.ppermute(block, "snap", [(i, (i + distance) % members) for i in range(members)])


def from_all(block):
    return jnp.stack([from_snap(block, i) for i in range(1, lax.axis_size("snap"))])


def shape(dims, kind):
    return jax.ShapeDtypeStruct(dims, kind)


def on_device(
    phasor_readings,
    reading_error_spread,
    starting_voltages,
    derivative_pieces,
    derivative_tile_position,
    frontier_voltage_pieces,
    holder_line_order,
    hub_line_order,
    reciprocal_normal_operator,
):
    snaps, lines = phasor_readings.shape
    states = starting_voltages.shape[1]
    own = states // BLK
    measure = derivative_pieces.shape[0]
    ties_table = frontier_voltage_pieces[0]
    ties = ties_table.shape[1]
    slots = own + 2 * ties
    members = lax.axis_size("snap")
    areas = lax.axis_size("area")
    everything = snaps * members
    held = reciprocal_normal_operator.shape[0] // BLK
    place = derivative_tile_position[0]
    cap = hub_line_order.shape[2]
    width = max(cap, BLK)
    chunks = areas * cap // width
    hub = hub_line_order[0].reshape(chunks, width)
    holder = holder_line_order[0].reshape(chunks, width)
    depth = (width // BLK) * snaps + 16

    message = call(
        pack_kernel,
        shape((chunks, depth, BLK), BF16),
        [VMEM, VMEM, VMEM],
        (phasor_readings, reading_error_spread.reshape(lines // BLK, BLK), hub),
        scratch=[pltpu.VMEM((chunks, width // BLK, BLK), jnp.int32)],
        name="pack_readings",
    )
    if cap < BLK:
        each = BLK // cap
        message = message.reshape(chunks, depth, each, cap).transpose(0, 2, 1, 3)
        message = message.reshape(areas, depth, cap)
    message = lax.all_to_all(message, "area", split_axis=0, concat_axis=0, tiled=True)
    if cap < BLK:
        message = message.reshape(chunks, each, depth, cap).transpose(0, 2, 1, 3)
        message = message.reshape(chunks, depth, BLK)

    group, lane = call(
        inverse_kernel,
        (shape((lines // BLK, BLK), jnp.int32),) * 2,
        [VMEM],
        (holder,),
        flops=10**9,
        name="invert_order",
    )
    x_others = from_all(starting_voltages)
    aug, to_lower, to_upper = call(
        first_states_kernel,
        (
            shape((own, everything, BLK), BF16),
            shape((ties, everything, BLK), BF16),
            shape((ties, everything, BLK), BF16),
        ),
        [VMEM, VMEM, SMEM],
        (starting_voltages, x_others, ties_table),
        name="first_states",
    )
    below = along_area(to_upper, 1)
    above = along_area(to_lower, -1)
    guess = call(
        predict_kernel,
        shape((everything, lines), F32),
        [VMEM, VMEM, VMEM, VMEM, SMEM],
        (aug, below, above, derivative_pieces, place),
        scratch=[pltpu.VMEM((slots, everything, BLK), BF16)],
        flops=10**9,
        name="predict",
    )
    readings, variance = call(
        unpack_kernel,
        (shape((snaps, lines), BF16), shape((1, lines), F32)),
        [VMEM, VMEM, VMEM],
        (message, group, lane),
        scratch=[
            pltpu.VMEM((chunks * (width // BLK), snaps, BLK), F32),
            pltpu.VMEM((chunks * (width // BLK), BLK), F32),
        ],
        name="unpack_readings",
    )
    reading_others = from_all(readings)
    grads = (
        shape((own, everything, BLK), F32),
        shape((ties, everything, BLK), F32),
        shape((ties, everything, BLK), F32),
    )
    total = pltpu.VMEM((slots, everything, BLK), F32)
    work = pltpu.VMEM((own, everything, BLK), F32)
    grad, grad_below, grad_above = call(
        pull_kernel,
        grads,
        [VMEM, VMEM, VMEM, VMEM, VMEM, SMEM],
        (guess, readings, reading_others, variance, derivative_pieces, place),
        scratch=[total],
        name="pull",
    )
    back_upper = along_area(grad_below, -1)
    back_lower = along_area(grad_above, 1)
    state, mine = call(
        first_update_kernel,
        (shape((held, everything, BLK), F32), shape((held, everything, BLK), BF16)),
        [VMEM, VMEM, VMEM, SMEM, VMEM, VMEM, VMEM],
        (
            grad, back_upper, back_lower, ties_table, reciprocal_normal_operator,
            starting_voltages, x_others,
        ),
        scratch=[work],
        name="first_update",
    )
    others = from_all(mine)
    aug, to_lower, to_upper = call(
        join_states_kernel,
        (
            shape((own, everything, BLK), BF16),
            shape((ties, everything, BLK), BF16),
            shape((ties, everything, BLK), BF16),
        ),
        [VMEM, VMEM, SMEM],
        (mine, others, ties_table),
        name="join_states",
    )
    below = along_area(to_upper, 1)
    above = along_area(to_lower, -1)
    grad, grad_below, grad_above = call(
        predict_pull_kernel,
        grads,
        [VMEM, VMEM, VMEM, VMEM, VMEM, VMEM, VMEM, SMEM],
        (aug, below, above, readings, reading_others, variance, derivative_pieces, place),
        scratch=[pltpu.VMEM((slots, everything, BLK), BF16), total],
        name="predict_pull",
    )
    back_upper = along_area(grad_below, -1)
    back_lower = along_area(grad_above, 1)
    kept, sent = call(
        last_update_kernel,
        (shape((snaps, held * BLK), F32), shape((members - 1, snaps, held * BLK), F32)),
        [VMEM, VMEM, VMEM, SMEM, VMEM, VMEM],
        (grad, back_upper, back_lower, ties_table, reciprocal_normal_operator, state),
        scratch=[work],
        name="last_update",
    )
    arrived = jnp.stack([from_snap(sent[i - 1], i) for i in range(1, members)])
    return call(
        finish_kernel,
        shape((snaps, states), F32),
        [VMEM, VMEM],
        (kept, arrived),
        name="finish",
    )


def solution(mesh):
    placed = (
        P("snap", "area"),
        P("area"),
        P("snap", "area"),
        P("area", None, None, None),
        P("area", None, None),
        P("area", None, None),
        P("area", None, None),
        P("area", None, None),
        P(("area", "snap"), None),
    )
    return jax.shard_map(
        on_device, mesh=mesh, in_specs=placed, out_specs=P("snap", "area"), check_vma=False
    )
```

```python
import functools

import jax
import jax.numpy as jnp
from jax import lax
from jax.experimental import pallas as pl
from jax.experimental.pallas import tpu as pltpu
from jax.sharding import PartitionSpec as P

BLK = 128
ITERS = 2
F32 = jnp.float32
BF16 = jnp.bfloat16
NT = (((1,), (1,)), ((), ()))
VMEM = pl.BlockSpec(memory_space=pltpu.VMEM)
SMEM = pl.BlockSpec(memory_space=pltpu.SMEM)


def call(kernel, outs, ins, args, scratch=(), flops=0, bytes_accessed=0, name=None):
    return pl.pallas_call(
        kernel,
        out_shape=outs,
        in_specs=ins,
        out_specs=jax.tree.map(lambda _: VMEM, outs),
        scratch_shapes=list(scratch),
        compiler_params=pltpu.CompilerParams(vmem_limit_bytes=40 * 1024 * 1024),
        cost_estimate=pl.CostEstimate(
            flops=flops, bytes_accessed=bytes_accessed, transcendentals=0
        ),
        name=name,
    )(*args)


def lane_gather(values, lanes):
    return jnp.take_along_axis(values, lanes, axis=1, mode="promise_in_bounds")


def rows_iota(shape):
    return lax.broadcasted_iota(jnp.int32, shape, 0)


def pack_kernel(z_ref, v_ref, hub_ref, out_ref, slot_ref):
    snaps, lines = z_ref.shape
    blocks = lines // BLK
    chunks, width = hub_ref.shape
    groups = width // BLK
    for d in range(chunks):
        for g in range(groups):
            slot_ref[d, g : g + 1] = hub_ref[d : d + 1, g * BLK : (g + 1) * BLK]

    def chunk(d, carry):
        tail = jnp.zeros((8, BLK), F32)
        for g in range(groups):
            slot = slot_ref[d, g : g + 1]
            high = jnp.right_shift(slot, 7)
            low = jnp.bitwise_and(slot, 127)
            lanes = jnp.broadcast_to(low, (snaps, BLK))
            block_of = jnp.broadcast_to(high, (snaps, BLK))
            picked = jnp.zeros((snaps, BLK), F32)
            for b in range(blocks):
                found = lane_gather(z_ref[:, b * BLK : (b + 1) * BLK], lanes)
                picked = jnp.where(block_of == b, found, picked)
            out_ref[d, g * snaps : (g + 1) * snaps, :] = picked
            found = lane_gather(v_ref[...], jnp.broadcast_to(low, (blocks, BLK)))
            mine = rows_iota((blocks, BLK)) == high
            variance = jnp.sum(jnp.where(mine, found, 0.0), axis=0, keepdims=True)
            tail = jnp.where(rows_iota((8, BLK)) == g, variance, tail)
        out_ref[d, groups * snaps :, :] = tail
        return carry

    lax.fori_loop(0, chunks, chunk, 0)


def inverse_kernel(own_ref, group_ref, lane_ref):
    chunks, width = own_ref.shape
    blocks = group_ref.shape[0]
    groups = width // BLK
    total = jnp.zeros((2 * blocks, BLK), F32)
    lane = lax.broadcasted_iota(jnp.int32, (2 * blocks, width), 1)
    row = rows_iota((2 * blocks, width))
    in_group = jnp.bitwise_and(lane, 127)
    group_in = jnp.right_shift(lane, 7)
    for d in range(chunks):
        owned = own_ref[d : d + 1, :]
        high = jnp.right_shift(owned, 7)
        low = jnp.bitwise_and(owned, 127)
        label = jnp.where(row < blocks, group_in + d * groups, in_group)
        hit = jnp.bitwise_and(row, blocks - 1) == high
        left = jnp.where(hit, label.astype(F32), 0.0).astype(BF16)
        right = jnp.where(rows_iota((BLK, width)) == low, 1.0, 0.0).astype(BF16)
        total += lax.dot_general(left, right, NT, preferred_element_type=F32)
    group_ref[...] = total[:blocks].astype(jnp.int32)
    lane_ref[...] = total[blocks:].astype(jnp.int32)


def unpack_kernel(message_ref, group_ref, lane_ref, z_ref, v_ref, variance_ref):
    chunks = message_ref.shape[0]
    snaps, lines = z_ref.shape
    blocks = lines // BLK
    groups = (message_ref.shape[1] - 8) // snaps
    for d in range(chunks):
        tail = message_ref[d, groups * snaps :, :]
        variance_ref[d * groups : (d + 1) * groups, :] = tail[:groups]
    total = chunks * groups

    def block(b, carry):
        group = group_ref[pl.ds(b, 1), :]
        lane = lane_ref[pl.ds(b, 1), :]
        lanes = jnp.broadcast_to(lane, (snaps, BLK))
        group_of = jnp.broadcast_to(group, (snaps, BLK))
        picked = jnp.zeros((snaps, BLK), F32)
        for g in range(total):
            rows = slice(g % groups * snaps, (g % groups + 1) * snaps)
            found = lane_gather(message_ref[g // groups, rows, :], lanes)
            picked = jnp.where(group_of == g, found, picked)
        columns = pl.ds(pl.multiple_of(b * BLK, BLK), BLK)
        z_ref[:, columns] = picked
        found = lane_gather(variance_ref[...], jnp.broadcast_to(lane, (total, BLK)))
        mine = rows_iota((total, BLK)) == group
        v_ref[:, columns] = jnp.sum(jnp.where(mine, found, 0.0), axis=0, keepdims=True)
        return carry

    lax.fori_loop(0, blocks, block, 0)


def split(ref):
    return [ref.at[i] for i in range(ref.shape[0])]


def parity():
    return lax.rem(lax.axis_index("area"), 2)


def pick(source, listing_ref, side, out_ref):
    for t in range(out_ref.shape[0]):
        b = listing_ref[side, t]
        block = source(jnp.maximum(b, 0))
        out_ref[t] = jnp.where(b >= 0, block, jnp.zeros_like(block))


def first_states_kernel(own_ref, others_ref, ties_ref, aug_ref, first_ref, second_ref):
    snaps = own_ref.shape[0]
    for b in range(aug_ref.shape[0]):
        columns = slice(b * BLK, (b + 1) * BLK)
        aug_ref[b, :snaps] = own_ref[:, columns].astype(BF16)
        for i in range(others_ref.shape[0]):
            aug_ref[b, (i + 1) * snaps : (i + 2) * snaps] = others_ref[i, :, columns].astype(BF16)
    pick(lambda b: aug_ref[b], ties_ref, 1 - parity(), first_ref)
    pick(lambda b: aug_ref[b], ties_ref, parity(), second_ref)


def join_states_kernel(mine_ref, others_ref, ties_ref, aug_ref, first_ref, second_ref):
    held, everything = mine_ref.shape[:2]
    members = others_ref.shape[0] + 1
    snaps = everything // members
    me = lax.axis_index("snap")
    aug_ref[pl.ds(me * held, held)] = mine_ref[...]
    for i in range(1, members):
        at = lax.rem(me + members - i, members) * held
        for j in range(members):
            to = (j - i) % members
            aug_ref[pl.ds(at, held), to * snaps : (to + 1) * snaps] = others_ref[
                i - 1, :, j * snaps : (j + 1) * snaps
            ]
    pick(lambda b: aug_ref[b], ties_ref, 1 - parity(), first_ref)
    pick(lambda b: aug_ref[b], ties_ref, parity(), second_ref)


def slots_into(slots_ref, aug_ref, first_ref, second_ref):
    own = aug_ref.shape[0]
    ties = first_ref.shape[0]
    slots_ref[:own] = aug_ref[...]
    slots_ref[pl.ds(own + ties * (1 - parity()), ties)] = first_ref[...]
    slots_ref[pl.ds(own + ties * parity(), ties)] = second_ref[...]


def predicted(j, slots_ref, tiles_ref, place_ref):
    touched = tiles_ref.shape[1]
    chosen = jnp.concatenate([slots_ref[place_ref[j, k]] for k in range(touched)], axis=1)
    weights = jnp.concatenate([tiles_ref[j, k] for k in range(touched)], axis=1)
    return lax.dot_general(chosen, weights, NT, preferred_element_type=F32)


def predict_kernel(aug_ref, first_ref, second_ref, tiles_ref, place_ref, out_ref, slots_ref):
    slots_into(slots_ref, aug_ref, first_ref, second_ref)
    for j in range(tiles_ref.shape[0]):
        out_ref[:, j * BLK : (j + 1) * BLK] = predicted(j, slots_ref, tiles_ref, place_ref)


def weigh(j, guess, z_ref, others_ref, v_ref):
    columns = slice(j * BLK, (j + 1) * BLK)
    readings = [z_ref[:, columns]] + [o[:, columns] for o in split(others_ref)]
    resid = jnp.concatenate(readings, axis=0) - guess
    spread = jnp.sum(resid * resid, axis=0, keepdims=True) / resid.shape[0]
    return (resid / (v_ref[:, columns] + spread)).astype(BF16)


def pull(weighted_ref, tiles_ref, place_ref, total_ref, own_ref, first_ref, second_ref):
    total_ref[...] = jnp.zeros_like(total_ref)
    touched = tiles_ref.shape[1]
    for j in range(tiles_ref.shape[0]):
        weighted = weighted_ref[:, j * BLK : (j + 1) * BLK]
        weights = jnp.concatenate([tiles_ref[j, k] for k in range(touched)], axis=1)
        part = jnp.dot(weighted, weights, preferred_element_type=F32)
        for k in range(touched):
            n = place_ref[j, k]
            total_ref[n] += part[:, k * BLK : (k + 1) * BLK]
    own = own_ref.shape[0]
    ties = first_ref.shape[0]
    own_ref[...] = total_ref[:own]
    first_ref[...] = total_ref[pl.ds(own + ties * (1 - parity()), ties)]
    second_ref[...] = total_ref[pl.ds(own + ties * parity(), ties)]


def pull_kernel(
    guess_ref, z_ref, others_ref, v_ref, tiles_ref, place_ref, own_ref, first_ref, second_ref,
    total_ref, weighted_ref,
):
    for j in range(tiles_ref.shape[0]):
        columns = slice(j * BLK, (j + 1) * BLK)
        weighted_ref[:, columns] = weigh(j, guess_ref[:, columns], z_ref, others_ref, v_ref)
    pull(weighted_ref, tiles_ref, place_ref, total_ref, own_ref, first_ref, second_ref)


def predict_pull_kernel(
    aug_ref, first_in_ref, second_in_ref, z_ref, others_ref, v_ref, tiles_ref, place_ref,
    own_ref, first_ref, second_ref, slots_ref, guess_ref, total_ref, weighted_ref,
):
    predict_kernel(aug_ref, first_in_ref, second_in_ref, tiles_ref, place_ref, guess_ref, slots_ref)
    pull_kernel(
        guess_ref, z_ref, others_ref, v_ref, tiles_ref, place_ref, own_ref, first_ref, second_ref,
        total_ref, weighted_ref,
    )


def full_gradient(grad_ref, back_first_ref, back_second_ref, ties_ref, work_ref):
    work_ref[...] = grad_ref[...]
    for side, back_ref in ((1 - parity(), back_first_ref), (parity(), back_second_ref)):
        for t in range(back_ref.shape[0]):
            b = ties_ref[side, t]

            @pl.when(b >= 0)
            def _(b=b, t=t, back_ref=back_ref):
                work_ref[b] += back_ref[t]

    return jnp.concatenate([work_ref[b].astype(BF16) for b in range(work_ref.shape[0])], axis=1)


def updates(gradient, gain_ref):
    step = min(2 * BLK, gain_ref.shape[0])
    for at in range(0, gain_ref.shape[0], step):
        rows = gain_ref[at : at + step, :]
        update = lax.dot_general(gradient, rows, NT, preferred_element_type=F32)
        for i in range(step // BLK):
            yield at // BLK + i, update[:, i * BLK : (i + 1) * BLK]


def first_update_kernel(
    grad_ref, back_first_ref, back_second_ref, ties_ref, gain_ref, x_ref, x_others_ref,
    state_ref, message_ref, work_ref,
):
    gradient = full_gradient(grad_ref, back_first_ref, back_second_ref, ties_ref, work_ref)
    held = state_ref.shape[0]
    me = lax.axis_index("snap")
    for i, update in updates(gradient, gain_ref):
        columns = pl.ds(pl.multiple_of((me * held + i) * BLK, BLK), BLK)
        parts = [x_ref[:, columns]] + [o[:, columns] for o in split(x_others_ref)]
        state = jnp.concatenate(parts, axis=0) + update
        state_ref[i] = state
        message_ref[i] = state.astype(BF16)


def last_update_kernel(
    grad_ref, back_first_ref, back_second_ref, ties_ref, gain_ref, state_ref, mine_ref, send_ref, work_ref
):
    gradient = full_gradient(grad_ref, back_first_ref, back_second_ref, ties_ref, work_ref)
    snaps = mine_ref.shape[0]
    for i, update in updates(gradient, gain_ref):
        state = state_ref[i] + update
        columns = slice(i * BLK, (i + 1) * BLK)
        mine_ref[:, columns] = state[:snaps]
        for j in range(send_ref.shape[0]):
            send_ref[j, :, columns] = state[(j + 1) * snaps : (j + 2) * snaps]


def finish_kernel(mine_ref, others_ref, out_ref):
    width = mine_ref.shape[1]
    members = others_ref.shape[0] + 1
    me = lax.axis_index("snap")
    out_ref[:, pl.ds(pl.multiple_of(me * width, BLK), width)] = mine_ref[...]
    for i in range(1, members):
        at = lax.rem(me + members - i, members) * width
        out_ref[:, pl.ds(pl.multiple_of(at, BLK), width)] = others_ref[i - 1]


def swap_pair(block, start):
    pairs = [(i, i + 1) for i in range(start, lax.axis_size("area") - 1, 2)]
    return lax.ppermute(block, "area", pairs + [(b, a) for a, b in pairs])


def with_neighbours(first, second):
    second = swap_pair(second, 1)
    return swap_pair(first, 0), second


def from_snap(block, distance):
    members = lax.axis_size("snap")
    return lax.ppermute(block, "snap", [(i, (i + distance) % members) for i in range(members)])


def from_all(block):
    return jnp.stack([from_snap(block, i) for i in range(1, lax.axis_size("snap"))])


def shape(dims, kind):
    return jax.ShapeDtypeStruct(dims, kind)


def on_device(
    phasor_readings,
    reading_error_spread,
    starting_voltages,
    derivative_pieces,
    derivative_tile_position,
    frontier_voltage_pieces,
    holder_line_order,
    hub_line_order,
    reciprocal_normal_operator,
):
    snaps, lines = phasor_readings.shape
    states = starting_voltages.shape[1]
    own = states // BLK
    measure = derivative_pieces.shape[0]
    ties_table = frontier_voltage_pieces[0]
    ties = ties_table.shape[1]
    slots = own + 2 * ties
    members = lax.axis_size("snap")
    areas = lax.axis_size("area")
    everything = snaps * members
    held = reciprocal_normal_operator.shape[0] // BLK
    place = derivative_tile_position[0]
    cap = hub_line_order.shape[2]
    width = max(cap, BLK)
    chunks = areas * cap // width
    hub = hub_line_order[0].reshape(chunks, width)
    holder = holder_line_order[0].reshape(chunks, width)
    depth = (width // BLK) * snaps + 8

    x_others = from_all(starting_voltages)
    message = call(
        pack_kernel,
        shape((chunks, depth, BLK), F32),
        [VMEM, VMEM, VMEM],
        (phasor_readings, reading_error_spread.reshape(lines // BLK, BLK), hub),
        scratch=[pltpu.VMEM((chunks, width // BLK, BLK), jnp.int32)],
        name="pack_readings",
    )
    if cap < BLK:
        each = BLK // cap
        message = message.reshape(chunks, depth, each, cap).transpose(0, 2, 1, 3)
        message = message.reshape(areas, depth, cap)
    message, x_others = lax.optimization_barrier((message, x_others))
    message = lax.all_to_all(message, "area", split_axis=0, concat_axis=0, tiled=True)
    if cap < BLK:
        message = message.reshape(chunks, each, depth, cap).transpose(0, 2, 1, 3)
        message = message.reshape(chunks, depth, BLK)

    group, lane = call(
        inverse_kernel,
        (shape((lines // BLK, BLK), jnp.int32),) * 2,
        [VMEM],
        (holder,),
        flops=10**9,
        name="invert_order",
    )
    aug, first, second = call(
        first_states_kernel,
        (
            shape((own, everything, BLK), BF16),
            shape((ties, everything, BLK), BF16),
            shape((ties, everything, BLK), BF16),
        ),
        [VMEM, VMEM, SMEM],
        (starting_voltages, x_others, ties_table),
        name="first_states",
    )
    first, second = with_neighbours(first, second)
    guess = call(
        predict_kernel,
        shape((everything, lines), F32),
        [VMEM, VMEM, VMEM, VMEM, SMEM],
        (aug, first, second, derivative_pieces, place),
        scratch=[pltpu.VMEM((slots, everything, BLK), BF16)],
        flops=10**9,
        name="predict",
    )
    message, guess = lax.optimization_barrier((message, guess))
    readings, variance = call(
        unpack_kernel,
        (shape((snaps, lines), F32), shape((1, lines), F32)),
        [VMEM, VMEM, VMEM],
        (message, group, lane),
        scratch=[pltpu.VMEM((chunks * (width // BLK), BLK), F32)],
        name="unpack_readings",
    )
    reading_others = from_all(readings)
    grads = (
        shape((own, everything, BLK), F32),
        shape((ties, everything, BLK), F32),
        shape((ties, everything, BLK), F32),
    )
    total = pltpu.VMEM((slots, everything, BLK), F32)
    work = pltpu.VMEM((own, everything, BLK), F32)
    grad, first, second = call(
        pull_kernel,
        grads,
        [VMEM, VMEM, VMEM, VMEM, VMEM, SMEM],
        (guess, readings, reading_others, variance, derivative_pieces, place),
        scratch=[total, pltpu.VMEM((everything, lines), BF16)],
        name="pull",
    )
    first, second = with_neighbours(first, second)
    state, mine = call(
        first_update_kernel,
        (shape((held, everything, BLK), F32), shape((held, everything, BLK), BF16)),
        [VMEM, VMEM, VMEM, SMEM, VMEM, VMEM, VMEM],
        (
            grad, first, second, ties_table, reciprocal_normal_operator,
            starting_voltages, x_others,
        ),
        scratch=[work],
        name="first_update",
    )
    others = from_all(mine)
    aug, first, second = call(
        join_states_kernel,
        (
            shape((own, everything, BLK), BF16),
            shape((ties, everything, BLK), BF16),
            shape((ties, everything, BLK), BF16),
        ),
        [VMEM, VMEM, SMEM],
        (mine, others, ties_table),
        name="join_states",
    )
    first, second = with_neighbours(first, second)
    grad, first, second = call(
        predict_pull_kernel,
        grads,
        [VMEM, VMEM, VMEM, VMEM, VMEM, VMEM, VMEM, SMEM],
        (aug, first, second, readings, reading_others, variance, derivative_pieces, place),
        scratch=[
            pltpu.VMEM((slots, everything, BLK), BF16),
            pltpu.VMEM((everything, lines), F32),
            total,
            pltpu.VMEM((everything, lines), BF16),
        ],
        name="predict_pull",
    )
    first, second = with_neighbours(first, second)
    kept, sent = call(
        last_update_kernel,
        (shape((snaps, held * BLK), F32), shape((members - 1, snaps, held * BLK), F32)),
        [VMEM, VMEM, VMEM, SMEM, VMEM, VMEM],
        (grad, first, second, ties_table, reciprocal_normal_operator, state),
        scratch=[work],
        name="last_update",
    )
    arrived = jnp.stack([from_snap(sent[i - 1], i) for i in range(1, members)])
    return call(
        finish_kernel,
        shape((snaps, states), F32),
        [VMEM, VMEM],
        (kept, arrived),
        name="finish",
    )


def solution(mesh):
    placed = (
        P("snap", "area"),
        P("area"),
        P("snap", "area"),
        P("area", None, None, None),
        P("area", None, None),
        P("area", None, None),
        P("area", None, None),
        P("area", None, None),
        P(("area", "snap"), None),
    )
    return jax.shard_map(
        on_device, mesh=mesh, in_specs=placed, out_specs=P("snap", "area"), check_vma=False
    )
```

```python
import functools

import jax
import jax.numpy as jnp
from jax import lax
from jax.experimental import pallas as pl
from jax.experimental.pallas import tpu as pltpu
from jax.sharding import PartitionSpec as P

BLK = 128
ITERS = 2
F32 = jnp.float32
BF16 = jnp.bfloat16
NT = (((1,), (1,)), ((), ()))
VMEM = pl.BlockSpec(memory_space=pltpu.VMEM)
ANY = pl.BlockSpec(memory_space=pl.ANY)
SMEM = pl.BlockSpec(memory_space=pltpu.SMEM)


def call(kernel, outs, ins, args, scratch=(), flops=0, bytes_accessed=0, name=None):
    return pl.pallas_call(
        kernel,
        out_shape=outs,
        in_specs=ins,
        out_specs=jax.tree.map(lambda _: VMEM, outs),
        scratch_shapes=list(scratch),
        compiler_params=pltpu.CompilerParams(vmem_limit_bytes=12 * 1024 * 1024),
        cost_estimate=pl.CostEstimate(
            flops=flops, bytes_accessed=bytes_accessed, transcendentals=0
        ),
        name=name,
    )(*args)


def lane_gather(values, lanes):
    return jnp.take_along_axis(values, lanes, axis=1, mode="promise_in_bounds")


def rows_iota(shape):
    return lax.broadcasted_iota(jnp.int32, shape, 0)


def pieces(refs):
    return [refs[0].at[i] for i in range(refs[0].shape[0])] if refs[0].ndim == 3 else list(refs)


def swapper(by_swaps):
    return lax.axis_index("area") if by_swaps else 0


def pack_kernel(by_swaps, z_in, v_in, hub_in, *refs):
    out_refs, (z_ref, v_ref, hub_ref, slot_ref, sems) = refs[:-5], refs[-5:]
    copies = [
        pltpu.make_async_copy(source, target, sems.at[i])
        for i, (source, target) in enumerate(((hub_in, hub_ref), (z_in, z_ref), (v_in, v_ref)))
    ]
    for copy in copies:
        copy.start()
    for copy in copies:
        copy.wait()
    snaps, lines = z_ref.shape
    blocks = lines // BLK
    chunks, width = hub_ref.shape
    groups = width // BLK
    for d in range(chunks):
        for g in range(groups):
            slot_ref[d, g : g + 1] = hub_ref[d : d + 1, g * BLK : (g + 1) * BLK]
    me = swapper(by_swaps)
    for m, out_ref in reversed(list(enumerate(pieces(out_refs)))):
        tail = jnp.zeros((8, BLK), F32)
        for g in range(groups):
            slot = slot_ref[jnp.bitwise_xor(me, m), g : g + 1]
            high = jnp.right_shift(slot, 7)
            low = jnp.bitwise_and(slot, 127)
            lanes = jnp.broadcast_to(low, (snaps, BLK))
            block_of = jnp.broadcast_to(high, (snaps, BLK))
            picked = jnp.zeros((snaps, BLK), F32)
            for b in range(blocks):
                found = lane_gather(z_ref[:, b * BLK : (b + 1) * BLK], lanes)
                picked = jnp.where(block_of == b, found, picked)
            out_ref[g * snaps : (g + 1) * snaps, :] = picked
            found = lane_gather(v_ref[...], jnp.broadcast_to(low, (blocks, BLK)))
            mine = rows_iota((blocks, BLK)) == high
            variance = jnp.sum(jnp.where(mine, found, 0.0), axis=0, keepdims=True)
            tail = jnp.where(rows_iota((8, BLK)) == g, variance, tail)
        out_ref[groups * snaps :, :] = tail


def inverse_kernel(own_ref, group_ref, lane_ref):
    chunks, width = own_ref.shape
    blocks = group_ref.shape[0]
    groups = width // BLK
    total = jnp.zeros((2 * blocks, BLK), F32)
    lane = lax.broadcasted_iota(jnp.int32, (2 * blocks, width), 1)
    row = rows_iota((2 * blocks, width))
    in_group = jnp.bitwise_and(lane, 127)
    group_in = jnp.right_shift(lane, 7)
    for d in range(chunks):
        owned = own_ref[d : d + 1, :]
        high = jnp.right_shift(owned, 7)
        low = jnp.bitwise_and(owned, 127)
        label = jnp.where(row < blocks, group_in + d * groups, in_group)
        hit = jnp.bitwise_and(row, blocks - 1) == high
        left = jnp.where(hit, label.astype(F32), 0.0).astype(BF16)
        right = jnp.where(rows_iota((BLK, width)) == low, 1.0, 0.0).astype(BF16)
        total += lax.dot_general(left, right, NT, preferred_element_type=F32)
    group_ref[...] = total[:blocks].astype(jnp.int32)
    lane_ref[...] = total[blocks:].astype(jnp.int32)


def unpack_kernel(by_swaps, start, group_ref, lane_ref, *refs):
    message_refs, (z_ref, v_ref, variance_ref) = pieces(refs[:-3][::-1]), refs[-3:]
    snaps, lines = z_ref.shape
    groups = (message_refs[0].shape[0] - 8) // snaps
    total = len(message_refs) * groups
    for m, message_ref in enumerate(message_refs):
        variance_ref[m * groups : (m + 1) * groups, :] = message_ref[groups * snaps :, :][:groups]
    me = swapper(by_swaps) * groups
    for b in range(lines // BLK):
        group = jnp.bitwise_xor(group_ref[start + b : start + b + 1, :], me)
        lane = lane_ref[start + b : start + b + 1, :]
        lanes = jnp.broadcast_to(lane, (snaps, BLK))
        group_of = jnp.broadcast_to(group, (snaps, BLK))
        picked = jnp.zeros((snaps, BLK), F32)
        for g in range(total):
            rows = slice(g % groups * snaps, (g % groups + 1) * snaps)
            found = lane_gather(message_refs[g // groups][rows, :], lanes)
            picked = jnp.where(group_of == g, found, picked)
        columns = slice(b * BLK, (b + 1) * BLK)
        z_ref[:, columns] = picked
        found = lane_gather(variance_ref[...], jnp.broadcast_to(lane, (total, BLK)))
        mine = rows_iota((total, BLK)) == group
        v_ref[:, columns] = jnp.sum(jnp.where(mine, found, 0.0), axis=0, keepdims=True)


def split(ref):
    return [ref.at[i] for i in range(ref.shape[0])]


def parity():
    return 1 - lax.rem(lax.axis_index("area"), 2)


def pick(source, listing_ref, side, out_ref):
    for t in range(out_ref.shape[0]):
        b = listing_ref[side, t]
        block = source(jnp.maximum(b, 0))
        out_ref[t] = jnp.where(b >= 0, block, jnp.zeros_like(block))


def first_states_kernel(own_ref, others_ref, ties_ref, aug_ref, first_ref, second_ref):
    snaps = own_ref.shape[0]
    for b in range(aug_ref.shape[0]):
        columns = slice(b * BLK, (b + 1) * BLK)
        aug_ref[b, :snaps] = own_ref[:, columns].astype(BF16)
        for i in range(others_ref.shape[0]):
            aug_ref[b, (i + 1) * snaps : (i + 2) * snaps] = others_ref[i, :, columns].astype(BF16)
    pick(lambda b: aug_ref[b], ties_ref, 1 - parity(), first_ref)
    pick(lambda b: aug_ref[b], ties_ref, parity(), second_ref)


def join_states_kernel(mine_ref, others_ref, ties_ref, aug_ref, first_ref, second_ref):
    held, everything = mine_ref.shape[:2]
    members = others_ref.shape[0] + 1
    snaps = everything // members
    me = lax.axis_index("snap")
    aug_ref[pl.ds(me * held, held)] = mine_ref[...]
    for i in range(1, members):
        at = lax.rem(me + members - i, members) * held
        for j in range(members):
            to = (j - i) % members
            aug_ref[pl.ds(at, held), to * snaps : (to + 1) * snaps] = others_ref[
                i - 1, :, j * snaps : (j + 1) * snaps
            ]
    pick(lambda b: aug_ref[b], ties_ref, 1 - parity(), first_ref)
    pick(lambda b: aug_ref[b], ties_ref, parity(), second_ref)


def slots_into(slots_ref, aug_ref, first_ref, second_ref):
    own = aug_ref.shape[0]
    ties = first_ref.shape[0]
    slots_ref[:own] = aug_ref[...]
    slots_ref[pl.ds(own + ties * (1 - parity()), ties)] = first_ref[...]
    slots_ref[pl.ds(own + ties * parity(), ties)] = second_ref[...]


def predicted(j, slots_ref, tiles_ref, place_ref):
    touched = tiles_ref.shape[1]
    chosen = jnp.concatenate([slots_ref[place_ref[k, j]] for k in range(touched)], axis=1)
    weights = jnp.concatenate([tiles_ref[j, k] for k in range(touched)], axis=1)
    return lax.dot_general(chosen, weights, NT, preferred_element_type=F32)


def predict_kernel(aug_ref, first_ref, second_ref, tiles_ref, place_ref, out_ref, slots_ref):
    slots_into(slots_ref, aug_ref, first_ref, second_ref)
    for j in range(tiles_ref.shape[0]):
        out_ref[:, j * BLK : (j + 1) * BLK] = predicted(j, slots_ref, tiles_ref, place_ref)


def weigh(j, guess, z_refs, others_refs, v_refs):
    each = z_refs[0].shape[1] // BLK
    z_ref, others_ref, v_ref = z_refs[j // each], others_refs[j // each], v_refs[j // each]
    columns = slice(j % each * BLK, (j % each + 1) * BLK)
    readings = [z_ref[:, columns]] + [o[:, columns] for o in split(others_ref)]
    resid = jnp.concatenate(readings, axis=0) - guess
    spread = jnp.sum(resid * resid, axis=0, keepdims=True) / resid.shape[0]
    return (resid / (v_ref[:, columns] + spread)).astype(BF16)


def pull(weighted_ref, tiles_ref, place_ref, total_ref, own_ref, first_ref, second_ref):
    total_ref[...] = jnp.zeros_like(total_ref)
    touched = tiles_ref.shape[1]
    for j in range(tiles_ref.shape[0]):
        weighted = weighted_ref[:, j * BLK : (j + 1) * BLK]
        weights = jnp.concatenate([tiles_ref[j, k] for k in range(touched)], axis=1)
        part = jnp.dot(weighted, weights, preferred_element_type=F32)
        for k in range(touched):
            n = place_ref[k, j]
            total_ref[n] += part[:, k * BLK : (k + 1) * BLK]
    own = own_ref.shape[0]
    ties = first_ref.shape[0]
    own_ref[...] = total_ref[:own]
    first_ref[...] = total_ref[pl.ds(own + ties * (1 - parity()), ties)]
    second_ref[...] = total_ref[pl.ds(own + ties * parity(), ties)]


def pull_kernel(
    guess_ref, z_refs, others_refs, v_refs, tiles_ref, place_ref, own_ref, first_ref, second_ref,
    total_ref, weighted_ref,
):
    for j in range(tiles_ref.shape[0]):
        columns = slice(j * BLK, (j + 1) * BLK)
        weighted_ref[:, columns] = weigh(j, guess_ref[:, columns], z_refs, others_refs, v_refs)
    pull(weighted_ref, tiles_ref, place_ref, total_ref, own_ref, first_ref, second_ref)


def predict_pull_kernel(
    aug_ref, first_in_ref, second_in_ref, z_refs, others_refs, v_refs, tiles_ref, place_ref,
    own_ref, first_ref, second_ref, slots_ref, guess_ref, total_ref, weighted_ref,
):
    predict_kernel(aug_ref, first_in_ref, second_in_ref, tiles_ref, place_ref, guess_ref, slots_ref)
    pull_kernel(
        guess_ref, z_refs, others_refs, v_refs, tiles_ref, place_ref, own_ref, first_ref, second_ref,
        total_ref, weighted_ref,
    )


def full_gradient(grad_ref, back_first_ref, back_second_ref, ties_ref, work_ref):
    work_ref[...] = grad_ref[...]
    for side, back_ref in ((1 - parity(), back_first_ref), (parity(), back_second_ref)):
        for t in range(back_ref.shape[0]):
            b = ties_ref[side, t]

            @pl.when(b >= 0)
            def _(b=b, t=t, back_ref=back_ref):
                work_ref[b] += back_ref[t]

    return jnp.concatenate([work_ref[b].astype(BF16) for b in range(work_ref.shape[0])], axis=1)


def updates(gradient, gain_ref):
    step = min(2 * BLK, gain_ref.shape[0])
    for at in range(0, gain_ref.shape[0], step):
        rows = gain_ref[at : at + step, :]
        update = lax.dot_general(gradient, rows, NT, preferred_element_type=F32)
        for i in range(step // BLK):
            yield at // BLK + i, update[:, i * BLK : (i + 1) * BLK]


def first_update_kernel(
    grad_ref, back_first_ref, back_second_ref, ties_ref, gain_ref, x_ref, x_others_ref,
    state_ref, message_ref, work_ref,
):
    gradient = full_gradient(grad_ref, back_first_ref, back_second_ref, ties_ref, work_ref)
    held = state_ref.shape[0]
    me = lax.axis_index("snap")
    for i, update in updates(gradient, gain_ref):
        columns = pl.ds(pl.multiple_of((me * held + i) * BLK, BLK), BLK)
        parts = [x_ref[:, columns]] + [o[:, columns] for o in split(x_others_ref)]
        state = jnp.concatenate(parts, axis=0) + update
        state_ref[i] = state
        message_ref[i] = state.astype(BF16)


def last_update_kernel(
    grad_ref, back_first_ref, back_second_ref, ties_ref, gain_ref, state_ref, mine_ref, send_ref, work_ref
):
    gradient = full_gradient(grad_ref, back_first_ref, back_second_ref, ties_ref, work_ref)
    snaps = mine_ref.shape[0]
    for i, update in updates(gradient, gain_ref):
        state = state_ref[i] + update
        columns = slice(i * BLK, (i + 1) * BLK)
        mine_ref[:, columns] = state[:snaps]
        for j in range(send_ref.shape[0]):
            send_ref[j, :, columns] = state[(j + 1) * snaps : (j + 2) * snaps]


def finish_kernel(mine_ref, others_ref, out_ref):
    width = mine_ref.shape[1]
    members = others_ref.shape[0] + 1
    me = lax.axis_index("snap")
    out_ref[:, pl.ds(pl.multiple_of(me * width, BLK), width)] = mine_ref[...]
    for i in range(1, members):
        at = lax.rem(me + members - i, members) * width
        out_ref[:, pl.ds(pl.multiple_of(at, BLK), width)] = others_ref[i - 1]


def swap_pair(block, start):
    pairs = [(i, i + 1) for i in range(start, lax.axis_size("area") - 1, 2)]
    return lax.ppermute(block, "area", pairs + [(b, a) for a, b in pairs])


def with_neighbours(first, second):
    return swap_pair(first, 1), swap_pair(second, 0)


def from_snap(block, distance):
    members = lax.axis_size("snap")
    return lax.ppermute(block, "snap", [(i, (i + distance) % members) for i in range(members)])


def from_all(block):
    return jnp.stack([from_snap(block, i) for i in range(1, lax.axis_size("snap"))])


def shape(dims, kind):
    return jax.ShapeDtypeStruct(dims, kind)


def on_device(
    phasor_readings,
    reading_error_spread,
    starting_voltages,
    derivative_pieces,
    derivative_tile_position,
    frontier_voltage_pieces,
    holder_line_order,
    hub_line_order,
    reciprocal_normal_operator,
):
    snaps, lines = phasor_readings.shape
    states = starting_voltages.shape[1]
    own = states // BLK
    measure = derivative_pieces.shape[0]
    ties_table = frontier_voltage_pieces[0]
    ties = ties_table.shape[1]
    slots = own + 2 * ties
    members = lax.axis_size("snap")
    areas = lax.axis_size("area")
    everything = snaps * members
    held = reciprocal_normal_operator.shape[0] // BLK
    place = derivative_tile_position[0].T
    cap = hub_line_order.shape[2]
    width = max(cap, BLK)
    chunks = areas * cap // width
    hub = hub_line_order[0].reshape(chunks, width)
    holder = holder_line_order[0].reshape(chunks, width)
    depth = (width // BLK) * snaps + 8

    x_others = from_all(starting_voltages)
    by_swaps = areas <= 16 and areas & (areas - 1) == 0 and cap >= BLK
    if by_swaps:
        packed = (shape((depth, BLK), F32),) * areas
    else:
        packed = (shape((chunks, depth, BLK), F32),)
    message = call(
        functools.partial(pack_kernel, by_swaps),
        packed,
        [ANY, ANY, ANY],
        (phasor_readings, reading_error_spread.reshape(lines // BLK, BLK), hub),
        scratch=[
            pltpu.VMEM((snaps, lines), F32),
            pltpu.VMEM((lines // BLK, BLK), F32),
            pltpu.VMEM((chunks, width), jnp.int32),
            pltpu.VMEM((chunks, width // BLK, BLK), jnp.int32),
            pltpu.SemaphoreType.DMA((3,)),
        ],
        name="pack_readings",
    )
    message, x_others = lax.optimization_barrier((message, x_others))
    if by_swaps:
        routes = [[(i, i ^ m) for i in range(areas)] for m in range(areas)]
        message = [
            lax.ppermute(message[m], "area", routes[m]) for m in reversed(range(1, areas))
        ] + [message[0]]
    else:
        message = message[0]
        each = width // cap
        if each > 1:
            message = message.reshape(chunks, depth, each, cap).transpose(0, 2, 1, 3)
            message = message.reshape(areas, depth, cap)
        message = lax.all_to_all(message, "area", split_axis=0, concat_axis=0, tiled=True)
        if each > 1:
            message = message.reshape(chunks, each, depth, cap).transpose(0, 2, 1, 3)
            message = message.reshape(chunks, depth, BLK)
        message = [message]

    group, lane = call(
        inverse_kernel,
        (shape((lines // BLK, BLK), jnp.int32),) * 2,
        [VMEM],
        (holder,),
        flops=10**9,
        name="invert_order",
    )
    aug, first, second = call(
        first_states_kernel,
        (
            shape((own, everything, BLK), BF16),
            shape((ties, everything, BLK), BF16),
            shape((ties, everything, BLK), BF16),
        ),
        [VMEM, VMEM, SMEM],
        (starting_voltages, x_others, ties_table),
        name="first_states",
    )
    first, second = with_neighbours(first, second)
    guess = call(
        predict_kernel,
        shape((everything, lines), F32),
        [VMEM, VMEM, VMEM, VMEM, SMEM],
        (aug, first, second, derivative_pieces, place),
        scratch=[pltpu.VMEM((slots, everything, BLK), BF16)],
        flops=10**9,
        name="predict",
    )
    message, guess = lax.optimization_barrier((message, guess))
    halves = []
    for part in range(2):
        halves.append(
            call(
                functools.partial(unpack_kernel, by_swaps, part * (lines // BLK // 2)),
                (shape((snaps, lines // 2), F32), shape((1, lines // 2), F32)),
                [VMEM, VMEM] + [VMEM] * len(message),
                (group, lane, *message),
                scratch=[pltpu.VMEM((chunks * (width // BLK), BLK), F32)],
                flops=2 * 10**9,
                name="unpack_readings",
            )
        )
    readings = [half[0] for half in halves]
    variance = [half[1] for half in halves]
    reading_others = [from_all(half) for half in readings]
    grads = (
        shape((own, everything, BLK), F32),
        shape((ties, everything, BLK), F32),
        shape((ties, everything, BLK), F32),
    )
    total = pltpu.VMEM((slots, everything, BLK), F32)
    work = pltpu.VMEM((own, everything, BLK), F32)
    grad, first, second = call(
        pull_kernel,
        grads,
        [VMEM, [VMEM] * 2, [VMEM] * 2, [VMEM] * 2, VMEM, SMEM],
        (guess, readings, reading_others, variance, derivative_pieces, place),
        scratch=[total, pltpu.VMEM((everything, lines), BF16)],
        name="pull",
    )
    first, second = with_neighbours(first, second)
    state, mine = call(
        first_update_kernel,
        (shape((held, everything, BLK), F32), shape((held, everything, BLK), BF16)),
        [VMEM, VMEM, VMEM, SMEM, VMEM, VMEM, VMEM],
        (
            grad, first, second, ties_table, reciprocal_normal_operator,
            starting_voltages, x_others,
        ),
        scratch=[work],
        name="first_update",
    )
    others = from_all(mine)
    aug, first, second = call(
        join_states_kernel,
        (
            shape((own, everything, BLK), BF16),
            shape((ties, everything, BLK), BF16),
            shape((ties, everything, BLK), BF16),
        ),
        [VMEM, VMEM, SMEM],
        (mine, others, ties_table),
        name="join_states",
    )
    first, second = with_neighbours(first, second)
    grad, first, second = call(
        predict_pull_kernel,
        grads,
        [VMEM, VMEM, VMEM, [VMEM] * 2, [VMEM] * 2, [VMEM] * 2, VMEM, SMEM],
        (aug, first, second, readings, reading_others, variance, derivative_pieces, place),
        scratch=[
            pltpu.VMEM((slots, everything, BLK), BF16),
            pltpu.VMEM((everything, lines), F32),
            total,
            pltpu.VMEM((everything, lines), BF16),
        ],
        name="predict_pull",
    )
    first, second = with_neighbours(first, second)
    kept, sent = call(
        last_update_kernel,
        (shape((snaps, held * BLK), F32), shape((members - 1, snaps, held * BLK), F32)),
        [VMEM, VMEM, VMEM, SMEM, VMEM, VMEM],
        (grad, first, second, ties_table, reciprocal_normal_operator, state),
        scratch=[work],
        name="last_update",
    )
    arrived = jnp.stack([from_snap(sent[i - 1], i) for i in range(1, members)])
    return call(
        finish_kernel,
        shape((snaps, states), F32),
        [VMEM, VMEM],
        (kept, arrived),
        name="finish",
    )


def solution(mesh):
    placed = (
        P("snap", "area"),
        P("area"),
        P("snap", "area"),
        P("area", None, None, None),
        P("area", None, None),
        P("area", None, None),
        P("area", None, None),
        P("area", None, None),
        P(("area", "snap"), None),
    )
    return jax.shard_map(
        on_device, mesh=mesh, in_specs=placed, out_specs=P("snap", "area"), check_vma=False
    )
```

```python
import functools

import jax
import jax.numpy as jnp
from jax import lax
from jax.experimental import pallas as pl
from jax.experimental.pallas import tpu as pltpu
from jax.sharding import PartitionSpec as P

BLK = 128
ITERS = 2
F32 = jnp.float32
BF16 = jnp.bfloat16
NT = (((1,), (1,)), ((), ()))
VMEM = pl.BlockSpec(memory_space=pltpu.VMEM)
HBM = pl.BlockSpec(memory_space=pltpu.HBM)
SMEM = pl.BlockSpec(memory_space=pltpu.SMEM)


def call(kernel, outs, ins, args, scratch=(), flops=0, bytes_accessed=0, name=None):
    return pl.pallas_call(
        kernel,
        out_shape=outs,
        in_specs=ins,
        out_specs=jax.tree.map(lambda _: VMEM, outs),
        scratch_shapes=list(scratch),
        compiler_params=pltpu.CompilerParams(vmem_limit_bytes=12 * 1024 * 1024),
        cost_estimate=pl.CostEstimate(
            flops=flops, bytes_accessed=bytes_accessed, transcendentals=0
        ),
        name=name,
    )(*args)


def lane_gather(values, lanes):
    return jnp.take_along_axis(values, lanes, axis=1, mode="promise_in_bounds")


def rows_iota(shape):
    return lax.broadcasted_iota(jnp.int32, shape, 0)


def pack_kernel(z_in, v_in, hub_in, out_ref, z_ref, v_ref, hub_ref, sems):
    copies = [
        pltpu.make_async_copy(source, target, sems.at[i])
        for i, (source, target) in enumerate(((hub_in, hub_ref), (z_in, z_ref), (v_in, v_ref)))
    ]
    for copy in copies:
        copy.start()
    for copy in copies:
        copy.wait()
    snaps, lines = z_ref.shape
    blocks = lines // BLK
    chunks, width = hub_ref.shape
    groups = width // BLK
    for d in range(chunks):
        tail = jnp.zeros((8, BLK), F32)
        for g in range(groups):
            slot = hub_ref[d : d + 1, g * BLK : (g + 1) * BLK]
            high = jnp.right_shift(slot, 7)
            low = jnp.bitwise_and(slot, 127)
            lanes = jnp.broadcast_to(low, (snaps, BLK))
            block_of = jnp.broadcast_to(high, (snaps, BLK))
            picked = jnp.zeros((snaps, BLK), F32)
            for b in range(blocks):
                found = lane_gather(z_ref[:, b * BLK : (b + 1) * BLK], lanes)
                picked = jnp.where(block_of == b, found, picked)
            out_ref[d, g * snaps : (g + 1) * snaps, :] = picked
            found = lane_gather(v_ref[...], jnp.broadcast_to(low, (blocks, BLK)))
            mine = rows_iota((blocks, BLK)) == high
            variance = jnp.sum(jnp.where(mine, found, 0.0), axis=0, keepdims=True)
            tail = jnp.where(rows_iota((8, BLK)) == g, variance, tail)
        out_ref[d, groups * snaps :, :] = tail


def inverse_kernel(own_ref, group_ref, lane_ref):
    chunks, width = own_ref.shape
    blocks = group_ref.shape[0]
    groups = width // BLK
    total = jnp.zeros((2 * blocks, BLK), F32)
    lane = lax.broadcasted_iota(jnp.int32, (2 * blocks, width), 1)
    row = rows_iota((2 * blocks, width))
    in_group = jnp.bitwise_and(lane, 127)
    group_in = jnp.right_shift(lane, 7)
    for d in range(chunks):
        owned = own_ref[d : d + 1, :]
        high = jnp.right_shift(owned, 7)
        low = jnp.bitwise_and(owned, 127)
        label = jnp.where(row < blocks, group_in + d * groups, in_group)
        hit = jnp.bitwise_and(row, blocks - 1) == high
        left = jnp.where(hit, label.astype(F32), 0.0).astype(BF16)
        right = jnp.where(rows_iota((BLK, width)) == low, 1.0, 0.0).astype(BF16)
        total += lax.dot_general(left, right, NT, preferred_element_type=F32)
    group_ref[...] = total[:blocks].astype(jnp.int32)
    lane_ref[...] = total[blocks:].astype(jnp.int32)


def unpack_kernel(start, group_ref, lane_ref, message_ref, z_ref, v_ref, variance_ref):
    snaps, lines = z_ref.shape
    chunks = message_ref.shape[0]
    groups = (message_ref.shape[1] - 8) // snaps
    total = chunks * groups
    for d in range(chunks):
        variance_ref[d * groups : (d + 1) * groups, :] = message_ref[d, groups * snaps :, :][:groups]
    for b in range(lines // BLK):
        group = group_ref[start + b : start + b + 1, :]
        lane = lane_ref[start + b : start + b + 1, :]
        lanes = jnp.broadcast_to(lane, (snaps, BLK))
        group_of = jnp.broadcast_to(group, (snaps, BLK))
        picked = jnp.zeros((snaps, BLK), F32)
        for g in range(total):
            rows = slice(g % groups * snaps, (g % groups + 1) * snaps)
            found = lane_gather(message_ref[g // groups, rows, :], lanes)
            picked = jnp.where(group_of == g, found, picked)
        columns = slice(b * BLK, (b + 1) * BLK)
        z_ref[:, columns] = picked
        found = lane_gather(variance_ref[...], jnp.broadcast_to(lane, (total, BLK)))
        mine = rows_iota((total, BLK)) == group
        v_ref[:, columns] = jnp.sum(jnp.where(mine, found, 0.0), axis=0, keepdims=True)


def split(ref):
    return [ref.at[i] for i in range(ref.shape[0])]


def parity():
    return 1 - lax.rem(lax.axis_index("area"), 2)


def pick(source, listing_ref, side, out_ref):
    for t in range(out_ref.shape[0]):
        b = listing_ref[side, t]
        block = source(jnp.maximum(b, 0))
        out_ref[t] = jnp.where(b >= 0, block, jnp.zeros_like(block))


def first_states_kernel(
    x_ref, own_ref, others_ref, ties_ref, aug_ref, first_ref, second_ref, sent_refs
):
    snaps = own_ref.shape[0]
    for b in range(aug_ref.shape[0]):
        columns = slice(b * BLK, (b + 1) * BLK)
        aug_ref[b, :snaps] = own_ref[:, columns]
        for i in range(others_ref.shape[0]):
            aug_ref[b, (i + 1) * snaps : (i + 2) * snaps] = others_ref[i, :, columns]
    pick(lambda b: aug_ref[b], ties_ref, 1 - parity(), first_ref)
    pick(lambda b: aug_ref[b], ties_ref, parity(), second_ref)
    members = len(sent_refs) + 1
    width = x_ref.shape[1] // members
    for i, sent_ref in enumerate(sent_refs, 1):
        at = lax.rem(lax.axis_index("snap") + i, members) * width
        sent_ref[...] = x_ref[:, pl.ds(pl.multiple_of(at, BLK), width)]


def join_states_kernel(mine_ref, others_ref, ties_ref, aug_ref, first_ref, second_ref):
    held, everything = mine_ref.shape[:2]
    members = others_ref.shape[0] + 1
    snaps = everything // members
    me = lax.axis_index("snap")
    aug_ref[pl.ds(me * held, held)] = mine_ref[...]
    for i in range(1, members):
        at = lax.rem(me + members - i, members) * held
        for j in range(members):
            to = (j - i) % members
            aug_ref[pl.ds(at, held), to * snaps : (to + 1) * snaps] = others_ref[
                i - 1, :, j * snaps : (j + 1) * snaps
            ]
    pick(lambda b: aug_ref[b], ties_ref, 1 - parity(), first_ref)
    pick(lambda b: aug_ref[b], ties_ref, parity(), second_ref)


def slots_into(slots_ref, aug_ref, first_ref, second_ref):
    own = aug_ref.shape[0]
    ties = first_ref.shape[0]
    slots_ref[:own] = aug_ref[...]
    slots_ref[pl.ds(own + ties * (1 - parity()), ties)] = first_ref[...]
    slots_ref[pl.ds(own + ties * parity(), ties)] = second_ref[...]


def predicted(j, slots_ref, tiles_ref, place_ref):
    touched = tiles_ref.shape[1]
    chosen = jnp.concatenate([slots_ref[place_ref[k, j]] for k in range(touched)], axis=1)
    weights = jnp.concatenate([tiles_ref[j, k] for k in range(touched)], axis=1)
    return lax.dot_general(chosen, weights, NT, preferred_element_type=F32)


def predict_kernel(aug_ref, first_ref, second_ref, tiles_ref, place_ref, out_ref, slots_ref):
    slots_into(slots_ref, aug_ref, first_ref, second_ref)
    for j in range(tiles_ref.shape[0]):
        out_ref[:, j * BLK : (j + 1) * BLK] = predicted(j, slots_ref, tiles_ref, place_ref)


def weigh(j, guess, z_refs, others_refs, v_refs):
    each = z_refs[0].shape[1] // BLK
    z_ref, others_ref, v_ref = z_refs[j // each], others_refs[j // each], v_refs[j // each]
    columns = slice(j % each * BLK, (j % each + 1) * BLK)
    readings = [z_ref[:, columns]] + [o[:, columns] for o in split(others_ref)]
    resid = jnp.concatenate(readings, axis=0) - guess
    spread = jnp.sum(resid * resid, axis=0, keepdims=True) / resid.shape[0]
    return (resid / (v_ref[:, columns] + spread)).astype(BF16)


def pull(weighted_ref, tiles_ref, place_ref, total_ref, own_ref, first_ref, second_ref):
    total_ref[...] = jnp.zeros_like(total_ref)
    touched = tiles_ref.shape[1]
    for j in range(tiles_ref.shape[0]):
        weighted = weighted_ref[:, j * BLK : (j + 1) * BLK]
        weights = jnp.concatenate([tiles_ref[j, k] for k in range(touched)], axis=1)
        part = jnp.dot(weighted, weights, preferred_element_type=F32)
        for k in range(touched):
            n = place_ref[k, j]
            total_ref[n] += part[:, k * BLK : (k + 1) * BLK]
    own = own_ref.shape[0]
    ties = first_ref.shape[0]
    own_ref[...] = total_ref[:own]
    first_ref[...] = total_ref[pl.ds(own + ties * (1 - parity()), ties)]
    second_ref[...] = total_ref[pl.ds(own + ties * parity(), ties)]


def pull_kernel(
    guess_ref, z_refs, others_refs, v_refs, tiles_ref, place_ref, own_ref, first_ref, second_ref,
    total_ref, weighted_ref,
):
    for j in range(tiles_ref.shape[0]):
        columns = slice(j * BLK, (j + 1) * BLK)
        weighted_ref[:, columns] = weigh(j, guess_ref[:, columns], z_refs, others_refs, v_refs)
    pull(weighted_ref, tiles_ref, place_ref, total_ref, own_ref, first_ref, second_ref)


def predict_pull_kernel(
    aug_ref, first_in_ref, second_in_ref, z_refs, others_refs, v_refs, tiles_ref, place_ref,
    own_ref, first_ref, second_ref, slots_ref, guess_ref, total_ref, weighted_ref,
):
    predict_kernel(aug_ref, first_in_ref, second_in_ref, tiles_ref, place_ref, guess_ref, slots_ref)
    pull_kernel(
        guess_ref, z_refs, others_refs, v_refs, tiles_ref, place_ref, own_ref, first_ref, second_ref,
        total_ref, weighted_ref,
    )


def full_gradient(grad_ref, back_first_ref, back_second_ref, ties_ref, work_ref):
    work_ref[...] = grad_ref[...]
    for side, back_ref in ((1 - parity(), back_first_ref), (parity(), back_second_ref)):
        for t in range(back_ref.shape[0]):
            b = ties_ref[side, t]

            @pl.when(b >= 0)
            def _(b=b, t=t, back_ref=back_ref):
                work_ref[b] += back_ref[t]

    return jnp.concatenate([work_ref[b].astype(BF16) for b in range(work_ref.shape[0])], axis=1)


def updates(gradient, gain_ref):
    step = min(2 * BLK, gain_ref.shape[0])
    for at in range(0, gain_ref.shape[0], step):
        rows = gain_ref[at : at + step, :]
        update = lax.dot_general(gradient, rows, NT, preferred_element_type=F32)
        for i in range(step // BLK):
            yield at // BLK + i, update[:, i * BLK : (i + 1) * BLK]


def first_update_kernel(
    grad_ref, back_first_ref, back_second_ref, ties_ref, gain_ref, x_ref, x_others_refs,
    state_ref, message_ref, work_ref,
):
    gradient = full_gradient(grad_ref, back_first_ref, back_second_ref, ties_ref, work_ref)
    held = state_ref.shape[0]
    me = lax.axis_index("snap")
    for i, update in updates(gradient, gain_ref):
        columns = pl.ds(pl.multiple_of((me * held + i) * BLK, BLK), BLK)
        parts = [x_ref[:, columns]] + [o[:, i * BLK : (i + 1) * BLK] for o in x_others_refs]
        state = jnp.concatenate(parts, axis=0) + update
        state_ref[i] = state
        message_ref[i] = state.astype(BF16)


def last_update_kernel(
    grad_ref, back_first_ref, back_second_ref, ties_ref, gain_ref, state_ref, mine_ref, send_ref, work_ref
):
    gradient = full_gradient(grad_ref, back_first_ref, back_second_ref, ties_ref, work_ref)
    snaps = mine_ref.shape[0]
    for i, update in updates(gradient, gain_ref):
        state = state_ref[i] + update
        columns = slice(i * BLK, (i + 1) * BLK)
        mine_ref[:, columns] = state[:snaps]
        for j in range(send_ref.shape[0]):
            send_ref[j, :, columns] = state[(j + 1) * snaps : (j + 2) * snaps]


def finish_kernel(mine_ref, others_ref, out_ref):
    width = mine_ref.shape[1]
    members = others_ref.shape[0] + 1
    me = lax.axis_index("snap")
    out_ref[:, pl.ds(pl.multiple_of(me * width, BLK), width)] = mine_ref[...]
    for i in range(1, members):
        at = lax.rem(me + members - i, members) * width
        out_ref[:, pl.ds(pl.multiple_of(at, BLK), width)] = others_ref[i - 1]


def swap_pair(block, start):
    pairs = [(i, i + 1) for i in range(start, lax.axis_size("area") - 1, 2)]
    return lax.ppermute(block, "area", pairs + [(b, a) for a, b in pairs])


def with_neighbours(first, second):
    return swap_pair(first, 1), swap_pair(second, 0)


def from_snap(block, distance):
    members = lax.axis_size("snap")
    return lax.ppermute(block, "snap", [(i, (i + distance) % members) for i in range(members)])


def from_all(block):
    return jnp.stack([from_snap(block, i) for i in range(1, lax.axis_size("snap"))])


def shape(dims, kind):
    return jax.ShapeDtypeStruct(dims, kind)


def on_device(
    phasor_readings,
    reading_error_spread,
    starting_voltages,
    derivative_pieces,
    derivative_tile_position,
    frontier_voltage_pieces,
    holder_line_order,
    hub_line_order,
    reciprocal_normal_operator,
):
    snaps, lines = phasor_readings.shape
    states = starting_voltages.shape[1]
    own = states // BLK
    measure = derivative_pieces.shape[0]
    ties_table = frontier_voltage_pieces[0]
    ties = ties_table.shape[1]
    slots = own + 2 * ties
    members = lax.axis_size("snap")
    areas = lax.axis_size("area")
    everything = snaps * members
    held = reciprocal_normal_operator.shape[0] // BLK
    place = derivative_tile_position[0].T
    cap = hub_line_order.shape[2]
    width = max(cap, BLK)
    chunks = areas * cap // width
    hub = hub_line_order[0].reshape(chunks, width)
    holder = holder_line_order[0].reshape(chunks, width)
    depth = (width // BLK) * snaps + 8

    rounded = starting_voltages.astype(BF16)
    rounded_others = from_all(rounded)
    message = call(
        pack_kernel,
        shape((chunks, depth, BLK), F32),
        [HBM, HBM, HBM],
        (phasor_readings, reading_error_spread.reshape(lines // BLK, BLK), hub),
        scratch=[
            pltpu.VMEM((snaps, lines), F32),
            pltpu.VMEM((lines // BLK, BLK), F32),
            pltpu.VMEM((chunks, width), jnp.int32),
            pltpu.SemaphoreType.DMA((3,)),
        ],
        name="pack_readings",
    )
    message, rounded_others = lax.optimization_barrier((message, rounded_others))
    each = width // cap
    if each > 1:
        message = message.reshape(chunks, depth, each, cap).transpose(0, 2, 1, 3)
        message = message.reshape(areas, depth, cap)
    message = lax.all_to_all(message, "area", split_axis=0, concat_axis=0, tiled=True)
    if each > 1:
        message = message.reshape(chunks, each, depth, cap).transpose(0, 2, 1, 3)
        message = message.reshape(chunks, depth, BLK)

    group, lane = call(
        inverse_kernel,
        (shape((lines // BLK, BLK), jnp.int32),) * 2,
        [VMEM],
        (holder,),
        flops=10**9,
        name="invert_order",
    )
    aug, first, second, x_sent = call(
        first_states_kernel,
        (
            shape((own, everything, BLK), BF16),
            shape((ties, everything, BLK), BF16),
            shape((ties, everything, BLK), BF16),
            [shape((snaps, held * BLK), F32)] * (members - 1),
        ),
        [VMEM, VMEM, VMEM, SMEM],
        (starting_voltages, rounded, rounded_others, ties_table),
        name="first_states",
    )
    x_others = [from_snap(sent, i) for i, sent in enumerate(x_sent, 1)]
    first, second = with_neighbours(first, second)
    guess = call(
        predict_kernel,
        shape((everything, lines), F32),
        [VMEM, VMEM, VMEM, VMEM, SMEM],
        (aug, first, second, derivative_pieces, place),
        scratch=[pltpu.VMEM((slots, everything, BLK), BF16)],
        flops=10**9,
        name="predict",
    )
    message, guess, x_others = lax.optimization_barrier((message, guess, x_others))
    halves = []
    for part in range(2):
        halves.append(
            call(
                functools.partial(unpack_kernel, part * (lines // BLK // 2)),
                (shape((snaps, lines // 2), F32), shape((1, lines // 2), F32)),
                [VMEM, VMEM, VMEM],
                (group, lane, message),
                scratch=[pltpu.VMEM((chunks * (width // BLK), BLK), F32)],
                flops=2 * 10**9,
                name="unpack_readings",
            )
        )
    readings = [half[0] for half in halves]
    variance = [half[1] for half in halves]
    reading_others = [from_all(half) for half in readings]
    grads = (
        shape((own, everything, BLK), F32),
        shape((ties, everything, BLK), F32),
        shape((ties, everything, BLK), F32),
    )
    total = pltpu.VMEM((slots, everything, BLK), F32)
    work = pltpu.VMEM((own, everything, BLK), F32)
    grad, first, second = call(
        pull_kernel,
        grads,
        [VMEM, [VMEM] * 2, [VMEM] * 2, [VMEM] * 2, VMEM, SMEM],
        (guess, readings, reading_others, variance, derivative_pieces, place),
        scratch=[total, pltpu.VMEM((everything, lines), BF16)],
        name="pull",
    )
    first, second = with_neighbours(first, second)
    state, mine = call(
        first_update_kernel,
        (shape((held, everything, BLK), F32), shape((held, everything, BLK), BF16)),
        [VMEM, VMEM, VMEM, SMEM, VMEM, VMEM, [VMEM] * (members - 1)],
        (
            grad, first, second, ties_table, reciprocal_normal_operator,
            starting_voltages, x_others,
        ),
        scratch=[work],
        name="first_update",
    )
    others = from_all(mine)
    aug, first, second = call(
        join_states_kernel,
        (
            shape((own, everything, BLK), BF16),
            shape((ties, everything, BLK), BF16),
            shape((ties, everything, BLK), BF16),
        ),
        [VMEM, VMEM, SMEM],
        (mine, others, ties_table),
        name="join_states",
    )
    first, second = with_neighbours(first, second)
    grad, first, second = call(
        predict_pull_kernel,
        grads,
        [VMEM, VMEM, VMEM, [VMEM] * 2, [VMEM] * 2, [VMEM] * 2, VMEM, SMEM],
        (aug, first, second, readings, reading_others, variance, derivative_pieces, place),
        scratch=[
            pltpu.VMEM((slots, everything, BLK), BF16),
            pltpu.VMEM((everything, lines), F32),
            total,
            pltpu.VMEM((everything, lines), BF16),
        ],
        name="predict_pull",
    )
    first, second = with_neighbours(first, second)
    kept, sent = call(
        last_update_kernel,
        (shape((snaps, held * BLK), F32), shape((members - 1, snaps, held * BLK), F32)),
        [VMEM, VMEM, VMEM, SMEM, VMEM, VMEM],
        (grad, first, second, ties_table, reciprocal_normal_operator, state),
        scratch=[work],
        name="last_update",
    )
    arrived = jnp.stack([from_snap(sent[i - 1], i) for i in range(1, members)])
    return call(
        finish_kernel,
        shape((snaps, states), F32),
        [VMEM, VMEM],
        (kept, arrived),
        name="finish",
    )


def solution(mesh):
    placed = (
        P("snap", "area"),
        P("area"),
        P("snap", "area"),
        P("area", None, None, None),
        P("area", None, None),
        P("area", None, None),
        P("area", None, None),
        P("area", None, None),
        P(("area", "snap"), None),
    )
    return jax.shard_map(
        on_device, mesh=mesh, in_specs=placed, out_specs=P("snap", "area"), check_vma=False
    )
```

```python
import functools

import jax
import jax.numpy as jnp
from jax import lax
from jax.experimental import pallas as pl
from jax.experimental.pallas import tpu as pltpu
from jax.sharding import PartitionSpec as P

BLK = 128
ITERS = 2
F32 = jnp.float32
BF16 = jnp.bfloat16
NT = (((1,), (1,)), ((), ()))
VMEM = pl.BlockSpec(memory_space=pltpu.VMEM)
HBM = pl.BlockSpec(memory_space=pltpu.HBM)
SMEM = pl.BlockSpec(memory_space=pltpu.SMEM)


def call(kernel, outs, ins, args, scratch=(), flops=0, mib=12, name=None):
    return pl.pallas_call(
        kernel,
        out_shape=outs,
        in_specs=ins,
        out_specs=jax.tree.map(lambda _: VMEM, outs),
        scratch_shapes=list(scratch),
        compiler_params=pltpu.CompilerParams(vmem_limit_bytes=mib * 1024 * 1024),
        cost_estimate=pl.CostEstimate(
            flops=flops, bytes_accessed=0, transcendentals=0
        ),
        name=name,
    )(*args)


def lane_gather(values, lanes):
    return jnp.take_along_axis(values, lanes, axis=1, mode="promise_in_bounds")


def rows_iota(shape):
    return lax.broadcasted_iota(jnp.int32, shape, 0)


def pack_kernel(z_in, v_in, hub_in, out_ref, z_ref, v_ref, hub_ref, sems):
    copies = [
        pltpu.make_async_copy(source, target, sems.at[i])
        for i, (source, target) in enumerate(((hub_in, hub_ref), (z_in, z_ref), (v_in, v_ref)))
    ]
    for copy in copies:
        copy.start()
    for copy in copies:
        copy.wait()
    snaps, lines = z_ref.shape
    blocks = lines // BLK
    chunks, width = hub_ref.shape
    groups = width // BLK
    for d in range(chunks):
        tail = jnp.zeros((8, BLK), F32)
        for g in range(groups):
            slot = hub_ref[d : d + 1, g * BLK : (g + 1) * BLK]
            high = jnp.right_shift(slot, 7)
            low = jnp.bitwise_and(slot, 127)
            lanes = jnp.broadcast_to(low, (snaps, BLK))
            block_of = jnp.broadcast_to(high, (snaps, BLK))
            picked = jnp.zeros((snaps, BLK), F32)
            for b in range(blocks):
                found = lane_gather(z_ref[:, b * BLK : (b + 1) * BLK], lanes)
                picked = jnp.where(block_of == b, found, picked)
            out_ref[d, g * snaps : (g + 1) * snaps, :] = picked
            found = lane_gather(v_ref[...], jnp.broadcast_to(low, (blocks, BLK)))
            mine = rows_iota((blocks, BLK)) == high
            variance = jnp.sum(jnp.where(mine, found, 0.0), axis=0, keepdims=True)
            tail = jnp.where(rows_iota((8, BLK)) == g, variance, tail)
        out_ref[d, groups * snaps :, :] = tail


def inverse_kernel(own_ref, group_ref, lane_ref):
    chunks, width = own_ref.shape
    blocks = group_ref.shape[0]
    groups = width // BLK
    total = jnp.zeros((2 * blocks, BLK), F32)
    lane = lax.broadcasted_iota(jnp.int32, (2 * blocks, width), 1)
    row = rows_iota((2 * blocks, width))
    in_group = jnp.bitwise_and(lane, 127)
    group_in = jnp.right_shift(lane, 7)
    for d in range(chunks):
        owned = own_ref[d : d + 1, :]
        high = jnp.right_shift(owned, 7)
        low = jnp.bitwise_and(owned, 127)
        label = jnp.where(row < blocks, group_in + d * groups, in_group)
        hit = jnp.bitwise_and(row, blocks - 1) == high
        left = jnp.where(hit, label.astype(F32), 0.0).astype(BF16)
        right = jnp.where(rows_iota((BLK, width)) == low, 1.0, 0.0).astype(BF16)
        total += lax.dot_general(left, right, NT, preferred_element_type=F32)
    group_ref[...] = total[:blocks].astype(jnp.int32)
    lane_ref[...] = total[blocks:].astype(jnp.int32)


def unpack_kernel(start, group_ref, lane_ref, message_ref, z_ref, v_ref, variance_ref):
    snaps, lines = z_ref.shape
    chunks = message_ref.shape[0]
    groups = (message_ref.shape[1] - 8) // snaps
    total = chunks * groups
    for d in range(chunks):
        variance_ref[d * groups : (d + 1) * groups, :] = message_ref[d, groups * snaps :, :][:groups]
    for b in range(lines // BLK):
        group = group_ref[start + b : start + b + 1, :]
        lane = lane_ref[start + b : start + b + 1, :]
        lanes = jnp.broadcast_to(lane, (snaps, BLK))
        group_of = jnp.broadcast_to(group, (snaps, BLK))
        picked = jnp.zeros((snaps, BLK), F32)
        for g in range(total):
            rows = slice(g % groups * snaps, (g % groups + 1) * snaps)
            found = lane_gather(message_ref[g // groups, rows, :], lanes)
            picked = jnp.where(group_of == g, found, picked)
        columns = slice(b * BLK, (b + 1) * BLK)
        z_ref[:, columns] = picked
        found = lane_gather(variance_ref[...], jnp.broadcast_to(lane, (total, BLK)))
        mine = rows_iota((total, BLK)) == group
        v_ref[:, columns] = jnp.sum(jnp.where(mine, found, 0.0), axis=0, keepdims=True)


def split(ref):
    return [ref.at[i] for i in range(ref.shape[0])]


def parity():
    return 1 - lax.rem(lax.axis_index("area"), 2)


def pick(blocks_ref, listing_ref, side, out_ref, start=0):
    held = blocks_ref.shape[0]
    for t in range(out_ref.shape[0]):
        b = listing_ref[side, t]
        at = b - start
        block = blocks_ref[jnp.clip(at, 0, held - 1)]
        here = (b >= 0) & (at >= 0) & (at < held)
        out_ref[t] = jnp.where(here, block, jnp.zeros_like(block))


def first_states_kernel(
    x_ref, own_ref, others_ref, ties_ref, aug_ref, first_ref, second_ref, sent_refs
):
    snaps = own_ref.shape[0]
    for b in range(aug_ref.shape[0]):
        columns = slice(b * BLK, (b + 1) * BLK)
        aug_ref[b, :snaps] = own_ref[:, columns]
        for i in range(others_ref.shape[0]):
            aug_ref[b, (i + 1) * snaps : (i + 2) * snaps] = others_ref[i, :, columns]
    pick(aug_ref, ties_ref, 1 - parity(), first_ref)
    pick(aug_ref, ties_ref, parity(), second_ref)
    members = len(sent_refs) + 1
    width = x_ref.shape[1] // members
    for i, sent_ref in enumerate(sent_refs, 1):
        at = lax.rem(lax.axis_index("snap") + i, members) * width
        sent_ref[...] = x_ref[:, pl.ds(pl.multiple_of(at, BLK), width)]


def slots_into(slots_ref, aug_ref, first_ref, second_ref):
    own = aug_ref.shape[0]
    ties = first_ref.shape[0]
    slots_ref[:own] = aug_ref[...]
    slots_ref[pl.ds(own + ties * (1 - parity()), ties)] = first_ref[...]
    slots_ref[pl.ds(own + ties * parity(), ties)] = second_ref[...]


def reordered(ref, distance, members):
    snaps = ref.shape[1] // members
    order = [(n + distance) % members for n in range(members)]
    return jnp.concatenate([ref[:, j * snaps : (j + 1) * snaps] for j in order], axis=1)


def join_states(slots_ref, mine_ref, others_refs, first_refs, second_refs):
    members = len(first_refs)
    held = mine_ref.shape[0]
    own = held * members
    ties = first_refs[0].shape[0]
    me = lax.axis_index("snap")
    slots_ref[pl.ds(me * held, held)] = mine_ref[...]
    for i, ref in enumerate(others_refs, 1):
        at = lax.rem(me + members - i, members) * held
        slots_ref[pl.ds(at, held)] = reordered(ref, i, members)
    for side, refs in ((1 - parity(), first_refs), (parity(), second_refs)):
        parts = [reordered(ref, i, members) for i, ref in enumerate(refs)]
        slots_ref[pl.ds(own + ties * side, ties)] = sum(parts[1:], parts[0])


def predicted(j, slots_ref, tiles_ref, place_ref):
    touched = tiles_ref.shape[1]
    chosen = jnp.concatenate([slots_ref[place_ref[k, j]] for k in range(touched)], axis=1)
    weights = jnp.concatenate([tiles_ref[j, k] for k in range(touched)], axis=1)
    return lax.dot_general(chosen, weights, NT, preferred_element_type=F32)


def predict_kernel(aug_ref, first_ref, second_ref, tiles_ref, place_ref, out_ref, slots_ref):
    slots_into(slots_ref, aug_ref, first_ref, second_ref)
    predict(tiles_ref, place_ref, out_ref, slots_ref)


def predict(tiles_ref, place_ref, out_ref, slots_ref):
    for j in range(tiles_ref.shape[0]):
        out_ref[:, j * BLK : (j + 1) * BLK] = predicted(j, slots_ref, tiles_ref, place_ref)


def weigh(j, guess, z_refs, others_refs, v_refs):
    each = z_refs[0].shape[1] // BLK
    z_ref, others_ref, v_ref = z_refs[j // each], others_refs[j // each], v_refs[j // each]
    columns = slice(j % each * BLK, (j % each + 1) * BLK)
    readings = [z_ref[:, columns]] + [o[:, columns] for o in split(others_ref)]
    resid = jnp.concatenate(readings, axis=0) - guess
    spread = jnp.sum(resid * resid, axis=0, keepdims=True) / resid.shape[0]
    return (resid / (v_ref[:, columns] + spread)).astype(BF16)


def pull(weighted_ref, tiles_ref, place_ref, total_ref, own_ref, first_ref, second_ref):
    total_ref[...] = jnp.zeros_like(total_ref)
    touched = tiles_ref.shape[1]
    for j in range(tiles_ref.shape[0]):
        weighted = weighted_ref[:, j * BLK : (j + 1) * BLK]
        weights = jnp.concatenate([tiles_ref[j, k] for k in range(touched)], axis=1)
        part = jnp.dot(weighted, weights, preferred_element_type=F32)
        for k in range(touched):
            n = place_ref[k, j]
            total_ref[n] += part[:, k * BLK : (k + 1) * BLK]
    own = own_ref.shape[0]
    ties = first_ref.shape[0]
    own_ref[...] = total_ref[:own]
    first_ref[...] = total_ref[pl.ds(own + ties * (1 - parity()), ties)]
    second_ref[...] = total_ref[pl.ds(own + ties * parity(), ties)]


def pull_kernel(
    guess_ref, z_refs, others_refs, v_refs, tiles_ref, place_ref, own_ref, first_ref, second_ref,
    total_ref, weighted_ref,
):
    for j in range(tiles_ref.shape[0]):
        columns = slice(j * BLK, (j + 1) * BLK)
        weighted_ref[:, columns] = weigh(j, guess_ref[:, columns], z_refs, others_refs, v_refs)
    pull(weighted_ref, tiles_ref, place_ref, total_ref, own_ref, first_ref, second_ref)


def predict_pull_kernel(
    first_refs, others_in_refs, second_refs, mine_ref, z_refs, others_refs, v_refs, tiles_ref, place_ref,
    own_ref, first_ref, second_ref, slots_ref, guess_ref, total_ref, weighted_ref,
):
    join_states(slots_ref, mine_ref, others_in_refs, first_refs, second_refs)
    predict(tiles_ref, place_ref, guess_ref, slots_ref)
    pull_kernel(
        guess_ref, z_refs, others_refs, v_refs, tiles_ref, place_ref, own_ref, first_ref, second_ref,
        total_ref, weighted_ref,
    )


def full_gradient(grad_ref, back_first_ref, back_second_ref, ties_ref, work_ref):
    work_ref[...] = grad_ref[...]
    for side, back_ref in ((1 - parity(), back_first_ref), (parity(), back_second_ref)):
        for t in range(back_ref.shape[0]):
            b = ties_ref[side, t]

            @pl.when(b >= 0)
            def _(b=b, t=t, back_ref=back_ref):
                work_ref[b] += back_ref[t]

    return jnp.concatenate([work_ref[b].astype(BF16) for b in range(work_ref.shape[0])], axis=1)


def updates(gradient, gain_ref):
    step = min(2 * BLK, gain_ref.shape[0])
    for at in range(0, gain_ref.shape[0], step):
        rows = gain_ref[at : at + step, :]
        update = lax.dot_general(gradient, rows, NT, preferred_element_type=F32)
        for i in range(step // BLK):
            yield at // BLK + i, update[:, i * BLK : (i + 1) * BLK]


def first_update_kernel(
    grad_ref, back_first_ref, back_second_ref, ties_ref, gain_ref, x_ref, x_others_refs,
    state_ref, message_ref, first_ref, second_ref, work_ref,
):
    gradient = full_gradient(grad_ref, back_first_ref, back_second_ref, ties_ref, work_ref)
    held = state_ref.shape[0]
    me = lax.axis_index("snap")
    for i, update in updates(gradient, gain_ref):
        columns = pl.ds(pl.multiple_of((me * held + i) * BLK, BLK), BLK)
        parts = [x_ref[:, columns]] + [o[:, i * BLK : (i + 1) * BLK] for o in x_others_refs]
        state = jnp.concatenate(parts, axis=0) + update
        state_ref[i] = state
        message_ref[i] = state.astype(BF16)
    pick(message_ref, ties_ref, 1 - parity(), first_ref, me * held)
    pick(message_ref, ties_ref, parity(), second_ref, me * held)


def last_update_kernel(
    grad_ref, back_first_ref, back_second_ref, ties_ref, gain_ref, state_ref, mine_ref, send_ref, work_ref
):
    gradient = full_gradient(grad_ref, back_first_ref, back_second_ref, ties_ref, work_ref)
    snaps = mine_ref.shape[0]
    for i, update in updates(gradient, gain_ref):
        state = state_ref[i] + update
        columns = slice(i * BLK, (i + 1) * BLK)
        mine_ref[:, columns] = state[:snaps]
        for j in range(send_ref.shape[0]):
            send_ref[j, :, columns] = state[(j + 1) * snaps : (j + 2) * snaps]


def finish_kernel(mine_ref, others_ref, out_ref):
    width = mine_ref.shape[1]
    members = others_ref.shape[0] + 1
    me = lax.axis_index("snap")
    out_ref[:, pl.ds(pl.multiple_of(me * width, BLK), width)] = mine_ref[...]
    for i in range(1, members):
        at = lax.rem(me + members - i, members) * width
        out_ref[:, pl.ds(pl.multiple_of(at, BLK), width)] = others_ref[i - 1]


def swap_pair(block, start, distance=0):
    members = lax.axis_size("snap")
    pairs = [(i, i + 1) for i in range(start, lax.axis_size("area") - 1, 2)]
    route = [
        (a * members + s, b * members + (s + distance) % members)
        for a, b in pairs + [(b, a) for a, b in pairs]
        for s in range(members)
    ]
    return lax.ppermute(block, ("area", "snap"), route)


def with_neighbours(first, second):
    return swap_pair(first, 1), swap_pair(second, 0)


def from_snap(block, distance):
    members = lax.axis_size("snap")
    return lax.ppermute(block, "snap", [(i, (i + distance) % members) for i in range(members)])


def from_all(block):
    return jnp.stack([from_snap(block, i) for i in range(1, lax.axis_size("snap"))])


def shape(dims, kind):
    return jax.ShapeDtypeStruct(dims, kind)


def on_device(
    phasor_readings,
    reading_error_spread,
    starting_voltages,
    derivative_pieces,
    derivative_tile_position,
    frontier_voltage_pieces,
    holder_line_order,
    hub_line_order,
    reciprocal_normal_operator,
):
    snaps, lines = phasor_readings.shape
    states = starting_voltages.shape[1]
    own = states // BLK
    measure = derivative_pieces.shape[0]
    ties_table = frontier_voltage_pieces[0]
    ties = ties_table.shape[1]
    slots = own + 2 * ties
    members = lax.axis_size("snap")
    areas = lax.axis_size("area")
    everything = snaps * members
    held = reciprocal_normal_operator.shape[0] // BLK
    place = derivative_tile_position[0].T
    cap = hub_line_order.shape[2]
    width = max(cap, BLK)
    chunks = areas * cap // width
    hub = hub_line_order[0].reshape(chunks, width)
    holder = holder_line_order[0].reshape(chunks, width)
    depth = (width // BLK) * snaps + 8

    rounded = starting_voltages.astype(BF16)
    rounded_others = from_all(rounded)
    message = call(
        pack_kernel,
        shape((chunks, depth, BLK), F32),
        [HBM, HBM, HBM],
        (phasor_readings, reading_error_spread.reshape(lines // BLK, BLK), hub),
        scratch=[
            pltpu.VMEM((snaps, lines), F32),
            pltpu.VMEM((lines // BLK, BLK), F32),
            pltpu.VMEM((chunks, width), jnp.int32),
            pltpu.SemaphoreType.DMA((3,)),
        ],
        mib=60,
        name="pack_readings",
    )
    message, rounded_others = lax.optimization_barrier((message, rounded_others))
    each = width // cap
    if each > 1:
        message = message.reshape(chunks, depth, each, cap).transpose(0, 2, 1, 3)
        message = message.reshape(areas, depth, cap)
    message = lax.all_to_all(message, "area", split_axis=0, concat_axis=0, tiled=True)
    if each > 1:
        message = message.reshape(chunks, each, depth, cap).transpose(0, 2, 1, 3)
        message = message.reshape(chunks, depth, BLK)

    group, lane = call(
        inverse_kernel,
        (shape((lines // BLK, BLK), jnp.int32),) * 2,
        [VMEM],
        (holder,),
        flops=10**9,
        name="invert_order",
    )
    aug, first, second, x_sent = call(
        first_states_kernel,
        (
            shape((own, everything, BLK), BF16),
            shape((ties, everything, BLK), BF16),
            shape((ties, everything, BLK), BF16),
            [shape((snaps, held * BLK), F32)] * (members - 1),
        ),
        [VMEM, VMEM, VMEM, SMEM],
        (starting_voltages, rounded, rounded_others, ties_table),
        name="first_states",
    )
    x_others = [from_snap(sent, i) for i, sent in enumerate(x_sent, 1)]
    first, second = with_neighbours(first, second)
    guess = call(
        predict_kernel,
        shape((everything, lines), F32),
        [VMEM, VMEM, VMEM, VMEM, SMEM],
        (aug, first, second, derivative_pieces, place),
        scratch=[pltpu.VMEM((slots, everything, BLK), BF16)],
        flops=10**9,
        name="predict",
    )
    message, guess, x_others = lax.optimization_barrier((message, guess, x_others))
    halves = []
    for part in range(2):
        halves.append(
            call(
                functools.partial(unpack_kernel, part * (lines // BLK // 2)),
                (shape((snaps, lines // 2), F32), shape((1, lines // 2), F32)),
                [VMEM, VMEM, VMEM],
                (group, lane, message),
                scratch=[pltpu.VMEM((chunks * (width // BLK), BLK), F32)],
                flops=2 * 10**9,
                name="unpack_readings",
            )
        )
    readings = [half[0] for half in halves]
    variance = [half[1] for half in halves]
    reading_others = [from_all(half) for half in readings]
    grads = (
        shape((own, everything, BLK), F32),
        shape((ties, everything, BLK), F32),
        shape((ties, everything, BLK), F32),
    )
    total = pltpu.VMEM((slots, everything, BLK), F32)
    work = pltpu.VMEM((own, everything, BLK), F32)
    grad, first, second = call(
        pull_kernel,
        grads,
        [VMEM, [VMEM] * 2, [VMEM] * 2, [VMEM] * 2, VMEM, SMEM],
        (guess, readings, reading_others, variance, derivative_pieces, place),
        scratch=[total, pltpu.VMEM((everything, lines), BF16)],
        name="pull",
    )
    arrived = with_neighbours(first, second)
    boundary = shape((ties, everything, BLK), BF16)
    state, mine, first, second = call(
        first_update_kernel,
        (
            shape((held, everything, BLK), F32),
            shape((held, everything, BLK), BF16),
            boundary,
            boundary,
        ),
        [VMEM, VMEM, VMEM, SMEM, VMEM, VMEM, [VMEM] * (members - 1)],
        (
            grad, *arrived, ties_table, reciprocal_normal_operator,
            starting_voltages, x_others,
        ),
        scratch=[work],
        name="first_update",
    )
    firsts = [swap_pair(first, 1, i) for i in range(members)]
    others = [from_snap(mine, i) for i in range(1, members)]
    seconds = [swap_pair(second, 0, i) for i in range(members)]
    grad, first, second = call(
        predict_pull_kernel,
        grads,
        [[VMEM] * members, [VMEM] * (members - 1), [VMEM] * members, VMEM]
        + [[VMEM] * 2, [VMEM] * 2, [VMEM] * 2, VMEM, SMEM],
        (firsts, others, seconds, mine, readings, reading_others, variance, derivative_pieces, place),
        scratch=[
            pltpu.VMEM((slots, everything, BLK), BF16),
            pltpu.VMEM((everything, lines), F32),
            total,
            pltpu.VMEM((everything, lines), BF16),
        ],
        name="predict_pull",
    )
    first, second = with_neighbours(first, second)
    kept, sent = call(
        last_update_kernel,
        (shape((snaps, held * BLK), F32), shape((members - 1, snaps, held * BLK), F32)),
        [VMEM, VMEM, VMEM, SMEM, VMEM, VMEM],
        (grad, first, second, ties_table, reciprocal_normal_operator, state),
        scratch=[work],
        name="last_update",
    )
    arrived = jnp.stack([from_snap(sent[i - 1], i) for i in range(1, members)])
    return call(
        finish_kernel,
        shape((snaps, states), F32),
        [VMEM, VMEM],
        (kept, arrived),
        name="finish",
    )


def solution(mesh):
    placed = (
        P("snap", "area"),
        P("area"),
        P("snap", "area"),
        P("area", None, None, None),
        P("area", None, None),
        P("area", None, None),
        P("area", None, None),
        P("area", None, None),
        P(("area", "snap"), None),
    )
    return jax.shard_map(
        on_device, mesh=mesh, in_specs=placed, out_specs=P("snap", "area"), check_vma=False
    )
```

```python
import functools

import jax
import jax.numpy as jnp
from jax import lax
from jax.experimental import pallas as pl
from jax.experimental.pallas import tpu as pltpu
from jax.sharding import PartitionSpec as P

BLK = 128
ITERS = 2
F32 = jnp.float32
BF16 = jnp.bfloat16
NT = (((1,), (1,)), ((), ()))
VMEM = pl.BlockSpec(memory_space=pltpu.VMEM)
HBM = pl.BlockSpec(memory_space=pltpu.HBM)
SMEM = pl.BlockSpec(memory_space=pltpu.SMEM)


def call(kernel, outs, ins, args, scratch=(), flops=0, mib=12, out_spec=VMEM, name=None):
    return pl.pallas_call(
        kernel,
        out_shape=outs,
        in_specs=ins,
        out_specs=jax.tree.map(lambda _: out_spec, outs),
        scratch_shapes=list(scratch),
        compiler_params=pltpu.CompilerParams(vmem_limit_bytes=mib * 1024 * 1024),
        cost_estimate=pl.CostEstimate(
            flops=flops, bytes_accessed=0, transcendentals=0
        ),
        name=name,
    )(*args)


def lane_gather(values, lanes):
    return jnp.take_along_axis(values, lanes, axis=1, mode="promise_in_bounds")


def rows_iota(shape):
    return lax.broadcasted_iota(jnp.int32, shape, 0)


def pack_kernel(z_in, v_in, hub_in, out, z_ref, v_ref, hub_ref, out_ref, sems, out_sems):
    copies = [
        pltpu.make_async_copy(source, target, sems.at[i])
        for i, (source, target) in enumerate(((hub_in, hub_ref), (z_in, z_ref), (v_in, v_ref)))
    ]
    for copy in copies:
        copy.start()
    for copy in copies:
        copy.wait()
    snaps, lines = z_ref.shape
    blocks = lines // BLK
    chunks, width = hub_ref.shape
    groups = width // BLK
    for d in range(chunks):
        tail = jnp.zeros((8, BLK), F32)
        for g in range(groups):
            slot = hub_ref[d : d + 1, g * BLK : (g + 1) * BLK]
            high = jnp.right_shift(slot, 7)
            low = jnp.bitwise_and(slot, 127)
            lanes = jnp.broadcast_to(low, (snaps, BLK))
            block_of = jnp.broadcast_to(high, (snaps, BLK))
            picked = jnp.zeros((snaps, BLK), F32)
            for b in range(blocks):
                found = lane_gather(z_ref[:, b * BLK : (b + 1) * BLK], lanes)
                picked = jnp.where(block_of == b, found, picked)
            out_ref[d, g * snaps : (g + 1) * snaps, :] = picked
            found = lane_gather(v_ref[...], jnp.broadcast_to(low, (blocks, BLK)))
            mine = rows_iota((blocks, BLK)) == high
            variance = jnp.sum(jnp.where(mine, found, 0.0), axis=0, keepdims=True)
            tail = jnp.where(rows_iota((8, BLK)) == g, variance, tail)
        out_ref[d, groups * snaps :, :] = tail
        pltpu.make_async_copy(out_ref.at[d], out.at[d], out_sems.at[d]).start()
    for d in range(chunks):
        pltpu.make_async_copy(out_ref.at[d], out.at[d], out_sems.at[d]).wait()


def inverse_kernel(own_ref, group_ref, lane_ref):
    chunks, width = own_ref.shape
    blocks = group_ref.shape[0]
    groups = width // BLK
    total = jnp.zeros((2 * blocks, BLK), F32)
    lane = lax.broadcasted_iota(jnp.int32, (2 * blocks, width), 1)
    row = rows_iota((2 * blocks, width))
    in_group = jnp.bitwise_and(lane, 127)
    group_in = jnp.right_shift(lane, 7)
    for d in range(chunks):
        owned = own_ref[d : d + 1, :]
        high = jnp.right_shift(owned, 7)
        low = jnp.bitwise_and(owned, 127)
        label = jnp.where(row < blocks, group_in + d * groups, in_group)
        hit = jnp.bitwise_and(row, blocks - 1) == high
        left = jnp.where(hit, label.astype(F32), 0.0).astype(BF16)
        right = jnp.where(rows_iota((BLK, width)) == low, 1.0, 0.0).astype(BF16)
        total += lax.dot_general(left, right, NT, preferred_element_type=F32)
    group_ref[...] = total[:blocks].astype(jnp.int32)
    lane_ref[...] = total[blocks:].astype(jnp.int32)


def unpack_kernel(start, group_ref, lane_ref, message_ref, z_ref, v_ref, variance_ref):
    snaps, lines = z_ref.shape
    chunks = message_ref.shape[0]
    groups = (message_ref.shape[1] - 8) // snaps
    total = chunks * groups
    for d in range(chunks):
        variance_ref[d * groups : (d + 1) * groups, :] = message_ref[d, groups * snaps :, :][:groups]
    for b in range(lines // BLK):
        group = group_ref[start + b : start + b + 1, :]
        lane = lane_ref[start + b : start + b + 1, :]
        lanes = jnp.broadcast_to(lane, (snaps, BLK))
        group_of = jnp.broadcast_to(group, (snaps, BLK))
        picked = jnp.zeros((snaps, BLK), F32)
        for g in range(total):
            rows = slice(g % groups * snaps, (g % groups + 1) * snaps)
            found = lane_gather(message_ref[g // groups, rows, :], lanes)
            picked = jnp.where(group_of == g, found, picked)
        columns = slice(b * BLK, (b + 1) * BLK)
        z_ref[:, columns] = picked
        found = lane_gather(variance_ref[...], jnp.broadcast_to(lane, (total, BLK)))
        mine = rows_iota((total, BLK)) == group
        v_ref[:, columns] = jnp.sum(jnp.where(mine, found, 0.0), axis=0, keepdims=True)


def split(ref):
    return [ref.at[i] for i in range(ref.shape[0])]


def parity():
    return 1 - lax.rem(lax.axis_index("area"), 2)


def pick(blocks_ref, listing_ref, side, out_ref, start=0):
    held = blocks_ref.shape[0]
    for t in range(out_ref.shape[0]):
        b = listing_ref[side, t]
        at = b - start
        block = blocks_ref[jnp.clip(at, 0, held - 1)]
        here = (b >= 0) & (at >= 0) & (at < held)
        out_ref[t] = jnp.where(here, block, jnp.zeros_like(block))


def first_states_kernel(
    x_ref, own_ref, others_ref, ties_ref, aug_ref, first_ref, second_ref, sent_refs
):
    snaps = own_ref.shape[0]
    for b in range(aug_ref.shape[0]):
        columns = slice(b * BLK, (b + 1) * BLK)
        aug_ref[b, :snaps] = own_ref[:, columns]
        for i in range(others_ref.shape[0]):
            aug_ref[b, (i + 1) * snaps : (i + 2) * snaps] = others_ref[i, :, columns]
    pick(aug_ref, ties_ref, 1 - parity(), first_ref)
    pick(aug_ref, ties_ref, parity(), second_ref)
    members = len(sent_refs) + 1
    width = x_ref.shape[1] // members
    for i, sent_ref in enumerate(sent_refs, 1):
        at = lax.rem(lax.axis_index("snap") + i, members) * width
        sent_ref[...] = x_ref[:, pl.ds(pl.multiple_of(at, BLK), width)]


def slots_into(slots_ref, aug_ref, first, second_ref):
    own = aug_ref.shape[0]
    ties = second_ref.shape[0]
    slots_ref[:own] = aug_ref[...]
    slots_ref[pl.ds(own + ties * (1 - parity()), ties)] = first
    slots_ref[pl.ds(own + ties * parity(), ties)] = second_ref[...]


def reordered(ref, distance, members):
    snaps = ref.shape[1] // members
    order = [(n + distance) % members for n in range(members)]
    return jnp.concatenate([ref[:, j * snaps : (j + 1) * snaps] for j in order], axis=1)


def join_states_kernel(mine_ref, others_refs, ties_ref, aug_ref, second_ref):
    members = len(others_refs) + 1
    held = mine_ref.shape[0]
    me = lax.axis_index("snap")
    aug_ref[pl.ds(me * held, held)] = mine_ref[...]
    for i, ref in enumerate(others_refs, 1):
        at = lax.rem(me + members - i, members) * held
        aug_ref[pl.ds(at, held)] = reordered(ref, i, members)
    pick(aug_ref, ties_ref, parity(), second_ref)


def predicted(j, slots_ref, tiles_ref, place_ref):
    touched = tiles_ref.shape[1]
    chosen = jnp.concatenate([slots_ref[place_ref[k, j]] for k in range(touched)], axis=1)
    weights = jnp.concatenate([tiles_ref[j, k] for k in range(touched)], axis=1)
    return lax.dot_general(chosen, weights, NT, preferred_element_type=F32)


def predict_kernel(aug_ref, first_ref, second_ref, tiles_ref, place_ref, out_ref, slots_ref):
    slots_into(slots_ref, aug_ref, first_ref[...], second_ref)
    predict(tiles_ref, place_ref, out_ref, slots_ref)


def predict(tiles_ref, place_ref, out_ref, slots_ref):
    for j in range(tiles_ref.shape[0]):
        out_ref[:, j * BLK : (j + 1) * BLK] = predicted(j, slots_ref, tiles_ref, place_ref)


def weigh(j, guess, z_refs, others_refs, v_refs):
    each = z_refs[0].shape[1] // BLK
    z_ref, others_ref, v_ref = z_refs[j // each], others_refs[j // each], v_refs[j // each]
    columns = slice(j % each * BLK, (j % each + 1) * BLK)
    readings = [z_ref[:, columns]] + [o[:, columns] for o in split(others_ref)]
    resid = jnp.concatenate(readings, axis=0) - guess
    spread = jnp.sum(resid * resid, axis=0, keepdims=True) / resid.shape[0]
    return (resid / (v_ref[:, columns] + spread)).astype(BF16)


def pull(weighted_ref, tiles_ref, place_ref, total_ref, own_ref, first_ref, second_ref):
    total_ref[...] = jnp.zeros_like(total_ref)
    touched = tiles_ref.shape[1]
    for j in range(tiles_ref.shape[0]):
        weighted = weighted_ref[:, j * BLK : (j + 1) * BLK]
        weights = jnp.concatenate([tiles_ref[j, k] for k in range(touched)], axis=1)
        part = jnp.dot(weighted, weights, preferred_element_type=F32)
        for k in range(touched):
            n = place_ref[k, j]
            total_ref[n] += part[:, k * BLK : (k + 1) * BLK]
    own = own_ref.shape[0]
    ties = first_ref.shape[0]
    own_ref[...] = total_ref[:own]
    first = total_ref[pl.ds(own + ties * (1 - parity()), ties)]
    second = total_ref[pl.ds(own + ties * parity(), ties)]
    first_ref[...] = first.astype(first_ref.dtype)
    second_ref[...] = second.astype(second_ref.dtype)


def pull_kernel(
    guess_ref, z_refs, others_refs, v_refs, tiles_ref, place_ref, own_ref, first_ref, second_ref,
    total_ref, weighted_ref,
):
    for j in range(tiles_ref.shape[0]):
        columns = slice(j * BLK, (j + 1) * BLK)
        weighted_ref[:, columns] = weigh(j, guess_ref[:, columns], z_refs, others_refs, v_refs)
    pull(weighted_ref, tiles_ref, place_ref, total_ref, own_ref, first_ref, second_ref)


def predict_pull_kernel(
    first_refs, aug_ref, second_in_ref, z_refs, others_refs, v_refs, tiles_ref, place_ref,
    own_ref, first_ref, second_ref, slots_ref, guess_ref, total_ref, weighted_ref,
):
    parts = [reordered(ref, i, len(first_refs)) for i, ref in enumerate(first_refs)]
    slots_into(slots_ref, aug_ref, sum(parts[1:], parts[0]), second_in_ref)
    predict(tiles_ref, place_ref, guess_ref, slots_ref)
    pull_kernel(
        guess_ref, z_refs, others_refs, v_refs, tiles_ref, place_ref, own_ref, first_ref, second_ref,
        total_ref, weighted_ref,
    )


def full_gradient(grad_ref, back_first_ref, back_second_ref, ties_ref, work_ref):
    work_ref[...] = grad_ref[...]
    for side, back_ref in ((1 - parity(), back_first_ref), (parity(), back_second_ref)):
        for t in range(back_ref.shape[0]):
            b = ties_ref[side, t]

            @pl.when(b >= 0)
            def _(b=b, t=t, back_ref=back_ref):
                work_ref[b] += back_ref[t].astype(F32)

    return jnp.concatenate([work_ref[b].astype(BF16) for b in range(work_ref.shape[0])], axis=1)


def updates(gradient, gain_ref):
    step = min(2 * BLK, gain_ref.shape[0])
    for at in range(0, gain_ref.shape[0], step):
        rows = gain_ref[at : at + step, :]
        update = lax.dot_general(gradient, rows, NT, preferred_element_type=F32)
        for i in range(step // BLK):
            yield at // BLK + i, update[:, i * BLK : (i + 1) * BLK]


def first_update_kernel(
    grad_ref, back_first_ref, back_second_ref, ties_ref, gain_ref, x_ref, x_others_refs,
    state_ref, message_ref, first_ref, work_ref,
):
    gradient = full_gradient(grad_ref, back_first_ref, back_second_ref, ties_ref, work_ref)
    held = state_ref.shape[0]
    me = lax.axis_index("snap")
    for i, update in updates(gradient, gain_ref):
        columns = pl.ds(pl.multiple_of((me * held + i) * BLK, BLK), BLK)
        parts = [x_ref[:, columns]] + [o[:, i * BLK : (i + 1) * BLK] for o in x_others_refs]
        state = jnp.concatenate(parts, axis=0) + update
        state_ref[i] = state
        message_ref[i] = state.astype(BF16)
    pick(message_ref, ties_ref, 1 - parity(), first_ref, me * held)


def last_update_kernel(
    grad_ref, back_first_ref, back_second_ref, ties_ref, gain_ref, state_ref, mine_ref, send_ref, work_ref
):
    gradient = full_gradient(grad_ref, back_first_ref, back_second_ref, ties_ref, work_ref)
    snaps = mine_ref.shape[0]
    for i, update in updates(gradient, gain_ref):
        state = state_ref[i] + update
        columns = slice(i * BLK, (i + 1) * BLK)
        mine_ref[:, columns] = state[:snaps]
        for j in range(send_ref.shape[0]):
            send_ref[j, :, columns] = state[(j + 1) * snaps : (j + 2) * snaps]


def finish_kernel(mine_ref, others_ref, out_ref):
    width = mine_ref.shape[1]
    members = others_ref.shape[0] + 1
    me = lax.axis_index("snap")
    out_ref[:, pl.ds(pl.multiple_of(me * width, BLK), width)] = mine_ref[...]
    for i in range(1, members):
        at = lax.rem(me + members - i, members) * width
        out_ref[:, pl.ds(pl.multiple_of(at, BLK), width)] = others_ref[i - 1]


def swap_pair(block, start):
    pairs = [(i, i + 1) for i in range(start, lax.axis_size("area") - 1, 2)]
    return lax.ppermute(block, "area", pairs + [(b, a) for a, b in pairs])


def with_neighbours(first, second):
    return swap_pair(first, 1), swap_pair(second, 0)


def from_snap(block, distance):
    members = lax.axis_size("snap")
    return lax.ppermute(block, "snap", [(i, (i + distance) % members) for i in range(members)])


def from_all(block):
    return jnp.stack([from_snap(block, i) for i in range(1, lax.axis_size("snap"))])


def shape(dims, kind):
    return jax.ShapeDtypeStruct(dims, kind)


def on_device(
    phasor_readings,
    reading_error_spread,
    starting_voltages,
    derivative_pieces,
    derivative_tile_position,
    frontier_voltage_pieces,
    holder_line_order,
    hub_line_order,
    reciprocal_normal_operator,
):
    snaps, lines = phasor_readings.shape
    states = starting_voltages.shape[1]
    own = states // BLK
    measure = derivative_pieces.shape[0]
    ties_table = frontier_voltage_pieces[0]
    ties = ties_table.shape[1]
    slots = own + 2 * ties
    members = lax.axis_size("snap")
    areas = lax.axis_size("area")
    everything = snaps * members
    held = reciprocal_normal_operator.shape[0] // BLK
    place = derivative_tile_position[0].T
    cap = hub_line_order.shape[2]
    width = max(cap, BLK)
    chunks = areas * cap // width
    hub = hub_line_order[0].reshape(chunks, width)
    holder = holder_line_order[0].reshape(chunks, width)
    depth = (width // BLK) * snaps + 8

    rounded = starting_voltages.astype(BF16)
    rounded_others = from_all(rounded)
    message = call(
        pack_kernel,
        shape((chunks, depth, BLK), F32),
        [HBM, HBM, HBM],
        (phasor_readings, reading_error_spread.reshape(lines // BLK, BLK), hub),
        scratch=[
            pltpu.VMEM((snaps, lines), F32),
            pltpu.VMEM((lines // BLK, BLK), F32),
            pltpu.VMEM((chunks, width), jnp.int32),
            pltpu.VMEM((chunks, depth, BLK), F32),
            pltpu.SemaphoreType.DMA((3,)),
            pltpu.SemaphoreType.DMA((chunks,)),
        ],
        out_spec=HBM,
        mib=60,
        name="pack_readings",
    )
    each = width // cap
    if each > 1:
        message = message.reshape(chunks, depth, each, cap).transpose(0, 2, 1, 3)
        message = message.reshape(areas, depth, cap)
    message = lax.all_to_all(message, "area", split_axis=0, concat_axis=0, tiled=True)
    if each > 1:
        message = message.reshape(chunks, each, depth, cap).transpose(0, 2, 1, 3)
        message = message.reshape(chunks, depth, BLK)

    group, lane = call(
        inverse_kernel,
        (shape((lines // BLK, BLK), jnp.int32),) * 2,
        [VMEM],
        (holder,),
        flops=10**9,
        name="invert_order",
    )
    aug, first, second, x_sent = call(
        first_states_kernel,
        (
            shape((own, everything, BLK), BF16),
            shape((ties, everything, BLK), BF16),
            shape((ties, everything, BLK), BF16),
            [shape((snaps, held * BLK), F32)] * (members - 1),
        ),
        [VMEM, VMEM, VMEM, SMEM],
        (starting_voltages, rounded, rounded_others, ties_table),
        name="first_states",
    )
    x_others = [from_snap(sent, i) for i, sent in enumerate(x_sent, 1)]
    first, second = with_neighbours(first, second)
    guess = call(
        predict_kernel,
        shape((everything, lines), F32),
        [VMEM, VMEM, VMEM, VMEM, SMEM],
        (aug, first, second, derivative_pieces, place),
        scratch=[pltpu.VMEM((slots, everything, BLK), BF16)],
        flops=10**9,
        name="predict",
    )
    message, guess, x_others = lax.optimization_barrier((message, guess, x_others))
    halves = []
    for part in range(2):
        halves.append(
            call(
                functools.partial(unpack_kernel, part * (lines // BLK // 2)),
                (shape((snaps, lines // 2), F32), shape((1, lines // 2), F32)),
                [VMEM, VMEM, VMEM],
                (group, lane, message),
                scratch=[pltpu.VMEM((chunks * (width // BLK), BLK), F32)],
                flops=2 * 10**9,
                name="unpack_readings",
            )
        )
    readings = [half[0] for half in halves]
    variance = [half[1] for half in halves]
    reading_others = [from_all(half) for half in readings]
    grads = (
        shape((own, everything, BLK), F32),
        shape((ties, everything, BLK), F32),
        shape((ties, everything, BLK), F32),
    )
    total = pltpu.VMEM((slots, everything, BLK), F32)
    work = pltpu.VMEM((own, everything, BLK), F32)
    grad, first, second = call(
        pull_kernel,
        grads,
        [VMEM, [VMEM] * 2, [VMEM] * 2, [VMEM] * 2, VMEM, SMEM],
        (guess, readings, reading_others, variance, derivative_pieces, place),
        scratch=[total, pltpu.VMEM((everything, lines), BF16)],
        name="pull",
    )
    arrived = with_neighbours(first, second)
    boundary = shape((ties, everything, BLK), BF16)
    state, mine, first = call(
        first_update_kernel,
        (
            shape((held, everything, BLK), F32),
            shape((held, everything, BLK), BF16),
            boundary,
        ),
        [VMEM, VMEM, VMEM, SMEM, VMEM, VMEM, [VMEM] * (members - 1)],
        (
            grad, *arrived, ties_table, reciprocal_normal_operator,
            starting_voltages, x_others,
        ),
        scratch=[work],
        name="first_update",
    )
    others = [from_snap(mine, i) for i in range(1, members)]
    first = swap_pair(first, 1)
    firsts = [first] + [from_snap(first, i) for i in range(1, members)]
    aug, second = call(
        join_states_kernel,
        (shape((own, everything, BLK), BF16), boundary),
        [VMEM, [VMEM] * (members - 1), SMEM],
        (mine, others, ties_table),
        name="join_states",
    )
    second = swap_pair(second, 0)
    grad, first, second = call(
        predict_pull_kernel,
        (grads[0], boundary, boundary),
        [[VMEM] * members, VMEM, VMEM, [VMEM] * 2, [VMEM] * 2, [VMEM] * 2, VMEM, SMEM],
        (firsts, aug, second, readings, reading_others, variance, derivative_pieces, place),
        scratch=[
            pltpu.VMEM((slots, everything, BLK), BF16),
            pltpu.VMEM((everything, lines), F32),
            total,
            pltpu.VMEM((everything, lines), BF16),
        ],
        name="predict_pull",
    )
    first, second = with_neighbours(first, second)
    kept, sent = call(
        last_update_kernel,
        (shape((snaps, held * BLK), F32), shape((members - 1, snaps, held * BLK), F32)),
        [VMEM, VMEM, VMEM, SMEM, VMEM, VMEM],
        (grad, first, second, ties_table, reciprocal_normal_operator, state),
        scratch=[work],
        name="last_update",
    )
    arrived = jnp.stack([from_snap(sent[i - 1], i) for i in range(1, members)])
    return call(
        finish_kernel,
        shape((snaps, states), F32),
        [VMEM, VMEM],
        (kept, arrived),
        name="finish",
    )


def solution(mesh):
    placed = (
        P("snap", "area"),
        P("area"),
        P("snap", "area"),
        P("area", None, None, None),
        P("area", None, None),
        P("area", None, None),
        P("area", None, None),
        P("area", None, None),
        P(("area", "snap"), None),
    )
    return jax.shard_map(
        on_device, mesh=mesh, in_specs=placed, out_specs=P("snap", "area"), check_vma=False
    )
```

```python
import functools

import jax
import jax.numpy as jnp
from jax import lax
from jax.experimental import pallas as pl
from jax.experimental.pallas import tpu as pltpu
from jax.sharding import PartitionSpec as P

BLK = 128
ITERS = 2
F32 = jnp.float32
BF16 = jnp.bfloat16
NT = (((1,), (1,)), ((), ()))
VMEM = pl.BlockSpec(memory_space=pltpu.VMEM)
HBM = pl.BlockSpec(memory_space=pltpu.HBM)
SMEM = pl.BlockSpec(memory_space=pltpu.SMEM)


def call(kernel, outs, ins, args, scratch=(), flops=0, mib=12, out_spec=VMEM, name=None):
    return pl.pallas_call(
        kernel,
        out_shape=outs,
        in_specs=ins,
        out_specs=jax.tree.map(lambda _: out_spec, outs),
        scratch_shapes=list(scratch),
        compiler_params=pltpu.CompilerParams(vmem_limit_bytes=mib * 1024 * 1024),
        cost_estimate=pl.CostEstimate(
            flops=flops, bytes_accessed=0, transcendentals=0
        ),
        name=name,
    )(*args)


def lane_gather(values, lanes):
    return jnp.take_along_axis(values, lanes, axis=1, mode="promise_in_bounds")


def rows_iota(shape):
    return lax.broadcasted_iota(jnp.int32, shape, 0)


def pack_kernel(z_in, v_in, hub_in, out, z_ref, v_ref, hub_ref, out_ref, sems, out_sems):
    copies = [
        pltpu.make_async_copy(source, target, sems.at[i])
        for i, (source, target) in enumerate(((hub_in, hub_ref), (z_in, z_ref), (v_in, v_ref)))
    ]
    for copy in copies:
        copy.start()
    for copy in copies:
        copy.wait()
    snaps, lines = z_ref.shape
    blocks = lines // BLK
    chunks, width = hub_ref.shape
    groups = width // BLK
    for d in range(chunks):
        tail = jnp.zeros((8, BLK), F32)
        for g in range(groups):
            slot = hub_ref[d : d + 1, g * BLK : (g + 1) * BLK]
            high = jnp.right_shift(slot, 7)
            low = jnp.bitwise_and(slot, 127)
            lanes = jnp.broadcast_to(low, (snaps, BLK))
            block_of = jnp.broadcast_to(high, (snaps, BLK))
            picked = jnp.zeros((snaps, BLK), F32)
            for b in range(blocks):
                found = lane_gather(z_ref[:, b * BLK : (b + 1) * BLK], lanes)
                picked = jnp.where(block_of == b, found, picked)
            out_ref[d, g * snaps : (g + 1) * snaps, :] = picked
            found = lane_gather(v_ref[...], jnp.broadcast_to(low, (blocks, BLK)))
            mine = rows_iota((blocks, BLK)) == high
            variance = jnp.sum(jnp.where(mine, found, 0.0), axis=0, keepdims=True)
            tail = jnp.where(rows_iota((8, BLK)) == g, variance, tail)
        out_ref[d, groups * snaps :, :] = tail
        pltpu.make_async_copy(out_ref.at[d], out.at[d], out_sems.at[d]).start()
    for d in range(chunks):
        pltpu.make_async_copy(out_ref.at[d], out.at[d], out_sems.at[d]).wait()


def inverse_kernel(own_ref, group_ref, lane_ref):
    chunks, width = own_ref.shape
    blocks = group_ref.shape[0]
    groups = width // BLK
    total = jnp.zeros((2 * blocks, BLK), F32)
    lane = lax.broadcasted_iota(jnp.int32, (2 * blocks, width), 1)
    row = rows_iota((2 * blocks, width))
    in_group = jnp.bitwise_and(lane, 127)
    group_in = jnp.right_shift(lane, 7)
    for d in range(chunks):
        owned = own_ref[d : d + 1, :]
        high = jnp.right_shift(owned, 7)
        low = jnp.bitwise_and(owned, 127)
        label = jnp.where(row < blocks, group_in + d * groups, in_group)
        hit = jnp.bitwise_and(row, blocks - 1) == high
        left = jnp.where(hit, label.astype(F32), 0.0).astype(BF16)
        right = jnp.where(rows_iota((BLK, width)) == low, 1.0, 0.0).astype(BF16)
        total += lax.dot_general(left, right, NT, preferred_element_type=F32)
    group_ref[...] = total[:blocks].astype(jnp.int32)
    lane_ref[...] = total[blocks:].astype(jnp.int32)


def unpack_kernel(start, group_ref, lane_ref, message_ref, z_ref, v_ref, variance_ref):
    snaps, lines = z_ref.shape
    chunks = message_ref.shape[0]
    groups = (message_ref.shape[1] - 8) // snaps
    total = chunks * groups
    for d in range(chunks):
        variance_ref[d * groups : (d + 1) * groups, :] = message_ref[d, groups * snaps :, :][:groups]
    for b in range(lines // BLK):
        group = group_ref[start + b : start + b + 1, :]
        lane = lane_ref[start + b : start + b + 1, :]
        lanes = jnp.broadcast_to(lane, (snaps, BLK))
        group_of = jnp.broadcast_to(group, (snaps, BLK))
        picked = jnp.zeros((snaps, BLK), F32)
        for g in range(total):
            rows = slice(g % groups * snaps, (g % groups + 1) * snaps)
            found = lane_gather(message_ref[g // groups, rows, :], lanes)
            picked = jnp.where(group_of == g, found, picked)
        columns = slice(b * BLK, (b + 1) * BLK)
        z_ref[:, columns] = picked
        found = lane_gather(variance_ref[...], jnp.broadcast_to(lane, (total, BLK)))
        mine = rows_iota((total, BLK)) == group
        v_ref[:, columns] = jnp.sum(jnp.where(mine, found, 0.0), axis=0, keepdims=True)


def split(ref):
    return [ref.at[i] for i in range(ref.shape[0])]


def parity():
    return 1 - lax.rem(lax.axis_index("area"), 2)


def pick(blocks_ref, listing_ref, side, out_ref, start=0):
    held = blocks_ref.shape[0]
    for t in range(out_ref.shape[0]):
        b = listing_ref[side, t]
        at = b - start
        block = blocks_ref[jnp.clip(at, 0, held - 1)]
        here = (b >= 0) & (at >= 0) & (at < held)
        out_ref[t] = jnp.where(here, block, jnp.zeros_like(block))


def first_states_kernel(own_ref, others_ref, ties_ref, aug_ref, first_ref, second_ref):
    snaps = own_ref.shape[0]
    for b in range(aug_ref.shape[0]):
        columns = slice(b * BLK, (b + 1) * BLK)
        aug_ref[b, :snaps] = own_ref[:, columns]
        for i in range(others_ref.shape[0]):
            aug_ref[b, (i + 1) * snaps : (i + 2) * snaps] = others_ref[i, :, columns]
    pick(aug_ref, ties_ref, 1 - parity(), first_ref)
    pick(aug_ref, ties_ref, parity(), second_ref)


def slots_into(slots_ref, aug_ref, first, second_ref):
    own = aug_ref.shape[0]
    ties = second_ref.shape[0]
    slots_ref[:own] = aug_ref[...]
    slots_ref[pl.ds(own + ties * (1 - parity()), ties)] = first
    slots_ref[pl.ds(own + ties * parity(), ties)] = second_ref[...]


def reordered(ref, distance, members):
    snaps = ref.shape[1] // members
    order = [(n + distance) % members for n in range(members)]
    return jnp.concatenate([ref[:, j * snaps : (j + 1) * snaps] for j in order], axis=1)


def join_states_kernel(mine_ref, others_refs, ties_ref, aug_ref, second_ref):
    members = len(others_refs) + 1
    held = mine_ref.shape[0]
    me = lax.axis_index("snap")
    aug_ref[pl.ds(me * held, held)] = mine_ref[...]
    for i, ref in enumerate(others_refs, 1):
        at = lax.rem(me + members - i, members) * held
        aug_ref[pl.ds(at, held)] = reordered(ref, i, members)
    pick(aug_ref, ties_ref, parity(), second_ref)


def predicted(j, slots_ref, tiles_ref, place_ref):
    touched = tiles_ref.shape[1]
    chosen = jnp.concatenate([slots_ref[place_ref[k, j]] for k in range(touched)], axis=1)
    weights = jnp.concatenate([tiles_ref[j, k] for k in range(touched)], axis=1)
    return lax.dot_general(chosen, weights, NT, preferred_element_type=F32)


def predict_kernel(aug_ref, first_ref, second_ref, tiles_ref, place_ref, out_ref, slots_ref):
    slots_into(slots_ref, aug_ref, first_ref[...], second_ref)
    predict(tiles_ref, place_ref, out_ref, slots_ref)


def predict(tiles_ref, place_ref, out_ref, slots_ref):
    for j in range(tiles_ref.shape[0]):
        out_ref[:, j * BLK : (j + 1) * BLK] = predicted(j, slots_ref, tiles_ref, place_ref)


def weigh(j, guess, z_refs, others_refs, v_refs):
    each = z_refs[0].shape[1] // BLK
    z_ref, others_ref, v_ref = z_refs[j // each], others_refs[j // each], v_refs[j // each]
    columns = slice(j % each * BLK, (j % each + 1) * BLK)
    readings = [z_ref[:, columns]] + [o[:, columns] for o in split(others_ref)]
    resid = jnp.concatenate(readings, axis=0) - guess
    spread = jnp.sum(resid * resid, axis=0, keepdims=True) / resid.shape[0]
    return (resid / (v_ref[:, columns] + spread)).astype(BF16)


def pull(weighted_ref, tiles_ref, place_ref, total_ref, own_ref, first_ref, second_ref):
    total_ref[...] = jnp.zeros_like(total_ref)
    touched = tiles_ref.shape[1]
    for j in range(tiles_ref.shape[0]):
        weighted = weighted_ref[:, j * BLK : (j + 1) * BLK]
        weights = jnp.concatenate([tiles_ref[j, k] for k in range(touched)], axis=1)
        part = jnp.dot(weighted, weights, preferred_element_type=F32)
        for k in range(touched):
            n = place_ref[k, j]
            total_ref[n] += part[:, k * BLK : (k + 1) * BLK]
    own = own_ref.shape[0]
    ties = first_ref.shape[0]
    own_ref[...] = total_ref[:own]
    first = total_ref[pl.ds(own + ties * (1 - parity()), ties)]
    second = total_ref[pl.ds(own + ties * parity(), ties)]
    first_ref[...] = first.astype(first_ref.dtype)
    second_ref[...] = second.astype(second_ref.dtype)


def pull_kernel(
    guess_ref, z_refs, others_refs, v_refs, tiles_ref, place_ref, own_ref, first_ref, second_ref,
    total_ref, weighted_ref,
):
    for j in range(tiles_ref.shape[0]):
        columns = slice(j * BLK, (j + 1) * BLK)
        weighted_ref[:, columns] = weigh(j, guess_ref[:, columns], z_refs, others_refs, v_refs)
    pull(weighted_ref, tiles_ref, place_ref, total_ref, own_ref, first_ref, second_ref)


def predict_pull_kernel(
    first_refs, aug_ref, second_in_ref, z_refs, others_refs, v_refs, tiles_ref, place_ref,
    own_ref, first_ref, second_ref, slots_ref, guess_ref, total_ref, weighted_ref,
):
    parts = [reordered(ref, i, len(first_refs)) for i, ref in enumerate(first_refs)]
    slots_into(slots_ref, aug_ref, sum(parts[1:], parts[0]), second_in_ref)
    predict(tiles_ref, place_ref, guess_ref, slots_ref)
    pull_kernel(
        guess_ref, z_refs, others_refs, v_refs, tiles_ref, place_ref, own_ref, first_ref, second_ref,
        total_ref, weighted_ref,
    )


def full_gradient(grad_ref, back_first_ref, back_second_ref, ties_ref, work_ref):
    work_ref[...] = grad_ref[...]
    for side, back_ref in ((1 - parity(), back_first_ref), (parity(), back_second_ref)):
        for t in range(back_ref.shape[0]):
            b = ties_ref[side, t]

            @pl.when(b >= 0)
            def _(b=b, t=t, back_ref=back_ref):
                work_ref[b] += back_ref[t].astype(F32)

    return jnp.concatenate([work_ref[b].astype(BF16) for b in range(work_ref.shape[0])], axis=1)


def updates(gradient, gain_ref):
    step = min(2 * BLK, gain_ref.shape[0])
    for at in range(0, gain_ref.shape[0], step):
        rows = gain_ref[at : at + step, :]
        update = lax.dot_general(gradient, rows, NT, preferred_element_type=F32)
        for i in range(step // BLK):
            yield at // BLK + i, update[:, i * BLK : (i + 1) * BLK]


def first_update_kernel(
    grad_ref, back_first_ref, back_second_ref, ties_ref, gain_ref, x_ref, x_others_refs,
    kept_ref, given_refs, message_ref, first_ref, work_ref,
):
    gradient = full_gradient(grad_ref, back_first_ref, back_second_ref, ties_ref, work_ref)
    held, snaps = kept_ref.shape[:2]
    me = lax.axis_index("snap")
    for i, update in updates(gradient, gain_ref):
        columns = pl.ds(pl.multiple_of((me * held + i) * BLK, BLK), BLK)
        parts = [x_ref[:, columns]] + [o[:, i * BLK : (i + 1) * BLK] for o in x_others_refs]
        state = jnp.concatenate(parts, axis=0) + update
        kept_ref[i] = state[:snaps]
        for j, given_ref in enumerate(given_refs, 1):
            given_ref[i] = state[j * snaps : (j + 1) * snaps]
        message_ref[i] = state.astype(BF16)
    pick(message_ref, ties_ref, 1 - parity(), first_ref, me * held)


def last_update_kernel(
    grad_ref, back_first_ref, back_second_ref, ties_ref, gain_ref, kept_ref, mine_ref, sent_refs, work_ref
):
    gradient = full_gradient(grad_ref, back_first_ref, back_second_ref, ties_ref, work_ref)
    snaps = mine_ref.shape[0]
    for i, update in updates(gradient, gain_ref):
        columns = slice(i * BLK, (i + 1) * BLK)
        mine_ref[:, columns] = kept_ref[i] + update[:snaps]
        for j, sent_ref in enumerate(sent_refs, 1):
            sent_ref[:, columns] = update[j * snaps : (j + 1) * snaps].astype(BF16)


def finish_kernel(mine_ref, states_refs, updates_refs, out_ref):
    width = mine_ref.shape[1]
    members = len(states_refs) + 1
    me = lax.axis_index("snap")
    out_ref[:, pl.ds(pl.multiple_of(me * width, BLK), width)] = mine_ref[...]
    for i, (state_ref, update_ref) in enumerate(zip(states_refs, updates_refs), 1):
        at = lax.rem(me + members - i, members) * width
        for b in range(width // BLK):
            update = update_ref[:, b * BLK : (b + 1) * BLK].astype(F32)
            columns = pl.ds(pl.multiple_of(at + b * BLK, BLK), BLK)
            out_ref[:, columns] = state_ref[b] + update


def swap_pair(block, start):
    pairs = [(i, i + 1) for i in range(start, lax.axis_size("area") - 1, 2)]
    return lax.ppermute(block, "area", pairs + [(b, a) for a, b in pairs])


def with_neighbours(first, second):
    return swap_pair(first, 1), swap_pair(second, 0)


def from_snap(block, distance):
    members = lax.axis_size("snap")
    return lax.ppermute(block, "snap", [(i, (i + distance) % members) for i in range(members)])


def from_all(block):
    return jnp.stack([from_snap(block, i) for i in range(1, lax.axis_size("snap"))])


def shape(dims, kind):
    return jax.ShapeDtypeStruct(dims, kind)


def on_device(
    phasor_readings,
    reading_error_spread,
    starting_voltages,
    derivative_pieces,
    derivative_tile_position,
    frontier_voltage_pieces,
    holder_line_order,
    hub_line_order,
    reciprocal_normal_operator,
):
    snaps, lines = phasor_readings.shape
    states = starting_voltages.shape[1]
    own = states // BLK
    measure = derivative_pieces.shape[0]
    ties_table = frontier_voltage_pieces[0]
    ties = ties_table.shape[1]
    slots = own + 2 * ties
    members = lax.axis_size("snap")
    areas = lax.axis_size("area")
    everything = snaps * members
    held = reciprocal_normal_operator.shape[0] // BLK
    place = derivative_tile_position[0].T
    cap = hub_line_order.shape[2]
    width = max(cap, BLK)
    chunks = areas * cap // width
    hub = hub_line_order[0].reshape(chunks, width)
    holder = holder_line_order[0].reshape(chunks, width)
    depth = (width // BLK) * snaps + 8

    rounded = starting_voltages.astype(BF16)
    rounded_others = from_all(rounded)
    message = call(
        pack_kernel,
        shape((chunks, depth, BLK), F32),
        [HBM, HBM, HBM],
        (phasor_readings, reading_error_spread.reshape(lines // BLK, BLK), hub),
        scratch=[
            pltpu.VMEM((snaps, lines), F32),
            pltpu.VMEM((lines // BLK, BLK), F32),
            pltpu.VMEM((chunks, width), jnp.int32),
            pltpu.VMEM((chunks, depth, BLK), F32),
            pltpu.SemaphoreType.DMA((3,)),
            pltpu.SemaphoreType.DMA((chunks,)),
        ],
        out_spec=HBM,
        mib=60,
        name="pack_readings",
    )
    each = width // cap
    if each > 1:
        message = message.reshape(chunks, depth, each, cap).transpose(0, 2, 1, 3)
        message = message.reshape(areas, depth, cap)
    message = lax.all_to_all(message, "area", split_axis=0, concat_axis=0, tiled=True)
    if each > 1:
        message = message.reshape(chunks, each, depth, cap).transpose(0, 2, 1, 3)
        message = message.reshape(chunks, depth, BLK)

    group, lane = call(
        inverse_kernel,
        (shape((lines // BLK, BLK), jnp.int32),) * 2,
        [VMEM],
        (holder,),
        flops=10**9,
        name="invert_order",
    )
    boundary = shape((ties, everything, BLK), BF16)
    aug, first, second = call(
        first_states_kernel,
        (
            shape((own, everything, BLK), BF16),
            boundary,
            boundary,
        ),
        [VMEM, VMEM, SMEM],
        (rounded, rounded_others, ties_table),
        name="first_states",
    )
    first, second = with_neighbours(first, second)
    guess = call(
        predict_kernel,
        shape((everything, lines), F32),
        [VMEM, VMEM, VMEM, VMEM, SMEM],
        (aug, first, second, derivative_pieces, place),
        scratch=[pltpu.VMEM((slots, everything, BLK), BF16)],
        flops=10**9,
        name="predict",
    )
    message, guess = lax.optimization_barrier((message, guess))
    halves = []
    for part in range(2):
        halves.append(
            call(
                functools.partial(unpack_kernel, part * (lines // BLK // 2)),
                (shape((snaps, lines // 2), F32), shape((1, lines // 2), F32)),
                [VMEM, VMEM, VMEM],
                (group, lane, message),
                scratch=[pltpu.VMEM((chunks * (width // BLK), BLK), F32)],
                flops=2 * 10**9,
                name="unpack_readings",
            )
        )
    readings = [half[0] for half in halves]
    variance = [half[1] for half in halves]
    reading_others = [from_all(half) for half in readings]
    grads = (
        shape((own, everything, BLK), F32),
        boundary,
        boundary,
    )
    total = pltpu.VMEM((slots, everything, BLK), F32)
    work = pltpu.VMEM((own, everything, BLK), F32)
    grad, first, second = call(
        pull_kernel,
        grads,
        [VMEM, [VMEM] * 2, [VMEM] * 2, [VMEM] * 2, VMEM, SMEM],
        (guess, readings, reading_others, variance, derivative_pieces, place),
        scratch=[total, pltpu.VMEM((everything, lines), BF16)],
        name="pull",
    )
    x_late, first, second = lax.optimization_barrier((starting_voltages, first, second))
    arrived = with_neighbours(first, second)
    me = lax.axis_index("snap")
    x_others = [
        from_snap(
            lax.dynamic_slice_in_dim(x_late, (me + i) % members * held * BLK, held * BLK, 1), i
        )
        for i in range(1, members)
    ]
    kept, given, mine, first = call(
        first_update_kernel,
        (
            shape((held, snaps, BLK), F32),
            [shape((held, snaps, BLK), F32)] * (members - 1),
            shape((held, everything, BLK), BF16),
            boundary,
        ),
        [VMEM, VMEM, VMEM, SMEM, VMEM, VMEM, [VMEM] * (members - 1)],
        (
            grad, *arrived, ties_table, reciprocal_normal_operator,
            starting_voltages, x_others,
        ),
        scratch=[work],
        name="first_update",
    )
    others = [from_snap(mine, i) for i in range(1, members)]
    first = swap_pair(first, 1)
    firsts = [first] + [from_snap(first, i) for i in range(1, members)]
    aug, second = call(
        join_states_kernel,
        (shape((own, everything, BLK), BF16), boundary),
        [VMEM, [VMEM] * (members - 1), SMEM],
        (mine, others, ties_table),
        name="join_states",
    )
    second = swap_pair(second, 0)
    grad, first, second = call(
        predict_pull_kernel,
        grads,
        [[VMEM] * members, VMEM, VMEM, [VMEM] * 2, [VMEM] * 2, [VMEM] * 2, VMEM, SMEM],
        (firsts, aug, second, readings, reading_others, variance, derivative_pieces, place),
        scratch=[
            pltpu.VMEM((slots, everything, BLK), BF16),
            pltpu.VMEM((everything, lines), F32),
            total,
            pltpu.VMEM((everything, lines), BF16),
        ],
        name="predict_pull",
    )
    given, first, second = lax.optimization_barrier((given, first, second))
    first, second = with_neighbours(first, second)
    states_in = [from_snap(block, i) for i, block in enumerate(given, 1)]
    mine, sent = call(
        last_update_kernel,
        (
            shape((snaps, held * BLK), F32),
            [shape((snaps, held * BLK), BF16)] * (members - 1),
        ),
        [VMEM, VMEM, VMEM, SMEM, VMEM, VMEM],
        (grad, first, second, ties_table, reciprocal_normal_operator, kept),
        scratch=[work],
        name="last_update",
    )
    return call(
        finish_kernel,
        shape((snaps, states), F32),
        [VMEM, [VMEM] * (members - 1), [VMEM] * (members - 1)],
        (mine, states_in, [from_snap(block, i) for i, block in enumerate(sent, 1)]),
        name="finish",
    )


def solution(mesh):
    placed = (
        P("snap", "area"),
        P("area"),
        P("snap", "area"),
        P("area", None, None, None),
        P("area", None, None),
        P("area", None, None),
        P("area", None, None),
        P("area", None, None),
        P(("area", "snap"), None),
    )
    return jax.shard_map(
        on_device, mesh=mesh, in_specs=placed, out_specs=P("snap", "area"), check_vma=False
    )
```

```python
import functools

import jax
import jax.numpy as jnp
from jax import lax
from jax.experimental import pallas as pl
from jax.experimental.pallas import tpu as pltpu
from jax.sharding import PartitionSpec as P

BLK = 128
ITERS = 2
F32 = jnp.float32
BF16 = jnp.bfloat16
NT = (((1,), (1,)), ((), ()))
VMEM = pl.BlockSpec(memory_space=pltpu.VMEM)
HBM = pl.BlockSpec(memory_space=pltpu.HBM)
SMEM = pl.BlockSpec(memory_space=pltpu.SMEM)


def call(kernel, outs, ins, args, scratch=(), flops=0, mib=12, out_spec=None, name=None):
    return pl.pallas_call(
        kernel,
        out_shape=outs,
        in_specs=ins,
        out_specs=jax.tree.map(lambda _: VMEM, outs) if out_spec is None else out_spec,
        scratch_shapes=list(scratch),
        compiler_params=pltpu.CompilerParams(vmem_limit_bytes=mib * 1024 * 1024),
        cost_estimate=pl.CostEstimate(
            flops=flops, bytes_accessed=0, transcendentals=0
        ),
        name=name,
    )(*args)


def lane_gather(values, lanes):
    return jnp.take_along_axis(values, lanes, axis=1, mode="promise_in_bounds")


def rows_iota(shape):
    return lax.broadcasted_iota(jnp.int32, shape, 0)


def pack_kernel(
    z_in, v_in, hub_in, x_in, out, rounded_ref, sent_refs,
    z_ref, v_ref, hub_ref, x_ref, out_ref, sems, out_sems, sent_sems,
):
    pairs = ((hub_in, hub_ref), (z_in, z_ref), (v_in, v_ref), (x_in, x_ref))
    copies = [
        pltpu.make_async_copy(source, target, sems.at[i])
        for i, (source, target) in enumerate(pairs)
    ]
    members = len(sent_refs) + 1
    part = x_in.shape[1] // members
    sends = []
    for i, sent_ref in enumerate(sent_refs, 1):
        at = lax.rem(lax.axis_index("snap") + i, members) * part
        source = x_in.at[:, pl.ds(pl.multiple_of(at, BLK), part)]
        sends.append(pltpu.make_async_copy(source, sent_ref, sent_sems.at[i - 1]))
    for copy in copies + sends:
        copy.start()
    for copy in copies:
        copy.wait()
    rounded_ref[...] = x_ref[...].astype(BF16)
    snaps, lines = z_ref.shape
    blocks = lines // BLK
    chunks, width = hub_ref.shape
    groups = width // BLK
    for d in range(chunks):
        tail = jnp.zeros((8, BLK), F32)
        for g in range(groups):
            slot = hub_ref[d : d + 1, g * BLK : (g + 1) * BLK]
            high = jnp.right_shift(slot, 7)
            low = jnp.bitwise_and(slot, 127)
            lanes = jnp.broadcast_to(low, (snaps, BLK))
            block_of = jnp.broadcast_to(high, (snaps, BLK))
            picked = jnp.zeros((snaps, BLK), F32)
            for b in range(blocks):
                found = lane_gather(z_ref[:, b * BLK : (b + 1) * BLK], lanes)
                picked = jnp.where(block_of == b, found, picked)
            out_ref[d, g * snaps : (g + 1) * snaps, :] = picked
            found = lane_gather(v_ref[...], jnp.broadcast_to(low, (blocks, BLK)))
            mine = rows_iota((blocks, BLK)) == high
            variance = jnp.sum(jnp.where(mine, found, 0.0), axis=0, keepdims=True)
            tail = jnp.where(rows_iota((8, BLK)) == g, variance, tail)
        out_ref[d, groups * snaps :, :] = tail
        pltpu.make_async_copy(out_ref.at[d], out.at[d], out_sems.at[d]).start()
    for d in range(chunks):
        pltpu.make_async_copy(out_ref.at[d], out.at[d], out_sems.at[d]).wait()
    for copy in sends:
        copy.wait()


def inverse_kernel(own_ref, group_ref, lane_ref):
    chunks, width = own_ref.shape
    blocks = group_ref.shape[0]
    groups = width // BLK
    total = jnp.zeros((2 * blocks, BLK), F32)
    lane = lax.broadcasted_iota(jnp.int32, (2 * blocks, width), 1)
    row = rows_iota((2 * blocks, width))
    in_group = jnp.bitwise_and(lane, 127)
    group_in = jnp.right_shift(lane, 7)
    for d in range(chunks):
        owned = own_ref[d : d + 1, :]
        high = jnp.right_shift(owned, 7)
        low = jnp.bitwise_and(owned, 127)
        label = jnp.where(row < blocks, group_in + d * groups, in_group)
        hit = jnp.bitwise_and(row, blocks - 1) == high
        left = jnp.where(hit, label.astype(F32), 0.0).astype(BF16)
        right = jnp.where(rows_iota((BLK, width)) == low, 1.0, 0.0).astype(BF16)
        total += lax.dot_general(left, right, NT, preferred_element_type=F32)
    group_ref[...] = total[:blocks].astype(jnp.int32)
    lane_ref[...] = total[blocks:].astype(jnp.int32)


def unpack_kernel(start, group_ref, lane_ref, message_ref, z_ref, v_ref, variance_ref):
    snaps, lines = z_ref.shape
    chunks = message_ref.shape[0]
    groups = (message_ref.shape[1] - 8) // snaps
    total = chunks * groups
    for d in range(chunks):
        variance_ref[d * groups : (d + 1) * groups, :] = message_ref[d, groups * snaps :, :][:groups]
    for b in range(lines // BLK):
        group = group_ref[start + b : start + b + 1, :]
        lane = lane_ref[start + b : start + b + 1, :]
        lanes = jnp.broadcast_to(lane, (snaps, BLK))
        group_of = jnp.broadcast_to(group, (snaps, BLK))
        picked = jnp.zeros((snaps, BLK), F32)
        for g in range(total):
            rows = slice(g % groups * snaps, (g % groups + 1) * snaps)
            found = lane_gather(message_ref[g // groups, rows, :], lanes)
            picked = jnp.where(group_of == g, found, picked)
        columns = slice(b * BLK, (b + 1) * BLK)
        z_ref[:, columns] = picked
        found = lane_gather(variance_ref[...], jnp.broadcast_to(lane, (total, BLK)))
        mine = rows_iota((total, BLK)) == group
        v_ref[:, columns] = jnp.sum(jnp.where(mine, found, 0.0), axis=0, keepdims=True)


def split(ref):
    return [ref.at[i] for i in range(ref.shape[0])]


def parity():
    return 1 - lax.rem(lax.axis_index("area"), 2)


def pick(blocks_ref, listing_ref, side, out_ref, start=0):
    held = blocks_ref.shape[0]
    for t in range(out_ref.shape[0]):
        b = listing_ref[side, t]
        at = b - start
        block = blocks_ref[jnp.clip(at, 0, held - 1)]
        here = (b >= 0) & (at >= 0) & (at < held)
        out_ref[t] = jnp.where(here, block, jnp.zeros_like(block))


def first_states_kernel(own_ref, others_ref, ties_ref, aug_ref, first_ref, second_ref):
    snaps = own_ref.shape[0]
    for b in range(aug_ref.shape[0]):
        columns = slice(b * BLK, (b + 1) * BLK)
        aug_ref[b, :snaps] = own_ref[:, columns]
        for i in range(others_ref.shape[0]):
            aug_ref[b, (i + 1) * snaps : (i + 2) * snaps] = others_ref[i, :, columns]
    pick(aug_ref, ties_ref, 1 - parity(), first_ref)
    pick(aug_ref, ties_ref, parity(), second_ref)


def slots_into(slots_ref, aug_ref, first, second_ref):
    own = aug_ref.shape[0]
    ties = second_ref.shape[0]
    slots_ref[:own] = aug_ref[...]
    slots_ref[pl.ds(own + ties * (1 - parity()), ties)] = first
    slots_ref[pl.ds(own + ties * parity(), ties)] = second_ref[...]


def reordered(ref, distance, members):
    snaps = ref.shape[1] // members
    order = [(n + distance) % members for n in range(members)]
    return jnp.concatenate([ref[:, j * snaps : (j + 1) * snaps] for j in order], axis=1)


def join_states_kernel(mine_ref, others_refs, ties_ref, aug_ref, second_ref):
    members = len(others_refs) + 1
    held = mine_ref.shape[0]
    me = lax.axis_index("snap")
    aug_ref[pl.ds(me * held, held)] = mine_ref[...]
    for i, ref in enumerate(others_refs, 1):
        at = lax.rem(me + members - i, members) * held
        aug_ref[pl.ds(at, held)] = reordered(ref, i, members)
    pick(aug_ref, ties_ref, parity(), second_ref)


def predicted(j, slots_ref, tiles_ref, place_ref):
    touched = tiles_ref.shape[1]
    chosen = jnp.concatenate([slots_ref[place_ref[k, j]] for k in range(touched)], axis=1)
    weights = jnp.concatenate([tiles_ref[j, k] for k in range(touched)], axis=1)
    return lax.dot_general(chosen, weights, NT, preferred_element_type=F32)


def predict_kernel(aug_ref, first_ref, second_ref, tiles_ref, place_ref, out_ref, slots_ref):
    slots_into(slots_ref, aug_ref, first_ref[...], second_ref)
    predict(tiles_ref, place_ref, out_ref, slots_ref)


def predict(tiles_ref, place_ref, out_ref, slots_ref):
    for j in range(tiles_ref.shape[0]):
        out_ref[:, j * BLK : (j + 1) * BLK] = predicted(j, slots_ref, tiles_ref, place_ref)


def weigh(j, guess, z_refs, others_refs, v_refs):
    each = z_refs[0].shape[1] // BLK
    z_ref, others_ref, v_ref = z_refs[j // each], others_refs[j // each], v_refs[j // each]
    columns = slice(j % each * BLK, (j % each + 1) * BLK)
    readings = [z_ref[:, columns]] + [o[:, columns] for o in split(others_ref)]
    resid = jnp.concatenate(readings, axis=0) - guess
    spread = jnp.sum(resid * resid, axis=0, keepdims=True) / resid.shape[0]
    return (resid / (v_ref[:, columns] + spread)).astype(BF16)


def pull(weighted_ref, tiles_ref, place_ref, total_ref, own_ref, first_ref, second_ref):
    total_ref[...] = jnp.zeros_like(total_ref)
    touched = tiles_ref.shape[1]
    for j in range(tiles_ref.shape[0]):
        weighted = weighted_ref[:, j * BLK : (j + 1) * BLK]
        weights = jnp.concatenate([tiles_ref[j, k] for k in range(touched)], axis=1)
        part = jnp.dot(weighted, weights, preferred_element_type=F32)
        for k in range(touched):
            n = place_ref[k, j]
            total_ref[n] += part[:, k * BLK : (k + 1) * BLK]
    own = own_ref.shape[0]
    ties = first_ref.shape[0]
    own_ref[...] = total_ref[:own]
    first = total_ref[pl.ds(own + ties * (1 - parity()), ties)]
    second = total_ref[pl.ds(own + ties * parity(), ties)]
    first_ref[...] = first.astype(first_ref.dtype)
    second_ref[...] = second.astype(second_ref.dtype)


def pull_kernel(
    guess_ref, z_refs, others_refs, v_refs, tiles_ref, place_ref, own_ref, first_ref, second_ref,
    total_ref, weighted_ref,
):
    for j in range(tiles_ref.shape[0]):
        columns = slice(j * BLK, (j + 1) * BLK)
        weighted_ref[:, columns] = weigh(j, guess_ref[:, columns], z_refs, others_refs, v_refs)
    pull(weighted_ref, tiles_ref, place_ref, total_ref, own_ref, first_ref, second_ref)


def predict_pull_kernel(
    first_refs, aug_ref, second_in_ref, z_refs, others_refs, v_refs, tiles_ref, place_ref,
    own_ref, first_ref, second_ref, slots_ref, guess_ref, total_ref, weighted_ref,
):
    parts = [reordered(ref, i, len(first_refs)) for i, ref in enumerate(first_refs)]
    slots_into(slots_ref, aug_ref, sum(parts[1:], parts[0]), second_in_ref)
    predict(tiles_ref, place_ref, guess_ref, slots_ref)
    pull_kernel(
        guess_ref, z_refs, others_refs, v_refs, tiles_ref, place_ref, own_ref, first_ref, second_ref,
        total_ref, weighted_ref,
    )


def full_gradient(grad_ref, back_first_ref, back_second_ref, ties_ref, work_ref):
    work_ref[...] = grad_ref[...]
    for side, back_ref in ((1 - parity(), back_first_ref), (parity(), back_second_ref)):
        for t in range(back_ref.shape[0]):
            b = ties_ref[side, t]

            @pl.when(b >= 0)
            def _(b=b, t=t, back_ref=back_ref):
                work_ref[b] += back_ref[t].astype(F32)

    return jnp.concatenate([work_ref[b].astype(BF16) for b in range(work_ref.shape[0])], axis=1)


def updates(gradient, gain_ref):
    step = min(2 * BLK, gain_ref.shape[0])
    for at in range(0, gain_ref.shape[0], step):
        rows = gain_ref[at : at + step, :]
        update = lax.dot_general(gradient, rows, NT, preferred_element_type=F32)
        for i in range(step // BLK):
            yield at // BLK + i, update[:, i * BLK : (i + 1) * BLK]


def first_update_kernel(
    grad_ref, back_first_ref, back_second_ref, ties_ref, gain_ref, x_ref, x_others_refs,
    kept_ref, given_refs, message_ref, first_ref, work_ref,
):
    gradient = full_gradient(grad_ref, back_first_ref, back_second_ref, ties_ref, work_ref)
    held, snaps = kept_ref.shape[:2]
    me = lax.axis_index("snap")
    for i, update in updates(gradient, gain_ref):
        columns = pl.ds(pl.multiple_of((me * held + i) * BLK, BLK), BLK)
        parts = [x_ref[:, columns]] + [o[:, i * BLK : (i + 1) * BLK] for o in x_others_refs]
        state = jnp.concatenate(parts, axis=0) + update
        kept_ref[i] = state[:snaps]
        for j, given_ref in enumerate(given_refs, 1):
            given_ref[i] = state[j * snaps : (j + 1) * snaps]
        message_ref[i] = state.astype(BF16)
    pick(message_ref, ties_ref, 1 - parity(), first_ref, me * held)


def last_update_kernel(
    grad_ref, back_first_ref, back_second_ref, ties_ref, gain_ref, kept_ref, mine_ref, sent_refs, work_ref
):
    gradient = full_gradient(grad_ref, back_first_ref, back_second_ref, ties_ref, work_ref)
    snaps = mine_ref.shape[0]
    for i, update in updates(gradient, gain_ref):
        columns = slice(i * BLK, (i + 1) * BLK)
        mine_ref[:, columns] = kept_ref[i] + update[:snaps]
        for j, sent_ref in enumerate(sent_refs, 1):
            sent_ref[:, columns] = update[j * snaps : (j + 1) * snaps].astype(BF16)


def finish_kernel(mine_ref, states_refs, updates_refs, out_ref):
    width = mine_ref.shape[1]
    members = len(states_refs) + 1
    me = lax.axis_index("snap")
    out_ref[:, pl.ds(pl.multiple_of(me * width, BLK), width)] = mine_ref[...]
    for i, (state_ref, update_ref) in enumerate(zip(states_refs, updates_refs), 1):
        at = lax.rem(me + members - i, members) * width
        for b in range(width // BLK):
            update = update_ref[:, b * BLK : (b + 1) * BLK].astype(F32)
            columns = pl.ds(pl.multiple_of(at + b * BLK, BLK), BLK)
            out_ref[:, columns] = state_ref[b] + update


def swap_pair(block, start):
    pairs = [(i, i + 1) for i in range(start, lax.axis_size("area") - 1, 2)]
    return lax.ppermute(block, "area", pairs + [(b, a) for a, b in pairs])


def with_neighbours(first, second):
    return swap_pair(first, 1), swap_pair(second, 0)


def from_snap(block, distance):
    members = lax.axis_size("snap")
    return lax.ppermute(block, "snap", [(i, (i + distance) % members) for i in range(members)])


def from_all(block):
    return jnp.stack([from_snap(block, i) for i in range(1, lax.axis_size("snap"))])


def shape(dims, kind):
    return jax.ShapeDtypeStruct(dims, kind)


def on_device(
    phasor_readings,
    reading_error_spread,
    starting_voltages,
    derivative_pieces,
    derivative_tile_position,
    frontier_voltage_pieces,
    holder_line_order,
    hub_line_order,
    reciprocal_normal_operator,
):
    snaps, lines = phasor_readings.shape
    states = starting_voltages.shape[1]
    own = states // BLK
    measure = derivative_pieces.shape[0]
    ties_table = frontier_voltage_pieces[0]
    ties = ties_table.shape[1]
    slots = own + 2 * ties
    members = lax.axis_size("snap")
    areas = lax.axis_size("area")
    everything = snaps * members
    held = reciprocal_normal_operator.shape[0] // BLK
    place = derivative_tile_position[0].T
    cap = hub_line_order.shape[2]
    width = max(cap, BLK)
    chunks = areas * cap // width
    hub = hub_line_order[0].reshape(chunks, width)
    holder = holder_line_order[0].reshape(chunks, width)
    depth = (width // BLK) * snaps + 8

    message, rounded, x_sent = call(
        pack_kernel,
        (
            shape((chunks, depth, BLK), F32),
            shape((snaps, states), BF16),
            [shape((snaps, held * BLK), F32)] * (members - 1),
        ),
        [HBM] * 4,
        (
            phasor_readings,
            reading_error_spread.reshape(lines // BLK, BLK),
            hub,
            starting_voltages,
        ),
        scratch=[
            pltpu.VMEM((snaps, lines), F32),
            pltpu.VMEM((lines // BLK, BLK), F32),
            pltpu.VMEM((chunks, width), jnp.int32),
            pltpu.VMEM((snaps, states), F32),
            pltpu.VMEM((chunks, depth, BLK), F32),
            pltpu.SemaphoreType.DMA((4,)),
            pltpu.SemaphoreType.DMA((chunks,)),
            pltpu.SemaphoreType.DMA((members,)),
        ],
        out_spec=(HBM, VMEM, [HBM] * (members - 1)),
        mib=60,
        name="pack_readings",
    )
    rounded_others = from_all(rounded)
    each = width // cap
    if each > 1:
        message = message.reshape(chunks, depth, each, cap).transpose(0, 2, 1, 3)
        message = message.reshape(areas, depth, cap)
    message = lax.all_to_all(message, "area", split_axis=0, concat_axis=0, tiled=True)
    if each > 1:
        message = message.reshape(chunks, each, depth, cap).transpose(0, 2, 1, 3)
        message = message.reshape(chunks, depth, BLK)

    group, lane = call(
        inverse_kernel,
        (shape((lines // BLK, BLK), jnp.int32),) * 2,
        [VMEM],
        (holder,),
        flops=10**9,
        name="invert_order",
    )
    boundary = shape((ties, everything, BLK), BF16)
    aug, first, second = call(
        first_states_kernel,
        (
            shape((own, everything, BLK), BF16),
            boundary,
            boundary,
        ),
        [VMEM, VMEM, SMEM],
        (rounded, rounded_others, ties_table),
        name="first_states",
    )
    first, second, x_sent = lax.optimization_barrier((first, second, x_sent))
    first, second = with_neighbours(first, second)
    x_others = [from_snap(block, i) for i, block in enumerate(x_sent, 1)]
    guess = call(
        predict_kernel,
        shape((everything, lines), F32),
        [VMEM, VMEM, VMEM, VMEM, SMEM],
        (aug, first, second, derivative_pieces, place),
        scratch=[pltpu.VMEM((slots, everything, BLK), BF16)],
        flops=10**9,
        name="predict",
    )
    message, guess, x_others = lax.optimization_barrier((message, guess, x_others))
    halves = []
    for part in range(2):
        halves.append(
            call(
                functools.partial(unpack_kernel, part * (lines // BLK // 2)),
                (shape((snaps, lines // 2), F32), shape((1, lines // 2), F32)),
                [VMEM, VMEM, VMEM],
                (group, lane, message),
                scratch=[pltpu.VMEM((chunks * (width // BLK), BLK), F32)],
                flops=2 * 10**9,
                name="unpack_readings",
            )
        )
    readings = [half[0] for half in halves]
    variance = [half[1] for half in halves]
    reading_others = [from_all(half) for half in readings]
    grads = (
        shape((own, everything, BLK), F32),
        boundary,
        boundary,
    )
    total = pltpu.VMEM((slots, everything, BLK), F32)
    work = pltpu.VMEM((own, everything, BLK), F32)
    grad, first, second = call(
        pull_kernel,
        grads,
        [VMEM, [VMEM] * 2, [VMEM] * 2, [VMEM] * 2, VMEM, SMEM],
        (guess, readings, reading_others, variance, derivative_pieces, place),
        scratch=[total, pltpu.VMEM((everything, lines), BF16)],
        name="pull",
    )
    arrived = with_neighbours(first, second)
    kept, given, mine, first = call(
        first_update_kernel,
        (
            shape((held, snaps, BLK), F32),
            [shape((held, snaps, BLK), F32)] * (members - 1),
            shape((held, everything, BLK), BF16),
            boundary,
        ),
        [VMEM, VMEM, VMEM, SMEM, VMEM, VMEM, [VMEM] * (members - 1)],
        (
            grad, *arrived, ties_table, reciprocal_normal_operator,
            starting_voltages, x_others,
        ),
        scratch=[work],
        name="first_update",
    )
    others = [from_snap(mine, i) for i in range(1, members)]
    first = swap_pair(first, 1)
    firsts = [first] + [from_snap(first, i) for i in range(1, members)]
    aug, second = call(
        join_states_kernel,
        (shape((own, everything, BLK), BF16), boundary),
        [VMEM, [VMEM] * (members - 1), SMEM],
        (mine, others, ties_table),
        name="join_states",
    )
    second = swap_pair(second, 0)
    grad, first, second = call(
        predict_pull_kernel,
        grads,
        [[VMEM] * members, VMEM, VMEM, [VMEM] * 2, [VMEM] * 2, [VMEM] * 2, VMEM, SMEM],
        (firsts, aug, second, readings, reading_others, variance, derivative_pieces, place),
        scratch=[
            pltpu.VMEM((slots, everything, BLK), BF16),
            pltpu.VMEM((everything, lines), F32),
            total,
            pltpu.VMEM((everything, lines), BF16),
        ],
        name="predict_pull",
    )
    given, first, second = lax.optimization_barrier((given, first, second))
    first, second = with_neighbours(first, second)
    states_in = [from_snap(block, i) for i, block in enumerate(given, 1)]
    mine, sent = call(
        last_update_kernel,
        (
            shape((snaps, held * BLK), F32),
            [shape((snaps, held * BLK), BF16)] * (members - 1),
        ),
        [VMEM, VMEM, VMEM, SMEM, VMEM, VMEM],
        (grad, first, second, ties_table, reciprocal_normal_operator, kept),
        scratch=[work],
        name="last_update",
    )
    return call(
        finish_kernel,
        shape((snaps, states), F32),
        [VMEM, [VMEM] * (members - 1), [VMEM] * (members - 1)],
        (mine, states_in, [from_snap(block, i) for i, block in enumerate(sent, 1)]),
        name="finish",
    )


def solution(mesh):
    placed = (
        P("snap", "area"),
        P("area"),
        P("snap", "area"),
        P("area", None, None, None),
        P("area", None, None),
        P("area", None, None),
        P("area", None, None),
        P("area", None, None),
        P(("area", "snap"), None),
    )
    return jax.shard_map(
        on_device, mesh=mesh, in_specs=placed, out_specs=P("snap", "area"), check_vma=False
    )
```

```python
import functools

import jax
import jax.numpy as jnp
from jax import lax
from jax.experimental import pallas as pl
from jax.experimental.pallas import tpu as pltpu
from jax.sharding import PartitionSpec as P

BLK = 128
ITERS = 2
F32 = jnp.float32
BF16 = jnp.bfloat16
NT = (((1,), (1,)), ((), ()))
VMEM = pl.BlockSpec(memory_space=pltpu.VMEM)
HBM = pl.BlockSpec(memory_space=pltpu.HBM)
SMEM = pl.BlockSpec(memory_space=pltpu.SMEM)


def call(kernel, outs, ins, args, scratch=(), flops=0, mib=12, out_spec=None, name=None):
    return pl.pallas_call(
        kernel,
        out_shape=outs,
        in_specs=ins,
        out_specs=jax.tree.map(lambda _: VMEM, outs) if out_spec is None else out_spec,
        scratch_shapes=list(scratch),
        compiler_params=pltpu.CompilerParams(vmem_limit_bytes=mib * 1024 * 1024),
        cost_estimate=pl.CostEstimate(
            flops=flops, bytes_accessed=0, transcendentals=0
        ),
        name=name,
    )(*args)


def lane_gather(values, lanes):
    return jnp.take_along_axis(values, lanes, axis=1, mode="promise_in_bounds")


def rows_iota(shape):
    return lax.broadcasted_iota(jnp.int32, shape, 0)


def pack_kernel(
    z_in, v_in, hub_in, x_in, ties_in, out, rounded_out, first_out, second_out, sent_outs,
    z_ref, v_ref, hub_ref, x_ref, ties_ref, out_ref, rounded_ref, first_ref, second_ref,
    sems, out_sems, sent_sems,
):
    pairs = (
        (x_in, x_ref), (ties_in, ties_ref), (hub_in, hub_ref), (z_in, z_ref), (v_in, v_ref)
    )
    copies = [
        pltpu.make_async_copy(source, target, sems.at[i])
        for i, (source, target) in enumerate(pairs)
    ]
    for copy in copies:
        copy.start()
    for copy in copies:
        copy.wait()
    for b in range(rounded_ref.shape[0]):
        rounded_ref[b] = x_ref[:, b * BLK : (b + 1) * BLK].astype(BF16)
    pick(rounded_ref, ties_ref, 1 - parity(), first_ref)
    pick(rounded_ref, ties_ref, parity(), second_ref)
    ready = [(first_ref, first_out), (second_ref, second_out), (rounded_ref, rounded_out)]
    members = len(sent_outs) + 1
    part = x_ref.shape[1] // members
    for i, sent_out in enumerate(sent_outs, 1):
        at = lax.rem(lax.axis_index("snap") + i, members) * part
        ready.append((x_ref.at[:, pl.ds(pl.multiple_of(at, BLK), part)], sent_out))
    sends = [
        pltpu.make_async_copy(source, target, sent_sems.at[i])
        for i, (source, target) in enumerate(ready)
    ]
    for copy in sends:
        copy.start()
    snaps, lines = z_ref.shape
    blocks = lines // BLK
    chunks, width = hub_ref.shape
    groups = width // BLK
    for d in range(chunks):
        tail = jnp.zeros((8, BLK), F32)
        for g in range(groups):
            slot = hub_ref[d : d + 1, g * BLK : (g + 1) * BLK]
            high = jnp.right_shift(slot, 7)
            low = jnp.bitwise_and(slot, 127)
            lanes = jnp.broadcast_to(low, (snaps, BLK))
            block_of = jnp.broadcast_to(high, (snaps, BLK))
            picked = jnp.zeros((snaps, BLK), F32)
            for b in range(blocks):
                found = lane_gather(z_ref[:, b * BLK : (b + 1) * BLK], lanes)
                picked = jnp.where(block_of == b, found, picked)
            out_ref[d, g * snaps : (g + 1) * snaps, :] = picked
            found = lane_gather(v_ref[...], jnp.broadcast_to(low, (blocks, BLK)))
            mine = rows_iota((blocks, BLK)) == high
            variance = jnp.sum(jnp.where(mine, found, 0.0), axis=0, keepdims=True)
            tail = jnp.where(rows_iota((8, BLK)) == g, variance, tail)
        out_ref[d, groups * snaps :, :] = tail
        pltpu.make_async_copy(out_ref.at[d], out.at[d], out_sems.at[d]).start()
    for d in range(chunks):
        pltpu.make_async_copy(out_ref.at[d], out.at[d], out_sems.at[d]).wait()
    for copy in sends:
        copy.wait()


def inverse_kernel(own_ref, group_ref, lane_ref):
    chunks, width = own_ref.shape
    blocks = group_ref.shape[0]
    groups = width // BLK
    total = jnp.zeros((2 * blocks, BLK), F32)
    lane = lax.broadcasted_iota(jnp.int32, (2 * blocks, width), 1)
    row = rows_iota((2 * blocks, width))
    in_group = jnp.bitwise_and(lane, 127)
    group_in = jnp.right_shift(lane, 7)
    for d in range(chunks):
        owned = own_ref[d : d + 1, :]
        high = jnp.right_shift(owned, 7)
        low = jnp.bitwise_and(owned, 127)
        label = jnp.where(row < blocks, group_in + d * groups, in_group)
        hit = jnp.bitwise_and(row, blocks - 1) == high
        left = jnp.where(hit, label.astype(F32), 0.0).astype(BF16)
        right = jnp.where(rows_iota((BLK, width)) == low, 1.0, 0.0).astype(BF16)
        total += lax.dot_general(left, right, NT, preferred_element_type=F32)
    group_ref[...] = total[:blocks].astype(jnp.int32)
    lane_ref[...] = total[blocks:].astype(jnp.int32)


def unpack_kernel(start, group_ref, lane_ref, message_ref, z_ref, v_ref, variance_ref):
    snaps, lines = z_ref.shape
    chunks = message_ref.shape[0]
    groups = (message_ref.shape[1] - 8) // snaps
    total = chunks * groups
    for d in range(chunks):
        variance_ref[d * groups : (d + 1) * groups, :] = message_ref[d, groups * snaps :, :][:groups]
    for b in range(lines // BLK):
        group = group_ref[start + b : start + b + 1, :]
        lane = lane_ref[start + b : start + b + 1, :]
        lanes = jnp.broadcast_to(lane, (snaps, BLK))
        group_of = jnp.broadcast_to(group, (snaps, BLK))
        picked = jnp.zeros((snaps, BLK), F32)
        for g in range(total):
            rows = slice(g % groups * snaps, (g % groups + 1) * snaps)
            found = lane_gather(message_ref[g // groups, rows, :], lanes)
            picked = jnp.where(group_of == g, found, picked)
        columns = slice(b * BLK, (b + 1) * BLK)
        z_ref[:, columns] = picked
        found = lane_gather(variance_ref[...], jnp.broadcast_to(lane, (total, BLK)))
        mine = rows_iota((total, BLK)) == group
        v_ref[:, columns] = jnp.sum(jnp.where(mine, found, 0.0), axis=0, keepdims=True)


def split(ref):
    return [ref.at[i] for i in range(ref.shape[0])]


def parity():
    return 1 - lax.rem(lax.axis_index("area"), 2)


def pick(blocks_ref, listing_ref, side, out_ref, start=0):
    held = blocks_ref.shape[0]
    for t in range(out_ref.shape[0]):
        b = listing_ref[side, t]
        at = b - start
        block = blocks_ref[jnp.clip(at, 0, held - 1)]
        here = (b >= 0) & (at >= 0) & (at < held)
        out_ref[t] = jnp.where(here, block, jnp.zeros_like(block))


def slots_into(slots_ref, aug_ref, first, second_ref):
    own = aug_ref.shape[0]
    ties = second_ref.shape[0]
    slots_ref[:own] = aug_ref[...]
    slots_ref[pl.ds(own + ties * (1 - parity()), ties)] = first
    slots_ref[pl.ds(own + ties * parity(), ties)] = second_ref[...]


def reordered(ref, distance, members):
    snaps = ref.shape[1] // members
    order = [(n - distance) % members for n in range(members)]
    return jnp.concatenate([ref[:, j * snaps : (j + 1) * snaps] for j in order], axis=1)


def join_states_kernel(mine_ref, others_refs, ties_ref, aug_ref, second_ref):
    members = len(others_refs) + 1
    held = mine_ref.shape[0]
    me = lax.axis_index("snap")
    aug_ref[pl.ds(me * held, held)] = mine_ref[...]
    for i, ref in enumerate(others_refs, 1):
        at = lax.rem(me + members - i, members) * held
        aug_ref[pl.ds(at, held)] = reordered(ref, i, members)
    pick(aug_ref, ties_ref, parity(), second_ref)


def predicted(j, slots_ref, tiles_ref, place_ref):
    touched = tiles_ref.shape[1]
    chosen = jnp.concatenate([slots_ref[place_ref[k, j]] for k in range(touched)], axis=1)
    weights = jnp.concatenate([tiles_ref[j, k] for k in range(touched)], axis=1)
    return lax.dot_general(chosen, weights, NT, preferred_element_type=F32)


def predict_kernel(
    first_refs, second_refs, own_refs, tiles_ref, place_ref, out_ref, slots_ref
):
    own, snaps = own_refs[0].shape[:2]
    ties = first_refs[0].shape[0]
    for i in range(len(own_refs)):
        rows = slice(i * snaps, (i + 1) * snaps)
        slots_ref[:own, rows] = own_refs[i][...]
        slots_ref[pl.ds(own + ties * (1 - parity()), ties), rows] = first_refs[i][...]
        slots_ref[pl.ds(own + ties * parity(), ties), rows] = second_refs[i][...]
    predict(tiles_ref, place_ref, out_ref, slots_ref)


def predict(tiles_ref, place_ref, out_ref, slots_ref):
    for j in range(tiles_ref.shape[0]):
        out_ref[:, j * BLK : (j + 1) * BLK] = predicted(j, slots_ref, tiles_ref, place_ref)


def weigh(j, guess, z_refs, others_refs, v_refs):
    each = z_refs[0].shape[1] // BLK
    z_ref, others_ref, v_ref = z_refs[j // each], others_refs[j // each], v_refs[j // each]
    columns = slice(j % each * BLK, (j % each + 1) * BLK)
    readings = [z_ref[:, columns]] + [o[:, columns] for o in split(others_ref)]
    resid = jnp.concatenate(readings, axis=0) - guess
    spread = jnp.sum(resid * resid, axis=0, keepdims=True) / resid.shape[0]
    return (resid / (v_ref[:, columns] + spread)).astype(BF16)


def pull(weighted_ref, tiles_ref, place_ref, total_ref, own_ref, first_ref, second_ref):
    total_ref[...] = jnp.zeros_like(total_ref)
    touched = tiles_ref.shape[1]
    for j in range(tiles_ref.shape[0]):
        weighted = weighted_ref[:, j * BLK : (j + 1) * BLK]
        weights = jnp.concatenate([tiles_ref[j, k] for k in range(touched)], axis=1)
        part = jnp.dot(weighted, weights, preferred_element_type=F32)
        for k in range(touched):
            n = place_ref[k, j]
            total_ref[n] += part[:, k * BLK : (k + 1) * BLK]
    own = own_ref.shape[0]
    ties = first_ref.shape[0]
    own_ref[...] = total_ref[:own]
    first = total_ref[pl.ds(own + ties * (1 - parity()), ties)]
    second = total_ref[pl.ds(own + ties * parity(), ties)]
    first_ref[...] = first.astype(first_ref.dtype)
    second_ref[...] = second.astype(second_ref.dtype)


def pull_kernel(
    guess_ref, z_refs, others_refs, v_refs, tiles_ref, place_ref, own_ref, first_ref, second_ref,
    total_ref, weighted_ref,
):
    for j in range(tiles_ref.shape[0]):
        columns = slice(j * BLK, (j + 1) * BLK)
        weighted_ref[:, columns] = weigh(j, guess_ref[:, columns], z_refs, others_refs, v_refs)
    pull(weighted_ref, tiles_ref, place_ref, total_ref, own_ref, first_ref, second_ref)


def predict_pull_kernel(
    first_refs, aug_ref, second_in_ref, z_refs, others_refs, v_refs, tiles_ref, place_ref,
    own_ref, first_ref, second_ref, slots_ref, guess_ref, total_ref, weighted_ref,
):
    parts = [reordered(ref, i, len(first_refs)) for i, ref in enumerate(first_refs)]
    slots_into(slots_ref, aug_ref, sum(parts[1:], parts[0]), second_in_ref)
    predict(tiles_ref, place_ref, guess_ref, slots_ref)
    pull_kernel(
        guess_ref, z_refs, others_refs, v_refs, tiles_ref, place_ref, own_ref, first_ref, second_ref,
        total_ref, weighted_ref,
    )


def full_gradient(grad_ref, back_first_ref, back_second_ref, ties_ref, work_ref):
    work_ref[...] = grad_ref[...]
    for side, back_ref in ((1 - parity(), back_first_ref), (parity(), back_second_ref)):
        for t in range(back_ref.shape[0]):
            b = ties_ref[side, t]

            @pl.when(b >= 0)
            def _(b=b, t=t, back_ref=back_ref):
                work_ref[b] += back_ref[t].astype(F32)

    return jnp.concatenate([work_ref[b].astype(BF16) for b in range(work_ref.shape[0])], axis=1)


def updates(gradient, gain_ref):
    step = min(2 * BLK, gain_ref.shape[0])
    for at in range(0, gain_ref.shape[0], step):
        rows = gain_ref[at : at + step, :]
        update = lax.dot_general(gradient, rows, NT, preferred_element_type=F32)
        for i in range(step // BLK):
            yield at // BLK + i, update[:, i * BLK : (i + 1) * BLK]


def first_update_kernel(
    grad_ref, back_first_ref, back_second_ref, ties_ref, gain_ref, x_ref, x_others_refs,
    kept_ref, given_refs, message_ref, first_ref, work_ref,
):
    gradient = full_gradient(grad_ref, back_first_ref, back_second_ref, ties_ref, work_ref)
    held, snaps = kept_ref.shape[:2]
    me = lax.axis_index("snap")
    for i, update in updates(gradient, gain_ref):
        columns = pl.ds(pl.multiple_of((me * held + i) * BLK, BLK), BLK)
        parts = [x_ref[:, columns]] + [o[:, i * BLK : (i + 1) * BLK] for o in x_others_refs]
        state = jnp.concatenate(parts, axis=0) + update
        kept_ref[i] = state[:snaps]
        for j, given_ref in enumerate(given_refs, 1):
            given_ref[i] = state[j * snaps : (j + 1) * snaps]
        message_ref[i] = state.astype(BF16)
    pick(message_ref, ties_ref, 1 - parity(), first_ref, me * held)


def last_update_kernel(
    grad_ref, back_first_ref, back_second_ref, ties_ref, gain_ref, kept_ref, mine_ref, sent_refs, work_ref
):
    gradient = full_gradient(grad_ref, back_first_ref, back_second_ref, ties_ref, work_ref)
    snaps = mine_ref.shape[0]
    for i, update in updates(gradient, gain_ref):
        columns = slice(i * BLK, (i + 1) * BLK)
        mine_ref[:, columns] = kept_ref[i] + update[:snaps]
        for j, sent_ref in enumerate(sent_refs, 1):
            sent_ref[:, columns] = update[j * snaps : (j + 1) * snaps].astype(BF16)


def finish_kernel(mine_ref, states_refs, updates_refs, out_ref):
    width = mine_ref.shape[1]
    members = len(states_refs) + 1
    me = lax.axis_index("snap")
    out_ref[:, pl.ds(pl.multiple_of(me * width, BLK), width)] = mine_ref[...]
    for i, (state_ref, update_ref) in enumerate(zip(states_refs, updates_refs), 1):
        at = lax.rem(me + i, members) * width
        for b in range(width // BLK):
            update = update_ref[:, b * BLK : (b + 1) * BLK].astype(F32)
            columns = pl.ds(pl.multiple_of(at + b * BLK, BLK), BLK)
            out_ref[:, columns] = state_ref[b] + update


def swap_pair(block, start):
    pairs = [(i, i + 1) for i in range(start, lax.axis_size("area") - 1, 2)]
    return lax.ppermute(block, "area", pairs + [(b, a) for a, b in pairs])


def with_neighbours(first, second):
    return swap_pair(first, 1), swap_pair(second, 0)


def from_snap(block, distance):
    members = lax.axis_size("snap")
    return lax.ppermute(block, "snap", [(i, (i + distance) % members) for i in range(members)])


def from_all(block):
    return jnp.stack([from_snap(block, i) for i in range(1, lax.axis_size("snap"))])


def shape(dims, kind):
    return jax.ShapeDtypeStruct(dims, kind)


def on_device(
    phasor_readings,
    reading_error_spread,
    starting_voltages,
    derivative_pieces,
    derivative_tile_position,
    frontier_voltage_pieces,
    holder_line_order,
    hub_line_order,
    reciprocal_normal_operator,
):
    snaps, lines = phasor_readings.shape
    states = starting_voltages.shape[1]
    own = states // BLK
    measure = derivative_pieces.shape[0]
    ties_table = frontier_voltage_pieces[0]
    ties = ties_table.shape[1]
    slots = own + 2 * ties
    members = lax.axis_size("snap")
    areas = lax.axis_size("area")
    everything = snaps * members
    held = reciprocal_normal_operator.shape[0] // BLK
    place = derivative_tile_position[0].T
    cap = hub_line_order.shape[2]
    width = max(cap, BLK)
    chunks = areas * cap // width
    hub = hub_line_order[0].reshape(chunks, width)
    holder = holder_line_order[0].reshape(chunks, width)
    depth = (width // BLK) * snaps + 8

    few = shape((ties, snaps, BLK), BF16)
    message, rounded, first, second, x_sent = call(
        pack_kernel,
        (
            shape((chunks, depth, BLK), F32),
            shape((own, snaps, BLK), BF16),
            few,
            few,
            [shape((snaps, held * BLK), F32)] * (members - 1),
        ),
        [HBM] * 5,
        (
            phasor_readings,
            reading_error_spread.reshape(lines // BLK, BLK),
            hub,
            starting_voltages,
            ties_table,
        ),
        scratch=[
            pltpu.VMEM((snaps, lines), F32),
            pltpu.VMEM((lines // BLK, BLK), F32),
            pltpu.VMEM((chunks, width), jnp.int32),
            pltpu.VMEM((snaps, states), F32),
            pltpu.SMEM(ties_table.shape, jnp.int32),
            pltpu.VMEM((chunks, depth, BLK), F32),
            pltpu.VMEM((own, snaps, BLK), BF16),
            pltpu.VMEM((ties, snaps, BLK), BF16),
            pltpu.VMEM((ties, snaps, BLK), BF16),
            pltpu.SemaphoreType.DMA((5,)),
            pltpu.SemaphoreType.DMA((chunks,)),
            pltpu.SemaphoreType.DMA((members + 2,)),
        ],
        out_spec=(HBM, HBM, HBM, HBM, [HBM] * (members - 1)),
        mib=60,
        name="pack_readings",
    )
    each = width // cap
    if each > 1:
        message = message.reshape(chunks, depth, each, cap).transpose(0, 2, 1, 3)
        message = message.reshape(areas, depth, cap)
    message = lax.all_to_all(message, "area", split_axis=0, concat_axis=0, tiled=True)
    if each > 1:
        message = message.reshape(chunks, each, depth, cap).transpose(0, 2, 1, 3)
        message = message.reshape(chunks, depth, BLK)

    group, lane = call(
        inverse_kernel,
        (shape((lines // BLK, BLK), jnp.int32),) * 2,
        [VMEM],
        (holder,),
        flops=10**9,
        name="invert_order",
    )
    boundary = shape((ties, everything, BLK), BF16)
    owns = [rounded] + [from_snap(rounded, i) for i in range(1, members)]
    first, second = with_neighbours(first, second)
    first, second, x_sent = lax.optimization_barrier((first, second, x_sent))
    firsts = [first] + [from_snap(first, i) for i in range(1, members)]
    seconds = [second] + [from_snap(second, i) for i in range(1, members)]
    x_others = [from_snap(block, i) for i, block in enumerate(x_sent, 1)]
    guess = call(
        predict_kernel,
        shape((everything, lines), F32),
        [[VMEM] * members, [VMEM] * members, [VMEM] * members, VMEM, SMEM],
        (firsts, seconds, owns, derivative_pieces, place),
        scratch=[pltpu.VMEM((slots, everything, BLK), BF16)],
        flops=10**9,
        name="predict",
    )
    message, guess, x_others = lax.optimization_barrier((message, guess, x_others))
    halves = []
    for part in range(2):
        halves.append(
            call(
                functools.partial(unpack_kernel, part * (lines // BLK // 2)),
                (shape((snaps, lines // 2), F32), shape((1, lines // 2), F32)),
                [VMEM, VMEM, VMEM],
                (group, lane, message),
                scratch=[pltpu.VMEM((chunks * (width // BLK), BLK), F32)],
                flops=2 * 10**9,
                name="unpack_readings",
            )
        )
    readings = [half[0] for half in halves]
    variance = [half[1] for half in halves]
    reading_others = [from_all(half) for half in readings]
    grads = (
        shape((own, everything, BLK), F32),
        boundary,
        boundary,
    )
    total = pltpu.VMEM((slots, everything, BLK), F32)
    work = pltpu.VMEM((own, everything, BLK), F32)
    grad, first, second = call(
        pull_kernel,
        grads,
        [VMEM, [VMEM] * 2, [VMEM] * 2, [VMEM] * 2, VMEM, SMEM],
        (guess, readings, reading_others, variance, derivative_pieces, place),
        scratch=[total, pltpu.VMEM((everything, lines), BF16)],
        name="pull",
    )
    arrived = with_neighbours(first, second)
    kept, given, mine, first = call(
        first_update_kernel,
        (
            shape((held, snaps, BLK), F32),
            [shape((held, snaps, BLK), F32)] * (members - 1),
            shape((held, everything, BLK), BF16),
            boundary,
        ),
        [VMEM, VMEM, VMEM, SMEM, VMEM, VMEM, [VMEM] * (members - 1)],
        (
            grad, *arrived, ties_table, reciprocal_normal_operator,
            starting_voltages, x_others,
        ),
        scratch=[work],
        name="first_update",
    )
    others = [from_snap(mine, i) for i in range(1, members)]
    first = swap_pair(first, 1)
    firsts = [first] + [from_snap(first, i) for i in range(1, members)]
    aug, second = call(
        join_states_kernel,
        (shape((own, everything, BLK), BF16), boundary),
        [VMEM, [VMEM] * (members - 1), SMEM],
        (mine, others, ties_table),
        name="join_states",
    )
    second = swap_pair(second, 0)
    grad, first, second = call(
        predict_pull_kernel,
        grads,
        [[VMEM] * members, VMEM, VMEM, [VMEM] * 2, [VMEM] * 2, [VMEM] * 2, VMEM, SMEM],
        (firsts, aug, second, readings, reading_others, variance, derivative_pieces, place),
        scratch=[
            pltpu.VMEM((slots, everything, BLK), BF16),
            pltpu.VMEM((everything, lines), F32),
            total,
            pltpu.VMEM((everything, lines), BF16),
        ],
        name="predict_pull",
    )
    given, first, second = lax.optimization_barrier((given, first, second))
    first, second = with_neighbours(first, second)
    states_in = [from_snap(block, -i) for i, block in enumerate(given, 1)]
    mine, sent = call(
        last_update_kernel,
        (
            shape((snaps, held * BLK), F32),
            [shape((snaps, held * BLK), BF16)] * (members - 1),
        ),
        [VMEM, VMEM, VMEM, SMEM, VMEM, VMEM],
        (grad, first, second, ties_table, reciprocal_normal_operator, kept),
        scratch=[work],
        name="last_update",
    )
    return call(
        finish_kernel,
        shape((snaps, states), F32),
        [VMEM, [VMEM] * (members - 1), [VMEM] * (members - 1)],
        (mine, states_in, [from_snap(block, -i) for i, block in enumerate(sent, 1)]),
        name="finish",
    )


def solution(mesh):
    placed = (
        P("snap", "area"),
        P("area"),
        P("snap", "area"),
        P("area", None, None, None),
        P("area", None, None),
        P("area", None, None),
        P("area", None, None),
        P("area", None, None),
        P(("area", "snap"), None),
    )
    return jax.shard_map(
        on_device, mesh=mesh, in_specs=placed, out_specs=P("snap", "area"), check_vma=False
    )
```

```python
import functools

import jax
import jax.numpy as jnp
from jax import lax
from jax.experimental import pallas as pl
from jax.experimental.pallas import tpu as pltpu
from jax.sharding import PartitionSpec as P

BLK = 128
ITERS = 2
F32 = jnp.float32
BF16 = jnp.bfloat16
NT = (((1,), (1,)), ((), ()))
VMEM = pl.BlockSpec(memory_space=pltpu.VMEM)
HBM = pl.BlockSpec(memory_space=pltpu.HBM)
SMEM = pl.BlockSpec(memory_space=pltpu.SMEM)


def call(kernel, outs, ins, args, scratch=(), flops=0, mib=12, out_spec=None, name=None):
    return pl.pallas_call(
        kernel,
        out_shape=outs,
        in_specs=ins,
        out_specs=jax.tree.map(lambda _: VMEM, outs) if out_spec is None else out_spec,
        scratch_shapes=list(scratch),
        compiler_params=pltpu.CompilerParams(vmem_limit_bytes=mib * 1024 * 1024),
        cost_estimate=pl.CostEstimate(
            flops=flops, bytes_accessed=0, transcendentals=0
        ),
        name=name,
    )(*args)


def lane_gather(values, lanes):
    return jnp.take_along_axis(values, lanes, axis=1, mode="promise_in_bounds")


def rows_iota(shape):
    return lax.broadcasted_iota(jnp.int32, shape, 0)


def pack_kernel(
    z_in, v_in, hub_in, x_in, out, rounded_out, sent_outs,
    z_ref, v_ref, hub_ref, x_ref, out_ref, rounded_ref,
    sems, out_sems, sent_sems,
):
    pairs = ((x_in, x_ref), (hub_in, hub_ref), (z_in, z_ref), (v_in, v_ref))
    copies = [
        pltpu.make_async_copy(source, target, sems.at[i])
        for i, (source, target) in enumerate(pairs)
    ]
    for copy in copies:
        copy.start()
    for copy in copies:
        copy.wait()
    for b in range(rounded_ref.shape[0]):
        rounded_ref[b] = x_ref[:, b * BLK : (b + 1) * BLK].astype(BF16)
    ready = [(rounded_ref, rounded_out)]
    members = len(sent_outs) + 1
    part = x_ref.shape[1] // members
    for i, sent_out in enumerate(sent_outs, 1):
        at = lax.rem(lax.axis_index("snap") + i, members) * part
        ready.append((x_ref.at[:, pl.ds(pl.multiple_of(at, BLK), part)], sent_out))
    sends = [
        pltpu.make_async_copy(source, target, sent_sems.at[i])
        for i, (source, target) in enumerate(ready)
    ]
    for copy in sends:
        copy.start()
    snaps, lines = z_ref.shape
    blocks = lines // BLK
    chunks, width = hub_ref.shape
    groups = width // BLK
    for d in range(chunks):
        tail = jnp.zeros((8, BLK), F32)
        for g in range(groups):
            slot = hub_ref[d : d + 1, g * BLK : (g + 1) * BLK]
            high = jnp.right_shift(slot, 7)
            low = jnp.bitwise_and(slot, 127)
            lanes = jnp.broadcast_to(low, (snaps, BLK))
            block_of = jnp.broadcast_to(high, (snaps, BLK))
            picked = jnp.zeros((snaps, BLK), F32)
            for b in range(blocks):
                found = lane_gather(z_ref[:, b * BLK : (b + 1) * BLK], lanes)
                picked = jnp.where(block_of == b, found, picked)
            out_ref[d, g * snaps : (g + 1) * snaps, :] = picked
            found = lane_gather(v_ref[...], jnp.broadcast_to(low, (blocks, BLK)))
            mine = rows_iota((blocks, BLK)) == high
            variance = jnp.sum(jnp.where(mine, found, 0.0), axis=0, keepdims=True)
            tail = jnp.where(rows_iota((8, BLK)) == g, variance, tail)
        out_ref[d, groups * snaps :, :] = tail
        pltpu.make_async_copy(out_ref.at[d], out.at[d], out_sems.at[d]).start()
    for d in range(chunks):
        pltpu.make_async_copy(out_ref.at[d], out.at[d], out_sems.at[d]).wait()
    for copy in sends:
        copy.wait()


def inverse_kernel(own_ref, group_ref, lane_ref):
    chunks, width = own_ref.shape
    blocks = group_ref.shape[0]
    groups = width // BLK
    total = jnp.zeros((2 * blocks, BLK), F32)
    lane = lax.broadcasted_iota(jnp.int32, (2 * blocks, width), 1)
    row = rows_iota((2 * blocks, width))
    in_group = jnp.bitwise_and(lane, 127)
    group_in = jnp.right_shift(lane, 7)
    for d in range(chunks):
        owned = own_ref[d : d + 1, :]
        high = jnp.right_shift(owned, 7)
        low = jnp.bitwise_and(owned, 127)
        label = jnp.where(row < blocks, group_in + d * groups, in_group)
        hit = jnp.bitwise_and(row, blocks - 1) == high
        left = jnp.where(hit, label.astype(F32), 0.0).astype(BF16)
        right = jnp.where(rows_iota((BLK, width)) == low, 1.0, 0.0).astype(BF16)
        total += lax.dot_general(left, right, NT, preferred_element_type=F32)
    group_ref[...] = total[:blocks].astype(jnp.int32)
    lane_ref[...] = total[blocks:].astype(jnp.int32)


def unpack_kernel(start, group_ref, lane_ref, message_ref, z_ref, v_ref, variance_ref):
    snaps, lines = z_ref.shape
    chunks = message_ref.shape[0]
    groups = (message_ref.shape[1] - 8) // snaps
    total = chunks * groups
    for d in range(chunks):
        variance_ref[d * groups : (d + 1) * groups, :] = message_ref[d, groups * snaps :, :][:groups]
    for b in range(lines // BLK):
        group = group_ref[start + b : start + b + 1, :]
        lane = lane_ref[start + b : start + b + 1, :]
        lanes = jnp.broadcast_to(lane, (snaps, BLK))
        group_of = jnp.broadcast_to(group, (snaps, BLK))
        picked = jnp.zeros((snaps, BLK), F32)
        for g in range(total):
            rows = slice(g % groups * snaps, (g % groups + 1) * snaps)
            found = lane_gather(message_ref[g // groups, rows, :], lanes)
            picked = jnp.where(group_of == g, found, picked)
        columns = slice(b * BLK, (b + 1) * BLK)
        z_ref[:, columns] = picked
        found = lane_gather(variance_ref[...], jnp.broadcast_to(lane, (total, BLK)))
        mine = rows_iota((total, BLK)) == group
        v_ref[:, columns] = jnp.sum(jnp.where(mine, found, 0.0), axis=0, keepdims=True)


def split(ref):
    return [ref.at[i] for i in range(ref.shape[0])]


def parity():
    return 1 - lax.rem(lax.axis_index("area"), 2)


def pick(blocks_ref, listing_ref, side, out_ref, start=0):
    held = blocks_ref.shape[0]
    for t in range(out_ref.shape[0]):
        b = listing_ref[side, t]
        at = b - start
        block = blocks_ref[jnp.clip(at, 0, held - 1)]
        here = (b >= 0) & (at >= 0) & (at < held)
        out_ref[t] = jnp.where(here, block, jnp.zeros_like(block))


def slots_into(slots_ref, aug_ref, first, second_ref):
    own = aug_ref.shape[0]
    ties = second_ref.shape[0]
    slots_ref[:own] = aug_ref[...]
    slots_ref[pl.ds(own + ties * (1 - parity()), ties)] = first
    slots_ref[pl.ds(own + ties * parity(), ties)] = second_ref[...]


def reordered(ref, distance, members):
    snaps = ref.shape[1] // members
    order = [(n - distance) % members for n in range(members)]
    return jnp.concatenate([ref[:, j * snaps : (j + 1) * snaps] for j in order], axis=1)


def join_states_kernel(mine_ref, others_refs, ties_ref, aug_ref, second_ref):
    members = len(others_refs) + 1
    held = mine_ref.shape[0]
    me = lax.axis_index("snap")
    aug_ref[pl.ds(me * held, held)] = mine_ref[...]
    for i, ref in enumerate(others_refs, 1):
        at = lax.rem(me + members - i, members) * held
        aug_ref[pl.ds(at, held)] = reordered(ref, i, members)
    pick(aug_ref, ties_ref, parity(), second_ref)


def predicted(j, slots_ref, tiles_ref, place_ref):
    touched = tiles_ref.shape[1]
    chosen = jnp.concatenate([slots_ref[place_ref[k, j]] for k in range(touched)], axis=1)
    weights = jnp.concatenate([tiles_ref[j, k] for k in range(touched)], axis=1)
    return lax.dot_general(chosen, weights, NT, preferred_element_type=F32)


def pick_kernel(own_refs, ties_ref, first_ref, second_ref):
    snaps = own_refs[0].shape[1]
    for i, own_ref in enumerate(own_refs):
        rows = slice(i * snaps, (i + 1) * snaps)
        pick(own_ref, ties_ref, 1 - parity(), first_ref.at[:, rows])
        pick(own_ref, ties_ref, parity(), second_ref.at[:, rows])


def predict_kernel(
    first_ref, second_ref, own_refs, tiles_ref, place_ref, out_ref, slots_ref
):
    own, snaps = own_refs[0].shape[:2]
    ties = first_ref.shape[0]
    for i, own_ref in enumerate(own_refs):
        slots_ref[:own, i * snaps : (i + 1) * snaps] = own_ref[...]
    slots_ref[pl.ds(own + ties * (1 - parity()), ties)] = first_ref[...]
    slots_ref[pl.ds(own + ties * parity(), ties)] = second_ref[...]
    predict(tiles_ref, place_ref, out_ref, slots_ref)


def predict(tiles_ref, place_ref, out_ref, slots_ref):
    for j in range(tiles_ref.shape[0]):
        out_ref[:, j * BLK : (j + 1) * BLK] = predicted(j, slots_ref, tiles_ref, place_ref)


def weigh(j, guess, z_refs, others_refs, v_refs):
    each = z_refs[0].shape[1] // BLK
    z_ref, others_ref, v_ref = z_refs[j // each], others_refs[j // each], v_refs[j // each]
    columns = slice(j % each * BLK, (j % each + 1) * BLK)
    readings = [z_ref[:, columns]] + [o[:, columns] for o in split(others_ref)]
    resid = jnp.concatenate(readings, axis=0) - guess
    spread = jnp.sum(resid * resid, axis=0, keepdims=True) / resid.shape[0]
    return (resid / (v_ref[:, columns] + spread)).astype(BF16)


def pull(weighted_ref, tiles_ref, place_ref, total_ref, own_ref, first_ref, second_ref):
    total_ref[...] = jnp.zeros_like(total_ref)
    touched = tiles_ref.shape[1]
    for j in range(tiles_ref.shape[0]):
        weighted = weighted_ref[:, j * BLK : (j + 1) * BLK]
        weights = jnp.concatenate([tiles_ref[j, k] for k in range(touched)], axis=1)
        part = jnp.dot(weighted, weights, preferred_element_type=F32)
        for k in range(touched):
            n = place_ref[k, j]
            total_ref[n] += part[:, k * BLK : (k + 1) * BLK]
    own = own_ref.shape[0]
    ties = first_ref.shape[0]
    own_ref[...] = total_ref[:own]
    first = total_ref[pl.ds(own + ties * (1 - parity()), ties)]
    second = total_ref[pl.ds(own + ties * parity(), ties)]
    first_ref[...] = first.astype(first_ref.dtype)
    second_ref[...] = second.astype(second_ref.dtype)


def pull_kernel(
    guess_ref, z_refs, others_refs, v_refs, tiles_ref, place_ref, own_ref, first_ref, second_ref,
    total_ref, weighted_ref,
):
    for j in range(tiles_ref.shape[0]):
        columns = slice(j * BLK, (j + 1) * BLK)
        weighted_ref[:, columns] = weigh(j, guess_ref[:, columns], z_refs, others_refs, v_refs)
    pull(weighted_ref, tiles_ref, place_ref, total_ref, own_ref, first_ref, second_ref)


def predict_pull_kernel(
    first_refs, aug_ref, second_in_ref, z_refs, others_refs, v_refs, tiles_ref, place_ref,
    own_ref, first_ref, second_ref, slots_ref, guess_ref, total_ref, weighted_ref,
):
    parts = [reordered(ref, i, len(first_refs)) for i, ref in enumerate(first_refs)]
    slots_into(slots_ref, aug_ref, sum(parts[1:], parts[0]), second_in_ref)
    predict(tiles_ref, place_ref, guess_ref, slots_ref)
    pull_kernel(
        guess_ref, z_refs, others_refs, v_refs, tiles_ref, place_ref, own_ref, first_ref, second_ref,
        total_ref, weighted_ref,
    )


def full_gradient(grad_ref, back_first_ref, back_second_ref, ties_ref, work_ref):
    work_ref[...] = grad_ref[...]
    for side, back_ref in ((1 - parity(), back_first_ref), (parity(), back_second_ref)):
        for t in range(back_ref.shape[0]):
            b = ties_ref[side, t]

            @pl.when(b >= 0)
            def _(b=b, t=t, back_ref=back_ref):
                work_ref[b] += back_ref[t].astype(F32)

    return jnp.concatenate([work_ref[b].astype(BF16) for b in range(work_ref.shape[0])], axis=1)


def updates(gradient, gain_ref):
    step = min(2 * BLK, gain_ref.shape[0])
    for at in range(0, gain_ref.shape[0], step):
        rows = gain_ref[at : at + step, :]
        update = lax.dot_general(gradient, rows, NT, preferred_element_type=F32)
        for i in range(step // BLK):
            yield at // BLK + i, update[:, i * BLK : (i + 1) * BLK]


def first_update_kernel(
    grad_ref, back_first_ref, back_second_ref, ties_ref, gain_ref, x_ref, x_others_refs,
    kept_ref, given_refs, message_ref, first_ref, work_ref,
):
    gradient = full_gradient(grad_ref, back_first_ref, back_second_ref, ties_ref, work_ref)
    held, snaps = kept_ref.shape[:2]
    me = lax.axis_index("snap")
    for i, update in updates(gradient, gain_ref):
        columns = pl.ds(pl.multiple_of((me * held + i) * BLK, BLK), BLK)
        parts = [x_ref[:, columns]] + [o[:, i * BLK : (i + 1) * BLK] for o in x_others_refs]
        state = jnp.concatenate(parts, axis=0) + update
        kept_ref[i] = state[:snaps]
        for j, given_ref in enumerate(given_refs, 1):
            given_ref[i] = state[j * snaps : (j + 1) * snaps]
        message_ref[i] = state.astype(BF16)
    pick(message_ref, ties_ref, 1 - parity(), first_ref, me * held)


def last_update_kernel(
    grad_ref, back_first_ref, back_second_ref, ties_ref, gain_ref, kept_ref, mine_ref, sent_refs, work_ref
):
    gradient = full_gradient(grad_ref, back_first_ref, back_second_ref, ties_ref, work_ref)
    snaps = mine_ref.shape[0]
    for i, update in updates(gradient, gain_ref):
        columns = slice(i * BLK, (i + 1) * BLK)
        mine_ref[:, columns] = kept_ref[i] + update[:snaps]
        for j, sent_ref in enumerate(sent_refs, 1):
            sent_ref[:, columns] = update[j * snaps : (j + 1) * snaps].astype(BF16)


def finish_kernel(mine_ref, states_refs, updates_refs, out_ref):
    width = mine_ref.shape[1]
    members = len(states_refs) + 1
    me = lax.axis_index("snap")
    out_ref[:, pl.ds(pl.multiple_of(me * width, BLK), width)] = mine_ref[...]
    for i, (state_ref, update_ref) in enumerate(zip(states_refs, updates_refs), 1):
        at = lax.rem(me + i, members) * width
        for b in range(width // BLK):
            update = update_ref[:, b * BLK : (b + 1) * BLK].astype(F32)
            columns = pl.ds(pl.multiple_of(at + b * BLK, BLK), BLK)
            out_ref[:, columns] = state_ref[b] + update


def swap_pair(block, start):
    pairs = [(i, i + 1) for i in range(start, lax.axis_size("area") - 1, 2)]
    return lax.ppermute(block, "area", pairs + [(b, a) for a, b in pairs])


def with_neighbours(first, second):
    return swap_pair(first, 1), swap_pair(second, 0)


def from_snap(block, distance):
    members = lax.axis_size("snap")
    return lax.ppermute(block, "snap", [(i, (i + distance) % members) for i in range(members)])


def from_all(block):
    return jnp.stack([from_snap(block, i) for i in range(1, lax.axis_size("snap"))])


def shape(dims, kind):
    return jax.ShapeDtypeStruct(dims, kind)


def on_device(
    phasor_readings,
    reading_error_spread,
    starting_voltages,
    derivative_pieces,
    derivative_tile_position,
    frontier_voltage_pieces,
    holder_line_order,
    hub_line_order,
    reciprocal_normal_operator,
):
    snaps, lines = phasor_readings.shape
    states = starting_voltages.shape[1]
    own = states // BLK
    measure = derivative_pieces.shape[0]
    ties_table = frontier_voltage_pieces[0]
    ties = ties_table.shape[1]
    slots = own + 2 * ties
    members = lax.axis_size("snap")
    areas = lax.axis_size("area")
    everything = snaps * members
    held = reciprocal_normal_operator.shape[0] // BLK
    place = derivative_tile_position[0].T
    cap = hub_line_order.shape[2]
    width = max(cap, BLK)
    chunks = areas * cap // width
    hub = hub_line_order[0].reshape(chunks, width)
    holder = holder_line_order[0].reshape(chunks, width)
    depth = (width // BLK) * snaps + 8

    message, rounded, x_sent = call(
        pack_kernel,
        (
            shape((chunks, depth, BLK), F32),
            shape((own, snaps, BLK), BF16),
            [shape((snaps, held * BLK), F32)] * (members - 1),
        ),
        [HBM] * 4,
        (
            phasor_readings,
            reading_error_spread.reshape(lines // BLK, BLK),
            hub,
            starting_voltages,
        ),
        scratch=[
            pltpu.VMEM((snaps, lines), F32),
            pltpu.VMEM((lines // BLK, BLK), F32),
            pltpu.VMEM((chunks, width), jnp.int32),
            pltpu.VMEM((snaps, states), F32),
            pltpu.VMEM((chunks, depth, BLK), F32),
            pltpu.VMEM((own, snaps, BLK), BF16),
            pltpu.SemaphoreType.DMA((4,)),
            pltpu.SemaphoreType.DMA((chunks,)),
            pltpu.SemaphoreType.DMA((members,)),
        ],
        out_spec=(HBM, HBM, [HBM] * (members - 1)),
        mib=60,
        name="pack_readings",
    )
    each = width // cap
    if each > 1:
        message = message.reshape(chunks, depth, each, cap).transpose(0, 2, 1, 3)
        message = message.reshape(areas, depth, cap)
    message = lax.all_to_all(message, "area", split_axis=0, concat_axis=0, tiled=True)
    if each > 1:
        message = message.reshape(chunks, each, depth, cap).transpose(0, 2, 1, 3)
        message = message.reshape(chunks, depth, BLK)

    group, lane = call(
        inverse_kernel,
        (shape((lines // BLK, BLK), jnp.int32),) * 2,
        [VMEM],
        (holder,),
        flops=10**9,
        name="invert_order",
    )
    boundary = shape((ties, everything, BLK), BF16)
    owns = [rounded] + [from_snap(rounded, i) for i in range(1, members)]
    first, second = call(
        pick_kernel,
        (boundary, boundary),
        [[VMEM] * members, SMEM],
        (owns, ties_table),
        name="pick_boundary",
    )
    first, second, x_sent = lax.optimization_barrier((first, second, x_sent))
    first, second = with_neighbours(first, second)
    x_others = [from_snap(block, i) for i, block in enumerate(x_sent, 1)]
    guess = call(
        predict_kernel,
        shape((everything, lines), F32),
        [VMEM, VMEM, [VMEM] * members, VMEM, SMEM],
        (first, second, owns, derivative_pieces, place),
        scratch=[pltpu.VMEM((slots, everything, BLK), BF16)],
        flops=10**9,
        name="predict",
    )
    message, guess, x_others = lax.optimization_barrier((message, guess, x_others))
    halves = []
    for part in range(2):
        halves.append(
            call(
                functools.partial(unpack_kernel, part * (lines // BLK // 2)),
                (shape((snaps, lines // 2), F32), shape((1, lines // 2), F32)),
                [VMEM, VMEM, VMEM],
                (group, lane, message),
                scratch=[pltpu.VMEM((chunks * (width // BLK), BLK), F32)],
                flops=2 * 10**9,
                name="unpack_readings",
            )
        )
    readings = [half[0] for half in halves]
    variance = [half[1] for half in halves]
    reading_others = [from_all(half) for half in readings]
    grads = (
        shape((own, everything, BLK), F32),
        boundary,
        boundary,
    )
    total = pltpu.VMEM((slots, everything, BLK), F32)
    work = pltpu.VMEM((own, everything, BLK), F32)
    grad, first, second = call(
        pull_kernel,
        grads,
        [VMEM, [VMEM] * 2, [VMEM] * 2, [VMEM] * 2, VMEM, SMEM],
        (guess, readings, reading_others, variance, derivative_pieces, place),
        scratch=[total, pltpu.VMEM((everything, lines), BF16)],
        name="pull",
    )
    arrived = with_neighbours(first, second)
    kept, given, mine, first = call(
        first_update_kernel,
        (
            shape((held, snaps, BLK), F32),
            [shape((held, snaps, BLK), F32)] * (members - 1),
            shape((held, everything, BLK), BF16),
            boundary,
        ),
        [VMEM, VMEM, VMEM, SMEM, VMEM, VMEM, [VMEM] * (members - 1)],
        (
            grad, *arrived, ties_table, reciprocal_normal_operator,
            starting_voltages, x_others,
        ),
        scratch=[work],
        name="first_update",
    )
    others = [from_snap(mine, i) for i in range(1, members)]
    first = swap_pair(first, 1)
    firsts = [first] + [from_snap(first, i) for i in range(1, members)]
    aug, second = call(
        join_states_kernel,
        (shape((own, everything, BLK), BF16), boundary),
        [VMEM, [VMEM] * (members - 1), SMEM],
        (mine, others, ties_table),
        name="join_states",
    )
    second = swap_pair(second, 0)
    grad, first, second = call(
        predict_pull_kernel,
        grads,
        [[VMEM] * members, VMEM, VMEM, [VMEM] * 2, [VMEM] * 2, [VMEM] * 2, VMEM, SMEM],
        (firsts, aug, second, readings, reading_others, variance, derivative_pieces, place),
        scratch=[
            pltpu.VMEM((slots, everything, BLK), BF16),
            pltpu.VMEM((everything, lines), F32),
            total,
            pltpu.VMEM((everything, lines), BF16),
        ],
        name="predict_pull",
    )
    given, first, second = lax.optimization_barrier((given, first, second))
    first, second = with_neighbours(first, second)
    states_in = [from_snap(block, -i) for i, block in enumerate(given, 1)]
    mine, sent = call(
        last_update_kernel,
        (
            shape((snaps, held * BLK), F32),
            [shape((snaps, held * BLK), BF16)] * (members - 1),
        ),
        [VMEM, VMEM, VMEM, SMEM, VMEM, VMEM],
        (grad, first, second, ties_table, reciprocal_normal_operator, kept),
        scratch=[work],
        name="last_update",
    )
    return call(
        finish_kernel,
        shape((snaps, states), F32),
        [VMEM, [VMEM] * (members - 1), [VMEM] * (members - 1)],
        (mine, states_in, [from_snap(block, -i) for i, block in enumerate(sent, 1)]),
        name="finish",
    )


def solution(mesh):
    placed = (
        P("snap", "area"),
        P("area"),
        P("snap", "area"),
        P("area", None, None, None),
        P("area", None, None),
        P("area", None, None),
        P("area", None, None),
        P("area", None, None),
        P(("area", "snap"), None),
    )
    return jax.shard_map(
        on_device, mesh=mesh, in_specs=placed, out_specs=P("snap", "area"), check_vma=False
    )
```

```python
import functools

import jax
import jax.numpy as jnp
from jax import lax
from jax.experimental import pallas as pl
from jax.experimental.pallas import tpu as pltpu
from jax.sharding import PartitionSpec as P

BLK = 128
ITERS = 2
F32 = jnp.float32
BF16 = jnp.bfloat16
NT = (((1,), (1,)), ((), ()))
VMEM = pl.BlockSpec(memory_space=pltpu.VMEM)
HBM = pl.BlockSpec(memory_space=pltpu.HBM)
SMEM = pl.BlockSpec(memory_space=pltpu.SMEM)


def call(kernel, outs, ins, args, scratch=(), flops=0, mib=12, out_spec=None, name=None):
    return pl.pallas_call(
        kernel,
        out_shape=outs,
        in_specs=ins,
        out_specs=jax.tree.map(lambda _: VMEM, outs) if out_spec is None else out_spec,
        scratch_shapes=list(scratch),
        compiler_params=pltpu.CompilerParams(vmem_limit_bytes=mib * 1024 * 1024),
        cost_estimate=pl.CostEstimate(
            flops=flops, bytes_accessed=0, transcendentals=0
        ),
        name=name,
    )(*args)


def lane_gather(values, lanes):
    return jnp.take_along_axis(values, lanes, axis=1, mode="promise_in_bounds")


def rows_iota(shape):
    return lax.broadcasted_iota(jnp.int32, shape, 0)


def pack_kernel(
    z_in, v_in, hub_in, x_in, out, rounded_out, sent_outs,
    z_ref, v_ref, hub_ref, x_ref, out_ref, rounded_ref,
    sems, out_sems, sent_sems,
):
    pairs = ((x_in, x_ref), (hub_in, hub_ref), (z_in, z_ref), (v_in, v_ref))
    copies = [
        pltpu.make_async_copy(source, target, sems.at[i])
        for i, (source, target) in enumerate(pairs)
    ]
    for copy in copies:
        copy.start()
    for copy in copies:
        copy.wait()
    for b in range(rounded_ref.shape[0]):
        rounded_ref[b] = x_ref[:, b * BLK : (b + 1) * BLK].astype(BF16)
    ready = [(rounded_ref, rounded_out)]
    members = len(sent_outs) + 1
    part = x_ref.shape[1] // members
    for i, sent_out in enumerate(sent_outs, 1):
        at = lax.rem(lax.axis_index("snap") + i, members) * part
        ready.append((x_ref.at[:, pl.ds(pl.multiple_of(at, BLK), part)], sent_out))
    sends = [
        pltpu.make_async_copy(source, target, sent_sems.at[i])
        for i, (source, target) in enumerate(ready)
    ]
    for copy in sends:
        copy.start()
    snaps, lines = z_ref.shape
    blocks = lines // BLK
    chunks, width = hub_ref.shape
    groups = width // BLK
    for d in range(chunks):
        tail = jnp.zeros((8, BLK), F32)
        for g in range(groups):
            slot = hub_ref[d : d + 1, g * BLK : (g + 1) * BLK]
            high = jnp.right_shift(slot, 7)
            low = jnp.bitwise_and(slot, 127)
            lanes = jnp.broadcast_to(low, (snaps, BLK))
            block_of = jnp.broadcast_to(high, (snaps, BLK))
            picked = jnp.zeros((snaps, BLK), F32)
            for b in range(blocks):
                found = lane_gather(z_ref[:, b * BLK : (b + 1) * BLK], lanes)
                picked = jnp.where(block_of == b, found, picked)
            out_ref[d, g * snaps : (g + 1) * snaps, :] = picked
            found = lane_gather(v_ref[...], jnp.broadcast_to(low, (blocks, BLK)))
            mine = rows_iota((blocks, BLK)) == high
            variance = jnp.sum(jnp.where(mine, found, 0.0), axis=0, keepdims=True)
            tail = jnp.where(rows_iota((8, BLK)) == g, variance, tail)
        out_ref[d, groups * snaps :, :] = tail
        pltpu.make_async_copy(out_ref.at[d], out.at[d], out_sems.at[d]).start()
    for d in range(chunks):
        pltpu.make_async_copy(out_ref.at[d], out.at[d], out_sems.at[d]).wait()
    for copy in sends:
        copy.wait()


def inverse_kernel(own_ref, handed_refs, group_ref, lane_ref, kept_refs):
    for handed_ref, kept_ref in zip(handed_refs, kept_refs):
        kept_ref[...] = handed_ref[...]
    chunks, width = own_ref.shape
    blocks = group_ref.shape[0]
    groups = width // BLK
    total = jnp.zeros((2 * blocks, BLK), F32)
    lane = lax.broadcasted_iota(jnp.int32, (2 * blocks, width), 1)
    row = rows_iota((2 * blocks, width))
    in_group = jnp.bitwise_and(lane, 127)
    group_in = jnp.right_shift(lane, 7)
    for d in range(chunks):
        owned = own_ref[d : d + 1, :]
        high = jnp.right_shift(owned, 7)
        low = jnp.bitwise_and(owned, 127)
        label = jnp.where(row < blocks, group_in + d * groups, in_group)
        hit = jnp.bitwise_and(row, blocks - 1) == high
        left = jnp.where(hit, label.astype(F32), 0.0).astype(BF16)
        right = jnp.where(rows_iota((BLK, width)) == low, 1.0, 0.0).astype(BF16)
        total += lax.dot_general(left, right, NT, preferred_element_type=F32)
    group_ref[...] = total[:blocks].astype(jnp.int32)
    lane_ref[...] = total[blocks:].astype(jnp.int32)


def unpack_kernel(start, group_ref, lane_ref, message_ref, z_ref, v_ref, variance_ref):
    snaps, lines = z_ref.shape
    chunks = message_ref.shape[0]
    groups = (message_ref.shape[1] - 8) // snaps
    total = chunks * groups
    for d in range(chunks):
        variance_ref[d * groups : (d + 1) * groups, :] = message_ref[d, groups * snaps :, :][:groups]
    for b in range(lines // BLK):
        group = group_ref[start + b : start + b + 1, :]
        lane = lane_ref[start + b : start + b + 1, :]
        lanes = jnp.broadcast_to(lane, (snaps, BLK))
        group_of = jnp.broadcast_to(group, (snaps, BLK))
        picked = jnp.zeros((snaps, BLK), F32)
        for g in range(total):
            rows = slice(g % groups * snaps, (g % groups + 1) * snaps)
            found = lane_gather(message_ref[g // groups, rows, :], lanes)
            picked = jnp.where(group_of == g, found, picked)
        columns = slice(b * BLK, (b + 1) * BLK)
        z_ref[:, columns] = picked
        found = lane_gather(variance_ref[...], jnp.broadcast_to(lane, (total, BLK)))
        mine = rows_iota((total, BLK)) == group
        v_ref[:, columns] = jnp.sum(jnp.where(mine, found, 0.0), axis=0, keepdims=True)


def split(ref):
    return [ref.at[i] for i in range(ref.shape[0])]


def parity():
    return 1 - lax.rem(lax.axis_index("area"), 2)


def pick(blocks_ref, listing_ref, side, out_ref, start=0):
    held = blocks_ref.shape[0]
    for t in range(out_ref.shape[0]):
        b = listing_ref[side, t]
        at = b - start
        block = blocks_ref[jnp.clip(at, 0, held - 1)]
        here = (b >= 0) & (at >= 0) & (at < held)
        out_ref[t] = jnp.where(here, block, jnp.zeros_like(block))


def slots_into(slots_ref, aug_ref, first, second_ref):
    own = aug_ref.shape[0]
    ties = second_ref.shape[0]
    slots_ref[:own] = aug_ref[...]
    slots_ref[pl.ds(own + ties * (1 - parity()), ties)] = first
    slots_ref[pl.ds(own + ties * parity(), ties)] = second_ref[...]


def reordered(ref, distance, members):
    snaps = ref.shape[1] // members
    order = [(n - distance) % members for n in range(members)]
    return jnp.concatenate([ref[:, j * snaps : (j + 1) * snaps] for j in order], axis=1)


def join_states_kernel(mine_ref, others_refs, ties_ref, aug_ref, second_ref):
    members = len(others_refs) + 1
    held = mine_ref.shape[0]
    me = lax.axis_index("snap")
    aug_ref[pl.ds(me * held, held)] = mine_ref[...]
    for i, ref in enumerate(others_refs, 1):
        at = lax.rem(me + members - i, members) * held
        aug_ref[pl.ds(at, held)] = reordered(ref, i, members)
    pick(aug_ref, ties_ref, parity(), second_ref)


def predicted(j, slots_ref, tiles_ref, place_ref):
    touched = tiles_ref.shape[1]
    chosen = jnp.concatenate([slots_ref[place_ref[k, j]] for k in range(touched)], axis=1)
    weights = jnp.concatenate([tiles_ref[j, k] for k in range(touched)], axis=1)
    return lax.dot_general(chosen, weights, NT, preferred_element_type=F32)


def pick_kernel(own_refs, ties_ref, first_ref, second_ref):
    snaps = own_refs[0].shape[1]
    for i, own_ref in enumerate(own_refs):
        rows = slice(i * snaps, (i + 1) * snaps)
        pick(own_ref, ties_ref, 1 - parity(), first_ref.at[:, rows])
        pick(own_ref, ties_ref, parity(), second_ref.at[:, rows])


def predict_kernel(
    first_ref, second_ref, own_refs, tiles_ref, place_ref, out_ref, slots_ref
):
    own, snaps = own_refs[0].shape[:2]
    ties = first_ref.shape[0]
    for i, own_ref in enumerate(own_refs):
        slots_ref[:own, i * snaps : (i + 1) * snaps] = own_ref[...]
    slots_ref[pl.ds(own + ties * (1 - parity()), ties)] = first_ref[...]
    slots_ref[pl.ds(own + ties * parity(), ties)] = second_ref[...]
    predict(tiles_ref, place_ref, out_ref, slots_ref)


def predict(tiles_ref, place_ref, out_ref, slots_ref):
    for j in range(tiles_ref.shape[0]):
        out_ref[:, j * BLK : (j + 1) * BLK] = predicted(j, slots_ref, tiles_ref, place_ref)


def weigh(j, guess, z_refs, others_refs, v_refs):
    each = z_refs[0].shape[1] // BLK
    z_ref, others_ref, v_ref = z_refs[j // each], others_refs[j // each], v_refs[j // each]
    columns = slice(j % each * BLK, (j % each + 1) * BLK)
    readings = [z_ref[:, columns]] + [o[:, columns] for o in split(others_ref)]
    resid = jnp.concatenate(readings, axis=0) - guess
    spread = jnp.sum(resid * resid, axis=0, keepdims=True) / resid.shape[0]
    return (resid / (v_ref[:, columns] + spread)).astype(BF16)


def pull(weighted_ref, tiles_ref, place_ref, total_ref, own_ref, first_ref, second_ref):
    total_ref[...] = jnp.zeros_like(total_ref)
    touched = tiles_ref.shape[1]
    for j in range(tiles_ref.shape[0]):
        weighted = weighted_ref[:, j * BLK : (j + 1) * BLK]
        weights = jnp.concatenate([tiles_ref[j, k] for k in range(touched)], axis=1)
        part = jnp.dot(weighted, weights, preferred_element_type=F32)
        for k in range(touched):
            n = place_ref[k, j]
            total_ref[n] += part[:, k * BLK : (k + 1) * BLK]
    own = own_ref.shape[0]
    ties = first_ref.shape[0]
    own_ref[...] = total_ref[:own]
    first = total_ref[pl.ds(own + ties * (1 - parity()), ties)]
    second = total_ref[pl.ds(own + ties * parity(), ties)]
    first_ref[...] = first.astype(first_ref.dtype)
    second_ref[...] = second.astype(second_ref.dtype)


def pull_kernel(
    guess_ref, z_refs, others_refs, v_refs, tiles_ref, place_ref, own_ref, first_ref, second_ref,
    total_ref, weighted_ref,
):
    for j in range(tiles_ref.shape[0]):
        columns = slice(j * BLK, (j + 1) * BLK)
        weighted_ref[:, columns] = weigh(j, guess_ref[:, columns], z_refs, others_refs, v_refs)
    pull(weighted_ref, tiles_ref, place_ref, total_ref, own_ref, first_ref, second_ref)


def predict_pull_kernel(
    first_refs, aug_ref, second_in_ref, z_refs, others_refs, v_refs, tiles_ref, place_ref,
    own_ref, first_ref, second_ref, slots_ref, guess_ref, total_ref, weighted_ref,
):
    parts = [reordered(ref, i, len(first_refs)) for i, ref in enumerate(first_refs)]
    slots_into(slots_ref, aug_ref, sum(parts[1:], parts[0]), second_in_ref)
    predict(tiles_ref, place_ref, guess_ref, slots_ref)
    pull_kernel(
        guess_ref, z_refs, others_refs, v_refs, tiles_ref, place_ref, own_ref, first_ref, second_ref,
        total_ref, weighted_ref,
    )


def full_gradient(grad_ref, back_first_ref, back_second_ref, ties_ref, work_ref):
    work_ref[...] = grad_ref[...]
    for side, back_ref in ((1 - parity(), back_first_ref), (parity(), back_second_ref)):
        for t in range(back_ref.shape[0]):
            b = ties_ref[side, t]

            @pl.when(b >= 0)
            def _(b=b, t=t, back_ref=back_ref):
                work_ref[b] += back_ref[t].astype(F32)

    return jnp.concatenate([work_ref[b].astype(BF16) for b in range(work_ref.shape[0])], axis=1)


def updates(gradient, gain_ref):
    step = min(2 * BLK, gain_ref.shape[0])
    for at in range(0, gain_ref.shape[0], step):
        rows = gain_ref[at : at + step, :]
        update = lax.dot_general(gradient, rows, NT, preferred_element_type=F32)
        for i in range(step // BLK):
            yield at // BLK + i, update[:, i * BLK : (i + 1) * BLK]


def first_update_kernel(
    grad_ref, back_first_ref, back_second_ref, ties_ref, gain_ref, x_ref, x_others_refs,
    kept_ref, given_refs, message_ref, first_ref, work_ref,
):
    gradient = full_gradient(grad_ref, back_first_ref, back_second_ref, ties_ref, work_ref)
    held, snaps = kept_ref.shape[:2]
    me = lax.axis_index("snap")
    for i, update in updates(gradient, gain_ref):
        columns = pl.ds(pl.multiple_of((me * held + i) * BLK, BLK), BLK)
        parts = [x_ref[:, columns]] + [o[:, i * BLK : (i + 1) * BLK] for o in x_others_refs]
        state = jnp.concatenate(parts, axis=0) + update
        kept_ref[i] = state[:snaps]
        for j, given_ref in enumerate(given_refs, 1):
            given_ref[i] = state[j * snaps : (j + 1) * snaps]
        message_ref[i] = state.astype(BF16)
    pick(message_ref, ties_ref, 1 - parity(), first_ref, me * held)


def last_update_kernel(
    grad_ref, back_first_ref, back_second_ref, ties_ref, gain_ref, kept_ref, mine_ref, sent_refs, work_ref
):
    gradient = full_gradient(grad_ref, back_first_ref, back_second_ref, ties_ref, work_ref)
    snaps = mine_ref.shape[0]
    for i, update in updates(gradient, gain_ref):
        columns = slice(i * BLK, (i + 1) * BLK)
        mine_ref[:, columns] = kept_ref[i] + update[:snaps]
        for j, sent_ref in enumerate(sent_refs, 1):
            sent_ref[:, columns] = update[j * snaps : (j + 1) * snaps].astype(BF16)


def finish_kernel(mine_ref, states_refs, updates_refs, out_ref):
    width = mine_ref.shape[1]
    members = len(states_refs) + 1
    me = lax.axis_index("snap")
    out_ref[:, pl.ds(pl.multiple_of(me * width, BLK), width)] = mine_ref[...]
    for i, (state_ref, update_ref) in enumerate(zip(states_refs, updates_refs), 1):
        at = lax.rem(me + i, members) * width
        for b in range(width // BLK):
            update = update_ref[:, b * BLK : (b + 1) * BLK].astype(F32)
            columns = pl.ds(pl.multiple_of(at + b * BLK, BLK), BLK)
            out_ref[:, columns] = state_ref[b] + update


def swap_pair(block, start):
    pairs = [(i, i + 1) for i in range(start, lax.axis_size("area") - 1, 2)]
    return lax.ppermute(block, "area", pairs + [(b, a) for a, b in pairs])


def with_neighbours(first, second):
    return swap_pair(first, 1), swap_pair(second, 0)


def from_snap(block, distance):
    members = lax.axis_size("snap")
    return lax.ppermute(block, "snap", [(i, (i + distance) % members) for i in range(members)])


def from_all(block):
    return jnp.stack([from_snap(block, i) for i in range(1, lax.axis_size("snap"))])


def shape(dims, kind):
    return jax.ShapeDtypeStruct(dims, kind)


def on_device(
    phasor_readings,
    reading_error_spread,
    starting_voltages,
    derivative_pieces,
    derivative_tile_position,
    frontier_voltage_pieces,
    holder_line_order,
    hub_line_order,
    reciprocal_normal_operator,
):
    snaps, lines = phasor_readings.shape
    states = starting_voltages.shape[1]
    own = states // BLK
    measure = derivative_pieces.shape[0]
    ties_table = frontier_voltage_pieces[0]
    ties = ties_table.shape[1]
    slots = own + 2 * ties
    members = lax.axis_size("snap")
    areas = lax.axis_size("area")
    everything = snaps * members
    held = reciprocal_normal_operator.shape[0] // BLK
    place = derivative_tile_position[0].T
    cap = hub_line_order.shape[2]
    width = max(cap, BLK)
    chunks = areas * cap // width
    hub = hub_line_order[0].reshape(chunks, width)
    holder = holder_line_order[0].reshape(chunks, width)
    depth = (width // BLK) * snaps + 8

    message, rounded, x_sent = call(
        pack_kernel,
        (
            shape((chunks, depth, BLK), F32),
            shape((own, snaps, BLK), BF16),
            [shape((snaps, held * BLK), F32)] * (members - 1),
        ),
        [HBM] * 4,
        (
            phasor_readings,
            reading_error_spread.reshape(lines // BLK, BLK),
            hub,
            starting_voltages,
        ),
        scratch=[
            pltpu.VMEM((snaps, lines), F32),
            pltpu.VMEM((lines // BLK, BLK), F32),
            pltpu.VMEM((chunks, width), jnp.int32),
            pltpu.VMEM((snaps, states), F32),
            pltpu.VMEM((chunks, depth, BLK), F32),
            pltpu.VMEM((own, snaps, BLK), BF16),
            pltpu.SemaphoreType.DMA((4,)),
            pltpu.SemaphoreType.DMA((chunks,)),
            pltpu.SemaphoreType.DMA((members,)),
        ],
        out_spec=(HBM, HBM, [HBM] * (members - 1)),
        mib=60,
        name="pack_readings",
    )
    each = width // cap
    if each > 1:
        message = message.reshape(chunks, depth, each, cap).transpose(0, 2, 1, 3)
        message = message.reshape(areas, depth, cap)
    message = lax.all_to_all(message, "area", split_axis=0, concat_axis=0, tiled=True)
    if each > 1:
        message = message.reshape(chunks, each, depth, cap).transpose(0, 2, 1, 3)
        message = message.reshape(chunks, depth, BLK)

    rounded_others = [from_snap(rounded, i) for i in range(1, members)]
    handed = [rounded, ties_table, place]
    table = shape((lines // BLK, BLK), jnp.int32)
    group, lane, (rounded, ties_table, place) = call(
        inverse_kernel,
        (table, table, [shape(a.shape, a.dtype) for a in handed]),
        [VMEM, [VMEM] * 3],
        (holder, handed),
        flops=10**9,
        name="invert_order",
    )
    boundary = shape((ties, everything, BLK), BF16)
    owns = [rounded] + rounded_others
    first, second = call(
        pick_kernel,
        (boundary, boundary),
        [[VMEM] * members, SMEM],
        (owns, ties_table),
        name="pick_boundary",
    )
    first, second, x_sent = lax.optimization_barrier((first, second, x_sent))
    first, second = with_neighbours(first, second)
    x_others = [from_snap(block, i) for i, block in enumerate(x_sent, 1)]
    guess = call(
        predict_kernel,
        shape((everything, lines), F32),
        [VMEM, VMEM, [VMEM] * members, VMEM, SMEM],
        (first, second, owns, derivative_pieces, place),
        scratch=[pltpu.VMEM((slots, everything, BLK), BF16)],
        flops=10**9,
        name="predict",
    )
    message, guess, x_others = lax.optimization_barrier((message, guess, x_others))
    halves = []
    for part in range(2):
        halves.append(
            call(
                functools.partial(unpack_kernel, part * (lines // BLK // 2)),
                (shape((snaps, lines // 2), F32), shape((1, lines // 2), F32)),
                [VMEM, VMEM, VMEM],
                (group, lane, message),
                scratch=[pltpu.VMEM((chunks * (width // BLK), BLK), F32)],
                flops=2 * 10**9,
                name="unpack_readings",
            )
        )
    readings = [half[0] for half in halves]
    variance = [half[1] for half in halves]
    reading_others = [from_all(half) for half in readings]
    grads = (
        shape((own, everything, BLK), F32),
        boundary,
        boundary,
    )
    total = pltpu.VMEM((slots, everything, BLK), F32)
    work = pltpu.VMEM((own, everything, BLK), F32)
    grad, first, second = call(
        pull_kernel,
        grads,
        [VMEM, [VMEM] * 2, [VMEM] * 2, [VMEM] * 2, VMEM, SMEM],
        (guess, readings, reading_others, variance, derivative_pieces, place),
        scratch=[total, pltpu.VMEM((everything, lines), BF16)],
        name="pull",
    )
    arrived = with_neighbours(first, second)
    kept, given, mine, first = call(
        first_update_kernel,
        (
            shape((held, snaps, BLK), F32),
            [shape((held, snaps, BLK), F32)] * (members - 1),
            shape((held, everything, BLK), BF16),
            boundary,
        ),
        [VMEM, VMEM, VMEM, SMEM, VMEM, VMEM, [VMEM] * (members - 1)],
        (
            grad, *arrived, ties_table, reciprocal_normal_operator,
            starting_voltages, x_others,
        ),
        scratch=[work],
        name="first_update",
    )
    others = [from_snap(mine, i) for i in range(1, members)]
    first = swap_pair(first, 1)
    firsts = [first] + [from_snap(first, i) for i in range(1, members)]
    aug, second = call(
        join_states_kernel,
        (shape((own, everything, BLK), BF16), boundary),
        [VMEM, [VMEM] * (members - 1), SMEM],
        (mine, others, ties_table),
        name="join_states",
    )
    second = swap_pair(second, 0)
    grad, first, second = call(
        predict_pull_kernel,
        grads,
        [[VMEM] * members, VMEM, VMEM, [VMEM] * 2, [VMEM] * 2, [VMEM] * 2, VMEM, SMEM],
        (firsts, aug, second, readings, reading_others, variance, derivative_pieces, place),
        scratch=[
            pltpu.VMEM((slots, everything, BLK), BF16),
            pltpu.VMEM((everything, lines), F32),
            total,
            pltpu.VMEM((everything, lines), BF16),
        ],
        name="predict_pull",
    )
    given, first, second = lax.optimization_barrier((given, first, second))
    first, second = with_neighbours(first, second)
    states_in = [from_snap(block, -i) for i, block in enumerate(given, 1)]
    mine, sent = call(
        last_update_kernel,
        (
            shape((snaps, held * BLK), F32),
            [shape((snaps, held * BLK), BF16)] * (members - 1),
        ),
        [VMEM, VMEM, VMEM, SMEM, VMEM, VMEM],
        (grad, first, second, ties_table, reciprocal_normal_operator, kept),
        scratch=[work],
        name="last_update",
    )
    return call(
        finish_kernel,
        shape((snaps, states), F32),
        [VMEM, [VMEM] * (members - 1), [VMEM] * (members - 1)],
        (mine, states_in, [from_snap(block, -i) for i, block in enumerate(sent, 1)]),
        name="finish",
    )


def solution(mesh):
    placed = (
        P("snap", "area"),
        P("area"),
        P("snap", "area"),
        P("area", None, None, None),
        P("area", None, None),
        P("area", None, None),
        P("area", None, None),
        P("area", None, None),
        P(("area", "snap"), None),
    )
    return jax.shard_map(
        on_device, mesh=mesh, in_specs=placed, out_specs=P("snap", "area"), check_vma=False
    )
```

```python
import functools

import jax
import jax.numpy as jnp
from jax import lax
from jax.experimental import pallas as pl
from jax.experimental.pallas import tpu as pltpu
from jax.sharding import PartitionSpec as P

BLK = 128
ITERS = 2
F32 = jnp.float32
BF16 = jnp.bfloat16
NT = (((1,), (1,)), ((), ()))
VMEM = pl.BlockSpec(memory_space=pltpu.VMEM)
HBM = pl.BlockSpec(memory_space=pltpu.HBM)
SMEM = pl.BlockSpec(memory_space=pltpu.SMEM)


def call(kernel, outs, ins, args, scratch=(), flops=0, mib=12, out_spec=None, name=None):
    return pl.pallas_call(
        kernel,
        out_shape=outs,
        in_specs=ins,
        out_specs=jax.tree.map(lambda _: VMEM, outs) if out_spec is None else out_spec,
        scratch_shapes=list(scratch),
        compiler_params=pltpu.CompilerParams(vmem_limit_bytes=mib * 1024 * 1024),
        cost_estimate=pl.CostEstimate(
            flops=flops, bytes_accessed=0, transcendentals=0
        ),
        name=name,
    )(*args)


def lane_gather(values, lanes):
    return jnp.take_along_axis(values, lanes, axis=1, mode="promise_in_bounds")


def rows_iota(shape):
    return lax.broadcasted_iota(jnp.int32, shape, 0)


def pack_kernel(
    z_in, v_in, hub_in, x_in, out, rounded_out, sent_outs,
    z_ref, v_ref, hub_ref, x_ref, out_ref, rounded_ref,
    sems, out_sems, sent_sems,
):
    pairs = ((x_in, x_ref), (hub_in, hub_ref), (z_in, z_ref), (v_in, v_ref))
    copies = [
        pltpu.make_async_copy(source, target, sems.at[i])
        for i, (source, target) in enumerate(pairs)
    ]
    for copy in copies:
        copy.start()
    for copy in copies:
        copy.wait()
    for b in range(rounded_ref.shape[0]):
        rounded_ref[b] = x_ref[:, b * BLK : (b + 1) * BLK].astype(BF16)
    ready = [(rounded_ref, rounded_out)]
    members = len(sent_outs) + 1
    part = x_ref.shape[1] // members
    for i, sent_out in enumerate(sent_outs, 1):
        at = lax.rem(lax.axis_index("snap") + i, members) * part
        ready.append((x_ref.at[:, pl.ds(pl.multiple_of(at, BLK), part)], sent_out))
    sends = [
        pltpu.make_async_copy(source, target, sent_sems.at[i])
        for i, (source, target) in enumerate(ready)
    ]
    for copy in sends:
        copy.start()
    snaps, lines = z_ref.shape
    blocks = lines // BLK
    chunks, width = hub_ref.shape
    groups = width // BLK
    for d in range(chunks):
        tail = jnp.zeros((8, BLK), F32)
        for g in range(groups):
            slot = hub_ref[d : d + 1, g * BLK : (g + 1) * BLK]
            high = jnp.right_shift(slot, 7)
            low = jnp.bitwise_and(slot, 127)
            lanes = jnp.broadcast_to(low, (snaps, BLK))
            block_of = jnp.broadcast_to(high, (snaps, BLK))
            picked = jnp.zeros((snaps, BLK), F32)
            for b in range(blocks):
                found = lane_gather(z_ref[:, b * BLK : (b + 1) * BLK], lanes)
                picked = jnp.where(block_of == b, found, picked)
            out_ref[d, g * snaps : (g + 1) * snaps, :] = picked
            found = lane_gather(v_ref[...], jnp.broadcast_to(low, (blocks, BLK)))
            mine = rows_iota((blocks, BLK)) == high
            variance = jnp.sum(jnp.where(mine, found, 0.0), axis=0, keepdims=True)
            tail = jnp.where(rows_iota((8, BLK)) == g, variance, tail)
        out_ref[d, groups * snaps :, :] = tail
        pltpu.make_async_copy(out_ref.at[d], out.at[d], out_sems.at[d]).start()
    for d in range(chunks):
        pltpu.make_async_copy(out_ref.at[d], out.at[d], out_sems.at[d]).wait()
    for copy in sends:
        copy.wait()


def inverse_kernel(own_ref, handed_refs, group_ref, lane_ref, kept_refs):
    for handed_ref, kept_ref in zip(handed_refs, kept_refs):
        kept_ref[...] = handed_ref[...]
    chunks, width = own_ref.shape
    blocks = group_ref.shape[0]
    groups = width // BLK
    total = jnp.zeros((2 * blocks, BLK), F32)
    lane = lax.broadcasted_iota(jnp.int32, (2 * blocks, width), 1)
    row = rows_iota((2 * blocks, width))
    in_group = jnp.bitwise_and(lane, 127)
    group_in = jnp.right_shift(lane, 7)
    for d in range(chunks):
        owned = own_ref[d : d + 1, :]
        high = jnp.right_shift(owned, 7)
        low = jnp.bitwise_and(owned, 127)
        label = jnp.where(row < blocks, group_in + d * groups, in_group)
        hit = jnp.bitwise_and(row, blocks - 1) == high
        left = jnp.where(hit, label.astype(F32), 0.0).astype(BF16)
        right = jnp.where(rows_iota((BLK, width)) == low, 1.0, 0.0).astype(BF16)
        total += lax.dot_general(left, right, NT, preferred_element_type=F32)
    group_ref[...] = total[:blocks].astype(jnp.int32)
    lane_ref[...] = total[blocks:].astype(jnp.int32)


def unpack_kernel(start, group_ref, lane_ref, message_ref, z_ref, v_ref, variance_ref):
    snaps, lines = z_ref.shape
    chunks = message_ref.shape[0]
    groups = (message_ref.shape[1] - 8) // snaps
    total = chunks * groups
    for d in range(chunks):
        variance_ref[d * groups : (d + 1) * groups, :] = message_ref[d, groups * snaps :, :][:groups]
    for b in range(lines // BLK):
        group = group_ref[start + b : start + b + 1, :]
        lane = lane_ref[start + b : start + b + 1, :]
        lanes = jnp.broadcast_to(lane, (snaps, BLK))
        group_of = jnp.broadcast_to(group, (snaps, BLK))
        picked = jnp.zeros((snaps, BLK), F32)
        for g in range(total):
            rows = slice(g % groups * snaps, (g % groups + 1) * snaps)
            found = lane_gather(message_ref[g // groups, rows, :], lanes)
            picked = jnp.where(group_of == g, found, picked)
        columns = slice(b * BLK, (b + 1) * BLK)
        z_ref[:, columns] = picked
        found = lane_gather(variance_ref[...], jnp.broadcast_to(lane, (total, BLK)))
        mine = rows_iota((total, BLK)) == group
        v_ref[:, columns] = jnp.sum(jnp.where(mine, found, 0.0), axis=0, keepdims=True)


def split(ref):
    return [ref.at[i] for i in range(ref.shape[0])]


def parity():
    return 1 - lax.rem(lax.axis_index("area"), 2)


def pick(blocks_ref, listing_ref, side, out_ref, start=0):
    held = blocks_ref.shape[0]
    for t in range(out_ref.shape[0]):
        b = listing_ref[side, t]
        at = b - start
        block = blocks_ref[jnp.clip(at, 0, held - 1)]
        here = (b >= 0) & (at >= 0) & (at < held)
        out_ref[t] = jnp.where(here, block, jnp.zeros_like(block))


def slots_into(slots_ref, aug_ref, first, second_ref):
    own = aug_ref.shape[0]
    ties = second_ref.shape[0]
    slots_ref[:own] = aug_ref[...]
    slots_ref[pl.ds(own + ties * (1 - parity()), ties)] = first
    slots_ref[pl.ds(own + ties * parity(), ties)] = second_ref[...]


def reordered(ref, distance, members):
    snaps = ref.shape[1] // members
    order = [(n - distance) % members for n in range(members)]
    return jnp.concatenate([ref[:, j * snaps : (j + 1) * snaps] for j in order], axis=1)


def join_states_kernel(mine_ref, others_refs, ties_ref, aug_ref, second_ref):
    members = len(others_refs) + 1
    held = mine_ref.shape[0]
    me = lax.axis_index("snap")
    aug_ref[pl.ds(me * held, held)] = mine_ref[...]
    for i, ref in enumerate(others_refs, 1):
        at = lax.rem(me + members - i, members) * held
        aug_ref[pl.ds(at, held)] = reordered(ref, i, members)
    pick(aug_ref, ties_ref, parity(), second_ref)


def predicted(j, slots_ref, tiles_ref, place_ref):
    touched = tiles_ref.shape[1]
    chosen = jnp.concatenate([slots_ref[place_ref[k, j]] for k in range(touched)], axis=1)
    weights = jnp.concatenate([tiles_ref[j, k] for k in range(touched)], axis=1)
    return lax.dot_general(chosen, weights, NT, preferred_element_type=F32)


def pick_kernel(own_refs, ties_ref, first_ref, second_ref):
    snaps = own_refs[0].shape[1]
    for i, own_ref in enumerate(own_refs):
        rows = slice(i * snaps, (i + 1) * snaps)
        pick(own_ref, ties_ref, 1 - parity(), first_ref.at[:, rows])
        pick(own_ref, ties_ref, parity(), second_ref.at[:, rows])


def predict_kernel(
    first_ref, second_ref, own_refs, tiles_ref, place_ref, out_ref, slots_ref
):
    own, snaps = own_refs[0].shape[:2]
    ties = first_ref.shape[0]
    for i, own_ref in enumerate(own_refs):
        slots_ref[:own, i * snaps : (i + 1) * snaps] = own_ref[...]
    slots_ref[pl.ds(own + ties * (1 - parity()), ties)] = first_ref[...]
    slots_ref[pl.ds(own + ties * parity(), ties)] = second_ref[...]
    predict(tiles_ref, place_ref, out_ref, slots_ref)


def predict(tiles_ref, place_ref, out_ref, slots_ref):
    for j in range(tiles_ref.shape[0]):
        out_ref[:, j * BLK : (j + 1) * BLK] = predicted(j, slots_ref, tiles_ref, place_ref)


def weigh(j, guess, z_refs, others_refs, v_refs):
    each = z_refs[0].shape[1] // BLK
    z_ref, others_ref, v_ref = z_refs[j // each], others_refs[j // each], v_refs[j // each]
    columns = slice(j % each * BLK, (j % each + 1) * BLK)
    readings = [z_ref[:, columns]] + [o[:, columns] for o in split(others_ref)]
    resid = jnp.concatenate(readings, axis=0) - guess
    spread = jnp.sum(resid * resid, axis=0, keepdims=True) / resid.shape[0]
    return (resid / (v_ref[:, columns] + spread)).astype(BF16)


def pull(weighted_ref, tiles_ref, place_ref, total_ref, own_ref, first_ref, second_ref):
    total_ref[...] = jnp.zeros_like(total_ref)
    touched = tiles_ref.shape[1]
    for j in range(tiles_ref.shape[0]):
        weighted = weighted_ref[:, j * BLK : (j + 1) * BLK]
        weights = jnp.concatenate([tiles_ref[j, k] for k in range(touched)], axis=1)
        part = jnp.dot(weighted, weights, preferred_element_type=F32)
        for k in range(touched):
            n = place_ref[k, j]
            total_ref[n] += part[:, k * BLK : (k + 1) * BLK]
    own = own_ref.shape[0]
    ties = first_ref.shape[0]
    own_ref[...] = total_ref[:own]
    first = total_ref[pl.ds(own + ties * (1 - parity()), ties)]
    second = total_ref[pl.ds(own + ties * parity(), ties)]
    first_ref[...] = first.astype(first_ref.dtype)
    second_ref[...] = second.astype(second_ref.dtype)


def pull_kernel(
    guess_ref, z_refs, others_refs, v_refs, tiles_ref, place_ref, own_ref, first_ref, second_ref,
    total_ref, weighted_ref,
):
    for j in range(tiles_ref.shape[0]):
        columns = slice(j * BLK, (j + 1) * BLK)
        weighted_ref[:, columns] = weigh(j, guess_ref[:, columns], z_refs, others_refs, v_refs)
    pull(weighted_ref, tiles_ref, place_ref, total_ref, own_ref, first_ref, second_ref)


def predict_pull_kernel(
    first_refs, aug_ref, second_in_ref, z_refs, others_refs, v_refs, tiles_ref, place_ref,
    own_ref, first_ref, second_ref, slots_ref, guess_ref, total_ref, weighted_ref,
):
    parts = [reordered(ref, i, len(first_refs)) for i, ref in enumerate(first_refs)]
    slots_into(slots_ref, aug_ref, sum(parts[1:], parts[0]), second_in_ref)
    predict(tiles_ref, place_ref, guess_ref, slots_ref)
    pull_kernel(
        guess_ref, z_refs, others_refs, v_refs, tiles_ref, place_ref, own_ref, first_ref, second_ref,
        total_ref, weighted_ref,
    )


def partial_update_kernel(grad_ref, ties_ref, gain_ref, part_ref):
    sides, ties = ties_ref.shape
    blocks = []
    for b in range(grad_ref.shape[0]):
        listed = ties_ref[0, 0] == b
        for side in range(sides):
            for t in range(ties):
                listed = listed | (ties_ref[side, t] == b)
        block = grad_ref[b]
        blocks.append(jnp.where(listed, jnp.zeros_like(block), block).astype(BF16))
    gradient = jnp.concatenate(blocks, axis=1)
    step = min(2 * BLK, gain_ref.shape[0])
    for at in range(0, gain_ref.shape[0], step):
        rows = gain_ref[at : at + step, :]
        part_ref[:, at : at + step] = lax.dot_general(
            gradient, rows, NT, preferred_element_type=F32
        )


def updates(part_ref, grad_ref, back_first_ref, back_second_ref, ties_ref, gain_ref, work_ref):
    ties = back_first_ref.shape[0]
    lists = [[ties_ref[side, t] for t in range(ties)] for side in (1 - parity(), parity())]
    for t, b in enumerate(lists[0]):
        block = grad_ref[jnp.maximum(b, 0)] + back_first_ref[t].astype(F32)
        work_ref[t] = jnp.where(b >= 0, block, jnp.zeros_like(block))
    for t, b in enumerate(lists[1]):
        at = ties + t
        for u, other in enumerate(lists[0]):
            at = jnp.where((b >= 0) & (other == b), u, at)
        block = grad_ref[jnp.maximum(b, 0)]
        alone = (b >= 0) & (at == ties + t)
        work_ref[ties + t] = jnp.where(alone, block, jnp.zeros_like(block))
        back = back_second_ref[t].astype(F32)
        work_ref[at] += jnp.where(b >= 0, back, jnp.zeros_like(back))
    listed = lists[0] + lists[1]
    gradient = jnp.concatenate([work_ref[n].astype(BF16) for n in range(len(listed))], axis=1)
    step = min(2 * BLK, gain_ref.shape[0])
    for at in range(0, gain_ref.shape[0], step):
        rows = [
            gain_ref[at : at + step, pl.ds(pl.multiple_of(jnp.maximum(b, 0) * BLK, BLK), BLK)]
            for b in listed
        ]
        update = part_ref[:, at : at + step] + lax.dot_general(
            gradient, jnp.concatenate(rows, axis=1), NT, preferred_element_type=F32
        )
        for i in range(step // BLK):
            yield at // BLK + i, update[:, i * BLK : (i + 1) * BLK]


def first_update_kernel(
    part_ref, grad_ref, back_first_ref, back_second_ref, ties_ref, gain_ref, x_ref, x_others_refs,
    kept_ref, given_refs, message_ref, first_ref, work_ref,
):
    held, snaps = kept_ref.shape[:2]
    me = lax.axis_index("snap")
    operands = part_ref, grad_ref, back_first_ref, back_second_ref, ties_ref, gain_ref, work_ref
    for i, update in updates(*operands):
        columns = pl.ds(pl.multiple_of((me * held + i) * BLK, BLK), BLK)
        parts = [x_ref[:, columns]] + [o[:, i * BLK : (i + 1) * BLK] for o in x_others_refs]
        state = jnp.concatenate(parts, axis=0) + update
        kept_ref[i] = state[:snaps]
        for j, given_ref in enumerate(given_refs, 1):
            given_ref[i] = state[j * snaps : (j + 1) * snaps]
        message_ref[i] = state.astype(BF16)
    pick(message_ref, ties_ref, 1 - parity(), first_ref, me * held)


def last_update_kernel(
    part_ref, grad_ref, back_first_ref, back_second_ref, ties_ref, gain_ref, kept_ref, mine_ref, sent_refs, work_ref
):
    snaps = mine_ref.shape[0]
    operands = part_ref, grad_ref, back_first_ref, back_second_ref, ties_ref, gain_ref, work_ref
    for i, update in updates(*operands):
        columns = slice(i * BLK, (i + 1) * BLK)
        mine_ref[:, columns] = kept_ref[i] + update[:snaps]
        for j, sent_ref in enumerate(sent_refs, 1):
            sent_ref[:, columns] = update[j * snaps : (j + 1) * snaps].astype(BF16)


def finish_kernel(mine_ref, states_refs, updates_refs, out_ref):
    width = mine_ref.shape[1]
    members = len(states_refs) + 1
    me = lax.axis_index("snap")
    out_ref[:, pl.ds(pl.multiple_of(me * width, BLK), width)] = mine_ref[...]
    for i, (state_ref, update_ref) in enumerate(zip(states_refs, updates_refs), 1):
        at = lax.rem(me + i, members) * width
        for b in range(width // BLK):
            update = update_ref[:, b * BLK : (b + 1) * BLK].astype(F32)
            columns = pl.ds(pl.multiple_of(at + b * BLK, BLK), BLK)
            out_ref[:, columns] = state_ref[b] + update


def swap_pair(block, start):
    pairs = [(i, i + 1) for i in range(start, lax.axis_size("area") - 1, 2)]
    return lax.ppermute(block, "area", pairs + [(b, a) for a, b in pairs])


def with_neighbours(first, second):
    return swap_pair(first, 1), swap_pair(second, 0)


def from_snap(block, distance):
    members = lax.axis_size("snap")
    return lax.ppermute(block, "snap", [(i, (i + distance) % members) for i in range(members)])


def from_all(block):
    return jnp.stack([from_snap(block, i) for i in range(1, lax.axis_size("snap"))])


def shape(dims, kind):
    return jax.ShapeDtypeStruct(dims, kind)


def on_device(
    phasor_readings,
    reading_error_spread,
    starting_voltages,
    derivative_pieces,
    derivative_tile_position,
    frontier_voltage_pieces,
    holder_line_order,
    hub_line_order,
    reciprocal_normal_operator,
):
    snaps, lines = phasor_readings.shape
    states = starting_voltages.shape[1]
    own = states // BLK
    measure = derivative_pieces.shape[0]
    ties_table = frontier_voltage_pieces[0]
    ties = ties_table.shape[1]
    slots = own + 2 * ties
    members = lax.axis_size("snap")
    areas = lax.axis_size("area")
    everything = snaps * members
    held = reciprocal_normal_operator.shape[0] // BLK
    place = derivative_tile_position[0].T
    cap = hub_line_order.shape[2]
    width = max(cap, BLK)
    chunks = areas * cap // width
    hub = hub_line_order[0].reshape(chunks, width)
    holder = holder_line_order[0].reshape(chunks, width)
    depth = (width // BLK) * snaps + 8

    message, rounded, x_sent = call(
        pack_kernel,
        (
            shape((chunks, depth, BLK), F32),
            shape((own, snaps, BLK), BF16),
            [shape((snaps, held * BLK), F32)] * (members - 1),
        ),
        [HBM] * 4,
        (
            phasor_readings,
            reading_error_spread.reshape(lines // BLK, BLK),
            hub,
            starting_voltages,
        ),
        scratch=[
            pltpu.VMEM((snaps, lines), F32),
            pltpu.VMEM((lines // BLK, BLK), F32),
            pltpu.VMEM((chunks, width), jnp.int32),
            pltpu.VMEM((snaps, states), F32),
            pltpu.VMEM((chunks, depth, BLK), F32),
            pltpu.VMEM((own, snaps, BLK), BF16),
            pltpu.SemaphoreType.DMA((4,)),
            pltpu.SemaphoreType.DMA((chunks,)),
            pltpu.SemaphoreType.DMA((members,)),
        ],
        out_spec=(HBM, HBM, [HBM] * (members - 1)),
        mib=60,
        name="pack_readings",
    )
    each = width // cap
    if each > 1:
        message = message.reshape(chunks, depth, each, cap).transpose(0, 2, 1, 3)
        message = message.reshape(areas, depth, cap)
    message = lax.all_to_all(message, "area", split_axis=0, concat_axis=0, tiled=True)
    if each > 1:
        message = message.reshape(chunks, each, depth, cap).transpose(0, 2, 1, 3)
        message = message.reshape(chunks, depth, BLK)

    rounded_others = [from_snap(rounded, i) for i in range(1, members)]
    handed = [rounded, ties_table, place]
    table = shape((lines // BLK, BLK), jnp.int32)
    group, lane, (rounded, ties_table, place) = call(
        inverse_kernel,
        (table, table, [shape(a.shape, a.dtype) for a in handed]),
        [VMEM, [VMEM] * 3],
        (holder, handed),
        flops=10**9,
        name="invert_order",
    )
    boundary = shape((ties, everything, BLK), BF16)
    owns = [rounded] + rounded_others
    first, second = call(
        pick_kernel,
        (boundary, boundary),
        [[VMEM] * members, SMEM],
        (owns, ties_table),
        name="pick_boundary",
    )
    first, second, x_sent = lax.optimization_barrier((first, second, x_sent))
    first, second = with_neighbours(first, second)
    x_others = [from_snap(block, i) for i, block in enumerate(x_sent, 1)]
    guess = call(
        predict_kernel,
        shape((everything, lines), F32),
        [VMEM, VMEM, [VMEM] * members, VMEM, SMEM],
        (first, second, owns, derivative_pieces, place),
        scratch=[pltpu.VMEM((slots, everything, BLK), BF16)],
        flops=10**9,
        name="predict",
    )
    message, guess = lax.optimization_barrier((message, guess))
    halves = []
    for part in range(2):
        halves.append(
            call(
                functools.partial(unpack_kernel, part * (lines // BLK // 2)),
                (shape((snaps, lines // 2), F32), shape((1, lines // 2), F32)),
                [VMEM, VMEM, VMEM],
                (group, lane, message),
                scratch=[pltpu.VMEM((chunks * (width // BLK), BLK), F32)],
                flops=2 * 10**9,
                name="unpack_readings",
            )
        )
    halves, x_others = lax.optimization_barrier((halves, x_others))
    readings = [half[0] for half in halves]
    variance = [half[1] for half in halves]
    reading_others = [from_all(half) for half in readings]
    grads = (
        shape((own, everything, BLK), F32),
        boundary,
        boundary,
    )
    total = pltpu.VMEM((slots, everything, BLK), F32)
    work = pltpu.VMEM((2 * ties, everything, BLK), F32)

    def partial_update(grad):
        return call(
            partial_update_kernel,
            shape((everything, held * BLK), F32),
            [VMEM, SMEM, VMEM],
            (grad, ties_table, reciprocal_normal_operator),
            flops=10**9,
            name="partial_update",
        )

    grad, first, second = call(
        pull_kernel,
        grads,
        [VMEM, [VMEM] * 2, [VMEM] * 2, [VMEM] * 2, VMEM, SMEM],
        (guess, readings, reading_others, variance, derivative_pieces, place),
        scratch=[total, pltpu.VMEM((everything, lines), BF16)],
        name="pull",
    )
    arrived = with_neighbours(first, second)
    kept, given, mine, first = call(
        first_update_kernel,
        (
            shape((held, snaps, BLK), F32),
            [shape((held, snaps, BLK), F32)] * (members - 1),
            shape((held, everything, BLK), BF16),
            boundary,
        ),
        [VMEM, VMEM, VMEM, VMEM, SMEM, VMEM, VMEM, [VMEM] * (members - 1)],
        (
            partial_update(grad), grad, *arrived, ties_table, reciprocal_normal_operator,
            starting_voltages, x_others,
        ),
        scratch=[work],
        name="first_update",
    )
    others = [from_snap(mine, i) for i in range(1, members)]
    first = swap_pair(first, 1)
    firsts = [first] + [from_snap(first, i) for i in range(1, members)]
    aug, second = call(
        join_states_kernel,
        (shape((own, everything, BLK), BF16), boundary),
        [VMEM, [VMEM] * (members - 1), SMEM],
        (mine, others, ties_table),
        name="join_states",
    )
    second = swap_pair(second, 0)
    grad, first, second = call(
        predict_pull_kernel,
        grads,
        [[VMEM] * members, VMEM, VMEM, [VMEM] * 2, [VMEM] * 2, [VMEM] * 2, VMEM, SMEM],
        (firsts, aug, second, readings, reading_others, variance, derivative_pieces, place),
        scratch=[
            pltpu.VMEM((slots, everything, BLK), BF16),
            pltpu.VMEM((everything, lines), F32),
            total,
            pltpu.VMEM((everything, lines), BF16),
        ],
        name="predict_pull",
    )
    given, first, second = lax.optimization_barrier((given, first, second))
    first, second = with_neighbours(first, second)
    states_in = [from_snap(block, -i) for i, block in enumerate(given, 1)]
    mine, sent = call(
        last_update_kernel,
        (
            shape((snaps, held * BLK), F32),
            [shape((snaps, held * BLK), BF16)] * (members - 1),
        ),
        [VMEM, VMEM, VMEM, VMEM, SMEM, VMEM, VMEM],
        (partial_update(grad), grad, first, second, ties_table, reciprocal_normal_operator, kept),
        scratch=[work],
        name="last_update",
    )
    return call(
        finish_kernel,
        shape((snaps, states), F32),
        [VMEM, [VMEM] * (members - 1), [VMEM] * (members - 1)],
        (mine, states_in, [from_snap(block, -i) for i, block in enumerate(sent, 1)]),
        name="finish",
    )


def solution(mesh):
    placed = (
        P("snap", "area"),
        P("area"),
        P("snap", "area"),
        P("area", None, None, None),
        P("area", None, None),
        P("area", None, None),
        P("area", None, None),
        P("area", None, None),
        P(("area", "snap"), None),
    )
    return jax.shard_map(
        on_device, mesh=mesh, in_specs=placed, out_specs=P("snap", "area"), check_vma=False
    )
```

```python
import functools

import jax
import jax.numpy as jnp
from jax import lax
from jax.experimental import pallas as pl
from jax.experimental.pallas import tpu as pltpu
from jax.sharding import PartitionSpec as P

BLK = 128
ITERS = 2
F32 = jnp.float32
BF16 = jnp.bfloat16
NT = (((1,), (1,)), ((), ()))
VMEM = pl.BlockSpec(memory_space=pltpu.VMEM)
HBM = pl.BlockSpec(memory_space=pltpu.HBM)
SMEM = pl.BlockSpec(memory_space=pltpu.SMEM)


def call(kernel, outs, ins, args, scratch=(), flops=0, mib=12, out_spec=None, name=None):
    return pl.pallas_call(
        kernel,
        out_shape=outs,
        in_specs=ins,
        out_specs=jax.tree.map(lambda _: VMEM, outs) if out_spec is None else out_spec,
        scratch_shapes=list(scratch),
        compiler_params=pltpu.CompilerParams(vmem_limit_bytes=mib * 1024 * 1024),
        cost_estimate=pl.CostEstimate(
            flops=flops, bytes_accessed=0, transcendentals=0
        ),
        name=name,
    )(*args)


def lane_gather(values, lanes):
    return jnp.take_along_axis(values, lanes, axis=1, mode="promise_in_bounds")


def rows_iota(shape):
    return lax.broadcasted_iota(jnp.int32, shape, 0)


def pack_kernel(
    z_in, v_in, hub_in, x_in, out, rounded_out, sent_outs,
    z_ref, v_ref, hub_ref, x_ref, out_ref, rounded_ref,
    sems, out_sems, sent_sems,
):
    pairs = ((x_in, x_ref), (hub_in, hub_ref), (z_in, z_ref), (v_in, v_ref))
    copies = [
        pltpu.make_async_copy(source, target, sems.at[i])
        for i, (source, target) in enumerate(pairs)
    ]
    for copy in copies:
        copy.start()
    for copy in copies:
        copy.wait()
    for b in range(rounded_ref.shape[0]):
        rounded_ref[b] = x_ref[:, b * BLK : (b + 1) * BLK].astype(BF16)
    ready = [(rounded_ref, rounded_out)]
    members = len(sent_outs) + 1
    part = x_ref.shape[1] // members
    for i, sent_out in enumerate(sent_outs, 1):
        at = lax.rem(lax.axis_index("snap") + i, members) * part
        ready.append((x_ref.at[:, pl.ds(pl.multiple_of(at, BLK), part)], sent_out))
    sends = [
        pltpu.make_async_copy(source, target, sent_sems.at[i])
        for i, (source, target) in enumerate(ready)
    ]
    for copy in sends:
        copy.start()
    snaps, lines = z_ref.shape
    blocks = lines // BLK
    chunks, width = hub_ref.shape
    groups = width // BLK
    for d in range(chunks):
        tail = jnp.zeros((8, BLK), F32)
        for g in range(groups):
            slot = hub_ref[d : d + 1, g * BLK : (g + 1) * BLK]
            high = jnp.right_shift(slot, 7)
            low = jnp.bitwise_and(slot, 127)
            lanes = jnp.broadcast_to(low, (snaps, BLK))
            block_of = jnp.broadcast_to(high, (snaps, BLK))
            picked = jnp.zeros((snaps, BLK), F32)
            for b in range(blocks):
                found = lane_gather(z_ref[:, b * BLK : (b + 1) * BLK], lanes)
                picked = jnp.where(block_of == b, found, picked)
            out_ref[d, g * snaps : (g + 1) * snaps, :] = picked
            found = lane_gather(v_ref[...], jnp.broadcast_to(low, (blocks, BLK)))
            mine = rows_iota((blocks, BLK)) == high
            variance = jnp.sum(jnp.where(mine, found, 0.0), axis=0, keepdims=True)
            tail = jnp.where(rows_iota((8, BLK)) == g, variance, tail)
        out_ref[d, groups * snaps :, :] = tail
        pltpu.make_async_copy(out_ref.at[d], out.at[d], out_sems.at[d]).start()
    for d in range(chunks):
        pltpu.make_async_copy(out_ref.at[d], out.at[d], out_sems.at[d]).wait()
    for copy in sends:
        copy.wait()


def inverse_kernel(own_ref, handed_refs, group_ref, lane_ref, kept_refs):
    for handed_ref, kept_ref in zip(handed_refs, kept_refs):
        kept_ref[...] = handed_ref[...]
    chunks, width = own_ref.shape
    blocks = group_ref.shape[0]
    groups = width // BLK
    total = jnp.zeros((2 * blocks, BLK), F32)
    lane = lax.broadcasted_iota(jnp.int32, (2 * blocks, width), 1)
    row = rows_iota((2 * blocks, width))
    in_group = jnp.bitwise_and(lane, 127)
    group_in = jnp.right_shift(lane, 7)
    for d in range(chunks):
        owned = own_ref[d : d + 1, :]
        high = jnp.right_shift(owned, 7)
        low = jnp.bitwise_and(owned, 127)
        label = jnp.where(row < blocks, group_in + d * groups, in_group)
        hit = jnp.bitwise_and(row, blocks - 1) == high
        left = jnp.where(hit, label.astype(F32), 0.0).astype(BF16)
        right = jnp.where(rows_iota((BLK, width)) == low, 1.0, 0.0).astype(BF16)
        total += lax.dot_general(left, right, NT, preferred_element_type=F32)
    group_ref[...] = total[:blocks].astype(jnp.int32)
    lane_ref[...] = total[blocks:].astype(jnp.int32)


def unpack_kernel(start, group_ref, lane_ref, message_ref, z_ref, v_ref, variance_ref):
    snaps, lines = z_ref.shape
    chunks = message_ref.shape[0]
    groups = (message_ref.shape[1] - 8) // snaps
    total = chunks * groups
    for d in range(chunks):
        variance_ref[d * groups : (d + 1) * groups, :] = message_ref[d, groups * snaps :, :][:groups]
    for b in range(lines // BLK):
        group = group_ref[start + b : start + b + 1, :]
        lane = lane_ref[start + b : start + b + 1, :]
        lanes = jnp.broadcast_to(lane, (snaps, BLK))
        group_of = jnp.broadcast_to(group, (snaps, BLK))
        picked = jnp.zeros((snaps, BLK), F32)
        for g in range(total):
            rows = slice(g % groups * snaps, (g % groups + 1) * snaps)
            found = lane_gather(message_ref[g // groups, rows, :], lanes)
            picked = jnp.where(group_of == g, found, picked)
        columns = slice(b * BLK, (b + 1) * BLK)
        z_ref[:, columns] = picked
        found = lane_gather(variance_ref[...], jnp.broadcast_to(lane, (total, BLK)))
        mine = rows_iota((total, BLK)) == group
        v_ref[:, columns] = jnp.sum(jnp.where(mine, found, 0.0), axis=0, keepdims=True)


def split(ref):
    return [ref.at[i] for i in range(ref.shape[0])]


def parity():
    return 1 - lax.rem(lax.axis_index("area"), 2)


def pick(blocks_ref, listing_ref, side, out_ref, start=0):
    held = blocks_ref.shape[0]
    for t in range(out_ref.shape[0]):
        b = listing_ref[side, t]
        at = b - start
        block = blocks_ref[jnp.clip(at, 0, held - 1)]
        here = (b >= 0) & (at >= 0) & (at < held)
        out_ref[t] = jnp.where(here, block, jnp.zeros_like(block))


def slots_into(slots_ref, aug_ref, first, second_ref):
    own = aug_ref.shape[0]
    ties = second_ref.shape[0]
    slots_ref[:own] = aug_ref[...]
    slots_ref[pl.ds(own + ties * (1 - parity()), ties)] = first
    slots_ref[pl.ds(own + ties * parity(), ties)] = second_ref[...]


def reordered(ref, distance, members):
    snaps = ref.shape[1] // members
    order = [(n - distance) % members for n in range(members)]
    return jnp.concatenate([ref[:, j * snaps : (j + 1) * snaps] for j in order], axis=1)


def join_states_kernel(mine_ref, others_refs, ties_ref, aug_ref, second_ref):
    members = len(others_refs) + 1
    held = mine_ref.shape[0]
    me = lax.axis_index("snap")
    aug_ref[pl.ds(me * held, held)] = mine_ref[...]
    for i, ref in enumerate(others_refs, 1):
        at = lax.rem(me + members - i, members) * held
        aug_ref[pl.ds(at, held)] = reordered(ref, i, members)
    pick(aug_ref, ties_ref, parity(), second_ref)


def predicted(j, slots_ref, tiles_ref, place_ref):
    touched = tiles_ref.shape[1]
    chosen = jnp.concatenate([slots_ref[place_ref[k, j]] for k in range(touched)], axis=1)
    weights = jnp.concatenate([tiles_ref[j, k] for k in range(touched)], axis=1)
    return lax.dot_general(chosen, weights, NT, preferred_element_type=F32)


def pick_kernel(own_refs, ties_ref, first_ref, second_ref):
    snaps = own_refs[0].shape[1]
    for i, own_ref in enumerate(own_refs):
        rows = slice(i * snaps, (i + 1) * snaps)
        pick(own_ref, ties_ref, 1 - parity(), first_ref.at[:, rows])
        pick(own_ref, ties_ref, parity(), second_ref.at[:, rows])


def predict_kernel(
    first_ref, second_ref, own_refs, tiles_ref, place_ref, out_ref, slots_ref
):
    own, snaps = own_refs[0].shape[:2]
    ties = first_ref.shape[0]
    for i, own_ref in enumerate(own_refs):
        slots_ref[:own, i * snaps : (i + 1) * snaps] = own_ref[...]
    slots_ref[pl.ds(own + ties * (1 - parity()), ties)] = first_ref[...]
    slots_ref[pl.ds(own + ties * parity(), ties)] = second_ref[...]
    predict(tiles_ref, place_ref, out_ref, slots_ref)


def predict(tiles_ref, place_ref, out_ref, slots_ref):
    for j in range(tiles_ref.shape[0]):
        out_ref[:, j * BLK : (j + 1) * BLK] = predicted(j, slots_ref, tiles_ref, place_ref)


def weigh(j, guess, z_refs, others_refs, v_refs):
    each = z_refs[0].shape[1] // BLK
    z_ref, others_ref, v_ref = z_refs[j // each], others_refs[j // each], v_refs[j // each]
    columns = slice(j % each * BLK, (j % each + 1) * BLK)
    readings = [z_ref[:, columns]] + [o[:, columns] for o in split(others_ref)]
    resid = jnp.concatenate(readings, axis=0) - guess
    spread = jnp.sum(resid * resid, axis=0, keepdims=True) / resid.shape[0]
    return (resid / (v_ref[:, columns] + spread)).astype(BF16)


def pull(weighted_ref, tiles_ref, place_ref, total_ref, own_ref, first_ref, second_ref):
    total_ref[...] = jnp.zeros_like(total_ref)
    touched = tiles_ref.shape[1]
    for j in range(tiles_ref.shape[0]):
        weighted = weighted_ref[:, j * BLK : (j + 1) * BLK]
        weights = jnp.concatenate([tiles_ref[j, k] for k in range(touched)], axis=1)
        part = jnp.dot(weighted, weights, preferred_element_type=F32)
        for k in range(touched):
            n = place_ref[k, j]
            total_ref[n] += part[:, k * BLK : (k + 1) * BLK]
    own = own_ref.shape[0]
    ties = first_ref.shape[0]
    own_ref[...] = total_ref[:own]
    first = total_ref[pl.ds(own + ties * (1 - parity()), ties)]
    second = total_ref[pl.ds(own + ties * parity(), ties)]
    first_ref[...] = first.astype(first_ref.dtype)
    second_ref[...] = second.astype(second_ref.dtype)


def pull_kernel(
    guess_ref, z_refs, others_refs, v_refs, tiles_ref, place_ref, own_ref, first_ref, second_ref,
    total_ref, weighted_ref,
):
    for j in range(tiles_ref.shape[0]):
        columns = slice(j * BLK, (j + 1) * BLK)
        weighted_ref[:, columns] = weigh(j, guess_ref[:, columns], z_refs, others_refs, v_refs)
    pull(weighted_ref, tiles_ref, place_ref, total_ref, own_ref, first_ref, second_ref)


def predict_pull_kernel(
    first_refs, aug_ref, second_in_ref, z_refs, others_refs, v_refs, tiles_ref, place_ref,
    own_ref, first_ref, second_ref, slots_ref, guess_ref, total_ref, weighted_ref,
):
    parts = [reordered(ref, i, len(first_refs)) for i, ref in enumerate(first_refs)]
    slots_into(slots_ref, aug_ref, sum(parts[1:], parts[0]), second_in_ref)
    predict(tiles_ref, place_ref, guess_ref, slots_ref)
    pull_kernel(
        guess_ref, z_refs, others_refs, v_refs, tiles_ref, place_ref, own_ref, first_ref, second_ref,
        total_ref, weighted_ref,
    )


def partial_update_kernel(grad_ref, ties_ref, gain_ref, part_ref):
    sides, ties = ties_ref.shape
    blocks = []
    for b in range(grad_ref.shape[0]):
        listed = ties_ref[0, 0] == b
        for side in range(sides):
            for t in range(ties):
                listed = listed | (ties_ref[side, t] == b)
        block = grad_ref[b]
        blocks.append(jnp.where(listed, jnp.zeros_like(block), block).astype(BF16))
    gradient = jnp.concatenate(blocks, axis=1)
    step = min(2 * BLK, gain_ref.shape[0])
    for at in range(0, gain_ref.shape[0], step):
        rows = gain_ref[at : at + step, :]
        part_ref[:, at : at + step] = lax.dot_general(
            gradient, rows, NT, preferred_element_type=F32
        )


def updates(part_ref, grad_ref, back_first_ref, back_second_ref, ties_ref, gain_ref, work_ref):
    ties = back_first_ref.shape[0]
    lists = [[ties_ref[side, t] for t in range(ties)] for side in (1 - parity(), parity())]
    for t, b in enumerate(lists[0]):
        block = grad_ref[jnp.maximum(b, 0)] + back_first_ref[t].astype(F32)
        work_ref[t] = jnp.where(b >= 0, block, jnp.zeros_like(block))
    for t, b in enumerate(lists[1]):
        at = ties + t
        for u, other in enumerate(lists[0]):
            at = jnp.where((b >= 0) & (other == b), u, at)
        block = grad_ref[jnp.maximum(b, 0)]
        alone = (b >= 0) & (at == ties + t)
        work_ref[ties + t] = jnp.where(alone, block, jnp.zeros_like(block))
        back = back_second_ref[t].astype(F32)
        work_ref[at] += jnp.where(b >= 0, back, jnp.zeros_like(back))
    listed = lists[0] + lists[1]
    gradient = jnp.concatenate([work_ref[n].astype(BF16) for n in range(len(listed))], axis=1)
    step = min(2 * BLK, gain_ref.shape[0])
    for at in range(0, gain_ref.shape[0], step):
        rows = [
            gain_ref[at : at + step, pl.ds(pl.multiple_of(jnp.maximum(b, 0) * BLK, BLK), BLK)]
            for b in listed
        ]
        update = part_ref[:, at : at + step] + lax.dot_general(
            gradient, jnp.concatenate(rows, axis=1), NT, preferred_element_type=F32
        )
        for i in range(step // BLK):
            yield at // BLK + i, update[:, i * BLK : (i + 1) * BLK]


def first_update_kernel(
    part_ref, grad_ref, back_first_ref, back_second_ref, ties_ref, gain_ref, x_ref, x_others_refs,
    kept_ref, given_refs, message_ref, first_ref, work_ref,
):
    held, snaps = kept_ref.shape[:2]
    me = lax.axis_index("snap")
    operands = part_ref, grad_ref, back_first_ref, back_second_ref, ties_ref, gain_ref, work_ref
    for i, update in updates(*operands):
        columns = pl.ds(pl.multiple_of((me * held + i) * BLK, BLK), BLK)
        parts = [x_ref[:, columns]] + [o[:, i * BLK : (i + 1) * BLK] for o in x_others_refs]
        state = jnp.concatenate(parts, axis=0) + update
        kept_ref[i] = state[:snaps]
        for j, given_ref in enumerate(given_refs, 1):
            given_ref[i] = state[j * snaps : (j + 1) * snaps]
        message_ref[i] = state.astype(BF16)
    pick(message_ref, ties_ref, 1 - parity(), first_ref, me * held)


def last_update_kernel(
    part_ref, grad_ref, back_first_ref, back_second_ref, ties_ref, gain_ref, kept_ref, mine_ref, sent_refs, work_ref
):
    snaps = mine_ref.shape[0]
    operands = part_ref, grad_ref, back_first_ref, back_second_ref, ties_ref, gain_ref, work_ref
    for i, update in updates(*operands):
        columns = slice(i * BLK, (i + 1) * BLK)
        mine_ref[:, columns] = kept_ref[i] + update[:snaps]
        for j, sent_ref in enumerate(sent_refs, 1):
            sent_ref[:, columns] = update[j * snaps : (j + 1) * snaps].astype(BF16)


def finish_kernel(mine_ref, states_refs, updates_refs, out_ref):
    width = mine_ref.shape[1]
    members = len(states_refs) + 1
    me = lax.axis_index("snap")
    out_ref[:, pl.ds(pl.multiple_of(me * width, BLK), width)] = mine_ref[...]
    for i, (state_ref, update_ref) in enumerate(zip(states_refs, updates_refs), 1):
        at = lax.rem(me + i, members) * width
        for b in range(width // BLK):
            update = update_ref[:, b * BLK : (b + 1) * BLK].astype(F32)
            columns = pl.ds(pl.multiple_of(at + b * BLK, BLK), BLK)
            out_ref[:, columns] = state_ref[b] + update


def swap_pair(block, start):
    pairs = [(i, i + 1) for i in range(start, lax.axis_size("area") - 1, 2)]
    return lax.ppermute(block, "area", pairs + [(b, a) for a, b in pairs])


def with_neighbours(first, second):
    return swap_pair(first, 1), swap_pair(second, 0)


def from_snap(block, distance):
    members = lax.axis_size("snap")
    return lax.ppermute(block, "snap", [(i, (i + distance) % members) for i in range(members)])


def from_all(block):
    return jnp.stack([from_snap(block, i) for i in range(1, lax.axis_size("snap"))])


def shape(dims, kind):
    return jax.ShapeDtypeStruct(dims, kind)


def on_device(
    phasor_readings,
    reading_error_spread,
    starting_voltages,
    derivative_pieces,
    derivative_tile_position,
    frontier_voltage_pieces,
    holder_line_order,
    hub_line_order,
    reciprocal_normal_operator,
):
    snaps, lines = phasor_readings.shape
    states = starting_voltages.shape[1]
    own = states // BLK
    measure = derivative_pieces.shape[0]
    ties_table = frontier_voltage_pieces[0]
    ties = ties_table.shape[1]
    slots = own + 2 * ties
    members = lax.axis_size("snap")
    areas = lax.axis_size("area")
    everything = snaps * members
    held = reciprocal_normal_operator.shape[0] // BLK
    place = derivative_tile_position[0].T
    cap = hub_line_order.shape[2]
    width = max(cap, BLK)
    chunks = areas * cap // width
    hub = hub_line_order[0].reshape(chunks, width)
    holder = holder_line_order[0].reshape(chunks, width)
    depth = (width // BLK) * snaps + 8

    message, rounded, x_sent = call(
        pack_kernel,
        (
            shape((chunks, depth, BLK), F32),
            shape((own, snaps, BLK), BF16),
            [shape((snaps, held * BLK), F32)] * (members - 1),
        ),
        [HBM] * 4,
        (
            phasor_readings,
            reading_error_spread.reshape(lines // BLK, BLK),
            hub,
            starting_voltages,
        ),
        scratch=[
            pltpu.VMEM((snaps, lines), F32),
            pltpu.VMEM((lines // BLK, BLK), F32),
            pltpu.VMEM((chunks, width), jnp.int32),
            pltpu.VMEM((snaps, states), F32),
            pltpu.VMEM((chunks, depth, BLK), F32),
            pltpu.VMEM((own, snaps, BLK), BF16),
            pltpu.SemaphoreType.DMA((4,)),
            pltpu.SemaphoreType.DMA((chunks,)),
            pltpu.SemaphoreType.DMA((members,)),
        ],
        out_spec=(HBM, HBM, [HBM] * (members - 1)),
        mib=60,
        name="pack_readings",
    )
    each = width // cap
    if each > 1:
        message = message.reshape(chunks, depth, each, cap).transpose(0, 2, 1, 3)
        message = message.reshape(areas, depth, cap)
    message = lax.all_to_all(message, "area", split_axis=0, concat_axis=0, tiled=True)
    if each > 1:
        message = message.reshape(chunks, each, depth, cap).transpose(0, 2, 1, 3)
        message = message.reshape(chunks, depth, BLK)

    rounded_others = [from_snap(rounded, i) for i in range(1, members)]
    handed = [rounded, ties_table, place]
    table = shape((lines // BLK, BLK), jnp.int32)
    group, lane, (rounded, ties_table, place) = call(
        inverse_kernel,
        (table, table, [shape(a.shape, a.dtype) for a in handed]),
        [VMEM, [VMEM] * 3],
        (holder, handed),
        flops=10**9,
        name="invert_order",
    )
    boundary = shape((ties, everything, BLK), BF16)
    owns = [rounded] + rounded_others
    first, second = call(
        pick_kernel,
        (boundary, boundary),
        [[VMEM] * members, SMEM],
        (owns, ties_table),
        name="pick_boundary",
    )
    first, second, x_sent = lax.optimization_barrier((first, second, x_sent))
    first, second = with_neighbours(first, second)
    x_others = [from_snap(block, i) for i, block in enumerate(x_sent, 1)]
    guess = call(
        predict_kernel,
        shape((everything, lines), F32),
        [VMEM, VMEM, [VMEM] * members, VMEM, SMEM],
        (first, second, owns, derivative_pieces, place),
        scratch=[pltpu.VMEM((slots, everything, BLK), BF16)],
        flops=10**9,
        name="predict",
    )
    message, guess = lax.optimization_barrier((message, guess))
    halves = []
    for part in range(2):
        halves.append(
            call(
                functools.partial(unpack_kernel, part * (lines // BLK // 2)),
                (shape((snaps, lines // 2), F32), shape((1, lines // 2), F32)),
                [VMEM, VMEM, VMEM],
                (group, lane, message),
                scratch=[pltpu.VMEM((chunks * (width // BLK), BLK), F32)],
                flops=2 * 10**9,
                name="unpack_readings",
            )
        )
    halves, x_others = lax.optimization_barrier((halves, x_others))
    readings = [half[0] for half in halves]
    variance = [half[1] for half in halves]
    reading_others = [from_all(half) for half in readings]
    grads = (
        shape((own, everything, BLK), F32),
        boundary,
        boundary,
    )
    total = pltpu.VMEM((slots, everything, BLK), F32)
    work = pltpu.VMEM((2 * ties, everything, BLK), F32)

    def partial_update(grad):
        return call(
            partial_update_kernel,
            shape((everything, held * BLK), F32),
            [VMEM, SMEM, VMEM],
            (grad, ties_table, reciprocal_normal_operator),
            flops=10**9,
            name="partial_update",
        )

    grad, first, second = call(
        pull_kernel,
        grads,
        [VMEM, [VMEM] * 2, [VMEM] * 2, [VMEM] * 2, VMEM, SMEM],
        (guess, readings, reading_others, variance, derivative_pieces, place),
        scratch=[total, pltpu.VMEM((everything, lines), BF16)],
        name="pull",
    )
    arrived = with_neighbours(first, second)
    kept, given, mine, first = call(
        first_update_kernel,
        (
            shape((held, snaps, BLK), F32),
            [shape((held, snaps, BLK), F32)] * (members - 1),
            shape((held, everything, BLK), BF16),
            boundary,
        ),
        [VMEM, VMEM, VMEM, VMEM, SMEM, VMEM, VMEM, [VMEM] * (members - 1)],
        (
            partial_update(grad), grad, *arrived, ties_table, reciprocal_normal_operator,
            starting_voltages, x_others,
        ),
        scratch=[work],
        name="first_update",
    )
    others = [from_snap(mine, i) for i in range(1, members)]
    first = swap_pair(first, 1)
    firsts = [first] + [from_snap(first, i) for i in range(1, members)]
    aug, second = call(
        join_states_kernel,
        (shape((own, everything, BLK), BF16), boundary),
        [VMEM, [VMEM] * (members - 1), SMEM],
        (mine, others, ties_table),
        name="join_states",
    )
    given, second = lax.optimization_barrier((given, second))
    second = swap_pair(second, 0)
    states_in = [from_snap(block, -i) for i, block in enumerate(given, 1)]
    grad, first, second = call(
        predict_pull_kernel,
        grads,
        [[VMEM] * members, VMEM, VMEM, [VMEM] * 2, [VMEM] * 2, [VMEM] * 2, VMEM, SMEM],
        (firsts, aug, second, readings, reading_others, variance, derivative_pieces, place),
        scratch=[
            pltpu.VMEM((slots, everything, BLK), BF16),
            pltpu.VMEM((everything, lines), F32),
            total,
            pltpu.VMEM((everything, lines), BF16),
        ],
        name="predict_pull",
    )
    grad, states_in = lax.optimization_barrier((grad, states_in))
    first, second = with_neighbours(first, second)
    mine, sent = call(
        last_update_kernel,
        (
            shape((snaps, held * BLK), F32),
            [shape((snaps, held * BLK), BF16)] * (members - 1),
        ),
        [VMEM, VMEM, VMEM, VMEM, SMEM, VMEM, VMEM],
        (partial_update(grad), grad, first, second, ties_table, reciprocal_normal_operator, kept),
        scratch=[work],
        name="last_update",
    )
    return call(
        finish_kernel,
        shape((snaps, states), F32),
        [VMEM, [VMEM] * (members - 1), [VMEM] * (members - 1)],
        (mine, states_in, [from_snap(block, -i) for i, block in enumerate(sent, 1)]),
        name="finish",
    )


def solution(mesh):
    placed = (
        P("snap", "area"),
        P("area"),
        P("snap", "area"),
        P("area", None, None, None),
        P("area", None, None),
        P("area", None, None),
        P("area", None, None),
        P("area", None, None),
        P(("area", "snap"), None),
    )
    return jax.shard_map(
        on_device, mesh=mesh, in_specs=placed, out_specs=P("snap", "area"), check_vma=False
    )
```

```python
import functools

import jax
import jax.numpy as jnp
from jax import lax
from jax.experimental import pallas as pl
from jax.experimental.pallas import tpu as pltpu
from jax.sharding import PartitionSpec as P

BLK = 128
ITERS = 2
F32 = jnp.float32
BF16 = jnp.bfloat16
NT = (((1,), (1,)), ((), ()))
VMEM = pl.BlockSpec(memory_space=pltpu.VMEM)
HBM = pl.BlockSpec(memory_space=pltpu.HBM)
SMEM = pl.BlockSpec(memory_space=pltpu.SMEM)


def call(kernel, outs, ins, args, scratch=(), flops=0, mib=12, out_spec=None, name=None):
    return pl.pallas_call(
        kernel,
        out_shape=outs,
        in_specs=ins,
        out_specs=jax.tree.map(lambda _: VMEM, outs) if out_spec is None else out_spec,
        scratch_shapes=list(scratch),
        compiler_params=pltpu.CompilerParams(vmem_limit_bytes=mib * 1024 * 1024),
        cost_estimate=pl.CostEstimate(
            flops=flops, bytes_accessed=0, transcendentals=0
        ),
        name=name,
    )(*args)


def lane_gather(values, lanes):
    return jnp.take_along_axis(values, lanes, axis=1, mode="promise_in_bounds")


def rows_iota(shape):
    return lax.broadcasted_iota(jnp.int32, shape, 0)


def pack_kernel(
    z_in, v_in, hub_in, x_in, out, rounded_out, sent_outs,
    z_ref, v_ref, hub_ref, x_ref, out_ref, rounded_ref,
    sems, out_sems, sent_sems,
):
    pairs = ((x_in, x_ref), (hub_in, hub_ref), (z_in, z_ref), (v_in, v_ref))
    copies = [
        pltpu.make_async_copy(source, target, sems.at[i])
        for i, (source, target) in enumerate(pairs)
    ]
    for copy in copies:
        copy.start()
    for copy in copies:
        copy.wait()
    for b in range(rounded_ref.shape[0]):
        rounded_ref[b] = x_ref[:, b * BLK : (b + 1) * BLK].astype(BF16)
    ready = [(rounded_ref, rounded_out)]
    members = len(sent_outs) + 1
    part = x_ref.shape[1] // members
    for i, sent_out in enumerate(sent_outs, 1):
        at = lax.rem(lax.axis_index("snap") + i, members) * part
        ready.append((x_ref.at[:, pl.ds(pl.multiple_of(at, BLK), part)], sent_out))
    sends = [
        pltpu.make_async_copy(source, target, sent_sems.at[i])
        for i, (source, target) in enumerate(ready)
    ]
    for copy in sends:
        copy.start()
    snaps, lines = z_ref.shape
    blocks = lines // BLK
    chunks, width = hub_ref.shape
    groups = width // BLK
    for d in range(chunks):
        tail = jnp.zeros((8, BLK), F32)
        for g in range(groups):
            slot = hub_ref[d : d + 1, g * BLK : (g + 1) * BLK]
            high = jnp.right_shift(slot, 7)
            low = jnp.bitwise_and(slot, 127)
            lanes = jnp.broadcast_to(low, (snaps, BLK))
            block_of = jnp.broadcast_to(high, (snaps, BLK))
            picked = jnp.zeros((snaps, BLK), F32)
            for b in range(blocks):
                found = lane_gather(z_ref[:, b * BLK : (b + 1) * BLK], lanes)
                picked = jnp.where(block_of == b, found, picked)
            out_ref[d, g * snaps : (g + 1) * snaps, :] = picked
            found = lane_gather(v_ref[...], jnp.broadcast_to(low, (blocks, BLK)))
            mine = rows_iota((blocks, BLK)) == high
            variance = jnp.sum(jnp.where(mine, found, 0.0), axis=0, keepdims=True)
            tail = jnp.where(rows_iota((8, BLK)) == g, variance, tail)
        out_ref[d, groups * snaps :, :] = tail
        pltpu.make_async_copy(out_ref.at[d], out.at[d], out_sems.at[d]).start()
    for d in range(chunks):
        pltpu.make_async_copy(out_ref.at[d], out.at[d], out_sems.at[d]).wait()
    for copy in sends:
        copy.wait()


def inverse_kernel(own_ref, handed_refs, group_ref, lane_ref, kept_refs):
    for handed_ref, kept_ref in zip(handed_refs, kept_refs):
        kept_ref[...] = handed_ref[...]
    chunks, width = own_ref.shape
    blocks = group_ref.shape[0]
    groups = width // BLK
    total = jnp.zeros((2 * blocks, BLK), F32)
    lane = lax.broadcasted_iota(jnp.int32, (2 * blocks, width), 1)
    row = rows_iota((2 * blocks, width))
    in_group = jnp.bitwise_and(lane, 127)
    group_in = jnp.right_shift(lane, 7)
    for d in range(chunks):
        owned = own_ref[d : d + 1, :]
        high = jnp.right_shift(owned, 7)
        low = jnp.bitwise_and(owned, 127)
        label = jnp.where(row < blocks, group_in + d * groups, in_group)
        hit = jnp.bitwise_and(row, blocks - 1) == high
        left = jnp.where(hit, label.astype(F32), 0.0).astype(BF16)
        right = jnp.where(rows_iota((BLK, width)) == low, 1.0, 0.0).astype(BF16)
        total += lax.dot_general(left, right, NT, preferred_element_type=F32)
    group_ref[...] = total[:blocks].astype(jnp.int32)
    lane_ref[...] = total[blocks:].astype(jnp.int32)


def unpack_kernel(start, group_ref, lane_ref, message_ref, z_ref, v_ref, variance_ref):
    snaps, lines = z_ref.shape
    chunks = message_ref.shape[0]
    groups = (message_ref.shape[1] - 8) // snaps
    total = chunks * groups
    for d in range(chunks):
        variance_ref[d * groups : (d + 1) * groups, :] = message_ref[d, groups * snaps :, :][:groups]
    for b in range(lines // BLK):
        group = group_ref[start + b : start + b + 1, :]
        lane = lane_ref[start + b : start + b + 1, :]
        lanes = jnp.broadcast_to(lane, (snaps, BLK))
        group_of = jnp.broadcast_to(group, (snaps, BLK))
        picked = jnp.zeros((snaps, BLK), F32)
        for g in range(total):
            rows = slice(g % groups * snaps, (g % groups + 1) * snaps)
            found = lane_gather(message_ref[g // groups, rows, :], lanes)
            picked = jnp.where(group_of == g, found, picked)
        columns = slice(b * BLK, (b + 1) * BLK)
        z_ref[:, columns] = picked
        found = lane_gather(variance_ref[...], jnp.broadcast_to(lane, (total, BLK)))
        mine = rows_iota((total, BLK)) == group
        v_ref[:, columns] = jnp.sum(jnp.where(mine, found, 0.0), axis=0, keepdims=True)


def split(ref):
    return [ref.at[i] for i in range(ref.shape[0])]


def parity():
    return 1 - lax.rem(lax.axis_index("area"), 2)


def pick(blocks_ref, listing_ref, side, out_ref, start=0):
    held = blocks_ref.shape[0]
    for t in range(out_ref.shape[0]):
        b = listing_ref[side, t]
        at = b - start
        block = blocks_ref[jnp.clip(at, 0, held - 1)]
        here = (b >= 0) & (at >= 0) & (at < held)
        out_ref[t] = jnp.where(here, block, jnp.zeros_like(block))


def slots_into(slots_ref, aug_ref, first, second_ref):
    own = aug_ref.shape[0]
    ties = second_ref.shape[0]
    slots_ref[:own] = aug_ref[...]
    slots_ref[pl.ds(own + ties * (1 - parity()), ties)] = first
    slots_ref[pl.ds(own + ties * parity(), ties)] = second_ref[...]


def reordered(ref, distance, members):
    snaps = ref.shape[1] // members
    order = [(n - distance) % members for n in range(members)]
    return jnp.concatenate([ref[:, j * snaps : (j + 1) * snaps] for j in order], axis=1)


def join_states_kernel(mine_ref, others_refs, ties_ref, aug_ref, second_ref):
    members = len(others_refs) + 1
    held = mine_ref.shape[0]
    me = lax.axis_index("snap")
    aug_ref[pl.ds(me * held, held)] = mine_ref[...]
    for i, ref in enumerate(others_refs, 1):
        at = lax.rem(me + members - i, members) * held
        aug_ref[pl.ds(at, held)] = reordered(ref, i, members)
    pick(aug_ref, ties_ref, parity(), second_ref)


def predicted(j, slots_ref, tiles_ref, place_ref):
    touched = tiles_ref.shape[1]
    chosen = jnp.concatenate([slots_ref[place_ref[k, j]] for k in range(touched)], axis=1)
    weights = jnp.concatenate([tiles_ref[j, k] for k in range(touched)], axis=1)
    return lax.dot_general(chosen, weights, NT, preferred_element_type=F32)


def pick_kernel(own_refs, ties_ref, first_ref, second_ref):
    snaps = own_refs[0].shape[1]
    for i, own_ref in enumerate(own_refs):
        rows = slice(i * snaps, (i + 1) * snaps)
        pick(own_ref, ties_ref, 1 - parity(), first_ref.at[:, rows])
        pick(own_ref, ties_ref, parity(), second_ref.at[:, rows])


def predict_kernel(
    first_ref, second_ref, own_refs, tiles_ref, place_ref, out_ref, slots_ref
):
    own, snaps = own_refs[0].shape[:2]
    ties = first_ref.shape[0]
    for i, own_ref in enumerate(own_refs):
        slots_ref[:own, i * snaps : (i + 1) * snaps] = own_ref[...]
    slots_ref[pl.ds(own + ties * (1 - parity()), ties)] = first_ref[...]
    slots_ref[pl.ds(own + ties * parity(), ties)] = second_ref[...]
    predict(tiles_ref, place_ref, out_ref, slots_ref)


def predict(tiles_ref, place_ref, out_ref, slots_ref):
    for j in range(tiles_ref.shape[0]):
        out_ref[:, j * BLK : (j + 1) * BLK] = predicted(j, slots_ref, tiles_ref, place_ref)


def weigh(j, guess, z_refs, others_refs, v_refs):
    each = z_refs[0].shape[1] // BLK
    z_ref, others_ref, v_ref = z_refs[j // each], others_refs[j // each], v_refs[j // each]
    columns = slice(j % each * BLK, (j % each + 1) * BLK)
    readings = [z_ref[:, columns]] + [o[:, columns] for o in split(others_ref)]
    resid = jnp.concatenate(readings, axis=0) - guess
    spread = jnp.sum(resid * resid, axis=0, keepdims=True) / resid.shape[0]
    return (resid / (v_ref[:, columns] + spread)).astype(BF16)


def pull(weighted_ref, tiles_ref, place_ref, total_ref, own_ref, first_ref, second_ref):
    total_ref[...] = jnp.zeros_like(total_ref)
    touched = tiles_ref.shape[1]
    for j in range(tiles_ref.shape[0]):
        weighted = weighted_ref[:, j * BLK : (j + 1) * BLK]
        weights = jnp.concatenate([tiles_ref[j, k] for k in range(touched)], axis=1)
        part = jnp.dot(weighted, weights, preferred_element_type=F32)
        for k in range(touched):
            n = place_ref[k, j]
            total_ref[n] += part[:, k * BLK : (k + 1) * BLK]
    own = own_ref.shape[0]
    ties = first_ref.shape[0]
    own_ref[...] = total_ref[:own]
    first = total_ref[pl.ds(own + ties * (1 - parity()), ties)]
    second = total_ref[pl.ds(own + ties * parity(), ties)]
    first_ref[...] = first.astype(first_ref.dtype)
    second_ref[...] = second.astype(second_ref.dtype)


def pull_kernel(
    guess_ref, z_refs, others_refs, v_refs, tiles_ref, place_ref, own_ref, first_ref, second_ref,
    total_ref, weighted_ref,
):
    for j in range(tiles_ref.shape[0]):
        columns = slice(j * BLK, (j + 1) * BLK)
        weighted_ref[:, columns] = weigh(j, guess_ref[:, columns], z_refs, others_refs, v_refs)
    pull(weighted_ref, tiles_ref, place_ref, total_ref, own_ref, first_ref, second_ref)


def predict_pull_kernel(
    first_refs, aug_ref, second_in_ref, z_refs, others_refs, v_refs, tiles_ref, place_ref,
    own_ref, first_ref, second_ref, slots_ref, guess_ref, total_ref, weighted_ref,
):
    parts = [reordered(ref, i, len(first_refs)) for i, ref in enumerate(first_refs)]
    slots_into(slots_ref, aug_ref, sum(parts[1:], parts[0]), second_in_ref)
    predict(tiles_ref, place_ref, guess_ref, slots_ref)
    pull_kernel(
        guess_ref, z_refs, others_refs, v_refs, tiles_ref, place_ref, own_ref, first_ref, second_ref,
        total_ref, weighted_ref,
    )


def partial_update_kernel(grad_ref, ties_ref, gain_ref, part_ref):
    sides, ties = ties_ref.shape
    blocks = []
    for b in range(grad_ref.shape[0]):
        listed = ties_ref[0, 0] == b
        for side in range(sides):
            for t in range(ties):
                listed = listed | (ties_ref[side, t] == b)
        block = grad_ref[b]
        blocks.append(jnp.where(listed, jnp.zeros_like(block), block).astype(BF16))
    gradient = jnp.concatenate(blocks, axis=1)
    step = min(2 * BLK, gain_ref.shape[0])
    for at in range(0, gain_ref.shape[0], step):
        rows = gain_ref[at : at + step, :]
        part_ref[:, at : at + step] = lax.dot_general(
            gradient, rows, NT, preferred_element_type=F32
        )


def updates(part_ref, grad_ref, back_first_ref, back_second_ref, ties_ref, gain_ref, work_ref):
    ties = back_first_ref.shape[0]
    lists = [[ties_ref[side, t] for t in range(ties)] for side in (1 - parity(), parity())]
    for t, b in enumerate(lists[0]):
        block = grad_ref[jnp.maximum(b, 0)] + back_first_ref[t].astype(F32)
        work_ref[t] = jnp.where(b >= 0, block, jnp.zeros_like(block))
    for t, b in enumerate(lists[1]):
        at = ties + t
        for u, other in enumerate(lists[0]):
            at = jnp.where((b >= 0) & (other == b), u, at)
        block = grad_ref[jnp.maximum(b, 0)]
        alone = (b >= 0) & (at == ties + t)
        work_ref[ties + t] = jnp.where(alone, block, jnp.zeros_like(block))
        back = back_second_ref[t].astype(F32)
        work_ref[at] += jnp.where(b >= 0, back, jnp.zeros_like(back))
    listed = lists[0] + lists[1]
    gradient = jnp.concatenate([work_ref[n].astype(BF16) for n in range(len(listed))], axis=1)
    step = min(2 * BLK, gain_ref.shape[0])
    for at in range(0, gain_ref.shape[0], step):
        rows = [
            gain_ref[at : at + step, pl.ds(pl.multiple_of(jnp.maximum(b, 0) * BLK, BLK), BLK)]
            for b in listed
        ]
        update = part_ref[:, at : at + step] + lax.dot_general(
            gradient, jnp.concatenate(rows, axis=1), NT, preferred_element_type=F32
        )
        for i in range(step // BLK):
            yield at // BLK + i, update[:, i * BLK : (i + 1) * BLK]


def first_update_kernel(
    part_ref, grad_ref, back_first_ref, back_second_ref, ties_ref, gain_ref, x_ref, x_others_refs,
    kept_ref, given_refs, message_ref, first_ref, work_ref,
):
    held, snaps = kept_ref.shape[:2]
    me = lax.axis_index("snap")
    operands = part_ref, grad_ref, back_first_ref, back_second_ref, ties_ref, gain_ref, work_ref
    for i, update in updates(*operands):
        columns = pl.ds(pl.multiple_of((me * held + i) * BLK, BLK), BLK)
        parts = [x_ref[:, columns]] + [o[:, i * BLK : (i + 1) * BLK] for o in x_others_refs]
        state = jnp.concatenate(parts, axis=0) + update
        kept_ref[i] = state[:snaps]
        for j, given_ref in enumerate(given_refs, 1):
            given_ref[i] = update[j * snaps : (j + 1) * snaps]
        message_ref[i] = state.astype(BF16)
    pick(message_ref, ties_ref, 1 - parity(), first_ref, me * held)


def last_update_kernel(
    part_ref, grad_ref, back_first_ref, back_second_ref, ties_ref, gain_ref, kept_ref, given_refs,
    mine_ref, sent_refs, work_ref,
):
    snaps = mine_ref.shape[0]
    operands = part_ref, grad_ref, back_first_ref, back_second_ref, ties_ref, gain_ref, work_ref
    for i, update in updates(*operands):
        columns = slice(i * BLK, (i + 1) * BLK)
        mine_ref[:, columns] = kept_ref[i] + update[:snaps]
        for j, (given_ref, sent_ref) in enumerate(zip(given_refs, sent_refs), 1):
            total = given_ref[i] + update[j * snaps : (j + 1) * snaps]
            sent_ref[:, columns] = total.astype(BF16)


def finish_kernel(mine_ref, x_ref, updates_refs, out_ref):
    width = mine_ref.shape[1]
    members = len(updates_refs) + 1
    me = lax.axis_index("snap")
    out_ref[:, pl.ds(pl.multiple_of(me * width, BLK), width)] = mine_ref[...]
    for i, update_ref in enumerate(updates_refs, 1):
        at = lax.rem(me + i, members) * width
        columns = pl.ds(pl.multiple_of(at, BLK), width)
        out_ref[:, columns] = x_ref[:, columns] + update_ref[...].astype(F32)


def swap_pair(block, start):
    pairs = [(i, i + 1) for i in range(start, lax.axis_size("area") - 1, 2)]
    return lax.ppermute(block, "area", pairs + [(b, a) for a, b in pairs])


def with_neighbours(first, second):
    return swap_pair(first, 1), swap_pair(second, 0)


def from_snap(block, distance):
    members = lax.axis_size("snap")
    return lax.ppermute(block, "snap", [(i, (i + distance) % members) for i in range(members)])


def from_all(block):
    return jnp.stack([from_snap(block, i) for i in range(1, lax.axis_size("snap"))])


def shape(dims, kind):
    return jax.ShapeDtypeStruct(dims, kind)


def on_device(
    phasor_readings,
    reading_error_spread,
    starting_voltages,
    derivative_pieces,
    derivative_tile_position,
    frontier_voltage_pieces,
    holder_line_order,
    hub_line_order,
    reciprocal_normal_operator,
):
    snaps, lines = phasor_readings.shape
    states = starting_voltages.shape[1]
    own = states // BLK
    measure = derivative_pieces.shape[0]
    ties_table = frontier_voltage_pieces[0]
    ties = ties_table.shape[1]
    slots = own + 2 * ties
    members = lax.axis_size("snap")
    areas = lax.axis_size("area")
    everything = snaps * members
    held = reciprocal_normal_operator.shape[0] // BLK
    place = derivative_tile_position[0].T
    cap = hub_line_order.shape[2]
    width = max(cap, BLK)
    chunks = areas * cap // width
    hub = hub_line_order[0].reshape(chunks, width)
    holder = holder_line_order[0].reshape(chunks, width)
    depth = (width // BLK) * snaps + 8

    message, rounded, x_sent = call(
        pack_kernel,
        (
            shape((chunks, depth, BLK), F32),
            shape((own, snaps, BLK), BF16),
            [shape((snaps, held * BLK), F32)] * (members - 1),
        ),
        [HBM] * 4,
        (
            phasor_readings,
            reading_error_spread.reshape(lines // BLK, BLK),
            hub,
            starting_voltages,
        ),
        scratch=[
            pltpu.VMEM((snaps, lines), F32),
            pltpu.VMEM((lines // BLK, BLK), F32),
            pltpu.VMEM((chunks, width), jnp.int32),
            pltpu.VMEM((snaps, states), F32),
            pltpu.VMEM((chunks, depth, BLK), F32),
            pltpu.VMEM((own, snaps, BLK), BF16),
            pltpu.SemaphoreType.DMA((4,)),
            pltpu.SemaphoreType.DMA((chunks,)),
            pltpu.SemaphoreType.DMA((members,)),
        ],
        out_spec=(HBM, HBM, [HBM] * (members - 1)),
        mib=60,
        name="pack_readings",
    )
    each = width // cap
    if each > 1:
        message = message.reshape(chunks, depth, each, cap).transpose(0, 2, 1, 3)
        message = message.reshape(areas, depth, cap)
    message = lax.all_to_all(message, "area", split_axis=0, concat_axis=0, tiled=True)
    if each > 1:
        message = message.reshape(chunks, each, depth, cap).transpose(0, 2, 1, 3)
        message = message.reshape(chunks, depth, BLK)

    rounded_others = [from_snap(rounded, i) for i in range(1, members)]
    handed = [rounded, ties_table, place]
    table = shape((lines // BLK, BLK), jnp.int32)
    group, lane, (rounded, ties_table, place) = call(
        inverse_kernel,
        (table, table, [shape(a.shape, a.dtype) for a in handed]),
        [VMEM, [VMEM] * 3],
        (holder, handed),
        flops=10**9,
        name="invert_order",
    )
    boundary = shape((ties, everything, BLK), BF16)
    owns = [rounded] + rounded_others
    first, second = call(
        pick_kernel,
        (boundary, boundary),
        [[VMEM] * members, SMEM],
        (owns, ties_table),
        name="pick_boundary",
    )
    first, second, x_sent = lax.optimization_barrier((first, second, x_sent))
    first, second = with_neighbours(first, second)
    x_others = [from_snap(block, i) for i, block in enumerate(x_sent, 1)]
    guess = call(
        predict_kernel,
        shape((everything, lines), F32),
        [VMEM, VMEM, [VMEM] * members, VMEM, SMEM],
        (first, second, owns, derivative_pieces, place),
        scratch=[pltpu.VMEM((slots, everything, BLK), BF16)],
        flops=10**9,
        name="predict",
    )
    message, guess = lax.optimization_barrier((message, guess))
    halves = []
    for part in range(2):
        halves.append(
            call(
                functools.partial(unpack_kernel, part * (lines // BLK // 2)),
                (shape((snaps, lines // 2), F32), shape((1, lines // 2), F32)),
                [VMEM, VMEM, VMEM],
                (group, lane, message),
                scratch=[pltpu.VMEM((chunks * (width // BLK), BLK), F32)],
                flops=2 * 10**9,
                name="unpack_readings",
            )
        )
    halves, x_others = lax.optimization_barrier((halves, x_others))
    readings = [half[0] for half in halves]
    variance = [half[1] for half in halves]
    reading_others = [from_all(half) for half in readings]
    grads = (
        shape((own, everything, BLK), F32),
        boundary,
        boundary,
    )
    total = pltpu.VMEM((slots, everything, BLK), F32)
    work = pltpu.VMEM((2 * ties, everything, BLK), F32)

    def partial_update(grad):
        return call(
            partial_update_kernel,
            shape((everything, held * BLK), F32),
            [VMEM, SMEM, VMEM],
            (grad, ties_table, reciprocal_normal_operator),
            flops=10**9,
            name="partial_update",
        )

    grad, first, second = call(
        pull_kernel,
        grads,
        [VMEM, [VMEM] * 2, [VMEM] * 2, [VMEM] * 2, VMEM, SMEM],
        (guess, readings, reading_others, variance, derivative_pieces, place),
        scratch=[total, pltpu.VMEM((everything, lines), BF16)],
        name="pull",
    )
    arrived = with_neighbours(first, second)
    kept, given, mine, first = call(
        first_update_kernel,
        (
            shape((held, snaps, BLK), F32),
            [shape((held, snaps, BLK), F32)] * (members - 1),
            shape((held, everything, BLK), BF16),
            boundary,
        ),
        [VMEM, VMEM, VMEM, VMEM, SMEM, VMEM, VMEM, [VMEM] * (members - 1)],
        (
            partial_update(grad), grad, *arrived, ties_table, reciprocal_normal_operator,
            starting_voltages, x_others,
        ),
        scratch=[work],
        name="first_update",
    )
    others = [from_snap(mine, i) for i in range(1, members)]
    first = swap_pair(first, 1)
    firsts = [first] + [from_snap(first, i) for i in range(1, members)]
    aug, second = call(
        join_states_kernel,
        (shape((own, everything, BLK), BF16), boundary),
        [VMEM, [VMEM] * (members - 1), SMEM],
        (mine, others, ties_table),
        name="join_states",
    )
    second = swap_pair(second, 0)
    grad, first, second = call(
        predict_pull_kernel,
        grads,
        [[VMEM] * members, VMEM, VMEM, [VMEM] * 2, [VMEM] * 2, [VMEM] * 2, VMEM, SMEM],
        (firsts, aug, second, readings, reading_others, variance, derivative_pieces, place),
        scratch=[
            pltpu.VMEM((slots, everything, BLK), BF16),
            pltpu.VMEM((everything, lines), F32),
            total,
            pltpu.VMEM((everything, lines), BF16),
        ],
        name="predict_pull",
    )
    first, second = with_neighbours(first, second)
    mine, sent = call(
        last_update_kernel,
        (
            shape((snaps, held * BLK), F32),
            [shape((snaps, held * BLK), BF16)] * (members - 1),
        ),
        [VMEM, VMEM, VMEM, VMEM, SMEM, VMEM, VMEM, [VMEM] * (members - 1)],
        (partial_update(grad), grad, first, second, ties_table, reciprocal_normal_operator, kept, given),
        scratch=[work],
        name="last_update",
    )
    return call(
        finish_kernel,
        shape((snaps, states), F32),
        [VMEM, VMEM, [VMEM] * (members - 1)],
        (mine, starting_voltages, [from_snap(block, -i) for i, block in enumerate(sent, 1)]),
        name="finish",
    )


def solution(mesh):
    placed = (
        P("snap", "area"),
        P("area"),
        P("snap", "area"),
        P("area", None, None, None),
        P("area", None, None),
        P("area", None, None),
        P("area", None, None),
        P("area", None, None),
        P(("area", "snap"), None),
    )
    return jax.shard_map(
        on_device, mesh=mesh, in_specs=placed, out_specs=P("snap", "area"), check_vma=False
    )
```

```python
import functools

import jax
import jax.numpy as jnp
from jax import lax
from jax.experimental import pallas as pl
from jax.experimental.pallas import tpu as pltpu
from jax.sharding import PartitionSpec as P

BLK = 128
ITERS = 2
F32 = jnp.float32
BF16 = jnp.bfloat16
NT = (((1,), (1,)), ((), ()))
VMEM = pl.BlockSpec(memory_space=pltpu.VMEM)
HBM = pl.BlockSpec(memory_space=pltpu.HBM)
SMEM = pl.BlockSpec(memory_space=pltpu.SMEM)


def call(kernel, outs, ins, args, scratch=(), flops=0, mib=12, out_spec=None, name=None):
    return pl.pallas_call(
        kernel,
        out_shape=outs,
        in_specs=ins,
        out_specs=jax.tree.map(lambda _: VMEM, outs) if out_spec is None else out_spec,
        scratch_shapes=list(scratch),
        compiler_params=pltpu.CompilerParams(vmem_limit_bytes=mib * 1024 * 1024),
        cost_estimate=pl.CostEstimate(
            flops=flops, bytes_accessed=0, transcendentals=0
        ),
        name=name,
    )(*args)


def lane_gather(values, lanes):
    return jnp.take_along_axis(values, lanes, axis=1, mode="promise_in_bounds")


def rows_iota(shape):
    return lax.broadcasted_iota(jnp.int32, shape, 0)


def pack_kernel(
    z_in, v_in, hub_in, x_in, out, rounded_out, sent_outs,
    z_ref, v_ref, hub_ref, x_ref, out_ref, rounded_ref,
    sems, out_sems, sent_sems,
):
    pairs = ((x_in, x_ref), (hub_in, hub_ref), (z_in, z_ref), (v_in, v_ref))
    copies = [
        pltpu.make_async_copy(source, target, sems.at[i])
        for i, (source, target) in enumerate(pairs)
    ]
    for copy in copies:
        copy.start()
    for copy in copies:
        copy.wait()
    for b in range(rounded_ref.shape[0]):
        rounded_ref[b] = x_ref[:, b * BLK : (b + 1) * BLK].astype(BF16)
    ready = [(rounded_ref, rounded_out)]
    members = len(sent_outs) + 1
    part = x_ref.shape[1] // members
    for i, sent_out in enumerate(sent_outs, 1):
        at = lax.rem(lax.axis_index("snap") + i, members) * part
        ready.append((x_ref.at[:, pl.ds(pl.multiple_of(at, BLK), part)], sent_out))
    sends = [
        pltpu.make_async_copy(source, target, sent_sems.at[i])
        for i, (source, target) in enumerate(ready)
    ]
    for copy in sends:
        copy.start()
    snaps, lines = z_ref.shape
    blocks = lines // BLK
    chunks, width = hub_ref.shape
    groups = width // BLK
    for d in range(chunks):
        tail = jnp.zeros((8, BLK), F32)
        for g in range(groups):
            slot = hub_ref[d : d + 1, g * BLK : (g + 1) * BLK]
            high = jnp.right_shift(slot, 7)
            low = jnp.bitwise_and(slot, 127)
            lanes = jnp.broadcast_to(low, (snaps, BLK))
            block_of = jnp.broadcast_to(high, (snaps, BLK))
            picked = jnp.zeros((snaps, BLK), F32)
            for b in range(blocks):
                found = lane_gather(z_ref[:, b * BLK : (b + 1) * BLK], lanes)
                picked = jnp.where(block_of == b, found, picked)
            out_ref[d, g * snaps : (g + 1) * snaps, :] = picked
            found = lane_gather(v_ref[...], jnp.broadcast_to(low, (blocks, BLK)))
            mine = rows_iota((blocks, BLK)) == high
            variance = jnp.sum(jnp.where(mine, found, 0.0), axis=0, keepdims=True)
            tail = jnp.where(rows_iota((8, BLK)) == g, variance, tail)
        out_ref[d, groups * snaps :, :] = tail
        pltpu.make_async_copy(out_ref.at[d], out.at[d], out_sems.at[d]).start()
    for d in range(chunks):
        pltpu.make_async_copy(out_ref.at[d], out.at[d], out_sems.at[d]).wait()
    for copy in sends:
        copy.wait()


def inverse_kernel(own_ref, handed_refs, group_ref, lane_ref, kept_refs):
    for handed_ref, kept_ref in zip(handed_refs, kept_refs):
        kept_ref[...] = handed_ref[...]
    chunks, width = own_ref.shape
    blocks = group_ref.shape[0]
    groups = width // BLK
    total = jnp.zeros((2 * blocks, BLK), F32)
    lane = lax.broadcasted_iota(jnp.int32, (2 * blocks, width), 1)
    row = rows_iota((2 * blocks, width))
    in_group = jnp.bitwise_and(lane, 127)
    group_in = jnp.right_shift(lane, 7)
    for d in range(chunks):
        owned = own_ref[d : d + 1, :]
        high = jnp.right_shift(owned, 7)
        low = jnp.bitwise_and(owned, 127)
        label = jnp.where(row < blocks, group_in + d * groups, in_group)
        hit = jnp.bitwise_and(row, blocks - 1) == high
        left = jnp.where(hit, label.astype(F32), 0.0).astype(BF16)
        right = jnp.where(rows_iota((BLK, width)) == low, 1.0, 0.0).astype(BF16)
        total += lax.dot_general(left, right, NT, preferred_element_type=F32)
    group_ref[...] = total[:blocks].astype(jnp.int32)
    lane_ref[...] = total[blocks:].astype(jnp.int32)


def unpack_kernel(start, group_ref, lane_ref, message_ref, z_ref, v_ref, variance_ref):
    snaps, lines = z_ref.shape
    chunks = message_ref.shape[0]
    groups = (message_ref.shape[1] - 8) // snaps
    total = chunks * groups
    for d in range(chunks):
        variance_ref[d * groups : (d + 1) * groups, :] = message_ref[d, groups * snaps :, :][:groups]
    for b in range(lines // BLK):
        group = group_ref[start + b : start + b + 1, :]
        lane = lane_ref[start + b : start + b + 1, :]
        lanes = jnp.broadcast_to(lane, (snaps, BLK))
        group_of = jnp.broadcast_to(group, (snaps, BLK))
        picked = jnp.zeros((snaps, BLK), F32)
        for g in range(total):
            rows = slice(g % groups * snaps, (g % groups + 1) * snaps)
            found = lane_gather(message_ref[g // groups, rows, :], lanes)
            picked = jnp.where(group_of == g, found, picked)
        columns = slice(b * BLK, (b + 1) * BLK)
        z_ref[:, columns] = picked
        found = lane_gather(variance_ref[...], jnp.broadcast_to(lane, (total, BLK)))
        mine = rows_iota((total, BLK)) == group
        v_ref[:, columns] = jnp.sum(jnp.where(mine, found, 0.0), axis=0, keepdims=True)


def split(ref):
    return [ref.at[i] for i in range(ref.shape[0])]


def parity():
    return 1 - lax.rem(lax.axis_index("area"), 2)


def pick(blocks_ref, listing_ref, side, out_ref, start=0):
    held = blocks_ref.shape[0]
    for t in range(out_ref.shape[0]):
        b = listing_ref[side, t]
        at = b - start
        block = blocks_ref[jnp.clip(at, 0, held - 1)]
        here = (b >= 0) & (at >= 0) & (at < held)
        out_ref[t] = jnp.where(here, block, jnp.zeros_like(block))


def slots_into(slots_ref, aug_ref, first, second_ref):
    own = aug_ref.shape[0]
    ties = second_ref.shape[0]
    slots_ref[:own] = aug_ref[...]
    slots_ref[pl.ds(own + ties * (1 - parity()), ties)] = first
    slots_ref[pl.ds(own + ties * parity(), ties)] = second_ref[...]


def reordered(ref, distance, members):
    snaps = ref.shape[1] // members
    order = [(n - distance) % members for n in range(members)]
    return jnp.concatenate([ref[:, j * snaps : (j + 1) * snaps] for j in order], axis=1)


def join_states_kernel(mine_ref, others_refs, ties_ref, aug_ref, second_ref):
    members = len(others_refs) + 1
    held = mine_ref.shape[0]
    me = lax.axis_index("snap")
    aug_ref[pl.ds(me * held, held)] = mine_ref[...]
    for i, ref in enumerate(others_refs, 1):
        at = lax.rem(me + members - i, members) * held
        aug_ref[pl.ds(at, held)] = reordered(ref, i, members)
    pick(aug_ref, ties_ref, parity(), second_ref)


def predicted(j, slots_ref, tiles_ref, place_ref):
    touched = tiles_ref.shape[1]
    chosen = jnp.concatenate([slots_ref[place_ref[k, j]] for k in range(touched)], axis=1)
    weights = jnp.concatenate([tiles_ref[j, k] for k in range(touched)], axis=1)
    return lax.dot_general(chosen, weights, NT, preferred_element_type=F32)


def pick_kernel(own_refs, ties_ref, first_ref, second_ref):
    snaps = own_refs[0].shape[1]
    for i, own_ref in enumerate(own_refs):
        rows = slice(i * snaps, (i + 1) * snaps)
        pick(own_ref, ties_ref, 1 - parity(), first_ref.at[:, rows])
        pick(own_ref, ties_ref, parity(), second_ref.at[:, rows])


def predict_kernel(
    first_ref, second_ref, own_refs, tiles_ref, place_ref, out_ref, slots_ref
):
    own, snaps = own_refs[0].shape[:2]
    ties = first_ref.shape[0]
    for i, own_ref in enumerate(own_refs):
        slots_ref[:own, i * snaps : (i + 1) * snaps] = own_ref[...]
    slots_ref[pl.ds(own + ties * (1 - parity()), ties)] = first_ref[...]
    slots_ref[pl.ds(own + ties * parity(), ties)] = second_ref[...]
    predict(tiles_ref, place_ref, out_ref, slots_ref)


def predict(tiles_ref, place_ref, out_ref, slots_ref):
    for j in range(tiles_ref.shape[0]):
        out_ref[:, j * BLK : (j + 1) * BLK] = predicted(j, slots_ref, tiles_ref, place_ref)


def weigh(j, guess, z_refs, others_refs, v_refs):
    part = 0
    while j >= z_refs[part].shape[1] // BLK:
        j -= z_refs[part].shape[1] // BLK
        part += 1
    z_ref, others_ref, v_ref = z_refs[part], others_refs[part], v_refs[part]
    columns = slice(j * BLK, (j + 1) * BLK)
    readings = [z_ref[:, columns]] + [o[:, columns] for o in split(others_ref)]
    resid = jnp.concatenate(readings, axis=0) - guess
    spread = jnp.sum(resid * resid, axis=0, keepdims=True) / resid.shape[0]
    return (resid / (v_ref[:, columns] + spread)).astype(BF16)


def pull(weighted_ref, tiles_ref, place_ref, total_ref, own_ref, first_ref, second_ref):
    total_ref[...] = jnp.zeros_like(total_ref)
    touched = tiles_ref.shape[1]
    for j in range(tiles_ref.shape[0]):
        weighted = weighted_ref[:, j * BLK : (j + 1) * BLK]
        weights = jnp.concatenate([tiles_ref[j, k] for k in range(touched)], axis=1)
        part = jnp.dot(weighted, weights, preferred_element_type=F32)
        for k in range(touched):
            n = place_ref[k, j]
            total_ref[n] += part[:, k * BLK : (k + 1) * BLK]
    own = own_ref.shape[0]
    ties = first_ref.shape[0]
    own_ref[...] = total_ref[:own]
    first = total_ref[pl.ds(own + ties * (1 - parity()), ties)]
    second = total_ref[pl.ds(own + ties * parity(), ties)]
    first_ref[...] = first.astype(first_ref.dtype)
    second_ref[...] = second.astype(second_ref.dtype)


def pull_kernel(
    guess_ref, z_refs, others_refs, v_refs, tiles_ref, place_ref, own_ref, first_ref, second_ref,
    total_ref, weighted_ref,
):
    for j in range(tiles_ref.shape[0]):
        columns = slice(j * BLK, (j + 1) * BLK)
        weighted_ref[:, columns] = weigh(j, guess_ref[:, columns], z_refs, others_refs, v_refs)
    pull(weighted_ref, tiles_ref, place_ref, total_ref, own_ref, first_ref, second_ref)


def predict_pull_kernel(
    first_refs, aug_ref, second_in_ref, z_refs, others_refs, v_refs, tiles_ref, place_ref,
    own_ref, first_ref, second_ref, slots_ref, guess_ref, total_ref, weighted_ref,
):
    parts = [reordered(ref, i, len(first_refs)) for i, ref in enumerate(first_refs)]
    slots_into(slots_ref, aug_ref, sum(parts[1:], parts[0]), second_in_ref)
    predict(tiles_ref, place_ref, guess_ref, slots_ref)
    pull_kernel(
        guess_ref, z_refs, others_refs, v_refs, tiles_ref, place_ref, own_ref, first_ref, second_ref,
        total_ref, weighted_ref,
    )


def partial_update_kernel(grad_ref, ties_ref, gain_ref, part_ref):
    sides, ties = ties_ref.shape
    blocks = []
    for b in range(grad_ref.shape[0]):
        listed = ties_ref[0, 0] == b
        for side in range(sides):
            for t in range(ties):
                listed = listed | (ties_ref[side, t] == b)
        block = grad_ref[b]
        blocks.append(jnp.where(listed, jnp.zeros_like(block), block).astype(BF16))
    gradient = jnp.concatenate(blocks, axis=1)
    step = min(2 * BLK, gain_ref.shape[0])
    for at in range(0, gain_ref.shape[0], step):
        rows = gain_ref[at : at + step, :]
        part_ref[:, at : at + step] = lax.dot_general(
            gradient, rows, NT, preferred_element_type=F32
        )


def updates(part_ref, grad_ref, back_first_ref, back_second_ref, ties_ref, gain_ref, work_ref):
    ties = back_first_ref.shape[0]
    lists = [[ties_ref[side, t] for t in range(ties)] for side in (1 - parity(), parity())]
    for t, b in enumerate(lists[0]):
        block = grad_ref[jnp.maximum(b, 0)] + back_first_ref[t].astype(F32)
        work_ref[t] = jnp.where(b >= 0, block, jnp.zeros_like(block))
    for t, b in enumerate(lists[1]):
        at = ties + t
        for u, other in enumerate(lists[0]):
            at = jnp.where((b >= 0) & (other == b), u, at)
        block = grad_ref[jnp.maximum(b, 0)]
        alone = (b >= 0) & (at == ties + t)
        work_ref[ties + t] = jnp.where(alone, block, jnp.zeros_like(block))
        back = back_second_ref[t].astype(F32)
        work_ref[at] += jnp.where(b >= 0, back, jnp.zeros_like(back))
    listed = lists[0] + lists[1]
    gradient = jnp.concatenate([work_ref[n].astype(BF16) for n in range(len(listed))], axis=1)
    step = min(2 * BLK, gain_ref.shape[0])
    for at in range(0, gain_ref.shape[0], step):
        rows = [
            gain_ref[at : at + step, pl.ds(pl.multiple_of(jnp.maximum(b, 0) * BLK, BLK), BLK)]
            for b in listed
        ]
        update = part_ref[:, at : at + step] + lax.dot_general(
            gradient, jnp.concatenate(rows, axis=1), NT, preferred_element_type=F32
        )
        for i in range(step // BLK):
            yield at // BLK + i, update[:, i * BLK : (i + 1) * BLK]


def first_update_kernel(
    part_ref, grad_ref, back_first_ref, back_second_ref, ties_ref, gain_ref, x_ref, x_others_refs,
    kept_ref, given_refs, message_ref, first_ref, work_ref,
):
    held, snaps = kept_ref.shape[:2]
    me = lax.axis_index("snap")
    operands = part_ref, grad_ref, back_first_ref, back_second_ref, ties_ref, gain_ref, work_ref
    for i, update in updates(*operands):
        columns = pl.ds(pl.multiple_of((me * held + i) * BLK, BLK), BLK)
        parts = [x_ref[:, columns]] + [o[:, i * BLK : (i + 1) * BLK] for o in x_others_refs]
        state = jnp.concatenate(parts, axis=0) + update
        kept_ref[i] = state[:snaps]
        for j, given_ref in enumerate(given_refs, 1):
            given_ref[i] = state[j * snaps : (j + 1) * snaps]
        message_ref[i] = state.astype(BF16)
    pick(message_ref, ties_ref, 1 - parity(), first_ref, me * held)


def last_update_kernel(
    part_ref, grad_ref, back_first_ref, back_second_ref, ties_ref, gain_ref, kept_ref, mine_ref, sent_refs, work_ref
):
    snaps = mine_ref.shape[0]
    operands = part_ref, grad_ref, back_first_ref, back_second_ref, ties_ref, gain_ref, work_ref
    for i, update in updates(*operands):
        columns = slice(i * BLK, (i + 1) * BLK)
        mine_ref[:, columns] = kept_ref[i] + update[:snaps]
        for j, sent_ref in enumerate(sent_refs, 1):
            sent_ref[:, columns] = update[j * snaps : (j + 1) * snaps].astype(BF16)


def finish_kernel(mine_ref, states_refs, updates_refs, out_ref):
    width = mine_ref.shape[1]
    members = len(states_refs) + 1
    me = lax.axis_index("snap")
    out_ref[:, pl.ds(pl.multiple_of(me * width, BLK), width)] = mine_ref[...]
    for i, (state_ref, update_ref) in enumerate(zip(states_refs, updates_refs), 1):
        at = lax.rem(me + i, members) * width
        for b in range(width // BLK):
            update = update_ref[:, b * BLK : (b + 1) * BLK].astype(F32)
            columns = pl.ds(pl.multiple_of(at + b * BLK, BLK), BLK)
            out_ref[:, columns] = state_ref[b] + update


def swap_pair(block, start):
    pairs = [(i, i + 1) for i in range(start, lax.axis_size("area") - 1, 2)]
    return lax.ppermute(block, "area", pairs + [(b, a) for a, b in pairs])


def with_neighbours(first, second):
    return swap_pair(first, 1), swap_pair(second, 0)


def from_snap(block, distance):
    members = lax.axis_size("snap")
    return lax.ppermute(block, "snap", [(i, (i + distance) % members) for i in range(members)])


def from_all(block):
    return jnp.stack([from_snap(block, i) for i in range(1, lax.axis_size("snap"))])


def shape(dims, kind):
    return jax.ShapeDtypeStruct(dims, kind)


def on_device(
    phasor_readings,
    reading_error_spread,
    starting_voltages,
    derivative_pieces,
    derivative_tile_position,
    frontier_voltage_pieces,
    holder_line_order,
    hub_line_order,
    reciprocal_normal_operator,
):
    snaps, lines = phasor_readings.shape
    states = starting_voltages.shape[1]
    own = states // BLK
    measure = derivative_pieces.shape[0]
    ties_table = frontier_voltage_pieces[0]
    ties = ties_table.shape[1]
    slots = own + 2 * ties
    members = lax.axis_size("snap")
    areas = lax.axis_size("area")
    everything = snaps * members
    held = reciprocal_normal_operator.shape[0] // BLK
    place = derivative_tile_position[0].T
    cap = hub_line_order.shape[2]
    width = max(cap, BLK)
    chunks = areas * cap // width
    hub = hub_line_order[0].reshape(chunks, width)
    holder = holder_line_order[0].reshape(chunks, width)
    depth = (width // BLK) * snaps + 8

    message, rounded, x_sent = call(
        pack_kernel,
        (
            shape((chunks, depth, BLK), F32),
            shape((own, snaps, BLK), BF16),
            [shape((snaps, held * BLK), F32)] * (members - 1),
        ),
        [HBM] * 4,
        (
            phasor_readings,
            reading_error_spread.reshape(lines // BLK, BLK),
            hub,
            starting_voltages,
        ),
        scratch=[
            pltpu.VMEM((snaps, lines), F32),
            pltpu.VMEM((lines // BLK, BLK), F32),
            pltpu.VMEM((chunks, width), jnp.int32),
            pltpu.VMEM((snaps, states), F32),
            pltpu.VMEM((chunks, depth, BLK), F32),
            pltpu.VMEM((own, snaps, BLK), BF16),
            pltpu.SemaphoreType.DMA((4,)),
            pltpu.SemaphoreType.DMA((chunks,)),
            pltpu.SemaphoreType.DMA((members,)),
        ],
        out_spec=(HBM, HBM, [HBM] * (members - 1)),
        mib=60,
        name="pack_readings",
    )
    each = width // cap
    if each > 1:
        message = message.reshape(chunks, depth, each, cap).transpose(0, 2, 1, 3)
        message = message.reshape(areas, depth, cap)
    message = lax.all_to_all(message, "area", split_axis=0, concat_axis=0, tiled=True)
    if each > 1:
        message = message.reshape(chunks, each, depth, cap).transpose(0, 2, 1, 3)
        message = message.reshape(chunks, depth, BLK)

    rounded_others = [from_snap(rounded, i) for i in range(1, members)]
    handed = [rounded, ties_table, place]
    table = shape((lines // BLK, BLK), jnp.int32)
    group, lane, (rounded, ties_table, place) = call(
        inverse_kernel,
        (table, table, [shape(a.shape, a.dtype) for a in handed]),
        [VMEM, [VMEM] * 3],
        (holder, handed),
        flops=10**9,
        name="invert_order",
    )
    boundary = shape((ties, everything, BLK), BF16)
    owns = [rounded] + rounded_others
    first, second = call(
        pick_kernel,
        (boundary, boundary),
        [[VMEM] * members, SMEM],
        (owns, ties_table),
        name="pick_boundary",
    )
    first, second, x_sent = lax.optimization_barrier((first, second, x_sent))
    first, second = with_neighbours(first, second)
    x_others = [from_snap(block, i) for i, block in enumerate(x_sent, 1)]
    guess = call(
        predict_kernel,
        shape((everything, lines), F32),
        [VMEM, VMEM, [VMEM] * members, VMEM, SMEM],
        (first, second, owns, derivative_pieces, place),
        scratch=[pltpu.VMEM((slots, everything, BLK), BF16)],
        flops=10**9,
        name="predict",
    )
    message, guess = lax.optimization_barrier((message, guess))
    blocks = lines // BLK
    cuts = (0, blocks // 4, blocks * 11 // 16, blocks)
    readings, variance, reading_others = [], [], []
    for part, (start, stop) in enumerate(zip(cuts, cuts[1:])):
        if part == 2:
            message, reading_others[0] = lax.optimization_barrier((message, reading_others[0]))
        some = call(
            functools.partial(unpack_kernel, start),
            (
                shape((snaps, (stop - start) * BLK), F32),
                shape((1, (stop - start) * BLK), F32),
            ),
            [VMEM, VMEM, VMEM],
            (group, lane, message),
            scratch=[pltpu.VMEM((chunks * (width // BLK), BLK), F32)],
            flops=2 * 10**9,
            name="unpack_readings",
        )
        if part == 1:
            some, x_others = lax.optimization_barrier((some, x_others))
        readings.append(some[0])
        variance.append(some[1])
        reading_others.append(from_all(some[0]))
    grads = (
        shape((own, everything, BLK), F32),
        boundary,
        boundary,
    )
    total = pltpu.VMEM((slots, everything, BLK), F32)
    work = pltpu.VMEM((2 * ties, everything, BLK), F32)

    def partial_update(grad):
        return call(
            partial_update_kernel,
            shape((everything, held * BLK), F32),
            [VMEM, SMEM, VMEM],
            (grad, ties_table, reciprocal_normal_operator),
            flops=10**9,
            name="partial_update",
        )

    grad, first, second = call(
        pull_kernel,
        grads,
        [VMEM, [VMEM] * 3, [VMEM] * 3, [VMEM] * 3, VMEM, SMEM],
        (guess, readings, reading_others, variance, derivative_pieces, place),
        scratch=[total, pltpu.VMEM((everything, lines), BF16)],
        name="pull",
    )
    arrived = with_neighbours(first, second)
    kept, given, mine, first = call(
        first_update_kernel,
        (
            shape((held, snaps, BLK), F32),
            [shape((held, snaps, BLK), F32)] * (members - 1),
            shape((held, everything, BLK), BF16),
            boundary,
        ),
        [VMEM, VMEM, VMEM, VMEM, SMEM, VMEM, VMEM, [VMEM] * (members - 1)],
        (
            partial_update(grad), grad, *arrived, ties_table, reciprocal_normal_operator,
            starting_voltages, x_others,
        ),
        scratch=[work],
        name="first_update",
    )
    others = [from_snap(mine, i) for i in range(1, members)]
    first = swap_pair(first, 1)
    firsts = [first] + [from_snap(first, i) for i in range(1, members)]
    aug, second = call(
        join_states_kernel,
        (shape((own, everything, BLK), BF16), boundary),
        [VMEM, [VMEM] * (members - 1), SMEM],
        (mine, others, ties_table),
        name="join_states",
    )
    second = swap_pair(second, 0)
    grad, first, second = call(
        predict_pull_kernel,
        grads,
        [[VMEM] * members, VMEM, VMEM, [VMEM] * 3, [VMEM] * 3, [VMEM] * 3, VMEM, SMEM],
        (firsts, aug, second, readings, reading_others, variance, derivative_pieces, place),
        scratch=[
            pltpu.VMEM((slots, everything, BLK), BF16),
            pltpu.VMEM((everything, lines), F32),
            total,
            pltpu.VMEM((everything, lines), BF16),
        ],
        name="predict_pull",
    )
    given, first, second = lax.optimization_barrier((given, first, second))
    first, second = with_neighbours(first, second)
    states_in = [from_snap(block, -i) for i, block in enumerate(given, 1)]
    mine, sent = call(
        last_update_kernel,
        (
            shape((snaps, held * BLK), F32),
            [shape((snaps, held * BLK), BF16)] * (members - 1),
        ),
        [VMEM, VMEM, VMEM, VMEM, SMEM, VMEM, VMEM],
        (partial_update(grad), grad, first, second, ties_table, reciprocal_normal_operator, kept),
        scratch=[work],
        name="last_update",
    )
    return call(
        finish_kernel,
        shape((snaps, states), F32),
        [VMEM, [VMEM] * (members - 1), [VMEM] * (members - 1)],
        (mine, states_in, [from_snap(block, -i) for i, block in enumerate(sent, 1)]),
        name="finish",
    )


def solution(mesh):
    placed = (
        P("snap", "area"),
        P("area"),
        P("snap", "area"),
        P("area", None, None, None),
        P("area", None, None),
        P("area", None, None),
        P("area", None, None),
        P("area", None, None),
        P(("area", "snap"), None),
    )
    return jax.shard_map(
        on_device, mesh=mesh, in_specs=placed, out_specs=P("snap", "area"), check_vma=False
    )
```

```python
import functools

import jax
import jax.numpy as jnp
from jax import lax
from jax.experimental import pallas as pl
from jax.experimental.pallas import tpu as pltpu
from jax.sharding import PartitionSpec as P

BLK = 128
ITERS = 2
F32 = jnp.float32
BF16 = jnp.bfloat16
NT = (((1,), (1,)), ((), ()))
VMEM = pl.BlockSpec(memory_space=pltpu.VMEM)
HBM = pl.BlockSpec(memory_space=pltpu.HBM)
SMEM = pl.BlockSpec(memory_space=pltpu.SMEM)


def call(kernel, outs, ins, args, scratch=(), flops=0, mib=12, out_spec=None, name=None):
    return pl.pallas_call(
        kernel,
        out_shape=outs,
        in_specs=ins,
        out_specs=jax.tree.map(lambda _: VMEM, outs) if out_spec is None else out_spec,
        scratch_shapes=list(scratch),
        compiler_params=pltpu.CompilerParams(vmem_limit_bytes=mib * 1024 * 1024),
        cost_estimate=pl.CostEstimate(
            flops=flops, bytes_accessed=0, transcendentals=0
        ),
        name=name,
    )(*args)


def lane_gather(values, lanes):
    return jnp.take_along_axis(values, lanes, axis=1, mode="promise_in_bounds")


def rows_iota(shape):
    return lax.broadcasted_iota(jnp.int32, shape, 0)


def pack_kernel(
    z_in, v_in, hub_in, x_in, out, rounded_out, sent_outs,
    z_ref, v_ref, hub_ref, x_ref, out_ref, rounded_ref,
    sems, out_sems, sent_sems,
):
    pairs = ((x_in, x_ref), (hub_in, hub_ref), (z_in, z_ref), (v_in, v_ref))
    copies = [
        pltpu.make_async_copy(source, target, sems.at[i])
        for i, (source, target) in enumerate(pairs)
    ]
    for copy in copies:
        copy.start()
    for copy in copies:
        copy.wait()
    for b in range(rounded_ref.shape[0]):
        rounded_ref[b] = x_ref[:, b * BLK : (b + 1) * BLK].astype(BF16)
    ready = [(rounded_ref, rounded_out)]
    members = len(sent_outs) + 1
    part = x_ref.shape[1] // members
    for i, sent_out in enumerate(sent_outs, 1):
        at = lax.rem(lax.axis_index("snap") + i, members) * part
        ready.append((x_ref.at[:, pl.ds(pl.multiple_of(at, BLK), part)], sent_out))
    sends = [
        pltpu.make_async_copy(source, target, sent_sems.at[i])
        for i, (source, target) in enumerate(ready)
    ]
    for copy in sends:
        copy.start()
    snaps, lines = z_ref.shape
    blocks = lines // BLK
    chunks, width = hub_ref.shape
    groups = width // BLK
    for d in range(chunks):
        tail = jnp.zeros((8, BLK), F32)
        for g in range(groups):
            slot = hub_ref[d : d + 1, g * BLK : (g + 1) * BLK]
            high = jnp.right_shift(slot, 7)
            low = jnp.bitwise_and(slot, 127)
            lanes = jnp.broadcast_to(low, (snaps, BLK))
            block_of = jnp.broadcast_to(high, (snaps, BLK))
            picked = jnp.zeros((snaps, BLK), F32)
            for b in range(blocks):
                found = lane_gather(z_ref[:, b * BLK : (b + 1) * BLK], lanes)
                picked = jnp.where(block_of == b, found, picked)
            out_ref[d, g * snaps : (g + 1) * snaps, :] = picked
            found = lane_gather(v_ref[...], jnp.broadcast_to(low, (blocks, BLK)))
            mine = rows_iota((blocks, BLK)) == high
            variance = jnp.sum(jnp.where(mine, found, 0.0), axis=0, keepdims=True)
            tail = jnp.where(rows_iota((8, BLK)) == g, variance, tail)
        out_ref[d, groups * snaps :, :] = tail
        pltpu.make_async_copy(out_ref.at[d], out.at[d], out_sems.at[d]).start()
    for d in range(chunks):
        pltpu.make_async_copy(out_ref.at[d], out.at[d], out_sems.at[d]).wait()
    for copy in sends:
        copy.wait()


def inverse_kernel(own_ref, handed_refs, group_ref, lane_ref, kept_refs):
    for handed_ref, kept_ref in zip(handed_refs, kept_refs):
        kept_ref[...] = handed_ref[...]
    chunks, width = own_ref.shape
    blocks = group_ref.shape[0]
    groups = width // BLK
    total = jnp.zeros((2 * blocks, BLK), F32)
    lane = lax.broadcasted_iota(jnp.int32, (2 * blocks, width), 1)
    row = rows_iota((2 * blocks, width))
    in_group = jnp.bitwise_and(lane, 127)
    group_in = jnp.right_shift(lane, 7)
    for d in range(chunks):
        owned = own_ref[d : d + 1, :]
        high = jnp.right_shift(owned, 7)
        low = jnp.bitwise_and(owned, 127)
        label = jnp.where(row < blocks, group_in + d * groups, in_group)
        hit = jnp.bitwise_and(row, blocks - 1) == high
        left = jnp.where(hit, label.astype(F32), 0.0).astype(BF16)
        right = jnp.where(rows_iota((BLK, width)) == low, 1.0, 0.0).astype(BF16)
        total += lax.dot_general(left, right, NT, preferred_element_type=F32)
    group_ref[...] = total[:blocks].astype(jnp.int32)
    lane_ref[...] = total[blocks:].astype(jnp.int32)


def unpack_kernel(start, group_ref, lane_ref, message_ref, z_ref, v_ref, variance_ref):
    snaps, lines = z_ref.shape
    chunks = message_ref.shape[0]
    groups = (message_ref.shape[1] - 8) // snaps
    total = chunks * groups
    for d in range(chunks):
        variance_ref[d * groups : (d + 1) * groups, :] = message_ref[d, groups * snaps :, :][:groups]
    for b in range(lines // BLK):
        group = group_ref[start + b : start + b + 1, :]
        lane = lane_ref[start + b : start + b + 1, :]
        lanes = jnp.broadcast_to(lane, (snaps, BLK))
        group_of = jnp.broadcast_to(group, (snaps, BLK))
        picked = jnp.zeros((snaps, BLK), F32)
        for g in range(total):
            rows = slice(g % groups * snaps, (g % groups + 1) * snaps)
            found = lane_gather(message_ref[g // groups, rows, :], lanes)
            picked = jnp.where(group_of == g, found, picked)
        columns = slice(b * BLK, (b + 1) * BLK)
        z_ref[:, columns] = picked
        found = lane_gather(variance_ref[...], jnp.broadcast_to(lane, (total, BLK)))
        mine = rows_iota((total, BLK)) == group
        v_ref[:, columns] = jnp.sum(jnp.where(mine, found, 0.0), axis=0, keepdims=True)


def split(ref):
    return [ref.at[i] for i in range(ref.shape[0])]


def parity():
    return 1 - lax.rem(lax.axis_index("area"), 2)


def pick(blocks_ref, listing_ref, side, out_ref, start=0):
    held = blocks_ref.shape[0]
    for t in range(out_ref.shape[0]):
        b = listing_ref[side, t]
        at = b - start
        block = blocks_ref[jnp.clip(at, 0, held - 1)]
        here = (b >= 0) & (at >= 0) & (at < held)
        out_ref[t] = jnp.where(here, block, jnp.zeros_like(block))


def slots_into(slots_ref, aug_ref, first, second_ref):
    own = aug_ref.shape[0]
    ties = second_ref.shape[0]
    slots_ref[:own] = aug_ref[...]
    slots_ref[pl.ds(own + ties * (1 - parity()), ties)] = first
    slots_ref[pl.ds(own + ties * parity(), ties)] = second_ref[...]


def reordered(ref, distance, members):
    snaps = ref.shape[1] // members
    order = [(n - distance) % members for n in range(members)]
    return jnp.concatenate([ref[:, j * snaps : (j + 1) * snaps] for j in order], axis=1)


def join_states_kernel(mine_ref, others_refs, ties_ref, aug_ref, second_ref):
    members = len(others_refs) + 1
    held = mine_ref.shape[0]
    me = lax.axis_index("snap")
    aug_ref[pl.ds(me * held, held)] = mine_ref[...]
    for i, ref in enumerate(others_refs, 1):
        at = lax.rem(me + members - i, members) * held
        aug_ref[pl.ds(at, held)] = reordered(ref, i, members)
    pick(aug_ref, ties_ref, parity(), second_ref)


def predicted(j, slots_ref, tiles_ref, place_ref):
    touched = tiles_ref.shape[1]
    chosen = jnp.concatenate([slots_ref[place_ref[k, j]] for k in range(touched)], axis=1)
    weights = jnp.concatenate([tiles_ref[j, k] for k in range(touched)], axis=1)
    return lax.dot_general(chosen, weights, NT, preferred_element_type=F32)


def pick_kernel(own_refs, ties_ref, first_ref, second_ref):
    snaps = own_refs[0].shape[1]
    for i, own_ref in enumerate(own_refs):
        rows = slice(i * snaps, (i + 1) * snaps)
        pick(own_ref, ties_ref, 1 - parity(), first_ref.at[:, rows])
        pick(own_ref, ties_ref, parity(), second_ref.at[:, rows])


def predict_kernel(
    first_ref, second_ref, own_refs, tiles_ref, place_ref, out_ref, slots_ref
):
    own, snaps = own_refs[0].shape[:2]
    ties = first_ref.shape[0]
    for i, own_ref in enumerate(own_refs):
        slots_ref[:own, i * snaps : (i + 1) * snaps] = own_ref[...]
    slots_ref[pl.ds(own + ties * (1 - parity()), ties)] = first_ref[...]
    slots_ref[pl.ds(own + ties * parity(), ties)] = second_ref[...]
    predict(tiles_ref, place_ref, out_ref, slots_ref)


def predict(tiles_ref, place_ref, out_ref, slots_ref):
    for j in range(tiles_ref.shape[0]):
        out_ref[:, j * BLK : (j + 1) * BLK] = predicted(j, slots_ref, tiles_ref, place_ref)


def weigh(j, guess, z_refs, others_refs, v_refs):
    part = 0
    while j >= z_refs[part].shape[1] // BLK:
        j -= z_refs[part].shape[1] // BLK
        part += 1
    z_ref, others_ref, v_ref = z_refs[part], others_refs[part], v_refs[part]
    columns = slice(j * BLK, (j + 1) * BLK)
    readings = [z_ref[:, columns]] + [o[:, columns] for o in split(others_ref)]
    resid = jnp.concatenate(readings, axis=0) - guess
    spread = jnp.sum(resid * resid, axis=0, keepdims=True) / resid.shape[0]
    return (resid / (v_ref[:, columns] + spread)).astype(BF16)


def pull(weighted_ref, tiles_ref, place_ref, total_ref, own_ref, first_ref, second_ref):
    total_ref[...] = jnp.zeros_like(total_ref)
    touched = tiles_ref.shape[1]
    for j in range(tiles_ref.shape[0]):
        weighted = weighted_ref[:, j * BLK : (j + 1) * BLK]
        weights = jnp.concatenate([tiles_ref[j, k] for k in range(touched)], axis=1)
        part = jnp.dot(weighted, weights, preferred_element_type=F32)
        for k in range(touched):
            n = place_ref[k, j]
            total_ref[n] += part[:, k * BLK : (k + 1) * BLK]
    own = own_ref.shape[0]
    ties = first_ref.shape[0]
    own_ref[...] = total_ref[:own]
    first = total_ref[pl.ds(own + ties * (1 - parity()), ties)]
    second = total_ref[pl.ds(own + ties * parity(), ties)]
    first_ref[...] = first.astype(first_ref.dtype)
    second_ref[...] = second.astype(second_ref.dtype)


def pull_kernel(
    guess_ref, z_refs, others_refs, v_refs, tiles_ref, place_ref, own_ref, first_ref, second_ref,
    total_ref, weighted_ref,
):
    for j in range(tiles_ref.shape[0]):
        columns = slice(j * BLK, (j + 1) * BLK)
        weighted_ref[:, columns] = weigh(j, guess_ref[:, columns], z_refs, others_refs, v_refs)
    pull(weighted_ref, tiles_ref, place_ref, total_ref, own_ref, first_ref, second_ref)


def predict_pull_kernel(
    first_refs, aug_ref, second_in_ref, z_refs, others_refs, v_refs, tiles_ref, place_ref,
    own_ref, first_ref, second_ref, slots_ref, guess_ref, total_ref, weighted_ref,
):
    parts = [reordered(ref, i, len(first_refs)) for i, ref in enumerate(first_refs)]
    slots_into(slots_ref, aug_ref, sum(parts[1:], parts[0]), second_in_ref)
    predict(tiles_ref, place_ref, guess_ref, slots_ref)
    pull_kernel(
        guess_ref, z_refs, others_refs, v_refs, tiles_ref, place_ref, own_ref, first_ref, second_ref,
        total_ref, weighted_ref,
    )


def partial_update_kernel(grad_ref, ties_ref, gain_ref, part_ref):
    sides, ties = ties_ref.shape
    blocks = []
    for b in range(grad_ref.shape[0]):
        listed = ties_ref[0, 0] == b
        for side in range(sides):
            for t in range(ties):
                listed = listed | (ties_ref[side, t] == b)
        block = grad_ref[b]
        blocks.append(jnp.where(listed, jnp.zeros_like(block), block).astype(BF16))
    gradient = jnp.concatenate(blocks, axis=1)
    step = min(2 * BLK, gain_ref.shape[0])
    for at in range(0, gain_ref.shape[0], step):
        rows = gain_ref[at : at + step, :]
        part_ref[:, at : at + step] = lax.dot_general(
            gradient, rows, NT, preferred_element_type=F32
        )


def updates(part_ref, grad_ref, back_first_ref, back_second_ref, ties_ref, gain_ref, work_ref):
    ties = back_first_ref.shape[0]
    lists = [[ties_ref[side, t] for t in range(ties)] for side in (1 - parity(), parity())]
    for t, b in enumerate(lists[0]):
        block = grad_ref[jnp.maximum(b, 0)] + back_first_ref[t].astype(F32)
        work_ref[t] = jnp.where(b >= 0, block, jnp.zeros_like(block))
    for t, b in enumerate(lists[1]):
        at = ties + t
        for u, other in enumerate(lists[0]):
            at = jnp.where((b >= 0) & (other == b), u, at)
        block = grad_ref[jnp.maximum(b, 0)]
        alone = (b >= 0) & (at == ties + t)
        work_ref[ties + t] = jnp.where(alone, block, jnp.zeros_like(block))
        back = back_second_ref[t].astype(F32)
        work_ref[at] += jnp.where(b >= 0, back, jnp.zeros_like(back))
    listed = lists[0] + lists[1]
    gradient = jnp.concatenate([work_ref[n].astype(BF16) for n in range(len(listed))], axis=1)
    step = min(2 * BLK, gain_ref.shape[0])
    for at in range(0, gain_ref.shape[0], step):
        rows = [
            gain_ref[at : at + step, pl.ds(pl.multiple_of(jnp.maximum(b, 0) * BLK, BLK), BLK)]
            for b in listed
        ]
        update = part_ref[:, at : at + step] + lax.dot_general(
            gradient, jnp.concatenate(rows, axis=1), NT, preferred_element_type=F32
        )
        for i in range(step // BLK):
            yield at // BLK + i, update[:, i * BLK : (i + 1) * BLK]


def first_update_kernel(
    part_ref, grad_ref, back_first_ref, back_second_ref, ties_ref, gain_ref, x_ref, x_others_refs,
    kept_ref, given_refs, message_ref, first_ref, work_ref,
):
    held, snaps = kept_ref.shape[:2]
    me = lax.axis_index("snap")
    operands = part_ref, grad_ref, back_first_ref, back_second_ref, ties_ref, gain_ref, work_ref
    for i, update in updates(*operands):
        columns = pl.ds(pl.multiple_of((me * held + i) * BLK, BLK), BLK)
        parts = [x_ref[:, columns]] + [o[:, i * BLK : (i + 1) * BLK] for o in x_others_refs]
        state = jnp.concatenate(parts, axis=0) + update
        kept_ref[i] = state[:snaps]
        for j, given_ref in enumerate(given_refs, 1):
            given_ref[i] = state[j * snaps : (j + 1) * snaps]
        message_ref[i] = state.astype(BF16)
    pick(message_ref, ties_ref, 1 - parity(), first_ref, me * held)


def last_update_kernel(
    part_ref, grad_ref, back_first_ref, back_second_ref, ties_ref, gain_ref, kept_ref, mine_ref, sent_refs, work_ref
):
    snaps = mine_ref.shape[0]
    operands = part_ref, grad_ref, back_first_ref, back_second_ref, ties_ref, gain_ref, work_ref
    for i, update in updates(*operands):
        columns = slice(i * BLK, (i + 1) * BLK)
        mine_ref[:, columns] = kept_ref[i] + update[:snaps]
        for j, sent_ref in enumerate(sent_refs, 1):
            sent_ref[:, columns] = update[j * snaps : (j + 1) * snaps].astype(BF16)


def finish_kernel(mine_ref, states_refs, updates_refs, out_ref):
    width = mine_ref.shape[1]
    members = len(states_refs) + 1
    me = lax.axis_index("snap")
    out_ref[:, pl.ds(pl.multiple_of(me * width, BLK), width)] = mine_ref[...]
    for i, (state_ref, update_ref) in enumerate(zip(states_refs, updates_refs), 1):
        at = lax.rem(me + i, members) * width
        for b in range(width // BLK):
            update = update_ref[:, b * BLK : (b + 1) * BLK].astype(F32)
            columns = pl.ds(pl.multiple_of(at + b * BLK, BLK), BLK)
            out_ref[:, columns] = state_ref[b] + update


def swap_pair(block, start):
    pairs = [(i, i + 1) for i in range(start, lax.axis_size("area") - 1, 2)]
    return lax.ppermute(block, "area", pairs + [(b, a) for a, b in pairs])


def with_neighbours(first, second):
    return swap_pair(first, 1), swap_pair(second, 0)


def from_snap(block, distance):
    members = lax.axis_size("snap")
    return lax.ppermute(block, "snap", [(i, (i + distance) % members) for i in range(members)])


def from_all(block):
    return jnp.stack([from_snap(block, i) for i in range(1, lax.axis_size("snap"))])


def shape(dims, kind):
    return jax.ShapeDtypeStruct(dims, kind)


def on_device(
    phasor_readings,
    reading_error_spread,
    starting_voltages,
    derivative_pieces,
    derivative_tile_position,
    frontier_voltage_pieces,
    holder_line_order,
    hub_line_order,
    reciprocal_normal_operator,
):
    snaps, lines = phasor_readings.shape
    states = starting_voltages.shape[1]
    own = states // BLK
    measure = derivative_pieces.shape[0]
    ties_table = frontier_voltage_pieces[0]
    ties = ties_table.shape[1]
    slots = own + 2 * ties
    members = lax.axis_size("snap")
    areas = lax.axis_size("area")
    everything = snaps * members
    held = reciprocal_normal_operator.shape[0] // BLK
    place = derivative_tile_position[0].T
    cap = hub_line_order.shape[2]
    width = max(cap, BLK)
    chunks = areas * cap // width
    hub = hub_line_order[0].reshape(chunks, width)
    holder = holder_line_order[0].reshape(chunks, width)
    depth = (width // BLK) * snaps + 8

    message, rounded, x_sent = call(
        pack_kernel,
        (
            shape((chunks, depth, BLK), F32),
            shape((own, snaps, BLK), BF16),
            [shape((snaps, held * BLK), F32)] * (members - 1),
        ),
        [HBM] * 4,
        (
            phasor_readings,
            reading_error_spread.reshape(lines // BLK, BLK),
            hub,
            starting_voltages,
        ),
        scratch=[
            pltpu.VMEM((snaps, lines), F32),
            pltpu.VMEM((lines // BLK, BLK), F32),
            pltpu.VMEM((chunks, width), jnp.int32),
            pltpu.VMEM((snaps, states), F32),
            pltpu.VMEM((chunks, depth, BLK), F32),
            pltpu.VMEM((own, snaps, BLK), BF16),
            pltpu.SemaphoreType.DMA((4,)),
            pltpu.SemaphoreType.DMA((chunks,)),
            pltpu.SemaphoreType.DMA((members,)),
        ],
        out_spec=(HBM, HBM, [HBM] * (members - 1)),
        mib=60,
        name="pack_readings",
    )
    each = width // cap
    if each > 1:
        message = message.reshape(chunks, depth, each, cap).transpose(0, 2, 1, 3)
        message = message.reshape(areas, depth, cap)
    message = lax.all_to_all(message, "area", split_axis=0, concat_axis=0, tiled=True)
    if each > 1:
        message = message.reshape(chunks, each, depth, cap).transpose(0, 2, 1, 3)
        message = message.reshape(chunks, depth, BLK)

    rounded_others = [from_snap(rounded, i) for i in range(1, members)]
    handed = [rounded, ties_table, place]
    table = shape((lines // BLK, BLK), jnp.int32)
    group, lane, (rounded, ties_table, place) = call(
        inverse_kernel,
        (table, table, [shape(a.shape, a.dtype) for a in handed]),
        [VMEM, [VMEM] * 3],
        (holder, handed),
        flops=10**9,
        name="invert_order",
    )
    boundary = shape((ties, everything, BLK), BF16)
    owns = [rounded] + rounded_others
    first, second = call(
        pick_kernel,
        (boundary, boundary),
        [[VMEM] * members, SMEM],
        (owns, ties_table),
        name="pick_boundary",
    )
    first, second, x_sent = lax.optimization_barrier((first, second, x_sent))
    first, second = with_neighbours(first, second)
    x_others = [from_snap(block, i) for i, block in enumerate(x_sent, 1)]
    guess = call(
        predict_kernel,
        shape((everything, lines), F32),
        [VMEM, VMEM, [VMEM] * members, VMEM, SMEM],
        (first, second, owns, derivative_pieces, place),
        scratch=[pltpu.VMEM((slots, everything, BLK), BF16)],
        flops=10**9,
        name="predict",
    )
    message, guess = lax.optimization_barrier((message, guess))
    blocks = lines // BLK
    cuts = (0, blocks * 3 // 16, blocks * 13 // 16, blocks)
    readings, variance, reading_others = [], [], []
    for part, (start, stop) in enumerate(zip(cuts, cuts[1:])):
        if part == 2:
            message, reading_others[0] = lax.optimization_barrier((message, reading_others[0]))
        some = call(
            functools.partial(unpack_kernel, start),
            (
                shape((snaps, (stop - start) * BLK), F32),
                shape((1, (stop - start) * BLK), F32),
            ),
            [VMEM, VMEM, VMEM],
            (group, lane, message),
            scratch=[pltpu.VMEM((chunks * (width // BLK), BLK), F32)],
            flops=2 * 10**9,
            name="unpack_readings",
        )
        if part == 1:
            some, x_others = lax.optimization_barrier((some, x_others))
        readings.append(some[0])
        variance.append(some[1])
        reading_others.append(from_all(some[0]))
    grads = (
        shape((own, everything, BLK), F32),
        boundary,
        boundary,
    )
    total = pltpu.VMEM((slots, everything, BLK), F32)
    work = pltpu.VMEM((2 * ties, everything, BLK), F32)

    def partial_update(grad):
        return call(
            partial_update_kernel,
            shape((everything, held * BLK), F32),
            [VMEM, SMEM, VMEM],
            (grad, ties_table, reciprocal_normal_operator),
            flops=10**9,
            name="partial_update",
        )

    grad, first, second = call(
        pull_kernel,
        grads,
        [VMEM, [VMEM] * 3, [VMEM] * 3, [VMEM] * 3, VMEM, SMEM],
        (guess, readings, reading_others, variance, derivative_pieces, place),
        scratch=[total, pltpu.VMEM((everything, lines), BF16)],
        name="pull",
    )
    arrived = with_neighbours(first, second)
    kept, given, mine, first = call(
        first_update_kernel,
        (
            shape((held, snaps, BLK), F32),
            [shape((held, snaps, BLK), F32)] * (members - 1),
            shape((held, everything, BLK), BF16),
            boundary,
        ),
        [VMEM, VMEM, VMEM, VMEM, SMEM, VMEM, VMEM, [VMEM] * (members - 1)],
        (
            partial_update(grad), grad, *arrived, ties_table, reciprocal_normal_operator,
            starting_voltages, x_others,
        ),
        scratch=[work],
        name="first_update",
    )
    others = [from_snap(mine, i) for i in range(1, members)]
    first = swap_pair(first, 1)
    firsts = [first] + [from_snap(first, i) for i in range(1, members)]
    aug, second = call(
        join_states_kernel,
        (shape((own, everything, BLK), BF16), boundary),
        [VMEM, [VMEM] * (members - 1), SMEM],
        (mine, others, ties_table),
        name="join_states",
    )
    second = swap_pair(second, 0)
    grad, first, second = call(
        predict_pull_kernel,
        grads,
        [[VMEM] * members, VMEM, VMEM, [VMEM] * 3, [VMEM] * 3, [VMEM] * 3, VMEM, SMEM],
        (firsts, aug, second, readings, reading_others, variance, derivative_pieces, place),
        scratch=[
            pltpu.VMEM((slots, everything, BLK), BF16),
            pltpu.VMEM((everything, lines), F32),
            total,
            pltpu.VMEM((everything, lines), BF16),
        ],
        name="predict_pull",
    )
    given, first, second = lax.optimization_barrier((given, first, second))
    first, second = with_neighbours(first, second)
    states_in = [from_snap(block, -i) for i, block in enumerate(given, 1)]
    mine, sent = call(
        last_update_kernel,
        (
            shape((snaps, held * BLK), F32),
            [shape((snaps, held * BLK), BF16)] * (members - 1),
        ),
        [VMEM, VMEM, VMEM, VMEM, SMEM, VMEM, VMEM],
        (partial_update(grad), grad, first, second, ties_table, reciprocal_normal_operator, kept),
        scratch=[work],
        name="last_update",
    )
    return call(
        finish_kernel,
        shape((snaps, states), F32),
        [VMEM, [VMEM] * (members - 1), [VMEM] * (members - 1)],
        (mine, states_in, [from_snap(block, -i) for i, block in enumerate(sent, 1)]),
        name="finish",
    )


def solution(mesh):
    placed = (
        P("snap", "area"),
        P("area"),
        P("snap", "area"),
        P("area", None, None, None),
        P("area", None, None),
        P("area", None, None),
        P("area", None, None),
        P("area", None, None),
        P(("area", "snap"), None),
    )
    return jax.shard_map(
        on_device, mesh=mesh, in_specs=placed, out_specs=P("snap", "area"), check_vma=False
    )
```

```python
import functools

import jax
import jax.numpy as jnp
from jax import lax
from jax.experimental import pallas as pl
from jax.experimental.pallas import tpu as pltpu
from jax.sharding import PartitionSpec as P

BLK = 128
ITERS = 2
F32 = jnp.float32
BF16 = jnp.bfloat16
NT = (((1,), (1,)), ((), ()))
VMEM = pl.BlockSpec(memory_space=pltpu.VMEM)
HBM = pl.BlockSpec(memory_space=pltpu.HBM)
SMEM = pl.BlockSpec(memory_space=pltpu.SMEM)


def call(kernel, outs, ins, args, scratch=(), flops=0, mib=12, out_spec=None, name=None):
    return pl.pallas_call(
        kernel,
        out_shape=outs,
        in_specs=ins,
        out_specs=jax.tree.map(lambda _: VMEM, outs) if out_spec is None else out_spec,
        scratch_shapes=list(scratch),
        compiler_params=pltpu.CompilerParams(vmem_limit_bytes=mib * 1024 * 1024),
        cost_estimate=pl.CostEstimate(
            flops=flops, bytes_accessed=0, transcendentals=0
        ),
        name=name,
    )(*args)


def lane_gather(values, lanes):
    return jnp.take_along_axis(values, lanes, axis=1, mode="promise_in_bounds")


def rows_iota(shape):
    return lax.broadcasted_iota(jnp.int32, shape, 0)


def pack_kernel(
    z_in, v_in, hub_in, x_in, out, rounded_out, sent_outs,
    z_ref, v_ref, hub_ref, x_ref, out_ref, rounded_ref,
    sems, out_sems, sent_sems,
):
    pairs = ((x_in, x_ref), (hub_in, hub_ref), (z_in, z_ref), (v_in, v_ref))
    copies = [
        pltpu.make_async_copy(source, target, sems.at[i])
        for i, (source, target) in enumerate(pairs)
    ]
    for copy in copies:
        copy.start()
    for copy in copies:
        copy.wait()
    for b in range(rounded_ref.shape[0]):
        rounded_ref[b] = x_ref[:, b * BLK : (b + 1) * BLK].astype(BF16)
    ready = [(rounded_ref, rounded_out)]
    members = len(sent_outs) + 1
    part = x_ref.shape[1] // members
    for i, sent_out in enumerate(sent_outs, 1):
        at = lax.rem(lax.axis_index("snap") + i, members) * part
        ready.append((x_ref.at[:, pl.ds(pl.multiple_of(at, BLK), part)], sent_out))
    sends = [
        pltpu.make_async_copy(source, target, sent_sems.at[i])
        for i, (source, target) in enumerate(ready)
    ]
    for copy in sends:
        copy.start()
    snaps, lines = z_ref.shape
    blocks = lines // BLK
    chunks, width = hub_ref.shape
    groups = width // BLK
    for d in range(chunks):
        tail = jnp.zeros((8, BLK), F32)
        for g in range(groups):
            slot = hub_ref[d : d + 1, g * BLK : (g + 1) * BLK]
            high = jnp.right_shift(slot, 7)
            low = jnp.bitwise_and(slot, 127)
            lanes = jnp.broadcast_to(low, (snaps, BLK))
            block_of = jnp.broadcast_to(high, (snaps, BLK))
            picked = jnp.zeros((snaps, BLK), F32)
            for b in range(blocks):
                found = lane_gather(z_ref[:, b * BLK : (b + 1) * BLK], lanes)
                picked = jnp.where(block_of == b, found, picked)
            out_ref[d, g * snaps : (g + 1) * snaps, :] = picked
            found = lane_gather(v_ref[...], jnp.broadcast_to(low, (blocks, BLK)))
            mine = rows_iota((blocks, BLK)) == high
            variance = jnp.sum(jnp.where(mine, found, 0.0), axis=0, keepdims=True)
            tail = jnp.where(rows_iota((8, BLK)) == g, variance, tail)
        out_ref[d, groups * snaps :, :] = tail
        pltpu.make_async_copy(out_ref.at[d], out.at[d], out_sems.at[d]).start()
    for d in range(chunks):
        pltpu.make_async_copy(out_ref.at[d], out.at[d], out_sems.at[d]).wait()
    for copy in sends:
        copy.wait()


def inverse_kernel(own_ref, handed_refs, group_ref, lane_ref, kept_refs):
    for handed_ref, kept_ref in zip(handed_refs, kept_refs):
        kept_ref[...] = handed_ref[...]
    chunks, width = own_ref.shape
    blocks = group_ref.shape[0]
    groups = width // BLK
    total = jnp.zeros((2 * blocks, BLK), F32)
    lane = lax.broadcasted_iota(jnp.int32, (2 * blocks, width), 1)
    row = rows_iota((2 * blocks, width))
    in_group = jnp.bitwise_and(lane, 127)
    group_in = jnp.right_shift(lane, 7)
    for d in range(chunks):
        owned = own_ref[d : d + 1, :]
        high = jnp.right_shift(owned, 7)
        low = jnp.bitwise_and(owned, 127)
        label = jnp.where(row < blocks, group_in + d * groups, in_group)
        hit = jnp.bitwise_and(row, blocks - 1) == high
        left = jnp.where(hit, label.astype(F32), 0.0).astype(BF16)
        right = jnp.where(rows_iota((BLK, width)) == low, 1.0, 0.0).astype(BF16)
        total += lax.dot_general(left, right, NT, preferred_element_type=F32)
    group_ref[...] = total[:blocks].astype(jnp.int32)
    lane_ref[...] = total[blocks:].astype(jnp.int32)


def unpack_kernel(start, group_ref, lane_ref, message_ref, z_ref, v_ref, variance_ref):
    snaps, lines = z_ref.shape
    chunks = message_ref.shape[0]
    groups = (message_ref.shape[1] - 8) // snaps
    total = chunks * groups
    for d in range(chunks):
        variance_ref[d * groups : (d + 1) * groups, :] = message_ref[d, groups * snaps :, :][:groups]
    for b in range(lines // BLK):
        group = group_ref[start + b : start + b + 1, :]
        lane = lane_ref[start + b : start + b + 1, :]
        lanes = jnp.broadcast_to(lane, (snaps, BLK))
        group_of = jnp.broadcast_to(group, (snaps, BLK))
        picked = jnp.zeros((snaps, BLK), F32)
        for g in range(total):
            rows = slice(g % groups * snaps, (g % groups + 1) * snaps)
            found = lane_gather(message_ref[g // groups, rows, :], lanes)
            picked = jnp.where(group_of == g, found, picked)
        columns = slice(b * BLK, (b + 1) * BLK)
        z_ref[:, columns] = picked
        found = lane_gather(variance_ref[...], jnp.broadcast_to(lane, (total, BLK)))
        mine = rows_iota((total, BLK)) == group
        v_ref[:, columns] = jnp.sum(jnp.where(mine, found, 0.0), axis=0, keepdims=True)


def split(ref):
    return [ref.at[i] for i in range(ref.shape[0])]


def parity():
    return 1 - lax.rem(lax.axis_index("area"), 2)


def pick(blocks_ref, listing_ref, side, out_ref, start=0):
    held = blocks_ref.shape[0]
    for t in range(out_ref.shape[0]):
        b = listing_ref[side, t]
        at = b - start
        block = blocks_ref[jnp.clip(at, 0, held - 1)]
        here = (b >= 0) & (at >= 0) & (at < held)
        out_ref[t] = jnp.where(here, block, jnp.zeros_like(block))


def slots_into(slots_ref, aug_ref, first, second_ref):
    own = aug_ref.shape[0]
    ties = second_ref.shape[0]
    slots_ref[:own] = aug_ref[...]
    slots_ref[pl.ds(own + ties * (1 - parity()), ties)] = first
    slots_ref[pl.ds(own + ties * parity(), ties)] = second_ref[...]


def reordered(ref, distance, members):
    snaps = ref.shape[1] // members
    order = [(n - distance) % members for n in range(members)]
    return jnp.concatenate([ref[:, j * snaps : (j + 1) * snaps] for j in order], axis=1)


def join_states_kernel(mine_ref, others_refs, ties_ref, aug_ref, second_ref):
    members = len(others_refs) + 1
    held = mine_ref.shape[0]
    me = lax.axis_index("snap")
    aug_ref[pl.ds(me * held, held)] = mine_ref[...]
    for i, ref in enumerate(others_refs, 1):
        at = lax.rem(me + members - i, members) * held
        aug_ref[pl.ds(at, held)] = reordered(ref, i, members)
    pick(aug_ref, ties_ref, parity(), second_ref)


def predicted(j, slots_ref, tiles_ref, place_ref):
    touched = tiles_ref.shape[1]
    chosen = jnp.concatenate([slots_ref[place_ref[k, j]] for k in range(touched)], axis=1)
    weights = jnp.concatenate([tiles_ref[j, k] for k in range(touched)], axis=1)
    return lax.dot_general(chosen, weights, NT, preferred_element_type=F32)


def pick_kernel(own_refs, ties_ref, first_ref, second_ref):
    snaps = own_refs[0].shape[1]
    for i, own_ref in enumerate(own_refs):
        rows = slice(i * snaps, (i + 1) * snaps)
        pick(own_ref, ties_ref, 1 - parity(), first_ref.at[:, rows])
        pick(own_ref, ties_ref, parity(), second_ref.at[:, rows])


def predict_kernel(
    first_ref, second_ref, own_refs, tiles_ref, place_ref, out_ref, slots_ref
):
    own, snaps = own_refs[0].shape[:2]
    ties = first_ref.shape[0]
    for i, own_ref in enumerate(own_refs):
        slots_ref[:own, i * snaps : (i + 1) * snaps] = own_ref[...]
    slots_ref[pl.ds(own + ties * (1 - parity()), ties)] = first_ref[...]
    slots_ref[pl.ds(own + ties * parity(), ties)] = second_ref[...]
    predict(tiles_ref, place_ref, out_ref, slots_ref)


def predict(tiles_ref, place_ref, out_ref, slots_ref):
    for j in range(tiles_ref.shape[0]):
        out_ref[:, j * BLK : (j + 1) * BLK] = predicted(j, slots_ref, tiles_ref, place_ref)


def weigh(j, guess, z_refs, others_refs, v_refs):
    part = 0
    while j >= z_refs[part].shape[1] // BLK:
        j -= z_refs[part].shape[1] // BLK
        part += 1
    z_ref, others_ref, v_ref = z_refs[part], others_refs[part], v_refs[part]
    columns = slice(j * BLK, (j + 1) * BLK)
    readings = [z_ref[:, columns]] + [o[:, columns] for o in split(others_ref)]
    resid = jnp.concatenate(readings, axis=0) - guess
    spread = jnp.sum(resid * resid, axis=0, keepdims=True) / resid.shape[0]
    return (resid / (v_ref[:, columns] + spread)).astype(BF16)


def pull(weighted_ref, tiles_ref, place_ref, total_ref, own_ref, first_ref, second_ref):
    total_ref[...] = jnp.zeros_like(total_ref)
    touched = tiles_ref.shape[1]
    for j in range(tiles_ref.shape[0]):
        weighted = weighted_ref[:, j * BLK : (j + 1) * BLK]
        weights = jnp.concatenate([tiles_ref[j, k] for k in range(touched)], axis=1)
        part = jnp.dot(weighted, weights, preferred_element_type=F32)
        for k in range(touched):
            n = place_ref[k, j]
            total_ref[n] += part[:, k * BLK : (k + 1) * BLK]
    own = own_ref.shape[0]
    ties = first_ref.shape[0]
    own_ref[...] = total_ref[:own]
    first = total_ref[pl.ds(own + ties * (1 - parity()), ties)]
    second = total_ref[pl.ds(own + ties * parity(), ties)]
    first_ref[...] = first.astype(first_ref.dtype)
    second_ref[...] = second.astype(second_ref.dtype)


def pull_kernel(
    guess_ref, z_refs, others_refs, v_refs, tiles_ref, place_ref, own_ref, first_ref, second_ref,
    total_ref, weighted_ref,
):
    for j in range(tiles_ref.shape[0]):
        columns = slice(j * BLK, (j + 1) * BLK)
        weighted_ref[:, columns] = weigh(j, guess_ref[:, columns], z_refs, others_refs, v_refs)
    pull(weighted_ref, tiles_ref, place_ref, total_ref, own_ref, first_ref, second_ref)


def predict_pull_kernel(
    first_refs, aug_ref, second_in_ref, z_refs, others_refs, v_refs, tiles_ref, place_ref,
    own_ref, first_ref, second_ref, slots_ref, guess_ref, total_ref, weighted_ref,
):
    parts = [reordered(ref, i, len(first_refs)) for i, ref in enumerate(first_refs)]
    slots_into(slots_ref, aug_ref, sum(parts[1:], parts[0]), second_in_ref)
    predict(tiles_ref, place_ref, guess_ref, slots_ref)
    pull_kernel(
        guess_ref, z_refs, others_refs, v_refs, tiles_ref, place_ref, own_ref, first_ref, second_ref,
        total_ref, weighted_ref,
    )


def partial_update_kernel(grad_ref, ties_ref, gain_ref, part_ref):
    sides, ties = ties_ref.shape
    blocks = []
    for b in range(grad_ref.shape[0]):
        listed = ties_ref[0, 0] == b
        for side in range(sides):
            for t in range(ties):
                listed = listed | (ties_ref[side, t] == b)
        block = grad_ref[b]
        blocks.append(jnp.where(listed, jnp.zeros_like(block), block).astype(BF16))
    gradient = jnp.concatenate(blocks, axis=1)
    step = min(2 * BLK, gain_ref.shape[0])
    for at in range(0, gain_ref.shape[0], step):
        rows = gain_ref[at : at + step, :]
        part_ref[:, at : at + step] = lax.dot_general(
            gradient, rows, NT, preferred_element_type=F32
        )


def updates(part_ref, grad_ref, back_first_ref, back_second_ref, ties_ref, gain_ref, work_ref):
    ties = back_first_ref.shape[0]
    lists = [[ties_ref[side, t] for t in range(ties)] for side in (1 - parity(), parity())]
    for t, b in enumerate(lists[0]):
        block = grad_ref[jnp.maximum(b, 0)] + back_first_ref[t].astype(F32)
        work_ref[t] = jnp.where(b >= 0, block, jnp.zeros_like(block))
    for t, b in enumerate(lists[1]):
        at = ties + t
        for u, other in enumerate(lists[0]):
            at = jnp.where((b >= 0) & (other == b), u, at)
        block = grad_ref[jnp.maximum(b, 0)]
        alone = (b >= 0) & (at == ties + t)
        work_ref[ties + t] = jnp.where(alone, block, jnp.zeros_like(block))
        back = back_second_ref[t].astype(F32)
        work_ref[at] += jnp.where(b >= 0, back, jnp.zeros_like(back))
    listed = lists[0] + lists[1]
    gradient = jnp.concatenate([work_ref[n].astype(BF16) for n in range(len(listed))], axis=1)
    step = min(2 * BLK, gain_ref.shape[0])
    for at in range(0, gain_ref.shape[0], step):
        rows = [
            gain_ref[at : at + step, pl.ds(pl.multiple_of(jnp.maximum(b, 0) * BLK, BLK), BLK)]
            for b in listed
        ]
        update = part_ref[:, at : at + step] + lax.dot_general(
            gradient, jnp.concatenate(rows, axis=1), NT, preferred_element_type=F32
        )
        for i in range(step // BLK):
            yield at // BLK + i, update[:, i * BLK : (i + 1) * BLK]


def first_update_kernel(
    part_ref, grad_ref, back_first_ref, back_second_ref, ties_ref, gain_ref, x_ref, x_others_refs,
    kept_ref, given_refs, message_ref, first_ref, work_ref,
):
    held, snaps = kept_ref.shape[:2]
    me = lax.axis_index("snap")
    operands = part_ref, grad_ref, back_first_ref, back_second_ref, ties_ref, gain_ref, work_ref
    for i, update in updates(*operands):
        columns = pl.ds(pl.multiple_of((me * held + i) * BLK, BLK), BLK)
        parts = [x_ref[:, columns]] + [o[:, i * BLK : (i + 1) * BLK] for o in x_others_refs]
        state = jnp.concatenate(parts, axis=0) + update
        kept_ref[i] = state[:snaps]
        for j, given_ref in enumerate(given_refs, 1):
            given_ref[i] = state[j * snaps : (j + 1) * snaps]
        message_ref[i] = state.astype(BF16)
    pick(message_ref, ties_ref, 1 - parity(), first_ref, me * held)


def last_update_kernel(
    part_ref, grad_ref, back_first_ref, back_second_ref, ties_ref, gain_ref, kept_ref, mine_ref, sent_refs, work_ref
):
    snaps = mine_ref.shape[0]
    operands = part_ref, grad_ref, back_first_ref, back_second_ref, ties_ref, gain_ref, work_ref
    for i, update in updates(*operands):
        columns = slice(i * BLK, (i + 1) * BLK)
        mine_ref[:, columns] = kept_ref[i] + update[:snaps]
        for j, sent_ref in enumerate(sent_refs, 1):
            sent_ref[:, columns] = update[j * snaps : (j + 1) * snaps].astype(BF16)


def finish_kernel(mine_ref, states_refs, updates_refs, out_ref):
    width = mine_ref.shape[1]
    members = len(states_refs) + 1
    me = lax.axis_index("snap")
    out_ref[:, pl.ds(pl.multiple_of(me * width, BLK), width)] = mine_ref[...]
    for i, (state_ref, update_ref) in enumerate(zip(states_refs, updates_refs), 1):
        at = lax.rem(me + i, members) * width
        for b in range(width // BLK):
            update = update_ref[:, b * BLK : (b + 1) * BLK].astype(F32)
            columns = pl.ds(pl.multiple_of(at + b * BLK, BLK), BLK)
            out_ref[:, columns] = state_ref[b] + update


def swap_pair(block, start):
    pairs = [(i, i + 1) for i in range(start, lax.axis_size("area") - 1, 2)]
    return lax.ppermute(block, "area", pairs + [(b, a) for a, b in pairs])


def with_neighbours(first, second):
    return swap_pair(first, 1), swap_pair(second, 0)


def from_snap(block, distance):
    members = lax.axis_size("snap")
    return lax.ppermute(block, "snap", [(i, (i + distance) % members) for i in range(members)])


def from_all(block):
    return jnp.stack([from_snap(block, i) for i in range(1, lax.axis_size("snap"))])


def shape(dims, kind):
    return jax.ShapeDtypeStruct(dims, kind)


def on_device(
    phasor_readings,
    reading_error_spread,
    starting_voltages,
    derivative_pieces,
    derivative_tile_position,
    frontier_voltage_pieces,
    holder_line_order,
    hub_line_order,
    reciprocal_normal_operator,
):
    snaps, lines = phasor_readings.shape
    states = starting_voltages.shape[1]
    own = states // BLK
    measure = derivative_pieces.shape[0]
    ties_table = frontier_voltage_pieces[0]
    ties = ties_table.shape[1]
    slots = own + 2 * ties
    members = lax.axis_size("snap")
    areas = lax.axis_size("area")
    everything = snaps * members
    held = reciprocal_normal_operator.shape[0] // BLK
    place = derivative_tile_position[0].T
    cap = hub_line_order.shape[2]
    width = max(cap, BLK)
    chunks = areas * cap // width
    hub = hub_line_order[0].reshape(chunks, width)
    holder = holder_line_order[0].reshape(chunks, width)
    depth = (width // BLK) * snaps + 8

    message, rounded, x_sent = call(
        pack_kernel,
        (
            shape((chunks, depth, BLK), F32),
            shape((own, snaps, BLK), BF16),
            [shape((snaps, held * BLK), F32)] * (members - 1),
        ),
        [HBM] * 4,
        (
            phasor_readings,
            reading_error_spread.reshape(lines // BLK, BLK),
            hub,
            starting_voltages,
        ),
        scratch=[
            pltpu.VMEM((snaps, lines), F32),
            pltpu.VMEM((lines // BLK, BLK), F32),
            pltpu.VMEM((chunks, width), jnp.int32),
            pltpu.VMEM((snaps, states), F32),
            pltpu.VMEM((chunks, depth, BLK), F32),
            pltpu.VMEM((own, snaps, BLK), BF16),
            pltpu.SemaphoreType.DMA((4,)),
            pltpu.SemaphoreType.DMA((chunks,)),
            pltpu.SemaphoreType.DMA((members,)),
        ],
        out_spec=(HBM, HBM, [HBM] * (members - 1)),
        mib=60,
        name="pack_readings",
    )
    each = width // cap
    if each > 1:
        message = message.reshape(chunks, depth, each, cap).transpose(0, 2, 1, 3)
        message = message.reshape(areas, depth, cap)
    message = lax.all_to_all(message, "area", split_axis=0, concat_axis=0, tiled=True)
    if each > 1:
        message = message.reshape(chunks, each, depth, cap).transpose(0, 2, 1, 3)
        message = message.reshape(chunks, depth, BLK)

    rounded_others = [from_snap(rounded, i) for i in range(1, members)]
    handed = [rounded, ties_table, place]
    table = shape((lines // BLK, BLK), jnp.int32)
    group, lane, (rounded, ties_table, place) = call(
        inverse_kernel,
        (table, table, [shape(a.shape, a.dtype) for a in handed]),
        [VMEM, [VMEM] * 3],
        (holder, handed),
        flops=10**9,
        name="invert_order",
    )
    boundary = shape((ties, everything, BLK), BF16)
    owns = [rounded] + rounded_others
    first, second = call(
        pick_kernel,
        (boundary, boundary),
        [[VMEM] * members, SMEM],
        (owns, ties_table),
        name="pick_boundary",
    )
    first, second, x_sent = lax.optimization_barrier((first, second, x_sent))
    first, second = with_neighbours(first, second)
    x_others = [from_snap(block, i) for i, block in enumerate(x_sent, 1)]
    guess = call(
        predict_kernel,
        shape((everything, lines), F32),
        [VMEM, VMEM, [VMEM] * members, VMEM, SMEM],
        (first, second, owns, derivative_pieces, place),
        scratch=[pltpu.VMEM((slots, everything, BLK), BF16)],
        flops=10**9,
        name="predict",
    )
    message, guess = lax.optimization_barrier((message, guess))
    blocks = lines // BLK
    cuts = (0, blocks * 11 // 16, blocks)
    readings, variance, reading_others = [], [], []
    for part, (start, stop) in enumerate(zip(cuts, cuts[1:])):
        if part == 2:
            message, reading_others[0] = lax.optimization_barrier((message, reading_others[0]))
        some = call(
            functools.partial(unpack_kernel, start),
            (
                shape((snaps, (stop - start) * BLK), F32),
                shape((1, (stop - start) * BLK), F32),
            ),
            [VMEM, VMEM, VMEM],
            (group, lane, message),
            scratch=[pltpu.VMEM((chunks * (width // BLK), BLK), F32)],
            flops=2 * 10**9,
            name="unpack_readings",
        )
        if part == 1:
            some, x_others = lax.optimization_barrier((some, x_others))
        readings.append(some[0])
        variance.append(some[1])
        reading_others.append(from_all(some[0]))
    grads = (
        shape((own, everything, BLK), F32),
        boundary,
        boundary,
    )
    total = pltpu.VMEM((slots, everything, BLK), F32)
    work = pltpu.VMEM((2 * ties, everything, BLK), F32)

    def partial_update(grad):
        return call(
            partial_update_kernel,
            shape((everything, held * BLK), F32),
            [VMEM, SMEM, VMEM],
            (grad, ties_table, reciprocal_normal_operator),
            flops=10**9,
            name="partial_update",
        )

    grad, first, second = call(
        pull_kernel,
        grads,
        [VMEM, [VMEM] * 2, [VMEM] * 2, [VMEM] * 2, VMEM, SMEM],
        (guess, readings, reading_others, variance, derivative_pieces, place),
        scratch=[total, pltpu.VMEM((everything, lines), BF16)],
        name="pull",
    )
    arrived = with_neighbours(first, second)
    kept, given, mine, first = call(
        first_update_kernel,
        (
            shape((held, snaps, BLK), F32),
            [shape((held, snaps, BLK), F32)] * (members - 1),
            shape((held, everything, BLK), BF16),
            boundary,
        ),
        [VMEM, VMEM, VMEM, VMEM, SMEM, VMEM, VMEM, [VMEM] * (members - 1)],
        (
            partial_update(grad), grad, *arrived, ties_table, reciprocal_normal_operator,
            starting_voltages, x_others,
        ),
        scratch=[work],
        name="first_update",
    )
    others = [from_snap(mine, i) for i in range(1, members)]
    first = swap_pair(first, 1)
    firsts = [first] + [from_snap(first, i) for i in range(1, members)]
    aug, second = call(
        join_states_kernel,
        (shape((own, everything, BLK), BF16), boundary),
        [VMEM, [VMEM] * (members - 1), SMEM],
        (mine, others, ties_table),
        name="join_states",
    )
    second = swap_pair(second, 0)
    grad, first, second = call(
        predict_pull_kernel,
        grads,
        [[VMEM] * members, VMEM, VMEM, [VMEM] * 2, [VMEM] * 2, [VMEM] * 2, VMEM, SMEM],
        (firsts, aug, second, readings, reading_others, variance, derivative_pieces, place),
        scratch=[
            pltpu.VMEM((slots, everything, BLK), BF16),
            pltpu.VMEM((everything, lines), F32),
            total,
            pltpu.VMEM((everything, lines), BF16),
        ],
        name="predict_pull",
    )
    given, first, second = lax.optimization_barrier((given, first, second))
    first, second = with_neighbours(first, second)
    states_in = [from_snap(block, -i) for i, block in enumerate(given, 1)]
    mine, sent = call(
        last_update_kernel,
        (
            shape((snaps, held * BLK), F32),
            [shape((snaps, held * BLK), BF16)] * (members - 1),
        ),
        [VMEM, VMEM, VMEM, VMEM, SMEM, VMEM, VMEM],
        (partial_update(grad), grad, first, second, ties_table, reciprocal_normal_operator, kept),
        scratch=[work],
        name="last_update",
    )
    return call(
        finish_kernel,
        shape((snaps, states), F32),
        [VMEM, [VMEM] * (members - 1), [VMEM] * (members - 1)],
        (mine, states_in, [from_snap(block, -i) for i, block in enumerate(sent, 1)]),
        name="finish",
    )


def solution(mesh):
    placed = (
        P("snap", "area"),
        P("area"),
        P("snap", "area"),
        P("area", None, None, None),
        P("area", None, None),
        P("area", None, None),
        P("area", None, None),
        P("area", None, None),
        P(("area", "snap"), None),
    )
    return jax.shard_map(
        on_device, mesh=mesh, in_specs=placed, out_specs=P("snap", "area"), check_vma=False
    )
```
